32 devices in a mesh: dp: 4 (over z), ctx: 4 (over y, x), tp: 2 (over core).
Axes of the slice: x: 2, y: 2, z: 4, core: 2. Of those that a mesh axis runs over, the one named last changes fastest.
Arguments:
- tokens: bfloat16 [16384, 768], P(('dp', 'ctx')), may hold values from -6 to 6
- cotangent: bfloat16 [16384, 768], P(('dp', 'ctx')), may hold values from -6 to 6
- device_fill: int32 [4, 4], P('dp'), may hold values from 1 to 4, 12 in all within a row
- seq_lengths: int32 [4, 3], P('dp'), may hold values from 1 to 3070, as said below
- norm_gain: bfloat16 [768], P('dp'), may hold values from 0.5 to 1.5
- w_z: bfloat16 [768, 1536], P('dp', 'tp'), may hold values from -0.21875 to 0.21875
- w_x: bfloat16 [768, 1536], P('dp', 'tp'), may hold values from -0.21875 to 0.21875
- w_bc: bfloat16 [768, 256], P('dp'), may hold values from -0.21875 to 0.21875
- w_dt: bfloat16 [768, 24], P('dp', 'tp'), may hold values from -0.21875 to 0.21875
- conv_x: bfloat16 [4, 24, 64], P(None, 'tp', 'dp'), may hold values from -3 to 3
- conv_x_bias: bfloat16 [24, 64], P('tp', 'dp'), may hold values from -3 to 3
- conv_bc: bfloat16 [4, 256], P(None, 'dp'), may hold values from -3 to 3
- bias_bc: bfloat16 [256], P('dp'), may hold values from -3 to 3
- dt_bias: float32 [24], P('tp'), may hold values from -7.6 to -3
- a_log: float32 [24], P('tp'), may hold values from -3.9 to 1.4
- skip_d: float32 [24], P('tp'), may hold values from 0.5 to 1.5
- gate_gain: bfloat16 [24, 64], P('tp', 'dp'), may hold values from 0.5 to 1.5
- w_out: bfloat16 [1536, 768], P('tp', 'dp'), may hold values from -0.15625 to 0.15625
Outputs:
- layer_out: float32 [16384, 768], P(('dp', 'ctx'), 'tp')
- grad_tokens: float32 [16384, 768], P(('dp', 'ctx'))
- grad_norm_gain: float32 [768], P('dp')
- grad_w_z: float32 [768, 1536], P('dp', 'tp')
- grad_w_x: float32 [768, 1536], P('dp', 'tp')
- grad_w_bc: float32 [768, 256], P('dp')
- grad_w_dt: float32 [768, 24], P('dp', 'tp')
- grad_conv_x: float32 [4, 24, 64], P(None, 'tp', 'dp')
- grad_conv_x_bias: float32 [24, 64], P('tp', 'dp')
- grad_conv_bc: float32 [4, 256], P(None, 'dp')
- grad_bias_bc: float32 [256], P('dp')
- grad_dt_bias: float32 [24], P('tp')
- grad_a_log: float32 [24], P('tp')
- grad_skip_d: float32 [24], P('tp')
- grad_gate_gain: float32 [24, 64], P('tp', 'dp')
- grad_w_out: float32 [1536, 768], P('tp', 'dp')
The draws below stay inside these ranges and needn't reach their ends.
Inputs may be any that keep to these rules, and one draw needn't show every extreme that they name: `device_fill`: A row sums to 12; used slots are a device's first ones. `seq_lengths`: A row's lengths sum to 3072; the first and the last are under 256.
All inputs are finite; a program needn't handle non-finite values.
Results may differ from the reference program's by a relative error of at most 0.029.
Values may be sent and summed in bfloat16 or wider, within the bound.
No kernel may reach another device: no remote copies, remote signals or barrier semaphores. Data moves between devices by JAX's collectives and lax.ppermute only.
A program may use at most 128 MiB of HBM per device.

```python
import math
from functools import partial
import jax
import jax.numpy as jnp
import numpy as np
from jax import lax

D = 768
HEADS = 24
HEADDIM = 64
STATE = 128
CONV = 4
BLOCK = 256
TOK_DEV = 1024
INNER = 1536
CAP_BLOCKS = 4
FILL_BLOCKS = 12
GROUP_TOKENS = 3072
TOKENS = 16384
N_DP = 4
N_CTX = 4


def draw_seq_lengths(key, part):
    key = jax.random.fold_in(key, 11)
    outer = jax.random.randint(key, (N_DP, 2), 1, BLOCK)
    chosen = jax.random.randint(jax.random.fold_in(key, 5), (), 0, N_DP)
    outer = jnp.where(jnp.arange(N_DP)[:, None] == chosen, 1, outer)
    middle = GROUP_TOKENS - outer[:, 0] - outer[:, 1]
    return jnp.stack([outer[:, 0], middle, outer[:, 1]], axis=1).astype(jnp.int32)


def level_of(own_key, shape, split, low, high):
    factor_of = 1.0
    for position, blocks in split:
        heights = jax.random.uniform(jax.random.fold_in(jax.random.fold_in(own_key, 6), position), (blocks,), jnp.float32, low / len(split), high / len(split))
        factor_of = factor_of * jnp.repeat(jnp.exp(heights), shape[position] // blocks).reshape((-1,) + (1,) * (len(shape) - 1 - position))
    return factor_of


def split_up(count, total, limit, skew):
    loads = [(1 << 20) // math.isqrt(standing ** skew) + 1 for standing in range(2, count + 1)]
    spare, holding = total - limit - (count - 1), [1] * (count - 1)
    while spare > 0:
        candidates = [i for i in range(count - 1) if holding[i] < limit]
        pool, left = sum([loads[i] for i in candidates]), spare
        for i in candidates:
            addition = min(limit - holding[i], max(1, left * loads[i] // pool), spare)
            holding[i] = holding[i] + addition
            spare = spare - addition
    return np.array([limit] + holding)


def uneven_parts(own_key, amount, total, most, slope):
    if amount == 2:
        one = jax.random.randint(own_key, (), max(1, total - most), min(most, total - 1) + 1)
        return jnp.stack([one, total - one])
    sizes = jnp.asarray(split_up(amount, total, most, slope), jnp.int32)
    twos = (amount - 1) // 2
    source_of, receiver = sizes[1:1 + 2 * twos:2], sizes[2:2 + 2 * twos:2]
    margin = jnp.minimum(source_of - 1, most - receiver)
    moved = jax.random.randint(jax.random.fold_in(own_key, 1), (twos,), 0, 1 << 20) % (margin + 1)
    sizes = sizes.at[1:1 + 2 * twos:2].set(source_of - moved).at[2:2 + 2 * twos:2].set(receiver + moved)
    return sizes[jax.random.permutation(jax.random.fold_in(own_key, 2), amount)]


def bell_draw(stream_key, shape, width, most, split=(), held_as=jnp.bfloat16):
    gain = level_of(stream_key, shape, split, -0.22, 0.18) if split else 1.0
    values = jax.random.normal(stream_key, shape, jnp.float32) * width * gain
    return jnp.minimum(jnp.maximum(values, -most), most).astype(held_as)


def setup_inputs(seed: int = 0) -> dict:
    streams_of = jax.random.split(jax.random.key(seed), 19)
    return {
        "tokens": bell_draw(streams_of[0], (TOKENS, D), 1.0, 6.0, ((0, 16),)),
        "cotangent": bell_draw(streams_of[1], (TOKENS, D), 1.0, 6.0, ((0, 16),)),
        "device_fill": jax.vmap(lambda own: uneven_parts(own, N_CTX, FILL_BLOCKS, CAP_BLOCKS, 2))(jax.random.split(streams_of[2], N_DP)).reshape((N_DP, N_CTX)).astype(jnp.int32),
        "seq_lengths": draw_seq_lengths(jax.random.fold_in(streams_of[18], 71), 0),
        "norm_gain": jnp.clip(1.0 + 0.1 * jax.random.normal(streams_of[4], (D,), jnp.float32), 0.5, 1.5).astype(jnp.bfloat16),
        "w_z": bell_draw(streams_of[5], (D, INNER), D ** -0.5, 0.21875, ((0, 4), (1, 2))),
        "w_x": bell_draw(streams_of[6], (D, INNER), D ** -0.5, 0.21875, ((0, 4), (1, 2))),
        "w_bc": bell_draw(streams_of[7], (D, 2 * STATE), D ** -0.5, 0.21875, ((0, 4),)),
        "w_dt": bell_draw(streams_of[8], (D, HEADS), D ** -0.5, 0.21875, ((0, 4), (1, 2))),
        "conv_x": bell_draw(streams_of[9], (CONV, HEADS, HEADDIM), CONV ** -0.5, 3.0, ((1, 2), (2, 4))),
        "conv_x_bias": bell_draw(streams_of[10], (HEADS, HEADDIM), 0.5, 3.0, ((0, 2), (1, 4))),
        "conv_bc": bell_draw(streams_of[11], (CONV, 2 * STATE), CONV ** -0.5, 3.0, ((1, 4),)),
        "bias_bc": bell_draw(streams_of[12], (2 * STATE,), 0.5, 3.0, ((0, 4),)),
        "dt_bias": jnp.clip(-7.6 + 4.6 * jax.random.uniform(streams_of[13], (HEADS,), jnp.float32) ** level_of(streams_of[13], (HEADS,), ((0, 2),), -0.2, 0.2), -7.6, -3.0),
        "a_log": jnp.clip(-3.9 + 5.3 * jax.random.uniform(streams_of[14], (HEADS,), jnp.float32) ** level_of(streams_of[14], (HEADS,), ((0, 2),), -0.2, 0.2), -3.9, 1.4),
        "skip_d": jnp.clip(0.5 + 1.0 * jax.random.uniform(streams_of[15], (HEADS,), jnp.float32) ** level_of(streams_of[15], (HEADS,), ((0, 2),), -0.2, 0.2), 0.5, 1.5),
        "gate_gain": jnp.clip(1.0 + 0.1 * jax.random.normal(streams_of[16], (HEADS, HEADDIM), jnp.float32), 0.5, 1.5).astype(jnp.bfloat16),
        "w_out": bell_draw(streams_of[17], (INNER, D), INNER ** -0.5, 0.15625, ((0, 2), (1, 4))),
    }


epsilon = 1e-05
highest = lax.Precision.HIGHEST

@jax.custom_vjp
def low(v):
    return lax.optimization_barrier(v.astype(jnp.bfloat16)).astype(jnp.float32)

@jax.custom_vjp
def low_back(v):
    return v

def low_keep(v):
    return (low(v), None)

def low_pass(kept, grad):
    return (grad,)

def back_keep(v):
    return (v, None)

def back_low(kept, grad):
    return (low(grad),)
low.defvjp(low_keep, low_pass)
low_back.defvjp(back_keep, back_low)

def segment_of(positions, seq_ends):
    found = lax.optimization_barrier(jnp.sum((positions[:, None] >= seq_ends[None, :]).astype(jnp.int32), axis=1))
    return jnp.where(positions < 0, -1, found).astype(jnp.int32)

def block_step(skip_d, state, items):
    x_conv, b_conv, c_conv, log_decay, step_size, segment, seg_before = items
    cum_decay = jnp.cumsum(log_decay, axis=0)
    gram = low_back(jnp.dot(c_conv, b_conv.T, precision=highest))
    index = jnp.arange(BLOCK)
    keep = ((segment[:, None] == segment[None, :]) & (index[:, None] >= index[None, :])).astype(jnp.float32)
    cum_heads = cum_decay.T
    diff = cum_heads[:, :, None] - cum_heads[:, None, :]
    kernel = jnp.exp(jnp.where(keep[None] > 0, diff, 0.0)) * keep[None]
    mixing = low(gram[None] * kernel * step_size.T[:, None, :])
    y_inner = jnp.einsum('htj,jhp->thp', mixing, x_conv, precision=highest)
    enter = jnp.exp(cum_decay) * (segment == seg_before).astype(jnp.float32)[:, None]
    state_low = low(state)
    state_read = low_back(jnp.einsum('tn,hpn->thp', c_conv, state_low, precision=highest))
    mixed = low_back(y_inner + enter[:, :, None] * state_read + skip_d[None, :, None] * x_conv)
    end_weight = jnp.exp(cum_decay[-1][None, :] - cum_decay) * (segment == segment[-1]).astype(jnp.float32)[:, None] * step_size
    weighted_b = low(end_weight.T[:, :, None] * b_conv[None])
    block_state = low_back(jnp.einsum('jhp,hjn->hpn', x_conv, weighted_b, precision=highest))
    decay = jnp.exp(cum_decay[-1]) * (segment[-1] == seg_before).astype(jnp.float32)
    return (decay[:, None, None] * state + block_state, mixed)

def group_forward(weights, slot_rows, fill_blocks, lengths):
    norm_gain, w_z, w_x, w_bc, w_dt, conv_x, conv_x_bias, conv_bc, bias_bc, dt_bias, a_log, skip_d, gate_gain, w_out = weights
    fill_rows = fill_blocks * BLOCK
    device_ends = jnp.cumsum(fill_rows)
    device_starts = device_ends - fill_rows
    positions = jnp.arange(GROUP_TOKENS)
    owner = lax.optimization_barrier(jnp.sum((positions[:, None] >= device_ends[None, :]).astype(jnp.int32), axis=1))
    matches = owner[:, None] == jnp.arange(N_CTX)[None, :]
    base_slot = lax.optimization_barrier(jnp.sum(jnp.where(matches, device_starts[None, :], 0), axis=1))
    slots = (owner * TOK_DEV + positions - base_slot).astype(jnp.int32)
    inputs = slot_rows[slots]
    seq_ends = jnp.cumsum(lengths)[:-1]
    segment = segment_of(positions, seq_ends)
    inv_rms = lax.rsqrt(lax.optimization_barrier(jnp.mean(inputs * inputs, axis=1, keepdims=True)) + epsilon)
    normed = low(inputs * inv_rms * norm_gain[None, :])
    z_raw = low_back(low(jnp.dot(normed, w_z, precision=highest)))
    x_raw = low_back(low(jnp.dot(normed, w_x, precision=highest)))
    bc_raw = low_back(low(jnp.dot(normed, w_bc, precision=highest)))
    dt_raw = low_back(low(jnp.dot(normed, w_dt, precision=highest)))
    conv_in = jnp.concatenate([x_raw, bc_raw], axis=1)
    padded = jnp.concatenate([jnp.zeros((CONV - 1, conv_in.shape[1]), jnp.float32), conv_in], axis=0)
    padded_segment = segment_of(jnp.arange(GROUP_TOKENS + CONV - 1) - (CONV - 1), seq_ends)
    taps = jnp.concatenate([conv_x.reshape(CONV, INNER), conv_bc], axis=1)
    shift_bias = jnp.concatenate([conv_x_bias.reshape(INNER), bias_bc])
    pre_act = shift_bias[None, :]
    for offset in range(CONV):
        same = (padded_segment[offset:offset + GROUP_TOKENS] == segment).astype(jnp.float32)[:, None]
        pre_act = pre_act + taps[offset][None, :] * padded[offset:offset + GROUP_TOKENS] * same
    activated = jax.nn.silu(pre_act)
    x_conv = low(activated[:, :INNER])
    b_conv = low(activated[:, INNER:INNER + STATE])
    c_conv = low(activated[:, INNER + STATE:])
    step_size = jax.nn.softplus(dt_raw + dt_bias[None, :])
    log_decay = -jnp.exp(a_log)[None, :] * step_size
    nblocks = GROUP_TOKENS // BLOCK
    seg_before = segment_of(jnp.arange(nblocks) * BLOCK - 1, seq_ends)
    items = (x_conv.reshape(nblocks, BLOCK, HEADS, HEADDIM), b_conv.reshape(nblocks, BLOCK, STATE), c_conv.reshape(nblocks, BLOCK, STATE), log_decay.reshape(nblocks, BLOCK, HEADS), step_size.reshape(nblocks, BLOCK, HEADS), segment.reshape(nblocks, BLOCK), seg_before)
    scan_step = jax.checkpoint(partial(block_step, skip_d))
    final_state, mixed = lax.scan(scan_step, jnp.zeros((HEADS, HEADDIM, STATE), jnp.float32), items)
    mixed_rows = mixed.reshape(GROUP_TOKENS, INNER)
    gated = mixed_rows * jax.nn.silu(z_raw)
    gate_inv = lax.rsqrt(lax.optimization_barrier(jnp.mean(gated * gated, axis=1, keepdims=True)) + epsilon)
    normal_out = low(gated * gate_inv * gate_gain.reshape(INNER)[None, :])
    branch = low_back(jnp.dot(normal_out, w_out, precision=highest))
    return slot_rows.at[slots].set(inputs + branch)

def reference(tokens, cotangent, device_fill, seq_lengths, norm_gain, w_z, w_x, w_bc, w_dt, conv_x, conv_x_bias, conv_bc, bias_bc, dt_bias, a_log, skip_d, gate_gain, w_out):
    weights = tuple((item.astype(jnp.float32) for item in (norm_gain, w_z, w_x, w_bc, w_dt, conv_x, conv_x_bias, conv_bc, bias_bc, dt_bias, a_log, skip_d, gate_gain, w_out)))

    def whole(weights, inputs):
        groups = inputs.reshape(N_DP, N_CTX * TOK_DEV, D)
        outputs = lax.map(lambda item: group_forward(weights, item[0], item[1], item[2]), (groups, device_fill, seq_lengths))
        return outputs.reshape(TOKENS, D)
    layer_out, pullback = jax.vjp(whole, weights, tokens.astype(jnp.float32))
    grads, grad_tokens = pullback(cotangent.astype(jnp.float32))
    return (layer_out, grad_tokens, grads[0], grads[1], grads[2], grads[3], grads[4], grads[5], grads[6], grads[7], grads[8], grads[9], grads[10], grads[11], grads[12], grads[13])
```

```python
import functools

import jax
import jax.numpy as jnp
from jax import lax
from jax.experimental import pallas as pl
from jax.experimental.pallas import tpu as pltpu
from jax.sharding import PartitionSpec as P

CONV = 4
BLOCK = 256
HEAD = 64
LANES = 128
EPS = 1e-05
VMEM = 56 * 1024 * 1024
F32 = jnp.float32
BF16 = jnp.bfloat16


def dot(left, right):
    return jnp.dot(left, right, preferred_element_type=F32)


def dot_tn(left, right):
    return lax.dot_general(left, right, (((0,), (0,)), ((), ())), preferred_element_type=F32)


def dot_nt(left, right):
    return lax.dot_general(left, right, (((1,), (1,)), ((), ())), preferred_element_type=F32)


def dot_exact(left, right):
    return jnp.dot(left, right, preferred_element_type=F32, precision=lax.Precision.HIGHEST)


def iota(shape, dim):
    return lax.broadcasted_iota(jnp.int32, shape, dim)


def sigmoid(value):
    return 1.0 / (1.0 + jnp.exp(-value))


def softplus(value):
    return jnp.maximum(value, 0.0) + jnp.log1p(jnp.exp(-jnp.abs(value)))


def split(value):
    high = value.astype(BF16)
    return high, (value - high.astype(F32)).astype(BF16)


def expand(value, spread):
    return dot(jnp.concatenate(split(value), axis=1), spread[...])


def reduce_heads(value, spread):
    high, low = split(value)
    pick = spread[:LANES, :]
    return dot_nt(high, pick) + dot_nt(low, pick)


def head_column(row, channels):
    shape = (channels, LANES)
    return jnp.sum(jnp.where(iota(shape, 0) // HEAD == iota(shape, 1), row, 0.0), axis=1, keepdims=True)


def xor(value, mask):
    return jnp.bitwise_xor(value, jnp.int32(mask))


class Place:
    def __init__(self, info, counts):
        devices, sequences = counts
        own = info[devices + sequences]
        self.ctx = own
        self.tp = info[devices + sequences + 1]
        self.dp = info[devices + sequences + 2]
        self.fill = jnp.int32(0)
        self.first = jnp.int32(0)
        for device in range(devices):
            rows = info[device] * BLOCK
            self.fill = self.fill + jnp.where(own == device, rows, 0)
            self.first = self.first + jnp.where(own > device, rows, 0)
        self.ends = []
        total = jnp.int32(0)
        for sequence in range(sequences - 1):
            total = total + info[devices + sequence]
            self.ends.append(total)

    def of(self, position):
        found = (position >= self.ends[0]).astype(jnp.int32)
        for end in self.ends[1:]:
            found = found + (position >= end).astype(jnp.int32)
        return jnp.where(position < 0, -1, found)

    def rows(self, index):
        return self.of(self.first + jnp.minimum(index, self.fill - 1))

    def before(self, block):
        position = self.first + jnp.minimum(block * BLOCK, self.fill) - 1
        found = jnp.int32(0)
        for end in self.ends:
            found = found + jnp.where(position >= end, 1, 0)
        return jnp.where(position < 0, -1, found)

    def last(self, block):
        position = self.first + jnp.minimum(block * BLOCK + BLOCK - 1, self.fill - 1)
        found = jnp.int32(0)
        for end in self.ends:
            found = found + jnp.where(position >= end, 1, 0)
        return found

    def column(self, block, shift=0):
        return self.rows(block * BLOCK + shift + iota((BLOCK, 1), 0))

    def valid(self, block):
        return (block * BLOCK + iota((BLOCK, 1), 0) < self.fill).astype(F32)

    def keep(self, block):
        down = self.rows(block * BLOCK + iota((BLOCK, BLOCK), 0))
        across = self.rows(block * BLOCK + iota((BLOCK, BLOCK), 1))
        return (down == across) & (iota((BLOCK, BLOCK), 0) >= iota((BLOCK, BLOCK), 1))


def step_sizes(place, block, pre_step, heads):
    lane = iota((BLOCK, LANES), 1)
    return jnp.where(lane < heads, softplus(pre_step), 0.0) * place.valid(block)


def end_weights(place, block, cum):
    same = (place.column(block) == place.last(block)).astype(F32)
    return jnp.exp(cum[BLOCK - 1 :, :] - cum) * same


def enter_weights(place, block, cum):
    return jnp.exp(cum) * (place.column(block) == place.before(block)).astype(F32)


def block_decay(place, block, cum):
    return jnp.exp(cum[BLOCK - 1 :, :]) * jnp.where(place.last(block) == place.before(block), 1.0, 0.0)


def decay_kernel(keep, cum, cum_rows, head):
    return jnp.exp(jnp.where(keep, cum[:, head : head + 1] - cum_rows[head : head + 1, :], -1e30))


def both_halves(pair):
    lane = iota(pair.shape, 1)
    zero = jnp.zeros_like(pair)
    return [jnp.where(lane < HEAD, pair, zero), jnp.where(lane >= HEAD, pair, zero)]


def same_mask(place, block, tap):
    return (place.column(block, tap - (CONV - 1)) == place.column(block)).astype(F32)


def conv_pre(place, block, ext, par, channels):
    total = par[4:5, :channels]
    for tap in range(CONV):
        first = 8 - (CONV - 1) + tap
        total = total + par[tap : tap + 1, :channels] * ext[first : first + BLOCK, :] * same_mask(
            place, block, tap
        )
    return total


def state_packet(state, decay):
    high, low = split(decay)
    row = iota((16, LANES), 0)
    tail = jnp.where(row == 0, high.astype(F32), jnp.where(row == 1, low.astype(F32), 0.0))
    return jnp.concatenate([state.astype(BF16), tail.astype(BF16)], axis=0)


def merge_packets(packets, inner):
    total = jnp.zeros((inner, LANES), F32)
    for packet in reversed(packets):
        tail = packet[inner : inner + 16, :].astype(F32)
        decay = tail[0:1, :] + tail[1:2, :]
        total = packet[:inner, :].astype(F32) + head_column(decay, inner) * total
    return total


def normalise(rows, gain):
    inv = lax.rsqrt(jnp.mean(rows * rows, axis=1, keepdims=True) + EPS)
    return rows * inv, inv, (rows * inv * gain).astype(BF16)


def piece_rows(place, dp_count, parts, rows):
    for part in range(parts):
        for block in range(dp_count):
            owner = xor(place.dp, block) * parts + (xor(place.ctx, part) if parts > 1 else 0)
            yield part, block, pl.multiple_of(owner * rows, rows)


def join_pieces(place, dp_count, parts, whole):
    if len(parts) == 1:
        whole[...] = parts[0][...]
        return
    rows = parts[0].shape[0] // dp_count
    for part, block, first in piece_rows(place, dp_count, len(parts), rows):
        whole[pl.ds(first, rows), :] = parts[part][block * rows : (block + 1) * rows, :]


def cut_pieces(place, dp_count, whole, parts, lanes):
    if len(parts) == 1:
        parts[0][:, lanes] = whole[...].astype(BF16)
        return
    rows = parts[0].shape[0] // dp_count
    for part, block, first in piece_rows(place, dp_count, len(parts), rows):
        parts[part][block * rows : (block + 1) * rows, lanes] = whole[pl.ds(first, rows), :].astype(BF16)


def join_parameters(place, vectors, skip, heads, par):
    shard = vectors[0].shape[1]
    each = HEAD // len(vectors)
    inner = heads * HEAD
    by_channel = jnp.zeros((16, inner), F32)
    in_order = jnp.zeros((16, shard * len(vectors)), F32)
    by_state = jnp.zeros((16, 2 * LANES), F32)
    states = 2 * LANES // len(vectors)
    for block, vector in enumerate(vectors):
        owner = xor(place.dp, block)
        source, target = iota((shard, inner), 0), iota((shard, inner), 1)
        pick = target == source // each * HEAD + owner * each + source % each
        by_channel = by_channel + dot(vector[...], pick.astype(BF16))
        source, target = iota((shard, in_order.shape[1]), 0), iota((shard, in_order.shape[1]), 1)
        in_order = in_order + dot(vector[...], (target == owner * shard + source).astype(BF16))
        source, target = iota((shard, 2 * LANES), 0), iota((shard, 2 * LANES), 1)
        pick = (target == owner * states + source) & (source < states)
        by_state = by_state + dot(vector[...], pick.astype(BF16))
    par[...] = jnp.zeros_like(par)
    par[0:5, :inner] = by_channel[0:5, :]
    par[0:5, inner:] = by_state[8:13, :]
    par[5:6, : in_order.shape[1]] = in_order[5:6, :]
    par[6:7, :inner] = by_channel[6:7, :]
    par[7:8, :inner] = skip


TAPS, NORM, GATE, STATE_TAPS, BY_HEAD = 12, 17, 18, 20, 25


def pack_parameters(dp_count, heads, small, gate, skip):
    inner = heads * HEAD
    each = HEAD // dp_count
    shard = inner // dp_count
    states = 2 * LANES // dp_count

    def lanes(pieces, columns):
        rows, at = [], 0
        for first, value in pieces:
            if first > at:
                rows.append(jnp.zeros((first - at, columns), F32))
            rows.append(value)
            at = first + value.shape[0]
        rows.append(jnp.zeros((LANES - at, columns), F32))
        return jnp.concatenate(rows, axis=0)

    source, target = iota((inner, inner), 0), iota((inner, inner), 1)
    inside = source % shard
    pick = target == inside // each * HEAD + source // shard * each + inside % each
    by_channel = lanes([(TAPS, small[0:5, :inner]), (GATE, gate)], inner)
    total = dot_nt(pick.astype(BF16), by_channel.astype(BF16))
    total = total + lanes([(NORM, small[5:6, :inner])], inner).T
    source, target = iota((inner, 2 * LANES), 0), iota((inner, 2 * LANES), 1)
    inside = source % shard
    pick = (target == source // shard * states + inside) & (inside < states)
    by_state = lanes([(STATE_TAPS, small[0:5, inner : inner + 2 * LANES])], 2 * LANES)
    total = total + dot_nt(pick.astype(BF16), by_state.astype(BF16))
    source, target = iota((inner, LANES), 0) % shard, iota((inner, LANES), 1)
    for index, row in enumerate((small[6:7, :LANES], small[7:8, :LANES], skip)):
        pick = (source == target + index * heads) & (target < heads)
        total = total + dot_nt(pick.astype(BF16), lanes([(BY_HEAD, row)], LANES).astype(BF16))
    return total


def forward_kernel(
    counts, heads, dp_count, part_count, info, *refs
):
    vectors = refs[:dp_count]
    parts = refs[dp_count : dp_count + part_count]
    (
        tok, halo, dtp, spread,
        w1, par, normed_o, halo_normed_o, halo_v_o, v_o, xc_o, bc_o, ypart_o, pre_o, cum_o, entry_o, decay_o,
        packet_o, ext, run, factor,
    ) = refs[dp_count + part_count :]
    forward_block(
        counts, heads, info, vectors, parts, tok, halo, w1, par, dtp, spread,
        normed_o, halo_normed_o, halo_v_o, v_o, xc_o, bc_o, ypart_o, pre_o, cum_o, entry_o, decay_o, packet_o,
        ext, run, factor,
    )


def forward_block(
    counts, heads, info, vectors, parts, tok, halo, w1, par, dtp, spread,
    normed_o, halo_normed_o, halo_v_o, v_o, xc_o, bc_o, ypart_o, pre_o, cum_o, entry_o, decay_o, packet_o,
    ext, run, factor,
):
    block = pl.program_id(0)
    place = Place(info, counts)
    inner = heads * HEAD
    state = LANES
    channels = inner + 2 * state
    width = tok.shape[1]

    @pl.when(block == 0)
    def _():
        join_pieces(place, len(vectors), parts, w1)
        join_parameters(place, vectors, expand(dtp[...], spread)[2:3, :], heads, par)

    gain = par[5:6, :width]
    _, _, normed = normalise(tok[...].astype(F32), gain)
    normed_o[...] = normed

    @pl.when(block == 0)
    def _():
        _, _, before = normalise(halo[...].astype(F32), gain)
        halo_normed_o[...] = before
        raw = dot(before, w1[:, :channels]).astype(BF16).astype(F32)
        ext[0:8, :] = raw[8:16, :]
        halo_v_o[...] = raw[8:16, :]
        run[...] = jnp.zeros_like(run)
        factor[...] = jnp.ones_like(factor)

    @pl.when(block > 0)
    def _():
        ext[0:8, :] = ext[BLOCK : BLOCK + 8, :]

    raw = dot(normed, w1[...])
    v = raw[:, :channels].astype(BF16)
    v_o[...] = v
    ext[8 : 8 + BLOCK, :] = v.astype(F32)
    pre = conv_pre(place, block, ext, par, channels)
    act = (pre * sigmoid(pre)).astype(BF16)
    xc = act[:, :inner]
    bq = act[:, inner : inner + state]
    cq = act[:, inner + state :]
    xc_o[...] = xc
    bc_o[...] = act[:, inner:]
    pre_step = raw[:, channels:].astype(BF16).astype(F32) + dtp[0:1, :]
    pre_o[...] = pre_step
    step = step_sizes(place, block, pre_step, heads)
    tri = (iota((BLOCK, BLOCK), 0) >= iota((BLOCK, BLOCK), 1)).astype(F32)
    cum = dot_exact(tri, -dtp[1:2, :] * step)
    cum_o[...] = cum
    cum_rows = cum.T
    step_rows = step.T
    gram = dot_nt(cq, bq)
    keep = place.keep(block)
    for pair in range(heads // 2):
        lanes = slice(pair * LANES, (pair + 1) * LANES)
        mixing = []
        for head in (2 * pair, 2 * pair + 1):
            weight = decay_kernel(keep, cum, cum_rows, head) * step_rows[head : head + 1, :]
            mixing.append((gram * weight).astype(BF16))
        x_pair = xc[:, lanes]
        y_pair = dot(jnp.concatenate(mixing, axis=1), jnp.concatenate(both_halves(x_pair), axis=0))
        ypart_o[:, lanes] = y_pair + par[7:8, lanes] * x_pair.astype(F32)
    weighted = (expand(end_weights(place, block, cum) * step, spread) * xc.astype(F32)).astype(BF16)
    block_state = dot_tn(weighted, bq)
    decay = block_decay(place, block, cum)
    entry_o[0] = run[...]
    total = head_column(decay, inner) * run[...] + block_state
    run[...] = total
    before = factor[0:1, :]
    row = iota((8, LANES), 0)
    decay_o[0] = jnp.where(row == 0, decay, jnp.where(row == 1, before, 0.0))
    after = before * decay
    factor[...] = jnp.broadcast_to(after, factor.shape)

    @pl.when(block == pl.num_programs(0) - 1)
    def _():
        packet_o[...] = state_packet(total, after)


def gate_matmul_kernel(counts, dp_count, info, *refs):
    shards = refs[:dp_count]
    normed, cot, w2, z_o, dn_o = refs[dp_count:]
    block = pl.program_id(0)
    place = Place(info, counts)
    inner = z_o.shape[1]
    shard = shards[0].shape[0]

    @pl.when(block == 0)
    def _():
        for offset in range(dp_count):
            first = pl.multiple_of(xor(place.dp, offset) * shard, shard)
            w2[pl.ds(first, shard), :] = shards[offset][...]

    z_o[...] = dot(normed[...], w2[:, :inner]).astype(BF16)
    grad = (cot[...].astype(F32) * place.valid(block)).astype(BF16)
    dn_o[...] = dot(grad, w2[:, inner:])


def apply_kernel(counts, packet_count, info, *refs):
    packets = refs[:packet_count]
    entry, decay, cum, bc, ypart, z, dn, par, spread, y_o, hb_o, h_o, stat_o, start = refs[packet_count:]
    block = pl.program_id(0)
    place = Place(info, counts)
    inner = z.shape[1]

    @pl.when(block == 0)
    def _():
        start[...] = merge_packets([packet[...] for packet in packets], inner)

    state = entry[0] + head_column(decay[0, 1:2, :], inner) * start[...]
    h_o[0] = state
    low = state.astype(BF16)
    hb_o[0] = low
    cq = bc[:, LANES:]
    y = ypart[...] + expand(enter_weights(place, block, cum[...]), spread) * dot_nt(cq, low)
    y_o[...] = y
    gate = z[...].astype(F32)
    gated = y * gate * sigmoid(gate)
    squares = jnp.sum(gated * gated, axis=1, keepdims=True)
    cross = jnp.sum(par[6:7, :inner] * dn[...] * gated, axis=1, keepdims=True)
    lane = iota((BLOCK, LANES), 1)
    both = jnp.where(lane == 0, squares, jnp.where(lane == 1, cross, 0.0))
    stat_o[...] = both.T[0:8, :]


def gate_back_kernel(
    counts, inner_all, info, stat, y, z, dn, cot, cum, bc, xc, hb, decay, wo, par, spread,
    keep_o, send_o, gwo_o, small_o, dy_o, dz_o, de_o, exit_o, packet_o,
    acc, run, factor,
):
    step = pl.program_id(0)
    block = pl.num_programs(0) - 1 - step
    place = Place(info, counts)
    inner = z.shape[1]
    width = cot.shape[1]
    half = width // 2

    @pl.when(step == 0)
    def _():
        acc[...] = jnp.zeros_like(acc)
        run[...] = jnp.zeros_like(run)
        factor[...] = jnp.ones_like(factor)
        small_o[...] = jnp.zeros_like(small_o)

    column = jnp.concatenate([stat[...], jnp.zeros((LANES - 8, BLOCK), F32)], axis=0).T
    inv = lax.rsqrt(column[:, 0:1] / inner_all + EPS)
    cross = column[:, 1:2]
    gain = par[6:7, :inner]
    gate = z[...].astype(F32)
    sig = sigmoid(gate)
    silu = gate * sig
    mixed = y[...]
    gated = mixed * silu
    normal = (gated * inv * gain).astype(BF16)
    own = pl.multiple_of(place.tp * half, half)
    other = pl.multiple_of((1 - place.tp) * half, half)
    keep_o[...] = dot_nt(normal, wo[pl.ds(own, half), :]).astype(BF16)
    send_o[...] = dot_nt(normal, wo[pl.ds(other, half), :]).astype(BF16)
    grad = (cot[...].astype(F32) * place.valid(block)).astype(BF16)
    acc[...] += dot_tn(grad, normal)
    back = dn[...]
    grad_gated = inv * (gain * back) - gated * (inv * inv * inv) * (cross / inner_all)
    dy = (grad_gated * silu).astype(BF16)
    dy_o[...] = dy
    dz_o[...] = (grad_gated * mixed * sig * (1.0 + gate * (1.0 - sig))).astype(BF16)
    dy_float = dy.astype(F32)
    cq = bc[:, LANES:]
    read = dot_nt(cq, hb[0])
    de_o[...] = reduce_heads(dy_float * read, spread)
    small_o[0:1, :] += jnp.sum(back * gated * inv, axis=0, keepdims=True)
    small_o[1:2, :] += jnp.sum(dy_float * xc[...].astype(F32), axis=0, keepdims=True)
    dq = (expand(enter_weights(place, block, cum[...]), spread) * dy_float).astype(BF16)
    exit_o[0] = run[...]
    here = decay[0, 0:1, :]
    total = head_column(here, inner) * run[...] + dot_tn(dq, cq)
    run[...] = total
    after = factor[0:1, :] * here
    factor[...] = jnp.broadcast_to(after, factor.shape)

    @pl.when(step == pl.num_programs(0) - 1)
    def _():
        packet_o[...] = state_packet(total, after)
        gwo_o[...] = acc[...].astype(BF16)


def intra_back_kernel(counts, heads, dp_count, info, *refs):
    dy, dz, xc, bc, cum, pre_step, hb, normed, wz, gwo, par, spread = refs[:12]
    dxc_o, dcq_o, dbq_o, rows_o, cols_o, dnz_o = refs[12:18]
    parts = refs[18:-2]
    acc, columns = refs[-2:]
    block = pl.program_id(0)
    place = Place(info, counts)
    inner = heads * HEAD

    @pl.when(block == 0)
    def _():
        acc[...] = jnp.zeros_like(acc)
        columns[...] = jnp.zeros_like(columns)

    bq = bc[:, :LANES]
    cq = bc[:, LANES:]
    cums = cum[...]
    step = step_sizes(place, block, pre_step[...], heads)
    cum_rows = cums.T
    step_rows = step.T
    gram = dot_nt(cq, bq)
    keep = place.keep(block)
    lane = iota((BLOCK, LANES), 1)
    grad_gram = jnp.zeros((BLOCK, BLOCK), F32)
    sums = jnp.zeros((BLOCK, LANES), F32)
    for pair in range(heads // 2):
        lanes = slice(pair * LANES, (pair + 1) * LANES)
        dy_pair = dy[:, lanes]
        x_pair = xc[:, lanes]
        halves = jnp.concatenate(both_halves(dy_pair), axis=0)
        grad_mixing = dot_nt(halves, x_pair)
        mixing = []
        for side in range(2):
            head = 2 * pair + side
            grad_m = grad_mixing[side * BLOCK : (side + 1) * BLOCK, :]
            kernel = decay_kernel(keep, cums, cum_rows, head)
            step_row = step_rows[head : head + 1, :]
            weight = kernel * step_row
            mixing.append((gram * weight).astype(BF16))
            grad_gram = grad_gram + grad_m * weight
            part = grad_m * gram * kernel
            columns[head : head + 1, :] = jnp.sum(part, axis=0, keepdims=True)
            sums = sums + jnp.where(lane == head, jnp.sum(part * step_row, axis=1, keepdims=True), 0.0)
        dx_pair = dot_tn(jnp.concatenate(mixing, axis=0), halves)
        dxc_o[:, lanes] = dx_pair + par[7:8, lanes] * dy_pair.astype(F32)
    grad_low = grad_gram.astype(BF16)
    dq = (expand(enter_weights(place, block, cums), spread) * dy[...].astype(F32)).astype(BF16)
    dcq_o[...] = dot(grad_low, bq) + dot(dq, hb[0])
    dbq_o[...] = dot_tn(grad_low, cq)
    rows_o[...] = sums
    cols_o[...] = columns[...].T
    dnz_o[...] = dot_nt(dz[...], wz[...])
    acc[...] += dot_tn(normed[...], dz[...])

    @pl.when(block == pl.num_programs(0) - 1)
    def _():
        cut_pieces(place, dp_count, acc, parts, slice(0, inner))
        cut_pieces(place, dp_count, gwo, parts, slice(inner, 2 * inner))


def state_back_kernel(counts, heads, dp_count, packet_count, part_count, info, *refs):
    packets = refs[:packet_count]
    (
        exits, h, xc, bc, cum, pre_step, de, dxc, dcq, dbq, rows, cols, decay, v, v_tail, halo_v, halo_normed,
        halo, tok, normed, dnz, small_gate, w1, par, dtp, spread,
        dn_o, dnh_o,
    ) = refs[packet_count : -6 - part_count]
    parts = refs[-6 - part_count : -6]
    start, factor, ext, grad_ext, acc, small_o = refs[-6:]
    step_id = pl.program_id(0)
    block = pl.num_programs(0) - 1 - step_id
    place = Place(info, counts)
    inner = heads * HEAD
    channels = inner + 2 * LANES
    width = tok.shape[1]

    @pl.when(step_id == 0)
    def _():
        start[...] = merge_packets([packet[...] for packet in packets], inner)
        factor[...] = jnp.ones_like(factor)
        acc[...] = jnp.zeros_like(acc)
        grad_ext[...] = jnp.zeros_like(grad_ext)
        small_o[...] = jnp.zeros_like(small_o)

    here = decay[0, 0:1, :]
    before = factor[0:1, :]
    grad_state = exits[0] + head_column(before, inner) * start[...]
    factor[...] = jnp.broadcast_to(before * here, factor.shape)
    shape = (inner, LANES)
    overlap = jnp.sum(grad_state * h[0], axis=1, keepdims=True)
    grad_decay = jnp.sum(
        jnp.where(iota(shape, 0) // HEAD == iota(shape, 1), overlap, 0.0), axis=0, keepdims=True
    )
    low = grad_state.astype(BF16)
    bq = bc[:, :LANES]
    cums = cum[...]
    x_float = xc[...].astype(F32)
    pre_dt = pre_step[...]
    valid = place.valid(block)
    step = step_sizes(place, block, pre_dt, heads)
    end_kernel = end_weights(place, block, cums)
    end_weight = end_kernel * step
    end_wide = expand(end_weight, spread)
    spread_b = dot_nt(bq, low)
    grad_x = dxc[...] + end_wide * spread_b
    grad_end = reduce_heads(x_float * spread_b, spread)
    grad_b = dbq[...] + dot((x_float * end_wide).astype(BF16), low)
    end_part = grad_end * end_weight
    last = iota((BLOCK, LANES), 0) == BLOCK - 1
    grad_cum = rows[...] - cols[...] * step - end_part + de[...] * enter_weights(place, block, cums)
    grad_cum = grad_cum + jnp.where(
        last, jnp.sum(end_part, axis=0, keepdims=True) + grad_decay * here, 0.0
    )
    upper = (iota((BLOCK, BLOCK), 0) <= iota((BLOCK, BLOCK), 1)).astype(F32)
    grad_log = dot_exact(upper, grad_cum)
    rates = dtp[1:2, :]
    grad_step = cols[...] + grad_end * end_kernel - rates * grad_log
    heads_lane = iota((BLOCK, LANES), 1) < heads
    grad_pre_dt = jnp.where(heads_lane, grad_step * sigmoid(pre_dt), 0.0) * valid
    small_o[6:7, :LANES] += jnp.sum(grad_pre_dt, axis=0, keepdims=True)
    small_o[7:8, :LANES] += jnp.sum(grad_log * (-rates * step), axis=0, keepdims=True)

    ext[8 : 8 + BLOCK, :] = v[...].astype(F32)

    @pl.when(block == 0)
    def _():
        ext[0:8, :] = halo_v[...]

    @pl.when(block > 0)
    def _():
        ext[0:8, :] = v_tail[...].astype(F32)[8:16, :]

    pre = conv_pre(place, block, ext, par, channels)
    sig = sigmoid(pre)
    slope = sig * (1.0 + pre * (1.0 - sig))
    grad_pre = jnp.concatenate([grad_x, grad_b, dcq[...]], axis=1) * slope
    small_o[4:5, :] += jnp.sum(grad_pre, axis=0, keepdims=True)
    carry = grad_ext[0:8, :]
    grad_ext[0 : BLOCK, :] = jnp.zeros((BLOCK, channels), F32)
    grad_ext[BLOCK : BLOCK + 8, :] = carry
    for tap in range(CONV):
        first = 8 - (CONV - 1) + tap
        masked = grad_pre * same_mask(place, block, tap)
        small_o[tap : tap + 1, :] += jnp.sum(masked * ext[first : first + BLOCK, :], axis=0, keepdims=True)
        grad_ext[first : first + BLOCK, :] += par[tap : tap + 1, :channels] * masked
    packed = jnp.concatenate([grad_ext[8 : 8 + BLOCK, :].astype(BF16), grad_pre_dt.astype(BF16)], axis=1)
    partial = dnz[...] + dot_nt(packed, w1[...])
    dn_o[...] = partial.astype(BF16)
    acc[...] += dot_tn(normed[...], packed)
    gain = par[5:6, :width]
    scaled, _, _ = normalise(tok[...].astype(F32), gain)
    small_o[5:6, :width] += jnp.sum(partial * scaled, axis=0, keepdims=True)

    @pl.when(block == 0)
    def _():
        back = jnp.concatenate([jnp.zeros((8, channels), F32), grad_ext[0:8, :]], axis=0).astype(BF16)
        halo_grad = dot_nt(back, w1[:, :channels])
        dnh_o[...] = halo_grad[8:16, :]
        halo_scaled, _, _ = normalise(halo[...].astype(F32), gain)
        small_o[5:6, :width] += jnp.sum(halo_grad * halo_scaled, axis=0, keepdims=True)
        acc[:, :channels] += dot_tn(halo_normed[...], back)
        skip = reduce_heads(jnp.broadcast_to(small_gate[1:2, :], (8, inner)), spread)[0:1, :]
        acc[:, channels:] += pack_parameters(dp_count, heads, small_o, small_gate[0:1, :], skip)
        cut_pieces(place, dp_count, acc, parts, slice(0, channels + LANES))


def finish_kernel(counts, info, own, other, halo_a, halo_b, tok, cot, par, grad_o):
    block = pl.program_id(0)
    place = Place(info, counts)
    width = tok.shape[1]
    grad = own[...].astype(F32) + other[...].astype(F32)
    is_last = jnp.where((block + 1) * BLOCK == place.fill, 1.0, 0.0)
    halo = (halo_a[...] + halo_b[...]) * is_last
    grad = jnp.concatenate([grad[: BLOCK - 8, :], grad[BLOCK - 8 :, :] + halo], axis=0)
    inputs = tok[...].astype(F32)
    inv = lax.rsqrt(jnp.mean(inputs * inputs, axis=1, keepdims=True) + EPS)
    scaled = par[5:6, :width] * grad
    inner_dot = jnp.sum(scaled * inputs, axis=1, keepdims=True)
    grad_o[...] = (
        inv * scaled - inputs * (inv * inv * inv) * (inner_dot / width) + cot[...].astype(F32)
    )


def unpack_gate_kernel(counts, part_count, info, *refs):
    parts = refs[:part_count]
    wz_o, wo_o, wide = refs[part_count:]
    place = Place(info, counts)
    shard, inner = wz_o.shape
    rows = shard // part_count
    for part in range(part_count):
        first = pl.multiple_of(xor(place.ctx, part) * rows, rows) if part_count > 1 else 0
        wz_o[pl.ds(first, rows), :] = parts[part][:, :inner].astype(F32)
        wide[pl.ds(first, rows), :] = parts[part][:, inner:].astype(F32)
    wo_o[...] = wide[...].T[:, :shard]


def unpack_input_kernel(counts, heads, part_count, info, *refs):
    parts = refs[:part_count]
    crosses = refs[part_count : 2 * part_count]
    (
        wx_o, wbc_o, wdt_o, norm_o, taps_o, bias_o, state_taps_o, state_bias_o, dt_bias_o, a_log_o, skip_o,
        gate_o, wide, cross,
    ) = refs[2 * part_count :]
    place = Place(info, counts)
    shard, inner = wx_o.shape
    channels = inner + 2 * LANES
    rows = shard // part_count
    for part in range(part_count):
        first = pl.multiple_of(xor(place.ctx, part) * rows, rows) if part_count > 1 else 0
        wide[pl.ds(first, rows), :] = parts[part][...].astype(F32)
        cross[pl.ds(first, rows), :] = crosses[part][...].astype(F32)
    wx_o[...] = wide[:shard, :inner]
    wbc_o[...] = wide[:shard, inner:channels] + cross[:shard, : 2 * LANES]
    wdt_o[...] = wide[:shard, channels : channels + heads]
    lane = iota((wide.shape[0], LANES), 1)
    both = (lane == NORM) | ((lane >= STATE_TAPS) & (lane < BY_HEAD))
    block = wide[:, channels:] + jnp.where(both, cross[:, 2 * LANES :], 0.0)
    lines = block.T
    each = gate_o.shape[1]
    size = lines.shape[1]
    source = iota((16, size), 1)
    inside = (source // each == iota((16, size), 0)) & (source < shard)
    place_in = (iota((size, LANES), 0) % each == iota((size, LANES), 1)).astype(BF16)

    def by_head(line):
        row = jnp.where(inside, lines[line : line + 1, :], 0.0).astype(BF16)
        return dot(row, place_in)[:heads, :each]

    for tap in range(CONV):
        taps_o[tap] = by_head(TAPS + tap)
    bias_o[...] = by_head(TAPS + CONV)
    gate_o[...] = by_head(GATE)
    norm_o[...] = lines[NORM : NORM + 1, :shard]
    states = state_bias_o.shape[1]
    state_taps_o[...] = lines[STATE_TAPS : STATE_TAPS + CONV, :states]
    state_bias_o[...] = lines[STATE_TAPS + CONV : STATE_TAPS + CONV + 1, :states]
    row = lines[BY_HEAD : BY_HEAD + 1, :]
    dt_bias_o[...] = row[:, :heads]
    a_log_o[...] = row[:, heads : 2 * heads]
    skip_o[...] = row[:, 2 * heads : 3 * heads]


def call(body, steps, info, operands, outputs, scratch=(), reverse=False):
    def at(index):
        return steps - 1 - index if reverse else index

    def spec(shape, kind):
        if kind == "rows":
            return pl.BlockSpec((BLOCK,) + tuple(shape[1:]), lambda i: (at(i), 0))
        if kind == "block":
            return pl.BlockSpec((1,) + tuple(shape[1:]), lambda i: (at(i), 0, 0))
        if kind == "lanes":
            return pl.BlockSpec((shape[0], BLOCK), lambda i: (0, at(i)))
        if kind == "tail":
            each = BLOCK // 16
            return pl.BlockSpec((16, shape[1]), lambda i: (jnp.maximum(at(i) * each - 1, 0), 0))
        if kind == "whole":
            return pl.BlockSpec(tuple(shape), lambda i: (0,) * len(shape))
        return kind

    return pl.pallas_call(
        body,
        grid=(steps,),
        in_specs=[pl.BlockSpec(memory_space=pltpu.SMEM)]
        + [spec(array.shape, kind) for array, kind in operands],
        out_specs=[spec(shape.shape, kind) for shape, kind in outputs],
        out_shape=[shape for shape, _ in outputs],
        scratch_shapes=list(scratch),
        compiler_params=pltpu.CompilerParams(
            dimension_semantics=("arbitrary",), vmem_limit_bytes=VMEM
        ),
    )(info, *[array for array, _ in operands])


def shifted(value, axis, steps):
    count = lax.axis_size(axis)
    first, last = max(0, -steps), min(count, count - steps)
    return lax.ppermute(value, axis, [(source, source + steps) for source in range(first, last)])


def swapped(value):
    return lax.ppermute(value, "tp", [(0, 1), (1, 0)])


def partnered(value, axis, mask):
    return lax.ppermute(value, axis, [(one, one ^ mask) for one in range(lax.axis_size(axis))])


def partnered_across(value, mask):
    size = 2 * lax.axis_size("ctx")
    return lax.ppermute(value, ("ctx", "tp"), [(one, one ^ (2 * mask + 1)) for one in range(size)])


def exchanged(value, axis):
    return [value] + [partnered(value, axis, mask) for mask in range(1, lax.axis_size(axis))]


def gather_rows(value, parts):
    if parts == 1:
        return [lax.all_gather(value, "dp", axis=0, tiled=True)]
    rows = value.shape[0] // parts
    own = lax.dynamic_slice_in_dim(value, lax.axis_index("ctx") * rows, rows, 0)
    return exchanged(jnp.concatenate(exchanged(own, "dp"), axis=0), "ctx")


def reduce_rows(pieces):
    if len(pieces) == 1:
        own = lax.psum_scatter(pieces[0], "dp", scatter_dimension=0, tiled=True)
        return lax.psum(own, "ctx")
    dp_count = lax.axis_size("dp")
    rows = pieces[0].shape[0] // dp_count
    total = pieces[0].astype(F32)
    for mask in range(1, len(pieces)):
        total = total + partnered(pieces[mask], "ctx", mask).astype(F32)
    own = total[:rows]
    for mask in range(1, dp_count):
        block = total[mask * rows : (mask + 1) * rows].astype(BF16)
        own = own + partnered(block, "dp", mask).astype(F32)
    return own.astype(BF16)


def body(
    tokens, cotangent, device_fill, seq_lengths, norm_gain, w_z, w_x, w_bc, w_dt,
    conv_x, conv_x_bias, conv_bc, bias_bc, dt_bias, a_log, skip_d, gate_gain, w_out,
):
    rows, width = tokens.shape
    heads = dt_bias.shape[0]
    inner = heads * HEAD
    channels = inner + 2 * LANES
    steps = rows // BLOCK
    shard = norm_gain.shape[0]
    dp_count = lax.axis_size("dp")
    ctx_count = lax.axis_size("ctx")
    tp_index = lax.axis_index("tp")
    counts = (ctx_count, seq_lengths.shape[1])

    parts = ctx_count if shard % (16 * ctx_count) == 0 else 1
    part_rows = shard // parts

    with jax.named_scope("gather_weights"):
        w1_parts = gather_rows(
            jnp.concatenate([w_x, w_bc, jnp.pad(w_dt, ((0, 0), (0, LANES - heads)))], axis=1), parts
        )
        vector = jnp.concatenate(
            [
                conv_x.reshape(CONV, shard),
                conv_x_bias.reshape(1, shard),
                norm_gain[None, :],
                gate_gain.reshape(1, shard),
                jnp.zeros((1, shard), BF16),
                jnp.pad(
                    jnp.concatenate([conv_bc, bias_bc[None, :]], axis=0),
                    ((0, 3), (0, shard - bias_bc.shape[0])),
                ),
            ],
            axis=0,
        )
        vectors = exchanged(vector, "dp")
        w2_shards = exchanged(jnp.concatenate([w_z, w_out.T], axis=1), "dp")

    dtp = jnp.pad(jnp.stack([dt_bias, jnp.exp(a_log), skip_d]), ((0, 5), (0, LANES - heads)))
    shape = (2 * LANES, inner)
    spread = (iota(shape, 0) % LANES == iota(shape, 1) // HEAD).astype(BF16)
    info = jnp.concatenate(
        [
            device_fill[0],
            seq_lengths[0],
            jnp.stack([lax.axis_index("ctx"), tp_index, lax.axis_index("dp")]).astype(jnp.int32),
        ]
    )
    fill = jnp.sum(jnp.where(jnp.arange(ctx_count) == lax.axis_index("ctx"), device_fill[0], 0)) * BLOCK
    halo = shifted(lax.dynamic_slice_in_dim(tokens, fill - 16, 16, 0), "ctx", 1)

    def out(shape, dtype, kind):
        return (jax.ShapeDtypeStruct(shape, dtype), kind)

    def row_out(columns, dtype):
        return out((rows, columns), dtype, "rows")

    state_out = out((steps, inner, LANES), F32, "block")
    packet_out = out((inner + 16, LANES), BF16, "whole")

    (w1, par, normed, halo_normed, halo_v, v, xc, bc, ypart, pre_step, cum, entry, decay, packet) = call(
        functools.partial(forward_kernel, counts, heads, dp_count, parts),
        steps,
        info,
        [(value, "whole") for value in vectors + w1_parts]
        + [(tokens, "rows"), (halo, "whole"), (dtp, "whole"), (spread, "whole")],
        [
            out((width, channels + LANES), BF16, "whole"),
            out((8, channels), F32, "whole"),
            row_out(width, BF16),
            out((16, width), BF16, "whole"),
            out((8, channels), F32, "whole"),
            row_out(channels, BF16),
            row_out(inner, BF16),
            row_out(2 * LANES, BF16),
            row_out(inner, F32),
            row_out(LANES, F32),
            row_out(LANES, F32),
            state_out,
            out((steps, 8, LANES), F32, "block"),
            packet_out,
        ],
        [
            pltpu.VMEM((8 + BLOCK, channels), F32),
            pltpu.VMEM((inner, LANES), F32),
            pltpu.VMEM((8, LANES), F32),
        ],
    )
    packets = [(shifted(packet, "ctx", step), "whole") for step in range(1, ctx_count)]
    wz_spec = pl.BlockSpec((width, inner), lambda i: (0, 0))
    wo_spec = pl.BlockSpec((width, inner), lambda i: (0, 1))
    w2, z, dn = call(
        functools.partial(gate_matmul_kernel, counts, dp_count),
        steps,
        info,
        [(value, "whole") for value in w2_shards] + [(normed, "rows"), (cotangent, "rows")],
        [out((width, 2 * inner), BF16, "whole"), row_out(inner, BF16), row_out(inner, F32)],
    )
    y, hb, h, stat = call(
        functools.partial(apply_kernel, counts, len(packets)),
        steps,
        info,
        packets
        + [
            (entry, "block"),
            (decay, "block"),
            (cum, "rows"),
            (bc, "rows"),
            (ypart, "rows"),
            (z, "rows"),
            (dn, "rows"),
            (par, "whole"),
            (spread, "whole"),
        ],
        [
            row_out(inner, F32),
            out((steps, inner, LANES), BF16, "block"),
            state_out,
            out((8, rows), F32, "lanes"),
        ],
        [pltpu.VMEM((inner, LANES), F32)],
    )
    stat = lax.psum(stat, "tp")
    inner_all = inner * lax.axis_size("tp")
    half = width // 2
    keep, send, gwo, small_gate, dy, dz, de, exits, packet = call(
        functools.partial(gate_back_kernel, counts, inner_all),
        steps,
        info,
        [
            (stat, "lanes"),
            (y, "rows"),
            (z, "rows"),
            (dn, "rows"),
            (cotangent, "rows"),
            (cum, "rows"),
            (bc, "rows"),
            (xc, "rows"),
            (hb, "block"),
            (decay, "block"),
            (w2, wo_spec),
            (par, "whole"),
            (spread, "whole"),
        ],
        [
            row_out(half, BF16),
            row_out(half, BF16),
            out((width, inner), BF16, "whole"),
            out((8, inner), F32, "whole"),
            row_out(inner, BF16),
            row_out(inner, BF16),
            row_out(LANES, F32),
            state_out,
            packet_out,
        ],
        [
            pltpu.VMEM((width, inner), F32),
            pltpu.VMEM((inner, LANES), F32),
            pltpu.VMEM((8, LANES), F32),
        ],
        reverse=True,
    )
    packets = [(shifted(packet, "ctx", -step), "whole") for step in range(1, ctx_count)]
    with jax.named_scope("layer_out"):
        received = swapped(send)
        own_inputs = lax.dynamic_slice_in_dim(tokens, tp_index * half, half, 1).astype(F32)
        valid = (jnp.arange(rows) < fill).astype(F32)[:, None]
        layer_out = own_inputs + (keep.astype(F32) + received.astype(F32)) * valid
    dxc, dcq, dbq, row_sums, col_sums, dnz, *g2 = call(
        functools.partial(intra_back_kernel, counts, heads, dp_count),
        steps,
        info,
        [
            (dy, "rows"),
            (dz, "rows"),
            (xc, "rows"),
            (bc, "rows"),
            (cum, "rows"),
            (pre_step, "rows"),
            (hb, "block"),
            (normed, "rows"),
            (w2, wz_spec),
            (gwo, "whole"),
            (par, "whole"),
            (spread, "whole"),
        ],
        [
            row_out(inner, F32),
            row_out(LANES, F32),
            row_out(LANES, F32),
            row_out(LANES, F32),
            row_out(LANES, F32),
            row_out(width, F32),
        ]
        + [out((width // parts, 2 * inner), BF16, "whole")] * parts,
        [pltpu.VMEM((width, inner), F32), pltpu.VMEM((LANES, BLOCK), F32)],
    )
    with jax.named_scope("reduce_gate_weights"):
        total2 = reduce_rows(g2)
        total2 = exchanged(total2, "ctx") if parts > 1 else [total2]
    partial, halo_grad, *g1 = call(
        functools.partial(state_back_kernel, counts, heads, dp_count, len(packets), parts),
        steps,
        info,
        packets
        + [
            (exits, "block"),
            (h, "block"),
            (xc, "rows"),
            (bc, "rows"),
            (cum, "rows"),
            (pre_step, "rows"),
            (de, "rows"),
            (dxc, "rows"),
            (dcq, "rows"),
            (dbq, "rows"),
            (row_sums, "rows"),
            (col_sums, "rows"),
            (decay, "block"),
            (v, "rows"),
            (v, "tail"),
            (halo_v, "whole"),
            (halo_normed, "whole"),
            (halo, "whole"),
            (tokens, "rows"),
            (normed, "rows"),
            (dnz, "rows"),
            (small_gate, "whole"),
            (w1, "whole"),
            (par, "whole"),
            (dtp, "whole"),
            (spread, "whole"),
        ],
        [
            row_out(width, BF16),
            out((8, width), F32, "whole"),
        ]
        + [out((width // parts, channels + LANES), BF16, "whole")] * parts,
        [
            pltpu.VMEM((inner, LANES), F32),
            pltpu.VMEM((8, LANES), F32),
            pltpu.VMEM((8 + BLOCK, channels), F32),
            pltpu.VMEM((8 + BLOCK, channels), F32),
            pltpu.VMEM((width, channels + LANES), F32),
            pltpu.VMEM((8, channels), F32),
        ],
        reverse=True,
    )
    other = swapped(partial)
    size = ctx_count * 2
    back = [(s, s - 2) for s in range(2, size)]
    cross = [(s, (s - 2) ^ 1) for s in range(2, size)]
    halo_a = lax.ppermute(halo_grad, ("ctx", "tp"), back)
    halo_b = lax.ppermute(halo_grad, ("ctx", "tp"), cross)
    with jax.named_scope("reduce_input_weights"):
        total1 = reduce_rows(g1)
        across = total1[:, inner:]
        if parts > 1:
            total1 = exchanged(total1, "ctx")
            across = [partnered_across(across, mask) for mask in range(parts)]
        else:
            total1, across = [total1], [swapped(across)]
    (grad_tokens,) = call(
        functools.partial(finish_kernel, counts),
        steps,
        info,
        [
            (partial, "rows"),
            (other, "rows"),
            (halo_a, "whole"),
            (halo_b, "whole"),
            (tokens, "rows"),
            (cotangent, "rows"),
            (par, "whole"),
        ],
        [row_out(width, F32)],
    )
    each = HEAD // dp_count
    part_bc = bias_bc.shape[0]
    tall = -(-shard // LANES) * LANES

    def final(*sizes):
        return out(sizes, F32, "whole")

    grad_wz, grad_wo = call(
        functools.partial(unpack_gate_kernel, counts, parts),
        1,
        info,
        [(value, "whole") for value in total2],
        [final(shard, inner), final(inner, shard)],
        [pltpu.VMEM((tall, inner), F32)],
    )
    (
        grad_wx, grad_wbc, grad_wdt, grad_norm, grad_taps, grad_bias, grad_state_taps, grad_state_bias,
        grad_dt_bias, grad_a_log, grad_skip, grad_gate,
    ) = call(
        functools.partial(unpack_input_kernel, counts, heads, parts),
        1,
        info,
        [(value, "whole") for value in total1 + across],
        [
            final(shard, inner),
            final(shard, 2 * LANES),
            final(shard, heads),
            final(1, shard),
            final(CONV, heads, each),
            final(heads, each),
            final(CONV, part_bc),
            final(1, part_bc),
            final(1, heads),
            final(1, heads),
            final(1, heads),
            final(heads, each),
        ],
        [pltpu.VMEM((tall, channels + LANES), F32), pltpu.VMEM((tall, 3 * LANES), F32)],
    )
    return (
        layer_out,
        grad_tokens,
        grad_norm[0],
        grad_wz,
        grad_wx,
        grad_wbc,
        grad_wdt,
        grad_taps,
        grad_bias,
        grad_state_taps,
        grad_state_bias[0],
        grad_dt_bias[0],
        grad_a_log[0],
        grad_skip[0],
        grad_gate,
        grad_wo,
    )


def solution(mesh):
    shards = P(("dp", "ctx"), None)
    return jax.shard_map(
        body,
        mesh=mesh,
        in_specs=(
            shards,
            shards,
            P("dp", None),
            P("dp", None),
            P("dp"),
            P("dp", "tp"),
            P("dp", "tp"),
            P("dp", None),
            P("dp", "tp"),
            P(None, "tp", "dp"),
            P("tp", "dp"),
            P(None, "dp"),
            P("dp"),
            P("tp"),
            P("tp"),
            P("tp"),
            P("tp", "dp"),
            P("tp", "dp"),
        ),
        out_specs=(
            P(("dp", "ctx"), "tp"),
            shards,
            P("dp"),
            P("dp", "tp"),
            P("dp", "tp"),
            P("dp", None),
            P("dp", "tp"),
            P(None, "tp", "dp"),
            P("tp", "dp"),
            P(None, "dp"),
            P("dp"),
            P("tp"),
            P("tp"),
            P("tp"),
            P("tp", "dp"),
            P("tp", "dp"),
        ),
        check_vma=False,
    )
```

```python
import functools

import jax
import jax.numpy as jnp
from jax import lax
from jax.experimental import pallas as pl
from jax.experimental.pallas import tpu as pltpu
from jax.sharding import PartitionSpec as P

CONV = 4
BLOCK = 256
HEAD = 64
LANES = 128
EPS = 1e-05
VMEM = 56 * 1024 * 1024
F32 = jnp.float32
BF16 = jnp.bfloat16


def dot(left, right):
    return jnp.dot(left, right, preferred_element_type=F32)


def dot_tn(left, right):
    return lax.dot_general(left, right, (((0,), (0,)), ((), ())), preferred_element_type=F32)


def dot_nt(left, right):
    return lax.dot_general(left, right, (((1,), (1,)), ((), ())), preferred_element_type=F32)


def dot_exact(left, right):
    return jnp.dot(left, right, preferred_element_type=F32, precision=lax.Precision.HIGHEST)


def iota(shape, dim):
    return lax.broadcasted_iota(jnp.int32, shape, dim)


def sigmoid(value):
    return 1.0 / (1.0 + jnp.exp(-value))


def softplus(value):
    return jnp.maximum(value, 0.0) + jnp.log1p(jnp.exp(-jnp.abs(value)))


def split(value):
    high = value.astype(BF16)
    return high, (value - high.astype(F32)).astype(BF16)


def expand(value, spread):
    return dot(jnp.concatenate(split(value), axis=1), spread[...])


def reduce_heads(value, spread):
    high, low = split(value)
    pick = spread[:LANES, :]
    return dot_nt(high, pick) + dot_nt(low, pick)


def head_column(row, channels):
    shape = (channels, LANES)
    return jnp.sum(jnp.where(iota(shape, 0) // HEAD == iota(shape, 1), row, 0.0), axis=1, keepdims=True)


def xor(value, mask):
    return jnp.bitwise_xor(value, jnp.int32(mask))


class Place:
    def __init__(self, info, counts):
        devices, sequences = counts
        own = info[devices + sequences]
        self.ctx = own
        self.tp = info[devices + sequences + 1]
        self.dp = info[devices + sequences + 2]
        self.fill = jnp.int32(0)
        self.first = jnp.int32(0)
        for device in range(devices):
            rows = info[device] * BLOCK
            self.fill = self.fill + jnp.where(own == device, rows, 0)
            self.first = self.first + jnp.where(own > device, rows, 0)
        self.ends = []
        total = jnp.int32(0)
        for sequence in range(sequences - 1):
            total = total + info[devices + sequence]
            self.ends.append(total)

    def of(self, position):
        found = (position >= self.ends[0]).astype(jnp.int32)
        for end in self.ends[1:]:
            found = found + (position >= end).astype(jnp.int32)
        return jnp.where(position < 0, -1, found)

    def rows(self, index):
        return self.of(self.first + jnp.minimum(index, self.fill - 1))

    def before(self, block):
        position = self.first + jnp.minimum(block * BLOCK, self.fill) - 1
        found = jnp.int32(0)
        for end in self.ends:
            found = found + jnp.where(position >= end, 1, 0)
        return jnp.where(position < 0, -1, found)

    def last(self, block):
        position = self.first + jnp.minimum(block * BLOCK + BLOCK - 1, self.fill - 1)
        found = jnp.int32(0)
        for end in self.ends:
            found = found + jnp.where(position >= end, 1, 0)
        return found

    def column(self, block, shift=0):
        return self.rows(block * BLOCK + shift + iota((BLOCK, 1), 0))

    def valid(self, block):
        return (block * BLOCK + iota((BLOCK, 1), 0) < self.fill).astype(F32)

    def keep(self, block):
        across = self.rows(block * BLOCK + iota((1, BLOCK), 1))
        return (self.column(block) == across) & (iota((BLOCK, BLOCK), 0) >= iota((BLOCK, BLOCK), 1))


def step_sizes(place, block, pre_step, heads):
    lane = iota((BLOCK, LANES), 1)
    return jnp.where(lane < heads, softplus(pre_step), 0.0) * place.valid(block)


def end_weights(place, block, cum):
    same = (place.column(block) == place.last(block)).astype(F32)
    return jnp.exp(cum[BLOCK - 1 :, :] - cum) * same


def enter_weights(place, block, cum):
    return jnp.exp(cum) * (place.column(block) == place.before(block)).astype(F32)


def block_decay(place, block, cum):
    return jnp.exp(cum[BLOCK - 1 :, :]) * jnp.where(place.last(block) == place.before(block), 1.0, 0.0)


def decay_kernel(keep, cum, cum_rows, head):
    return jnp.exp(jnp.where(keep, cum[:, head : head + 1] - cum_rows[head : head + 1, :], -1e30))


def both_halves(pair):
    lane = iota(pair.shape, 1)
    zero = jnp.zeros_like(pair)
    return [jnp.where(lane < HEAD, pair, zero), jnp.where(lane >= HEAD, pair, zero)]


def same_mask(place, block, tap):
    return (place.column(block, tap - (CONV - 1)) == place.column(block)).astype(F32)


def conv_pre(place, block, ext, par, channels):
    total = par[4:5, :channels]
    for tap in range(CONV):
        first = 8 - (CONV - 1) + tap
        total = total + par[tap : tap + 1, :channels] * ext[first : first + BLOCK, :] * same_mask(
            place, block, tap
        )
    return total


def state_packet(state, decay):
    high, low = split(decay)
    row = iota((16, LANES), 0)
    tail = jnp.where(row == 0, high.astype(F32), jnp.where(row == 1, low.astype(F32), 0.0))
    return jnp.concatenate([state.astype(BF16), tail.astype(BF16)], axis=0)


def merge_packets(packets, inner):
    total = jnp.zeros((inner, LANES), F32)
    for packet in reversed(packets):
        tail = packet[inner : inner + 16, :].astype(F32)
        decay = tail[0:1, :] + tail[1:2, :]
        total = packet[:inner, :].astype(F32) + head_column(decay, inner) * total
    return total


def normalise(rows, gain):
    inv = lax.rsqrt(jnp.mean(rows * rows, axis=1, keepdims=True) + EPS)
    return rows * inv, inv, (rows * inv * gain).astype(BF16)


def piece_rows(place, dp_count, parts, rows):
    for part in range(parts):
        for block in range(dp_count):
            owner = xor(place.dp, block) * parts + (xor(place.ctx, part) if parts > 1 else 0)
            yield part, block, pl.multiple_of(owner * rows, rows)


def join_pieces(place, dp_count, parts, whole):
    columns = parts[0].shape[1]
    if len(parts) == 1:
        whole[:, :columns] = parts[0][...]
        return
    rows = parts[0].shape[0] // dp_count
    for part, block, first in piece_rows(place, dp_count, len(parts), rows):
        whole[pl.ds(first, rows), :columns] = parts[part][block * rows : (block + 1) * rows, :]


def cut_pieces(place, dp_count, whole, parts, lanes):
    if len(parts) == 1:
        parts[0][:, lanes] = whole[...].astype(BF16)
        return
    rows = parts[0].shape[0] // dp_count
    for part, block, first in piece_rows(place, dp_count, len(parts), rows):
        parts[part][block * rows : (block + 1) * rows, lanes] = whole[pl.ds(first, rows), :].astype(BF16)


def join_parameters(place, vectors, skip, heads, par, w1):
    shard = vectors[0].shape[1]
    each = HEAD // len(vectors)
    inner = heads * HEAD
    by_channel = jnp.zeros((16, inner), F32)
    in_order = jnp.zeros((16, shard * len(vectors)), F32)
    by_state = jnp.zeros((16, 2 * LANES), F32)
    states = 2 * LANES // len(vectors)
    eye = (iota((16, LANES), 0) == iota((16, LANES), 1)).astype(BF16)
    for block, vector in enumerate(vectors):
        owner = xor(place.dp, block)
        first = pl.multiple_of(owner * shard, shard)
        w1[pl.ds(first, shard), inner + 2 * LANES :] = dot_tn(vector[16:32, :], eye).astype(BF16)
        source, target = iota((shard, inner), 0), iota((shard, inner), 1)
        pick = target == source // each * HEAD + owner * each + source % each
        by_channel = by_channel + dot(vector[0:16, :], pick.astype(BF16))
        source, target = iota((shard, in_order.shape[1]), 0), iota((shard, in_order.shape[1]), 1)
        in_order = in_order + dot(vector[0:16, :], (target == owner * shard + source).astype(BF16))
        source, target = iota((shard, 2 * LANES), 0), iota((shard, 2 * LANES), 1)
        pick = (target == owner * states + source) & (source < states)
        by_state = by_state + dot(vector[0:16, :], pick.astype(BF16))
    par[...] = jnp.zeros_like(par)
    par[0:5, :inner] = by_channel[0:5, :]
    par[0:5, inner:] = by_state[8:13, :]
    par[5:6, : in_order.shape[1]] = in_order[5:6, :]
    par[6:7, :inner] = by_channel[6:7, :]
    par[7:8, :inner] = skip


TAPS, NORM, GATE, STATE_TAPS, BY_HEAD = 12, 17, 18, 20, 25


def pack_parameters(dp_count, heads, small, gate, skip):
    inner = heads * HEAD
    each = HEAD // dp_count
    shard = inner // dp_count
    states = 2 * LANES // dp_count

    def lanes(pieces, columns):
        rows, at = [], 0
        for first, value in pieces:
            if first > at:
                rows.append(jnp.zeros((first - at, columns), F32))
            rows.append(value)
            at = first + value.shape[0]
        rows.append(jnp.zeros((LANES - at, columns), F32))
        return jnp.concatenate(rows, axis=0)

    source, target = iota((inner, inner), 0), iota((inner, inner), 1)
    inside = source % shard
    pick = target == inside // each * HEAD + source // shard * each + inside % each
    by_channel = lanes([(TAPS, small[0:5, :inner]), (GATE, gate)], inner)
    total = dot_nt(pick.astype(BF16), by_channel.astype(BF16))
    total = total + lanes([(NORM, small[5:6, :inner])], inner).T
    source, target = iota((inner, 2 * LANES), 0), iota((inner, 2 * LANES), 1)
    inside = source % shard
    pick = (target == source // shard * states + inside) & (inside < states)
    by_state = lanes([(STATE_TAPS, small[0:5, inner : inner + 2 * LANES])], 2 * LANES)
    total = total + dot_nt(pick.astype(BF16), by_state.astype(BF16))
    source, target = iota((inner, LANES), 0) % shard, iota((inner, LANES), 1)
    for index, row in enumerate((small[6:7, :LANES], small[7:8, :LANES], skip)):
        pick = (source == target + index * heads) & (target < heads)
        total = total + dot_nt(pick.astype(BF16), lanes([(BY_HEAD, row)], LANES).astype(BF16))
    return total


def forward_kernel(
    counts, heads, dp_count, part_count, info, *refs
):
    vectors = refs[:dp_count]
    parts = refs[dp_count : dp_count + part_count]
    (
        tok, halo, dtp, spread,
        w1, par, normed_o, halo_normed_o, halo_v_o, v_o, xc_o, bc_o, ypart_o, pre_o, cum_o, entry_o, decay_o,
        packet_o, ext, run, factor,
    ) = refs[dp_count + part_count :]
    forward_block(
        counts, heads, info, vectors, parts, tok, halo, w1, par, dtp, spread,
        normed_o, halo_normed_o, halo_v_o, v_o, xc_o, bc_o, ypart_o, pre_o, cum_o, entry_o, decay_o, packet_o,
        ext, run, factor,
    )


def forward_block(
    counts, heads, info, vectors, parts, tok, halo, w1, par, dtp, spread,
    normed_o, halo_normed_o, halo_v_o, v_o, xc_o, bc_o, ypart_o, pre_o, cum_o, entry_o, decay_o, packet_o,
    ext, run, factor,
):
    block = pl.program_id(0)
    place = Place(info, counts)
    inner = heads * HEAD
    state = LANES
    channels = inner + 2 * state
    width = tok.shape[1]

    @pl.when(block == 0)
    def _():
        join_pieces(place, len(vectors), parts, w1)
        join_parameters(place, vectors, expand(dtp[...], spread)[2:3, :], heads, par, w1)

    gain = par[5:6, :width]
    _, _, normed = normalise(tok[...].astype(F32), gain)
    normed_o[...] = normed

    @pl.when(block == 0)
    def _():
        _, _, before = normalise(halo[...].astype(F32), gain)
        halo_normed_o[...] = before
        raw = dot(before, w1[:, :channels]).astype(BF16).astype(F32)
        ext[0:8, :] = raw[8:16, :]
        halo_v_o[...] = raw[8:16, :]
        run[...] = jnp.zeros_like(run)
        factor[...] = jnp.ones_like(factor)

    @pl.when(block > 0)
    def _():
        ext[0:8, :] = ext[BLOCK : BLOCK + 8, :]

    raw = dot(normed, w1[...])
    v = raw[:, :channels].astype(BF16)
    v_o[...] = v
    ext[8 : 8 + BLOCK, :] = v.astype(F32)
    pre = conv_pre(place, block, ext, par, channels)
    act = (pre * sigmoid(pre)).astype(BF16)
    xc = act[:, :inner]
    bq = act[:, inner : inner + state]
    cq = act[:, inner + state :]
    xc_o[...] = xc
    bc_o[...] = act[:, inner:]
    pre_step = raw[:, channels:].astype(BF16).astype(F32) + dtp[0:1, :]
    pre_o[...] = pre_step
    step = step_sizes(place, block, pre_step, heads)
    tri = (iota((BLOCK, BLOCK), 0) >= iota((BLOCK, BLOCK), 1)).astype(F32)
    cum = dot_exact(tri, -dtp[1:2, :] * step)
    cum_o[...] = cum
    cum_rows = cum.T
    step_rows = step.T
    gram = dot_nt(cq, bq)
    keep = place.keep(block)
    for pair in range(heads // 2):
        lanes = slice(pair * LANES, (pair + 1) * LANES)
        mixing = []
        for head in (2 * pair, 2 * pair + 1):
            weight = decay_kernel(keep, cum, cum_rows, head) * step_rows[head : head + 1, :]
            mixing.append((gram * weight).astype(BF16))
        x_pair = xc[:, lanes]
        y_pair = dot(jnp.concatenate(mixing, axis=1), jnp.concatenate(both_halves(x_pair), axis=0))
        ypart_o[:, lanes] = y_pair + par[7:8, lanes] * x_pair.astype(F32)
    weighted = (expand(end_weights(place, block, cum) * step, spread) * xc.astype(F32)).astype(BF16)
    block_state = dot_tn(weighted, bq)
    decay = block_decay(place, block, cum)
    entry_o[0] = run[...]
    total = head_column(decay, inner) * run[...] + block_state
    run[...] = total
    before = factor[0:1, :]
    row = iota((8, LANES), 0)
    decay_o[0] = jnp.where(row == 0, decay, jnp.where(row == 1, before, 0.0))
    after = before * decay
    factor[...] = jnp.broadcast_to(after, factor.shape)

    @pl.when(block == pl.num_programs(0) - 1)
    def _():
        packet_o[...] = state_packet(total, after)


def gate_matmul_kernel(counts, dp_count, info, *refs):
    shards = refs[:dp_count]
    normed, cot, w2, z_o, dn_o = refs[dp_count:]
    block = pl.program_id(0)
    place = Place(info, counts)
    inner = z_o.shape[1]
    shard = shards[0].shape[0]

    @pl.when(block == 0)
    def _():
        for offset in range(dp_count):
            first = pl.multiple_of(xor(place.dp, offset) * shard, shard)
            w2[pl.ds(first, shard), :] = shards[offset][...]

    z_o[...] = dot(normed[...], w2[:, :inner]).astype(BF16)
    grad = (cot[...].astype(F32) * place.valid(block)).astype(BF16)
    dn_o[...] = dot(grad, w2[:, inner:])


def apply_kernel(counts, packet_count, info, *refs):
    packets = refs[:packet_count]
    entry, decay, cum, bc, ypart, z, dn, par, spread, y_o, hb_o, h_o, stat_o, start = refs[packet_count:]
    block = pl.program_id(0)
    place = Place(info, counts)
    inner = z.shape[1]

    @pl.when(block == 0)
    def _():
        start[...] = merge_packets([packet[...] for packet in packets], inner)

    state = entry[0] + head_column(decay[0, 1:2, :], inner) * start[...]
    h_o[0] = state
    low = state.astype(BF16)
    hb_o[0] = low
    cq = bc[:, LANES:]
    y = ypart[...] + expand(enter_weights(place, block, cum[...]), spread) * dot_nt(cq, low)
    y_o[...] = y
    gate = z[...].astype(F32)
    gated = y * gate * sigmoid(gate)
    squares = jnp.sum(gated * gated, axis=1, keepdims=True)
    cross = jnp.sum(par[6:7, :inner] * dn[...] * gated, axis=1, keepdims=True)
    lane = iota((BLOCK, LANES), 1)
    both = jnp.where(lane == 0, squares, jnp.where(lane == 1, cross, 0.0))
    stat_o[...] = both.T[0:8, :]


def gate_back_kernel(
    counts, inner_all, info, stat, y, z, dn, cot, cum, bc, xc, hb, decay, wo, par, spread,
    keep_o, send_o, gwo_o, small_o, dy_o, dz_o, de_o, exit_o, packet_o,
    acc, run, factor,
):
    step = pl.program_id(0)
    block = pl.num_programs(0) - 1 - step
    place = Place(info, counts)
    inner = z.shape[1]
    width = cot.shape[1]
    half = width // 2

    @pl.when(step == 0)
    def _():
        acc[...] = jnp.zeros_like(acc)
        run[...] = jnp.zeros_like(run)
        factor[...] = jnp.ones_like(factor)
        small_o[...] = jnp.zeros_like(small_o)

    column = jnp.concatenate([stat[...], jnp.zeros((LANES - 8, BLOCK), F32)], axis=0).T
    inv = lax.rsqrt(column[:, 0:1] / inner_all + EPS)
    cross = column[:, 1:2]
    gain = par[6:7, :inner]
    gate = z[...].astype(F32)
    sig = sigmoid(gate)
    silu = gate * sig
    mixed = y[...]
    gated = mixed * silu
    normal = (gated * inv * gain).astype(BF16)
    own = pl.multiple_of(place.tp * half, half)
    other = pl.multiple_of((1 - place.tp) * half, half)
    keep_o[...] = dot_nt(normal, wo[pl.ds(own, half), :]).astype(BF16)
    send_o[...] = dot_nt(normal, wo[pl.ds(other, half), :]).astype(BF16)
    grad = (cot[...].astype(F32) * place.valid(block)).astype(BF16)
    acc[...] += dot_tn(grad, normal)
    back = dn[...]
    grad_gated = inv * (gain * back) - gated * (inv * inv * inv) * (cross / inner_all)
    dy = (grad_gated * silu).astype(BF16)
    dy_o[...] = dy
    dz_o[...] = (grad_gated * mixed * sig * (1.0 + gate * (1.0 - sig))).astype(BF16)
    dy_float = dy.astype(F32)
    cq = bc[:, LANES:]
    read = dot_nt(cq, hb[0])
    de_o[...] = reduce_heads(dy_float * read, spread)
    small_o[0:1, :] += jnp.sum(back * gated * inv, axis=0, keepdims=True)
    small_o[1:2, :] += jnp.sum(dy_float * xc[...].astype(F32), axis=0, keepdims=True)
    dq = (expand(enter_weights(place, block, cum[...]), spread) * dy_float).astype(BF16)
    exit_o[0] = run[...]
    here = decay[0, 0:1, :]
    total = head_column(here, inner) * run[...] + dot_tn(dq, cq)
    run[...] = total
    after = factor[0:1, :] * here
    factor[...] = jnp.broadcast_to(after, factor.shape)

    @pl.when(step == pl.num_programs(0) - 1)
    def _():
        packet_o[...] = state_packet(total, after)
        gwo_o[...] = acc[...].astype(BF16)


def intra_back_kernel(counts, heads, dp_count, info, *refs):
    dy, dz, xc, bc, cum, pre_step, hb, normed, wz, gwo, par, spread = refs[:12]
    dxc_o, dcq_o, dbq_o, rows_o, cols_o, dnz_o = refs[12:18]
    parts = refs[18:-2]
    acc, columns = refs[-2:]
    block = pl.program_id(0)
    place = Place(info, counts)
    inner = heads * HEAD

    @pl.when(block == 0)
    def _():
        acc[...] = jnp.zeros_like(acc)
        columns[...] = jnp.zeros_like(columns)

    bq = bc[:, :LANES]
    cq = bc[:, LANES:]
    cums = cum[...]
    step = step_sizes(place, block, pre_step[...], heads)
    cum_rows = cums.T
    step_rows = step.T
    gram = dot_nt(cq, bq)
    keep = place.keep(block)
    lane = iota((BLOCK, LANES), 1)
    grad_gram = jnp.zeros((BLOCK, BLOCK), F32)
    sums = jnp.zeros((BLOCK, LANES), F32)
    for pair in range(heads // 2):
        lanes = slice(pair * LANES, (pair + 1) * LANES)
        dy_pair = dy[:, lanes]
        x_pair = xc[:, lanes]
        halves = jnp.concatenate(both_halves(dy_pair), axis=0)
        grad_mixing = dot_nt(halves, x_pair)
        mixing = []
        for side in range(2):
            head = 2 * pair + side
            grad_m = grad_mixing[side * BLOCK : (side + 1) * BLOCK, :]
            kernel = decay_kernel(keep, cums, cum_rows, head)
            step_row = step_rows[head : head + 1, :]
            weight = kernel * step_row
            mixing.append((gram * weight).astype(BF16))
            grad_gram = grad_gram + grad_m * weight
            part = grad_m * gram * kernel
            columns[head : head + 1, :] = jnp.sum(part, axis=0, keepdims=True)
            sums = sums + jnp.where(lane == head, jnp.sum(part * step_row, axis=1, keepdims=True), 0.0)
        dx_pair = dot_tn(jnp.concatenate(mixing, axis=0), halves)
        dxc_o[:, lanes] = dx_pair + par[7:8, lanes] * dy_pair.astype(F32)
    grad_low = grad_gram.astype(BF16)
    dq = (expand(enter_weights(place, block, cums), spread) * dy[...].astype(F32)).astype(BF16)
    dcq_o[...] = dot(grad_low, bq) + dot(dq, hb[0])
    dbq_o[...] = dot_tn(grad_low, cq)
    rows_o[...] = sums
    cols_o[...] = columns[...].T
    dnz_o[...] = dot_nt(dz[...], wz[...])
    acc[...] += dot_tn(normed[...], dz[...])

    @pl.when(block == pl.num_programs(0) - 1)
    def _():
        cut_pieces(place, dp_count, acc, parts, slice(0, inner))
        cut_pieces(place, dp_count, gwo, parts, slice(inner, 2 * inner))


def state_back_kernel(counts, heads, dp_count, packet_count, part_count, info, *refs):
    packets = refs[:packet_count]
    (
        exits, h, xc, bc, cum, pre_step, de, dxc, dcq, dbq, rows, cols, decay, v, v_tail, halo_v, halo_normed,
        halo, tok, normed, dnz, small_gate, w1, par, dtp, spread,
        dn_o, dnh_o,
    ) = refs[packet_count : -6 - part_count]
    parts = refs[-6 - part_count : -6]
    start, factor, ext, grad_ext, acc, small_o = refs[-6:]
    step_id = pl.program_id(0)
    block = pl.num_programs(0) - 1 - step_id
    place = Place(info, counts)
    inner = heads * HEAD
    channels = inner + 2 * LANES
    width = tok.shape[1]

    @pl.when(step_id == 0)
    def _():
        start[...] = merge_packets([packet[...] for packet in packets], inner)
        factor[...] = jnp.ones_like(factor)
        acc[...] = jnp.zeros_like(acc)
        grad_ext[...] = jnp.zeros_like(grad_ext)
        small_o[...] = jnp.zeros_like(small_o)

    here = decay[0, 0:1, :]
    before = factor[0:1, :]
    grad_state = exits[0] + head_column(before, inner) * start[...]
    factor[...] = jnp.broadcast_to(before * here, factor.shape)
    shape = (inner, LANES)
    overlap = jnp.sum(grad_state * h[0], axis=1, keepdims=True)
    grad_decay = jnp.sum(
        jnp.where(iota(shape, 0) // HEAD == iota(shape, 1), overlap, 0.0), axis=0, keepdims=True
    )
    low = grad_state.astype(BF16)
    bq = bc[:, :LANES]
    cums = cum[...]
    x_float = xc[...].astype(F32)
    pre_dt = pre_step[...]
    valid = place.valid(block)
    step = step_sizes(place, block, pre_dt, heads)
    end_kernel = end_weights(place, block, cums)
    end_weight = end_kernel * step
    end_wide = expand(end_weight, spread)
    spread_b = dot_nt(bq, low)
    grad_x = dxc[...] + end_wide * spread_b
    grad_end = reduce_heads(x_float * spread_b, spread)
    grad_b = dbq[...] + dot((x_float * end_wide).astype(BF16), low)
    end_part = grad_end * end_weight
    last = iota((BLOCK, LANES), 0) == BLOCK - 1
    grad_cum = rows[...] - cols[...] * step - end_part + de[...] * enter_weights(place, block, cums)
    grad_cum = grad_cum + jnp.where(
        last, jnp.sum(end_part, axis=0, keepdims=True) + grad_decay * here, 0.0
    )
    upper = (iota((BLOCK, BLOCK), 0) <= iota((BLOCK, BLOCK), 1)).astype(F32)
    grad_log = dot_exact(upper, grad_cum)
    rates = dtp[1:2, :]
    grad_step = cols[...] + grad_end * end_kernel - rates * grad_log
    heads_lane = iota((BLOCK, LANES), 1) < heads
    grad_pre_dt = jnp.where(heads_lane, grad_step * sigmoid(pre_dt), 0.0) * valid
    small_o[6:7, :LANES] += jnp.sum(grad_pre_dt, axis=0, keepdims=True)
    small_o[7:8, :LANES] += jnp.sum(grad_log * (-rates * step), axis=0, keepdims=True)

    ext[8 : 8 + BLOCK, :] = v[...].astype(F32)

    @pl.when(block == 0)
    def _():
        ext[0:8, :] = halo_v[...]

    @pl.when(block > 0)
    def _():
        ext[0:8, :] = v_tail[...].astype(F32)[8:16, :]

    pre = conv_pre(place, block, ext, par, channels)
    sig = sigmoid(pre)
    slope = sig * (1.0 + pre * (1.0 - sig))
    grad_pre = jnp.concatenate([grad_x, grad_b, dcq[...]], axis=1) * slope
    small_o[4:5, :] += jnp.sum(grad_pre, axis=0, keepdims=True)
    carry = grad_ext[0:8, :]
    grad_ext[0 : BLOCK, :] = jnp.zeros((BLOCK, channels), F32)
    grad_ext[BLOCK : BLOCK + 8, :] = carry
    for tap in range(CONV):
        first = 8 - (CONV - 1) + tap
        masked = grad_pre * same_mask(place, block, tap)
        small_o[tap : tap + 1, :] += jnp.sum(masked * ext[first : first + BLOCK, :], axis=0, keepdims=True)
        grad_ext[first : first + BLOCK, :] += par[tap : tap + 1, :channels] * masked
    packed = jnp.concatenate([grad_ext[8 : 8 + BLOCK, :].astype(BF16), grad_pre_dt.astype(BF16)], axis=1)
    partial = dnz[...] + dot_nt(packed, w1[...])
    dn_o[...] = partial.astype(BF16)
    acc[...] += dot_tn(normed[...], packed)
    gain = par[5:6, :width]
    scaled, _, _ = normalise(tok[...].astype(F32), gain)
    small_o[5:6, :width] += jnp.sum(partial * scaled, axis=0, keepdims=True)

    @pl.when(block == 0)
    def _():
        back = jnp.concatenate([jnp.zeros((8, channels), F32), grad_ext[0:8, :]], axis=0).astype(BF16)
        halo_grad = dot_nt(back, w1[:, :channels])
        dnh_o[...] = halo_grad[8:16, :]
        halo_scaled, _, _ = normalise(halo[...].astype(F32), gain)
        small_o[5:6, :width] += jnp.sum(halo_grad * halo_scaled, axis=0, keepdims=True)
        acc[:, :channels] += dot_tn(halo_normed[...], back)
        skip = reduce_heads(jnp.broadcast_to(small_gate[1:2, :], (8, inner)), spread)[0:1, :]
        acc[:, channels:] += pack_parameters(dp_count, heads, small_o, small_gate[0:1, :], skip)
        cut_pieces(place, dp_count, acc, parts, slice(0, channels + LANES))


def finish_kernel(counts, info, own, other, halo_a, halo_b, tok, cot, par, grad_o):
    block = pl.program_id(0)
    place = Place(info, counts)
    width = tok.shape[1]
    grad = own[...].astype(F32) + other[...].astype(F32)
    is_last = jnp.where((block + 1) * BLOCK == place.fill, 1.0, 0.0)
    halo = (halo_a[...] + halo_b[...]) * is_last
    grad = jnp.concatenate([grad[: BLOCK - 8, :], grad[BLOCK - 8 :, :] + halo], axis=0)
    inputs = tok[...].astype(F32)
    inv = lax.rsqrt(jnp.mean(inputs * inputs, axis=1, keepdims=True) + EPS)
    scaled = par[5:6, :width] * grad
    inner_dot = jnp.sum(scaled * inputs, axis=1, keepdims=True)
    grad_o[...] = (
        inv * scaled - inputs * (inv * inv * inv) * (inner_dot / width) + cot[...].astype(F32)
    )


def unpack_gate_kernel(counts, part_count, info, *refs):
    parts = refs[:part_count]
    wz_o, wo_o = refs[part_count:]
    place = Place(info, counts)
    shard, inner = wz_o.shape
    rows = shard // part_count
    for part in range(part_count):
        first = pl.multiple_of(xor(place.ctx, part) * rows, rows) if part_count > 1 else 0
        wz_o[pl.ds(first, rows), :] = parts[part][:, :inner].astype(F32)
        wo_o[pl.ds(first, rows), :] = parts[part][:, inner:].astype(F32)


def unpack_input_kernel(counts, heads, part_count, info, *refs):
    parts = refs[:part_count]
    (
        wx_o, wbc_o, wdt_o, norm_o, taps_o, bias_o, state_taps_o, state_bias_o, dt_bias_o, a_log_o, skip_o,
        gate_o, wide,
    ) = refs[part_count:]
    place = Place(info, counts)
    shard, inner = wx_o.shape
    channels = inner + 2 * LANES
    rows = shard // part_count
    for part in range(part_count):
        first = pl.multiple_of(xor(place.ctx, part) * rows, rows) if part_count > 1 else 0
        wide[pl.ds(first, rows), :] = parts[part][...].astype(F32)
    wx_o[...] = wide[:shard, :inner]
    wbc_o[...] = wide[:shard, inner:channels]
    lines = wide[:, channels:].T
    wdt_o[...] = lines[:heads, :shard]
    each = gate_o.shape[1]
    size = lines.shape[1]
    source = iota((16, size), 1)
    inside = (source // each == iota((16, size), 0)) & (source < shard)
    place_in = (iota((size, LANES), 0) % each == iota((size, LANES), 1)).astype(BF16)

    def by_head(line):
        row = jnp.where(inside, lines[line : line + 1, :], 0.0).astype(BF16)
        return dot(row, place_in)[:heads, :each]

    for tap in range(CONV):
        taps_o[:, tap, :] = by_head(TAPS + tap)
    bias_o[...] = by_head(TAPS + CONV)
    gate_o[...] = by_head(GATE)
    norm_o[...] = lines[NORM : NORM + 1, :shard]
    states = state_bias_o.shape[1]
    state_taps_o[...] = lines[STATE_TAPS : STATE_TAPS + CONV, :states]
    state_bias_o[...] = lines[STATE_TAPS + CONV : STATE_TAPS + CONV + 1, :states]
    row = lines[BY_HEAD : BY_HEAD + 1, :]
    dt_bias_o[...] = row[:, :heads]
    a_log_o[...] = row[:, heads : 2 * heads]
    skip_o[...] = row[:, 2 * heads : 3 * heads]


def call(body, steps, info, operands, outputs, scratch=(), reverse=False, micros=1):
    def at(index):
        return steps - 1 - index if reverse else index

    def spec(shape, kind):
        if kind == "rows":
            return pl.BlockSpec((BLOCK,) + tuple(shape[1:]), lambda i: (at(i), 0))
        if kind == "block":
            return pl.BlockSpec((1,) + tuple(shape[1:]), lambda i: (at(i), 0, 0))
        if kind == "lanes":
            return pl.BlockSpec((shape[0], BLOCK), lambda i: (0, at(i)))
        if kind == "tail":
            each = BLOCK // 16
            return pl.BlockSpec((16, shape[1]), lambda i: (jnp.maximum(at(i) * each - 1, 0), 0))
        if kind == "whole":
            return pl.BlockSpec(tuple(shape), lambda i: (0,) * len(shape))
        return kind

    return pl.pallas_call(
        body,
        grid=(steps,),
        in_specs=[pl.BlockSpec(memory_space=pltpu.SMEM)]
        + [spec(array.shape, kind) for array, kind in operands],
        out_specs=[spec(shape.shape, kind) for shape, kind in outputs],
        out_shape=[shape for shape, _ in outputs],
        scratch_shapes=list(scratch),
        compiler_params=pltpu.CompilerParams(
            dimension_semantics=("arbitrary",), vmem_limit_bytes=VMEM
        ),
        cost_estimate=pl.CostEstimate(
            flops=micros * 1_100_000_000, bytes_accessed=micros * 3_500_000, transcendentals=0
        ),
    )(info, *[array for array, _ in operands])


def shifted(value, axis, steps):
    count = lax.axis_size(axis)
    first, last = max(0, -steps), min(count, count - steps)
    return lax.ppermute(value, axis, [(source, source + steps) for source in range(first, last)])


def swapped(value):
    return lax.ppermute(value, "tp", [(0, 1), (1, 0)])


def partnered(value, axis, mask):
    return lax.ppermute(value, axis, [(one, one ^ mask) for one in range(lax.axis_size(axis))])


def exchanged(value, axis):
    return [value] + [partnered(value, axis, mask) for mask in range(1, lax.axis_size(axis))]


def gather_rows(value, parts):
    if parts == 1:
        return [lax.all_gather(value, "dp", axis=0, tiled=True)], ()
    rows = value.shape[0] // parts
    own = lax.dynamic_slice_in_dim(value, lax.axis_index("ctx") * rows, rows, 0)
    joined = jnp.concatenate(exchanged(own, "dp"), axis=0)
    return exchanged(joined, "ctx"), joined


def reduce_rows(pieces):
    if len(pieces) == 1:
        own = lax.psum_scatter(pieces[0], "dp", scatter_dimension=0, tiled=True)
        return lax.psum(own, "ctx")
    dp_count = lax.axis_size("dp")
    rows = pieces[0].shape[0] // dp_count
    total = pieces[0].astype(F32)
    for mask in range(1, len(pieces)):
        total = total + partnered(pieces[mask], "ctx", mask).astype(F32)
    own = total[:rows]
    for mask in range(1, dp_count):
        block = total[mask * rows : (mask + 1) * rows].astype(BF16)
        own = own + partnered(block, "dp", mask).astype(F32)
    return own.astype(BF16)


def body(
    tokens, cotangent, device_fill, seq_lengths, norm_gain, w_z, w_x, w_bc, w_dt,
    conv_x, conv_x_bias, conv_bc, bias_bc, dt_bias, a_log, skip_d, gate_gain, w_out,
):
    rows, width = tokens.shape
    heads = dt_bias.shape[0]
    inner = heads * HEAD
    channels = inner + 2 * LANES
    steps = rows // BLOCK
    shard = norm_gain.shape[0]
    dp_count = lax.axis_size("dp")
    ctx_count = lax.axis_size("ctx")
    tp_index = lax.axis_index("tp")
    counts = (ctx_count, seq_lengths.shape[1])

    parts = ctx_count if shard % (16 * ctx_count) == 0 else 1
    part_rows = shard // parts

    with jax.named_scope("gather_weights"):
        w1_parts, arrived = gather_rows(jnp.concatenate([w_x, w_bc], axis=1), parts)
        vector = jnp.concatenate(
            [
                conv_x.reshape(CONV, shard),
                conv_x_bias.reshape(1, shard),
                norm_gain[None, :],
                gate_gain.reshape(1, shard),
                jnp.zeros((1, shard), BF16),
                jnp.pad(
                    jnp.concatenate([conv_bc, bias_bc[None, :]], axis=0),
                    ((0, 3), (0, shard - bias_bc.shape[0])),
                ),
                jnp.pad(w_dt.T, ((0, 16 - heads), (0, 0))),
            ],
            axis=0,
        )
        vectors = exchanged(vector, "dp")
        shard2 = jnp.concatenate([w_z, w_out.T], axis=1)
        shard2, _ = lax.optimization_barrier((shard2, arrived))
        w2_shards = exchanged(shard2, "dp")

    dtp = jnp.pad(jnp.stack([dt_bias, jnp.exp(a_log), skip_d]), ((0, 5), (0, LANES - heads)))
    shape = (2 * LANES, inner)
    spread = (iota(shape, 0) % LANES == iota(shape, 1) // HEAD).astype(BF16)
    info = jnp.concatenate(
        [
            device_fill[0],
            seq_lengths[0],
            jnp.stack([lax.axis_index("ctx"), tp_index, lax.axis_index("dp")]).astype(jnp.int32),
        ]
    )
    fill = jnp.sum(jnp.where(jnp.arange(ctx_count) == lax.axis_index("ctx"), device_fill[0], 0)) * BLOCK
    halo = shifted(lax.dynamic_slice_in_dim(tokens, fill - 16, 16, 0), "ctx", 1)

    def out(shape, dtype, kind):
        return (jax.ShapeDtypeStruct(shape, dtype), kind)

    def row_out(columns, dtype):
        return out((rows, columns), dtype, "rows")

    state_out = out((steps, inner, LANES), F32, "block")
    packet_out = out((inner + 16, LANES), BF16, "whole")

    (w1, par, normed, halo_normed, halo_v, v, xc, bc, ypart, pre_step, cum, entry, decay, packet) = call(
        functools.partial(forward_kernel, counts, heads, dp_count, parts),
        steps,
        info,
        [(value, "whole") for value in vectors + w1_parts]
        + [(tokens, "rows"), (halo, "whole"), (dtp, "whole"), (spread, "whole")],
        [
            out((width, channels + LANES), BF16, "whole"),
            out((8, channels), F32, "whole"),
            row_out(width, BF16),
            out((16, width), BF16, "whole"),
            out((8, channels), F32, "whole"),
            row_out(channels, BF16),
            row_out(inner, BF16),
            row_out(2 * LANES, BF16),
            row_out(inner, F32),
            row_out(LANES, F32),
            row_out(LANES, F32),
            state_out,
            out((steps, 8, LANES), F32, "block"),
            packet_out,
        ],
        [
            pltpu.VMEM((8 + BLOCK, channels), F32),
            pltpu.VMEM((inner, LANES), F32),
            pltpu.VMEM((8, LANES), F32),
        ],
        micros=20,
    )
    packets = [(shifted(packet, "ctx", step), "whole") for step in range(1, ctx_count)]
    wz_spec = pl.BlockSpec((width, inner), lambda i: (0, 0))
    wo_spec = pl.BlockSpec((width, inner), lambda i: (0, 1))
    w2, z, dn = call(
        functools.partial(gate_matmul_kernel, counts, dp_count),
        steps,
        info,
        [(value, "whole") for value in w2_shards] + [(normed, "rows"), (cotangent, "rows")],
        [out((width, 2 * inner), BF16, "whole"), row_out(inner, BF16), row_out(inner, F32)],
        micros=7,
    )
    y, hb, h, stat = call(
        functools.partial(apply_kernel, counts, len(packets)),
        steps,
        info,
        packets
        + [
            (entry, "block"),
            (decay, "block"),
            (cum, "rows"),
            (bc, "rows"),
            (ypart, "rows"),
            (z, "rows"),
            (dn, "rows"),
            (par, "whole"),
            (spread, "whole"),
        ],
        [
            row_out(inner, F32),
            out((steps, inner, LANES), BF16, "block"),
            state_out,
            out((8, rows), F32, "lanes"),
        ],
        [pltpu.VMEM((inner, LANES), F32)],
        micros=8,
    )
    stat = lax.psum(stat, "tp")
    inner_all = inner * lax.axis_size("tp")
    half = width // 2
    keep, send, gwo, small_gate, dy, dz, de, exits, packet = call(
        functools.partial(gate_back_kernel, counts, inner_all),
        steps,
        info,
        [
            (stat, "lanes"),
            (y, "rows"),
            (z, "rows"),
            (dn, "rows"),
            (cotangent, "rows"),
            (cum, "rows"),
            (bc, "rows"),
            (xc, "rows"),
            (hb, "block"),
            (decay, "block"),
            (w2, wo_spec),
            (par, "whole"),
            (spread, "whole"),
        ],
        [
            row_out(half, BF16),
            row_out(half, BF16),
            out((width, inner), BF16, "whole"),
            out((8, inner), F32, "whole"),
            row_out(inner, BF16),
            row_out(inner, BF16),
            row_out(LANES, F32),
            state_out,
            packet_out,
        ],
        [
            pltpu.VMEM((width, inner), F32),
            pltpu.VMEM((inner, LANES), F32),
            pltpu.VMEM((8, LANES), F32),
        ],
        reverse=True,
        micros=15,
    )
    packets = [(shifted(packet, "ctx", -step), "whole") for step in range(1, ctx_count)]
    with jax.named_scope("layer_out"):
        received = swapped(send)
        own_inputs = lax.dynamic_slice_in_dim(tokens, tp_index * half, half, 1).astype(F32)
        valid = (jnp.arange(rows) < fill).astype(F32)[:, None]
        layer_out = own_inputs + (keep.astype(F32) + received.astype(F32)) * valid
    dxc, dcq, dbq, row_sums, col_sums, dnz, *g2 = call(
        functools.partial(intra_back_kernel, counts, heads, dp_count),
        steps,
        info,
        [
            (dy, "rows"),
            (dz, "rows"),
            (xc, "rows"),
            (bc, "rows"),
            (cum, "rows"),
            (pre_step, "rows"),
            (hb, "block"),
            (normed, "rows"),
            (w2, wz_spec),
            (gwo, "whole"),
            (par, "whole"),
            (spread, "whole"),
        ],
        [
            row_out(inner, F32),
            row_out(LANES, F32),
            row_out(LANES, F32),
            row_out(LANES, F32),
            row_out(LANES, F32),
            row_out(width, F32),
        ]
        + [out((width // parts, 2 * inner), BF16, "whole")] * parts,
        [pltpu.VMEM((width, inner), F32), pltpu.VMEM((LANES, BLOCK), F32)],
        micros=18,
    )
    with jax.named_scope("reduce_gate_weights"):
        total2 = reduce_rows(g2)
        total2 = exchanged(total2, "ctx") if parts > 1 else [total2]
    partial, halo_grad, *g1 = call(
        functools.partial(state_back_kernel, counts, heads, dp_count, len(packets), parts),
        steps,
        info,
        packets
        + [
            (exits, "block"),
            (h, "block"),
            (xc, "rows"),
            (bc, "rows"),
            (cum, "rows"),
            (pre_step, "rows"),
            (de, "rows"),
            (dxc, "rows"),
            (dcq, "rows"),
            (dbq, "rows"),
            (row_sums, "rows"),
            (col_sums, "rows"),
            (decay, "block"),
            (v, "rows"),
            (v, "tail"),
            (halo_v, "whole"),
            (halo_normed, "whole"),
            (halo, "whole"),
            (tokens, "rows"),
            (normed, "rows"),
            (dnz, "rows"),
            (small_gate, "whole"),
            (w1, "whole"),
            (par, "whole"),
            (dtp, "whole"),
            (spread, "whole"),
        ],
        [
            row_out(width, BF16),
            out((8, width), F32, "whole"),
        ]
        + [out((width // parts, channels + LANES), BF16, "whole")] * parts,
        [
            pltpu.VMEM((inner, LANES), F32),
            pltpu.VMEM((8, LANES), F32),
            pltpu.VMEM((8 + BLOCK, channels), F32),
            pltpu.VMEM((8 + BLOCK, channels), F32),
            pltpu.VMEM((width, channels + LANES), F32),
            pltpu.VMEM((8, channels), F32),
        ],
        reverse=True,
        micros=28,
    )
    other = swapped(partial)
    size = ctx_count * 2
    back = [(s, s - 2) for s in range(2, size)]
    cross = [(s, (s - 2) ^ 1) for s in range(2, size)]
    halo_a = lax.ppermute(halo_grad, ("ctx", "tp"), back)
    halo_b = lax.ppermute(halo_grad, ("ctx", "tp"), cross)
    with jax.named_scope("reduce_input_weights"):
        total1 = reduce_rows(g1)
        across = swapped(total1[:, inner:])
        lane = jnp.arange(3 * LANES) - 2 * LANES
        both = (lane < 0) | (lane == NORM) | ((lane >= STATE_TAPS) & (lane < BY_HEAD))
        summed = total1[:, inner:] + jnp.where(both[None, :], across, 0)
        total1 = jnp.concatenate([total1[:, :inner], summed], axis=1)
        total1 = exchanged(total1, "ctx") if parts > 1 else [total1]
    (grad_tokens,) = call(
        functools.partial(finish_kernel, counts),
        steps,
        info,
        [
            (partial, "rows"),
            (other, "rows"),
            (halo_a, "whole"),
            (halo_b, "whole"),
            (tokens, "rows"),
            (cotangent, "rows"),
            (par, "whole"),
        ],
        [row_out(width, F32)],
        micros=5,
    )
    each = HEAD // dp_count
    part_bc = bias_bc.shape[0]
    tall = -(-shard // LANES) * LANES

    def final(*sizes):
        return out(sizes, F32, "whole")

    grad_wz, grad_wo = call(
        functools.partial(unpack_gate_kernel, counts, parts),
        1,
        info,
        [(value, "whole") for value in total2],
        [final(shard, inner), final(shard, inner)],
        micros=2,
    )
    (
        grad_wx, grad_wbc, grad_wdt, grad_norm, grad_taps, grad_bias, grad_state_taps, grad_state_bias,
        grad_dt_bias, grad_a_log, grad_skip, grad_gate,
    ) = call(
        functools.partial(unpack_input_kernel, counts, heads, parts),
        1,
        info,
        [(value, "whole") for value in total1],
        [
            final(shard, inner),
            final(shard, 2 * LANES),
            final(heads, shard),
            final(1, shard),
            final(heads, CONV, each),
            final(heads, each),
            final(CONV, part_bc),
            final(1, part_bc),
            final(1, heads),
            final(1, heads),
            final(1, heads),
            final(heads, each),
        ],
        [pltpu.VMEM((tall, channels + LANES), F32)],
        micros=2,
    )
    return (
        layer_out,
        grad_tokens,
        grad_norm[0],
        grad_wz,
        grad_wx,
        grad_wbc,
        grad_wdt.T,
        grad_taps.transpose(1, 0, 2),
        grad_bias,
        grad_state_taps,
        grad_state_bias[0],
        grad_dt_bias[0],
        grad_a_log[0],
        grad_skip[0],
        grad_gate,
        grad_wo.T,
    )


def solution(mesh):
    shards = P(("dp", "ctx"), None)
    return jax.shard_map(
        body,
        mesh=mesh,
        in_specs=(
            shards,
            shards,
            P("dp", None),
            P("dp", None),
            P("dp"),
            P("dp", "tp"),
            P("dp", "tp"),
            P("dp", None),
            P("dp", "tp"),
            P(None, "tp", "dp"),
            P("tp", "dp"),
            P(None, "dp"),
            P("dp"),
            P("tp"),
            P("tp"),
            P("tp"),
            P("tp", "dp"),
            P("tp", "dp"),
        ),
        out_specs=(
            P(("dp", "ctx"), "tp"),
            shards,
            P("dp"),
            P("dp", "tp"),
            P("dp", "tp"),
            P("dp", None),
            P("dp", "tp"),
            P(None, "tp", "dp"),
            P("tp", "dp"),
            P(None, "dp"),
            P("dp"),
            P("tp"),
            P("tp"),
            P("tp"),
            P("tp", "dp"),
            P("tp", "dp"),
        ),
        check_vma=False,
    )
```

```python
import functools

import jax
import jax.numpy as jnp
from jax import lax
from jax.experimental import pallas as pl
from jax.experimental.pallas import tpu as pltpu
from jax.sharding import PartitionSpec as P

CONV = 4
BLOCK = 256
HEAD = 64
LANES = 128
EPS = 1e-05
VMEM = 56 * 1024 * 1024
F32 = jnp.float32
BF16 = jnp.bfloat16


def dot(left, right):
    return jnp.dot(left, right, preferred_element_type=F32)


def dot_tn(left, right):
    return lax.dot_general(left, right, (((0,), (0,)), ((), ())), preferred_element_type=F32)


def dot_nt(left, right):
    return lax.dot_general(left, right, (((1,), (1,)), ((), ())), preferred_element_type=F32)


def dot_exact(left, right):
    return jnp.dot(left, right, preferred_element_type=F32, precision=lax.Precision.HIGHEST)


def iota(shape, dim):
    return lax.broadcasted_iota(jnp.int32, shape, dim)


def sigmoid(value):
    return 1.0 / (1.0 + jnp.exp(-value))


def softplus(value):
    return jnp.maximum(value, 0.0) + jnp.log1p(jnp.exp(-jnp.abs(value)))


def split(value):
    high = value.astype(BF16)
    return high, (value - high.astype(F32)).astype(BF16)


def expand(value, spread):
    return dot(jnp.concatenate(split(value), axis=1), spread[...])


def reduce_heads(value, spread):
    high, low = split(value)
    pick = spread[:LANES, :]
    return dot_nt(high, pick) + dot_nt(low, pick)


def head_column(row, channels):
    shape = (channels, LANES)
    return jnp.sum(jnp.where(iota(shape, 0) // HEAD == iota(shape, 1), row, 0.0), axis=1, keepdims=True)


def xor(value, mask):
    return jnp.bitwise_xor(value, jnp.int32(mask))


class Place:
    def __init__(self, info, counts):
        devices, sequences = counts
        own = info[devices + sequences]
        self.ctx = own
        self.tp = info[devices + sequences + 1]
        self.dp = info[devices + sequences + 2]
        self.fill = jnp.int32(0)
        self.first = jnp.int32(0)
        for device in range(devices):
            rows = info[device] * BLOCK
            self.fill = self.fill + jnp.where(own == device, rows, 0)
            self.first = self.first + jnp.where(own > device, rows, 0)
        self.ends = []
        total = jnp.int32(0)
        for sequence in range(sequences - 1):
            total = total + info[devices + sequence]
            self.ends.append(total)

    def of(self, position):
        found = (position >= self.ends[0]).astype(jnp.int32)
        for end in self.ends[1:]:
            found = found + (position >= end).astype(jnp.int32)
        return jnp.where(position < 0, -1, found)

    def rows(self, index):
        return self.of(self.first + jnp.minimum(index, self.fill - 1))

    def before(self, block):
        position = self.first + jnp.minimum(block * BLOCK, self.fill) - 1
        found = jnp.int32(0)
        for end in self.ends:
            found = found + jnp.where(position >= end, 1, 0)
        return jnp.where(position < 0, -1, found)

    def last(self, block):
        position = self.first + jnp.minimum(block * BLOCK + BLOCK - 1, self.fill - 1)
        found = jnp.int32(0)
        for end in self.ends:
            found = found + jnp.where(position >= end, 1, 0)
        return found

    def column(self, block, shift=0):
        return self.rows(block * BLOCK + shift + iota((BLOCK, 1), 0))

    def valid(self, block):
        return (block * BLOCK + iota((BLOCK, 1), 0) < self.fill).astype(F32)

    def keep(self, block):
        across = self.rows(block * BLOCK + iota((1, BLOCK), 1))
        return (self.column(block) == across) & (iota((BLOCK, BLOCK), 0) >= iota((BLOCK, BLOCK), 1))


def step_sizes(place, block, pre_step, heads):
    lane = iota((BLOCK, LANES), 1)
    return jnp.where(lane < heads, softplus(pre_step), 0.0) * place.valid(block)


def end_weights(place, block, cum):
    same = (place.column(block) == place.last(block)).astype(F32)
    return jnp.exp(cum[BLOCK - 1 :, :] - cum) * same


def enter_weights(place, block, cum):
    return jnp.exp(cum) * (place.column(block) == place.before(block)).astype(F32)


def block_decay(place, block, cum):
    return jnp.exp(cum[BLOCK - 1 :, :]) * jnp.where(place.last(block) == place.before(block), 1.0, 0.0)


def decay_kernel(keep, cum, cum_rows, head):
    return jnp.exp(jnp.where(keep, cum[:, head : head + 1] - cum_rows[head : head + 1, :], -1e30))


def both_halves(pair):
    lane = iota(pair.shape, 1)
    zero = jnp.zeros_like(pair)
    return [jnp.where(lane < HEAD, pair, zero), jnp.where(lane >= HEAD, pair, zero)]


def same_mask(place, block, tap):
    return (place.column(block, tap - (CONV - 1)) == place.column(block)).astype(F32)


def conv_pre(place, block, ext, par, channels):
    total = par[4:5, :channels]
    for tap in range(CONV):
        first = 8 - (CONV - 1) + tap
        total = total + par[tap : tap + 1, :channels] * ext[first : first + BLOCK, :] * same_mask(
            place, block, tap
        )
    return total


def state_packet(state, decay):
    high, low = split(decay)
    row = iota((16, LANES), 0)
    tail = jnp.where(row == 0, high.astype(F32), jnp.where(row == 1, low.astype(F32), 0.0))
    return jnp.concatenate([state.astype(BF16), tail.astype(BF16)], axis=0)


def merge_packets(packets, inner):
    total = jnp.zeros((inner, LANES), F32)
    for packet in reversed(packets):
        tail = packet[inner : inner + 16, :].astype(F32)
        decay = tail[0:1, :] + tail[1:2, :]
        total = packet[:inner, :].astype(F32) + head_column(decay, inner) * total
    return total


def normalise(rows, gain):
    inv = lax.rsqrt(jnp.mean(rows * rows, axis=1, keepdims=True) + EPS)
    return rows * inv, inv, (rows * inv * gain).astype(BF16)


def piece_rows(place, dp_count, parts, rows):
    for part in range(parts):
        for block in range(dp_count):
            owner = xor(place.dp, block) * parts + (xor(place.ctx, part) if parts > 1 else 0)
            yield part, block, pl.multiple_of(owner * rows, rows)


def join_pieces(place, dp_count, parts, whole):
    columns = parts[0].shape[1]
    if len(parts) == 1:
        whole[:, :columns] = parts[0][...]
        return
    rows = parts[0].shape[0] // dp_count
    for part, block, first in piece_rows(place, dp_count, len(parts), rows):
        whole[pl.ds(first, rows), :columns] = parts[part][block * rows : (block + 1) * rows, :]


def cut_pieces(place, dp_count, whole, parts, lanes):
    if len(parts) == 1:
        parts[0][:, lanes] = whole[...].astype(BF16)
        return
    rows = parts[0].shape[0] // dp_count
    for part, block, first in piece_rows(place, dp_count, len(parts), rows):
        parts[part][block * rows : (block + 1) * rows, lanes] = whole[pl.ds(first, rows), :].astype(BF16)


def join_parameters(place, vectors, skip, heads, par, w1):
    shard = vectors[0].shape[1]
    each = HEAD // len(vectors)
    inner = heads * HEAD
    by_channel = jnp.zeros((16, inner), F32)
    in_order = jnp.zeros((16, shard * len(vectors)), F32)
    by_state = jnp.zeros((16, 2 * LANES), F32)
    states = 2 * LANES // len(vectors)
    eye = (iota((16, LANES), 0) == iota((16, LANES), 1)).astype(BF16)
    for block, vector in enumerate(vectors):
        owner = xor(place.dp, block)
        first = pl.multiple_of(owner * shard, shard)
        w1[pl.ds(first, shard), inner + 2 * LANES :] = dot_tn(vector[16:32, :], eye).astype(BF16)
        source, target = iota((shard, inner), 0), iota((shard, inner), 1)
        pick = target == source // each * HEAD + owner * each + source % each
        by_channel = by_channel + dot(vector[0:16, :], pick.astype(BF16))
        source, target = iota((shard, in_order.shape[1]), 0), iota((shard, in_order.shape[1]), 1)
        in_order = in_order + dot(vector[0:16, :], (target == owner * shard + source).astype(BF16))
        source, target = iota((shard, 2 * LANES), 0), iota((shard, 2 * LANES), 1)
        pick = (target == owner * states + source) & (source < states)
        by_state = by_state + dot(vector[0:16, :], pick.astype(BF16))
    par[...] = jnp.zeros_like(par)
    par[0:5, :inner] = by_channel[0:5, :]
    par[0:5, inner:] = by_state[8:13, :]
    par[5:6, : in_order.shape[1]] = in_order[5:6, :]
    par[6:7, :inner] = by_channel[6:7, :]
    par[7:8, :inner] = skip


TAPS, NORM, GATE, STATE_TAPS, BY_HEAD = 12, 17, 18, 20, 25


def pack_parameters(dp_count, heads, small, gate, skip):
    inner = heads * HEAD
    each = HEAD // dp_count
    shard = inner // dp_count
    states = 2 * LANES // dp_count

    def lanes(pieces, columns):
        rows, at = [], 0
        for first, value in pieces:
            if first > at:
                rows.append(jnp.zeros((first - at, columns), F32))
            rows.append(value)
            at = first + value.shape[0]
        rows.append(jnp.zeros((LANES - at, columns), F32))
        return jnp.concatenate(rows, axis=0)

    source, target = iota((inner, inner), 0), iota((inner, inner), 1)
    inside = source % shard
    pick = target == inside // each * HEAD + source // shard * each + inside % each
    by_channel = lanes([(TAPS, small[0:5, :inner]), (GATE, gate)], inner)
    total = dot_nt(pick.astype(BF16), by_channel.astype(BF16))
    total = total + lanes([(NORM, small[5:6, :inner])], inner).T
    source, target = iota((inner, 2 * LANES), 0), iota((inner, 2 * LANES), 1)
    inside = source % shard
    pick = (target == source // shard * states + inside) & (inside < states)
    by_state = lanes([(STATE_TAPS, small[0:5, inner : inner + 2 * LANES])], 2 * LANES)
    total = total + dot_nt(pick.astype(BF16), by_state.astype(BF16))
    source, target = iota((inner, LANES), 0) % shard, iota((inner, LANES), 1)
    for index, row in enumerate((small[6:7, :LANES], small[7:8, :LANES], skip)):
        pick = (source == target + index * heads) & (target < heads)
        total = total + dot_nt(pick.astype(BF16), lanes([(BY_HEAD, row)], LANES).astype(BF16))
    return total


def forward_kernel(
    counts, heads, dp_count, part_count, info, *refs
):
    vectors = refs[:dp_count]
    parts = refs[dp_count : dp_count + part_count]
    (
        tok, halo, dtp, spread,
        w1, par, normed_o, halo_normed_o, halo_v_o, v_o, xc_o, bc_o, ypart_o, pre_o, cum_o, entry_o, decay_o,
        packet_o, ext, run, factor,
    ) = refs[dp_count + part_count :]
    forward_block(
        counts, heads, info, vectors, parts, tok, halo, w1, par, dtp, spread,
        normed_o, halo_normed_o, halo_v_o, v_o, xc_o, bc_o, ypart_o, pre_o, cum_o, entry_o, decay_o, packet_o,
        ext, run, factor,
    )


def forward_block(
    counts, heads, info, vectors, parts, tok, halo, w1, par, dtp, spread,
    normed_o, halo_normed_o, halo_v_o, v_o, xc_o, bc_o, ypart_o, pre_o, cum_o, entry_o, decay_o, packet_o,
    ext, run, factor,
):
    block = pl.program_id(0)
    place = Place(info, counts)
    inner = heads * HEAD
    state = LANES
    channels = inner + 2 * state
    width = tok.shape[1]

    @pl.when(block == 0)
    def _():
        join_pieces(place, len(vectors), parts, w1)
        join_parameters(place, vectors, expand(dtp[...], spread)[2:3, :], heads, par, w1)

    gain = par[5:6, :width]
    _, _, normed = normalise(tok[...].astype(F32), gain)
    normed_o[...] = normed

    @pl.when(block == 0)
    def _():
        _, _, before = normalise(halo[...].astype(F32), gain)
        halo_normed_o[...] = before
        raw = dot(before, w1[:, :channels]).astype(BF16).astype(F32)
        ext[0:8, :] = raw[8:16, :]
        halo_v_o[...] = raw[8:16, :]
        run[...] = jnp.zeros_like(run)
        factor[...] = jnp.ones_like(factor)

    @pl.when(block > 0)
    def _():
        ext[0:8, :] = ext[BLOCK : BLOCK + 8, :]

    raw = dot(normed, w1[...])
    v = raw[:, :channels].astype(BF16)
    v_o[...] = v
    ext[8 : 8 + BLOCK, :] = v.astype(F32)
    pre = conv_pre(place, block, ext, par, channels)
    act = (pre * sigmoid(pre)).astype(BF16)
    xc = act[:, :inner]
    bq = act[:, inner : inner + state]
    cq = act[:, inner + state :]
    xc_o[...] = xc
    bc_o[...] = act[:, inner:]
    pre_step = raw[:, channels:].astype(BF16).astype(F32) + dtp[0:1, :]
    pre_o[...] = pre_step
    step = step_sizes(place, block, pre_step, heads)
    tri = (iota((BLOCK, BLOCK), 0) >= iota((BLOCK, BLOCK), 1)).astype(F32)
    cum = dot_exact(tri, -dtp[1:2, :] * step)
    cum_o[...] = cum
    cum_rows = cum.T
    step_rows = step.T
    gram = dot_nt(cq, bq)
    keep = place.keep(block)
    for pair in range(heads // 2):
        lanes = slice(pair * LANES, (pair + 1) * LANES)
        mixing = []
        for head in (2 * pair, 2 * pair + 1):
            weight = decay_kernel(keep, cum, cum_rows, head) * step_rows[head : head + 1, :]
            mixing.append((gram * weight).astype(BF16))
        x_pair = xc[:, lanes]
        y_pair = dot(jnp.concatenate(mixing, axis=1), jnp.concatenate(both_halves(x_pair), axis=0))
        ypart_o[:, lanes] = y_pair + par[7:8, lanes] * x_pair.astype(F32)
    weighted = (expand(end_weights(place, block, cum) * step, spread) * xc.astype(F32)).astype(BF16)
    block_state = dot_tn(weighted, bq)
    decay = block_decay(place, block, cum)
    entry_o[0] = run[...]
    total = head_column(decay, inner) * run[...] + block_state
    run[...] = total
    before = factor[0:1, :]
    row = iota((8, LANES), 0)
    decay_o[0] = jnp.where(row == 0, decay, jnp.where(row == 1, before, 0.0))
    after = before * decay
    factor[...] = jnp.broadcast_to(after, factor.shape)

    @pl.when(block == pl.num_programs(0) - 1)
    def _():
        packet_o[...] = state_packet(total, after)


def gate_matmul_kernel(counts, info, normed, cot, w2, z_o, dn_o):
    block = pl.program_id(0)
    place = Place(info, counts)
    inner = z_o.shape[1]
    z_o[...] = dot(normed[...], w2[:, :inner]).astype(BF16)
    grad = (cot[...].astype(F32) * place.valid(block)).astype(BF16)
    dn_o[...] = dot(grad, w2[:, inner:])


def apply_kernel(counts, packet_count, info, *refs):
    packets = refs[:packet_count]
    entry, decay, cum, bc, ypart, z, dn, par, spread, y_o, hb_o, h_o, stat_o, start = refs[packet_count:]
    block = pl.program_id(0)
    place = Place(info, counts)
    inner = z.shape[1]

    @pl.when(block == 0)
    def _():
        start[...] = merge_packets([packet[...] for packet in packets], inner)

    state = entry[0] + head_column(decay[0, 1:2, :], inner) * start[...]
    h_o[0] = state
    low = state.astype(BF16)
    hb_o[0] = low
    cq = bc[:, LANES:]
    y = ypart[...] + expand(enter_weights(place, block, cum[...]), spread) * dot_nt(cq, low)
    y_o[...] = y
    gate = z[...].astype(F32)
    gated = y * gate * sigmoid(gate)
    squares = jnp.sum(gated * gated, axis=1, keepdims=True)
    cross = jnp.sum(par[6:7, :inner] * dn[...] * gated, axis=1, keepdims=True)
    lane = iota((BLOCK, LANES), 1)
    both = jnp.where(lane == 0, squares, jnp.where(lane == 1, cross, 0.0))
    stat_o[...] = both.T[0:8, :]


def gate_back_kernel(
    counts, inner_all, info, stat, y, z, dn, cot, cum, bc, xc, hb, decay, normed, wo, par, spread,
    keep_o, send_o, g2_o, small_o, dy_o, dz_o, de_o, exit_o, packet_o,
    acc, run, factor,
):
    step = pl.program_id(0)
    block = pl.num_programs(0) - 1 - step
    place = Place(info, counts)
    inner = z.shape[1]
    width = cot.shape[1]
    half = width // 2

    @pl.when(step == 0)
    def _():
        acc[...] = jnp.zeros_like(acc)
        run[...] = jnp.zeros_like(run)
        factor[...] = jnp.ones_like(factor)
        small_o[...] = jnp.zeros_like(small_o)

    column = jnp.concatenate([stat[...], jnp.zeros((LANES - 8, BLOCK), F32)], axis=0).T
    inv = lax.rsqrt(column[:, 0:1] / inner_all + EPS)
    cross = column[:, 1:2]
    gain = par[6:7, :inner]
    gate = z[...].astype(F32)
    sig = sigmoid(gate)
    silu = gate * sig
    mixed = y[...]
    gated = mixed * silu
    normal = (gated * inv * gain).astype(BF16)
    own = pl.multiple_of(place.tp * half, half)
    other = pl.multiple_of((1 - place.tp) * half, half)
    keep_o[...] = dot_nt(normal, wo[pl.ds(own, half), :]).astype(BF16)
    send_o[...] = dot_nt(normal, wo[pl.ds(other, half), :]).astype(BF16)
    grad = (cot[...].astype(F32) * place.valid(block)).astype(BF16)
    acc[:, inner:] += dot_tn(grad, normal)
    back = dn[...]
    grad_gated = inv * (gain * back) - gated * (inv * inv * inv) * (cross / inner_all)
    dy = (grad_gated * silu).astype(BF16)
    dy_o[...] = dy
    dz = (grad_gated * mixed * sig * (1.0 + gate * (1.0 - sig))).astype(BF16)
    dz_o[...] = dz
    acc[:, :inner] += dot_tn(normed[...], dz)
    dy_float = dy.astype(F32)
    cq = bc[:, LANES:]
    read = dot_nt(cq, hb[0])
    de_o[...] = reduce_heads(dy_float * read, spread)
    small_o[0:1, :] += jnp.sum(back * gated * inv, axis=0, keepdims=True)
    small_o[1:2, :] += jnp.sum(dy_float * xc[...].astype(F32), axis=0, keepdims=True)
    dq = (expand(enter_weights(place, block, cum[...]), spread) * dy_float).astype(BF16)
    exit_o[0] = run[...]
    here = decay[0, 0:1, :]
    total = head_column(here, inner) * run[...] + dot_tn(dq, cq)
    run[...] = total
    after = factor[0:1, :] * here
    factor[...] = jnp.broadcast_to(after, factor.shape)

    @pl.when(step == pl.num_programs(0) - 1)
    def _():
        packet_o[...] = state_packet(total, after)
        g2_o[...] = acc[...].astype(BF16)


def intra_back_kernel(
    counts, heads, info, dy, dz, xc, bc, cum, pre_step, hb, wz, par, spread,
    dxc_o, dcq_o, dbq_o, rows_o, cols_o, dnz_o,
    columns,
):
    block = pl.program_id(0)
    place = Place(info, counts)

    @pl.when(block == 0)
    def _():
        columns[...] = jnp.zeros_like(columns)

    bq = bc[:, :LANES]
    cq = bc[:, LANES:]
    cums = cum[...]
    step = step_sizes(place, block, pre_step[...], heads)
    cum_rows = cums.T
    step_rows = step.T
    gram = dot_nt(cq, bq)
    keep = place.keep(block)
    lane = iota((BLOCK, LANES), 1)
    grad_gram = jnp.zeros((BLOCK, BLOCK), F32)
    sums = jnp.zeros((BLOCK, LANES), F32)
    for pair in range(heads // 2):
        lanes = slice(pair * LANES, (pair + 1) * LANES)
        dy_pair = dy[:, lanes]
        x_pair = xc[:, lanes]
        halves = jnp.concatenate(both_halves(dy_pair), axis=0)
        grad_mixing = dot_nt(halves, x_pair)
        mixing = []
        for side in range(2):
            head = 2 * pair + side
            grad_m = grad_mixing[side * BLOCK : (side + 1) * BLOCK, :]
            kernel = decay_kernel(keep, cums, cum_rows, head)
            step_row = step_rows[head : head + 1, :]
            weight = kernel * step_row
            mixing.append((gram * weight).astype(BF16))
            grad_gram = grad_gram + grad_m * weight
            part = grad_m * gram * kernel
            columns[head : head + 1, :] = jnp.sum(part, axis=0, keepdims=True)
            sums = sums + jnp.where(lane == head, jnp.sum(part * step_row, axis=1, keepdims=True), 0.0)
        dx_pair = dot_tn(jnp.concatenate(mixing, axis=0), halves)
        dxc_o[:, lanes] = dx_pair + par[7:8, lanes] * dy_pair.astype(F32)
    grad_low = grad_gram.astype(BF16)
    dq = (expand(enter_weights(place, block, cums), spread) * dy[...].astype(F32)).astype(BF16)
    dcq_o[...] = dot(grad_low, bq) + dot(dq, hb[0])
    dbq_o[...] = dot_tn(grad_low, cq)
    rows_o[...] = sums
    cols_o[...] = columns[...].T
    dnz_o[...] = dot_nt(dz[...], wz[...])


def state_back_kernel(counts, heads, dp_count, packet_count, part_count, info, *refs):
    packets = refs[:packet_count]
    (
        exits, h, xc, bc, cum, pre_step, de, dxc, dcq, dbq, rows, cols, decay, v, v_tail, halo_v, halo_normed,
        halo, tok, normed, dnz, small_gate, w1, par, dtp, spread,
        dn_o, dnh_o,
    ) = refs[packet_count : -6 - part_count]
    parts = refs[-6 - part_count : -6]
    start, factor, ext, grad_ext, acc, small_o = refs[-6:]
    step_id = pl.program_id(0)
    block = pl.num_programs(0) - 1 - step_id
    place = Place(info, counts)
    inner = heads * HEAD
    channels = inner + 2 * LANES
    width = tok.shape[1]

    @pl.when(step_id == 0)
    def _():
        start[...] = merge_packets([packet[...] for packet in packets], inner)
        factor[...] = jnp.ones_like(factor)
        acc[...] = jnp.zeros_like(acc)
        grad_ext[...] = jnp.zeros_like(grad_ext)
        small_o[...] = jnp.zeros_like(small_o)

    here = decay[0, 0:1, :]
    before = factor[0:1, :]
    grad_state = exits[0] + head_column(before, inner) * start[...]
    factor[...] = jnp.broadcast_to(before * here, factor.shape)
    shape = (inner, LANES)
    overlap = jnp.sum(grad_state * h[0], axis=1, keepdims=True)
    grad_decay = jnp.sum(
        jnp.where(iota(shape, 0) // HEAD == iota(shape, 1), overlap, 0.0), axis=0, keepdims=True
    )
    low = grad_state.astype(BF16)
    bq = bc[:, :LANES]
    cums = cum[...]
    x_float = xc[...].astype(F32)
    pre_dt = pre_step[...]
    valid = place.valid(block)
    step = step_sizes(place, block, pre_dt, heads)
    end_kernel = end_weights(place, block, cums)
    end_weight = end_kernel * step
    end_wide = expand(end_weight, spread)
    spread_b = dot_nt(bq, low)
    grad_x = dxc[...] + end_wide * spread_b
    grad_end = reduce_heads(x_float * spread_b, spread)
    grad_b = dbq[...] + dot((x_float * end_wide).astype(BF16), low)
    end_part = grad_end * end_weight
    last = iota((BLOCK, LANES), 0) == BLOCK - 1
    grad_cum = rows[...] - cols[...] * step - end_part + de[...] * enter_weights(place, block, cums)
    grad_cum = grad_cum + jnp.where(
        last, jnp.sum(end_part, axis=0, keepdims=True) + grad_decay * here, 0.0
    )
    upper = (iota((BLOCK, BLOCK), 0) <= iota((BLOCK, BLOCK), 1)).astype(F32)
    grad_log = dot_exact(upper, grad_cum)
    rates = dtp[1:2, :]
    grad_step = cols[...] + grad_end * end_kernel - rates * grad_log
    heads_lane = iota((BLOCK, LANES), 1) < heads
    grad_pre_dt = jnp.where(heads_lane, grad_step * sigmoid(pre_dt), 0.0) * valid
    small_o[6:7, :LANES] += jnp.sum(grad_pre_dt, axis=0, keepdims=True)
    small_o[7:8, :LANES] += jnp.sum(grad_log * (-rates * step), axis=0, keepdims=True)

    ext[8 : 8 + BLOCK, :] = v[...].astype(F32)

    @pl.when(block == 0)
    def _():
        ext[0:8, :] = halo_v[...]

    @pl.when(block > 0)
    def _():
        ext[0:8, :] = v_tail[...].astype(F32)[8:16, :]

    pre = conv_pre(place, block, ext, par, channels)
    sig = sigmoid(pre)
    slope = sig * (1.0 + pre * (1.0 - sig))
    grad_pre = jnp.concatenate([grad_x, grad_b, dcq[...]], axis=1) * slope
    small_o[4:5, :] += jnp.sum(grad_pre, axis=0, keepdims=True)
    carry = grad_ext[0:8, :]
    grad_ext[0 : BLOCK, :] = jnp.zeros((BLOCK, channels), F32)
    grad_ext[BLOCK : BLOCK + 8, :] = carry
    for tap in range(CONV):
        first = 8 - (CONV - 1) + tap
        masked = grad_pre * same_mask(place, block, tap)
        small_o[tap : tap + 1, :] += jnp.sum(masked * ext[first : first + BLOCK, :], axis=0, keepdims=True)
        grad_ext[first : first + BLOCK, :] += par[tap : tap + 1, :channels] * masked
    packed = jnp.concatenate([grad_ext[8 : 8 + BLOCK, :].astype(BF16), grad_pre_dt.astype(BF16)], axis=1)
    partial = dnz[...] + dot_nt(packed, w1[...])
    dn_o[...] = partial.astype(BF16)
    acc[...] += dot_tn(normed[...], packed)
    gain = par[5:6, :width]
    scaled, _, _ = normalise(tok[...].astype(F32), gain)
    small_o[5:6, :width] += jnp.sum(partial * scaled, axis=0, keepdims=True)

    @pl.when(block == 0)
    def _():
        back = jnp.concatenate([jnp.zeros((8, channels), F32), grad_ext[0:8, :]], axis=0).astype(BF16)
        halo_grad = dot_nt(back, w1[:, :channels])
        dnh_o[...] = halo_grad[8:16, :]
        halo_scaled, _, _ = normalise(halo[...].astype(F32), gain)
        small_o[5:6, :width] += jnp.sum(halo_grad * halo_scaled, axis=0, keepdims=True)
        acc[:, :channels] += dot_tn(halo_normed[...], back)
        skip = reduce_heads(jnp.broadcast_to(small_gate[1:2, :], (8, inner)), spread)[0:1, :]
        acc[:, channels:] += pack_parameters(dp_count, heads, small_o, small_gate[0:1, :], skip)
        cut_pieces(place, dp_count, acc, parts, slice(0, channels + LANES))


def finish_kernel(counts, info, own, other, halo_a, halo_b, tok, cot, par, grad_o):
    block = pl.program_id(0)
    place = Place(info, counts)
    width = tok.shape[1]
    grad = own[...].astype(F32) + other[...].astype(F32)
    is_last = jnp.where((block + 1) * BLOCK == place.fill, 1.0, 0.0)
    halo = (halo_a[...] + halo_b[...]) * is_last
    grad = jnp.concatenate([grad[: BLOCK - 8, :], grad[BLOCK - 8 :, :] + halo], axis=0)
    inputs = tok[...].astype(F32)
    inv = lax.rsqrt(jnp.mean(inputs * inputs, axis=1, keepdims=True) + EPS)
    scaled = par[5:6, :width] * grad
    inner_dot = jnp.sum(scaled * inputs, axis=1, keepdims=True)
    grad_o[...] = (
        inv * scaled - inputs * (inv * inv * inv) * (inner_dot / width) + cot[...].astype(F32)
    )


def unpack_input_kernel(counts, heads, part_count, info, *refs):
    parts = refs[:part_count]
    (
        wx_o, wbc_o, wdt_o, norm_o, taps_o, bias_o, state_taps_o, state_bias_o, dt_bias_o, a_log_o, skip_o,
        gate_o, wide,
    ) = refs[part_count:]
    place = Place(info, counts)
    shard, inner = wx_o.shape
    channels = inner + 2 * LANES
    rows = shard // part_count
    for part in range(part_count):
        first = pl.multiple_of(xor(place.ctx, part) * rows, rows) if part_count > 1 else 0
        wide[pl.ds(first, rows), :] = parts[part][...].astype(F32)
    wx_o[...] = wide[:shard, :inner]
    wbc_o[...] = wide[:shard, inner:channels]
    lines = wide[:, channels:].T
    wdt_o[...] = lines[:heads, :shard]
    each = gate_o.shape[1]
    size = lines.shape[1]
    source = iota((16, size), 1)
    inside = (source // each == iota((16, size), 0)) & (source < shard)
    place_in = (iota((size, LANES), 0) % each == iota((size, LANES), 1)).astype(BF16)

    def by_head(line):
        row = jnp.where(inside, lines[line : line + 1, :], 0.0).astype(BF16)
        return dot(row, place_in)[:heads, :each]

    for tap in range(CONV):
        taps_o[:, tap, :] = by_head(TAPS + tap)
    bias_o[...] = by_head(TAPS + CONV)
    gate_o[...] = by_head(GATE)
    norm_o[...] = lines[NORM : NORM + 1, :shard]
    states = state_bias_o.shape[1]
    state_taps_o[...] = lines[STATE_TAPS : STATE_TAPS + CONV, :states]
    state_bias_o[...] = lines[STATE_TAPS + CONV : STATE_TAPS + CONV + 1, :states]
    row = lines[BY_HEAD : BY_HEAD + 1, :]
    dt_bias_o[...] = row[:, :heads]
    a_log_o[...] = row[:, heads : 2 * heads]
    skip_o[...] = row[:, 2 * heads : 3 * heads]


def call(body, steps, info, operands, outputs, scratch=(), reverse=False, micros=1):
    def at(index):
        return steps - 1 - index if reverse else index

    def spec(shape, kind):
        if kind == "rows":
            return pl.BlockSpec((BLOCK,) + tuple(shape[1:]), lambda i: (at(i), 0))
        if kind == "block":
            return pl.BlockSpec((1,) + tuple(shape[1:]), lambda i: (at(i), 0, 0))
        if kind == "lanes":
            return pl.BlockSpec((shape[0], BLOCK), lambda i: (0, at(i)))
        if kind == "tail":
            each = BLOCK // 16
            return pl.BlockSpec((16, shape[1]), lambda i: (jnp.maximum(at(i) * each - 1, 0), 0))
        if kind == "whole":
            return pl.BlockSpec(tuple(shape), lambda i: (0,) * len(shape))
        return kind

    return pl.pallas_call(
        body,
        grid=(steps,),
        in_specs=[pl.BlockSpec(memory_space=pltpu.SMEM)]
        + [spec(array.shape, kind) for array, kind in operands],
        out_specs=[spec(shape.shape, kind) for shape, kind in outputs],
        out_shape=[shape for shape, _ in outputs],
        scratch_shapes=list(scratch),
        compiler_params=pltpu.CompilerParams(
            dimension_semantics=("arbitrary",), vmem_limit_bytes=VMEM
        ),
        cost_estimate=pl.CostEstimate(
            flops=micros * 1_100_000_000, bytes_accessed=micros * 3_500_000, transcendentals=0
        ),
    )(info, *[array for array, _ in operands])


def shifted(value, axis, steps):
    count = lax.axis_size(axis)
    first, last = max(0, -steps), min(count, count - steps)
    return lax.ppermute(value, axis, [(source, source + steps) for source in range(first, last)])


def swapped(value):
    return lax.ppermute(value, "tp", [(0, 1), (1, 0)])


def partnered(value, axis, mask):
    return lax.ppermute(value, axis, [(one, one ^ mask) for one in range(lax.axis_size(axis))])


def exchanged(value, axis):
    return [value] + [partnered(value, axis, mask) for mask in range(1, lax.axis_size(axis))]


def gather_rows(value, parts):
    if parts == 1:
        return [lax.all_gather(value, "dp", axis=0, tiled=True)]
    rows = value.shape[0] // parts
    own = lax.dynamic_slice_in_dim(value, lax.axis_index("ctx") * rows, rows, 0)
    joined = jnp.concatenate(exchanged(own, "dp"), axis=0)
    return exchanged(joined, "ctx")


def reduce_rows(pieces):
    if len(pieces) == 1:
        own = lax.psum_scatter(pieces[0], "dp", scatter_dimension=0, tiled=True)
        return lax.psum(own, "ctx")
    dp_count = lax.axis_size("dp")
    rows = pieces[0].shape[0] // dp_count
    total = pieces[0].astype(F32)
    for mask in range(1, len(pieces)):
        total = total + partnered(pieces[mask], "ctx", mask).astype(F32)
    own = total[:rows]
    for mask in range(1, dp_count):
        block = total[mask * rows : (mask + 1) * rows].astype(BF16)
        own = own + partnered(block, "dp", mask).astype(F32)
    return own.astype(BF16)


def body(
    tokens, cotangent, device_fill, seq_lengths, norm_gain, w_z, w_x, w_bc, w_dt,
    conv_x, conv_x_bias, conv_bc, bias_bc, dt_bias, a_log, skip_d, gate_gain, w_out,
):
    rows, width = tokens.shape
    heads = dt_bias.shape[0]
    inner = heads * HEAD
    channels = inner + 2 * LANES
    steps = rows // BLOCK
    shard = norm_gain.shape[0]
    dp_count = lax.axis_size("dp")
    ctx_count = lax.axis_size("ctx")
    tp_index = lax.axis_index("tp")
    counts = (ctx_count, seq_lengths.shape[1])

    parts = ctx_count if shard % (16 * ctx_count) == 0 else 1
    part_rows = shard // parts

    with jax.named_scope("gather_weights"):
        w1_parts = gather_rows(jnp.concatenate([w_x, w_bc], axis=1), parts)
        vector = jnp.concatenate(
            [
                conv_x.reshape(CONV, shard),
                conv_x_bias.reshape(1, shard),
                norm_gain[None, :],
                gate_gain.reshape(1, shard),
                jnp.zeros((1, shard), BF16),
                jnp.pad(
                    jnp.concatenate([conv_bc, bias_bc[None, :]], axis=0),
                    ((0, 3), (0, shard - bias_bc.shape[0])),
                ),
                jnp.pad(w_dt.T, ((0, 16 - heads), (0, 0))),
            ],
            axis=0,
        )
        vectors = exchanged(vector, "dp")
        w2 = lax.all_gather(jnp.concatenate([w_z, w_out.T], axis=1), "dp", axis=0, tiled=True)

    dtp = jnp.pad(jnp.stack([dt_bias, jnp.exp(a_log), skip_d]), ((0, 5), (0, LANES - heads)))
    shape = (2 * LANES, inner)
    spread = (iota(shape, 0) % LANES == iota(shape, 1) // HEAD).astype(BF16)
    info = jnp.concatenate(
        [
            device_fill[0],
            seq_lengths[0],
            jnp.stack([lax.axis_index("ctx"), tp_index, lax.axis_index("dp")]).astype(jnp.int32),
        ]
    )
    fill = jnp.sum(jnp.where(jnp.arange(ctx_count) == lax.axis_index("ctx"), device_fill[0], 0)) * BLOCK
    halo = shifted(lax.dynamic_slice_in_dim(tokens, fill - 16, 16, 0), "ctx", 1)

    def out(shape, dtype, kind):
        return (jax.ShapeDtypeStruct(shape, dtype), kind)

    def row_out(columns, dtype):
        return out((rows, columns), dtype, "rows")

    state_out = out((steps, inner, LANES), F32, "block")
    packet_out = out((inner + 16, LANES), BF16, "whole")

    (w1, par, normed, halo_normed, halo_v, v, xc, bc, ypart, pre_step, cum, entry, decay, packet) = call(
        functools.partial(forward_kernel, counts, heads, dp_count, parts),
        steps,
        info,
        [(value, "whole") for value in vectors + w1_parts]
        + [(tokens, "rows"), (halo, "whole"), (dtp, "whole"), (spread, "whole")],
        [
            out((width, channels + LANES), BF16, "whole"),
            out((8, channels), F32, "whole"),
            row_out(width, BF16),
            out((16, width), BF16, "whole"),
            out((8, channels), F32, "whole"),
            row_out(channels, BF16),
            row_out(inner, BF16),
            row_out(2 * LANES, BF16),
            row_out(inner, F32),
            row_out(LANES, F32),
            row_out(LANES, F32),
            state_out,
            out((steps, 8, LANES), F32, "block"),
            packet_out,
        ],
        [
            pltpu.VMEM((8 + BLOCK, channels), F32),
            pltpu.VMEM((inner, LANES), F32),
            pltpu.VMEM((8, LANES), F32),
        ],
        micros=20,
    )
    packets = [(shifted(packet, "ctx", step), "whole") for step in range(1, ctx_count)]
    wz_spec = pl.BlockSpec((width, inner), lambda i: (0, 0))
    wo_spec = pl.BlockSpec((width, inner), lambda i: (0, 1))
    z, dn = call(
        functools.partial(gate_matmul_kernel, counts),
        steps,
        info,
        [(normed, "rows"), (cotangent, "rows"), (w2, "whole")],
        [row_out(inner, BF16), row_out(inner, F32)],
        micros=7,
    )
    y, hb, h, stat = call(
        functools.partial(apply_kernel, counts, len(packets)),
        steps,
        info,
        packets
        + [
            (entry, "block"),
            (decay, "block"),
            (cum, "rows"),
            (bc, "rows"),
            (ypart, "rows"),
            (z, "rows"),
            (dn, "rows"),
            (par, "whole"),
            (spread, "whole"),
        ],
        [
            row_out(inner, F32),
            out((steps, inner, LANES), BF16, "block"),
            state_out,
            out((8, rows), F32, "lanes"),
        ],
        [pltpu.VMEM((inner, LANES), F32)],
        micros=8,
    )
    stat = lax.psum(stat, "tp")
    inner_all = inner * lax.axis_size("tp")
    half = width // 2
    keep, send, g2, small_gate, dy, dz, de, exits, packet = call(
        functools.partial(gate_back_kernel, counts, inner_all),
        steps,
        info,
        [
            (stat, "lanes"),
            (y, "rows"),
            (z, "rows"),
            (dn, "rows"),
            (cotangent, "rows"),
            (cum, "rows"),
            (bc, "rows"),
            (xc, "rows"),
            (hb, "block"),
            (decay, "block"),
            (normed, "rows"),
            (w2, wo_spec),
            (par, "whole"),
            (spread, "whole"),
        ],
        [
            row_out(half, BF16),
            row_out(half, BF16),
            out((width, 2 * inner), BF16, "whole"),
            out((8, inner), F32, "whole"),
            row_out(inner, BF16),
            row_out(inner, BF16),
            row_out(LANES, F32),
            state_out,
            packet_out,
        ],
        [
            pltpu.VMEM((width, 2 * inner), F32),
            pltpu.VMEM((inner, LANES), F32),
            pltpu.VMEM((8, LANES), F32),
        ],
        reverse=True,
        micros=16,
    )
    with jax.named_scope("reduce_gate_weights"):
        total2 = lax.psum_scatter(g2, "dp", scatter_dimension=0, tiled=True)
        total2 = lax.psum(total2, "ctx").astype(F32)
    packets = [(shifted(packet, "ctx", -step), "whole") for step in range(1, ctx_count)]
    with jax.named_scope("layer_out"):
        received = swapped(send)
        own_inputs = lax.dynamic_slice_in_dim(tokens, tp_index * half, half, 1).astype(F32)
        valid = (jnp.arange(rows) < fill).astype(F32)[:, None]
        layer_out = own_inputs + (keep.astype(F32) + received.astype(F32)) * valid
    dxc, dcq, dbq, row_sums, col_sums, dnz = call(
        functools.partial(intra_back_kernel, counts, heads),
        steps,
        info,
        [
            (dy, "rows"),
            (dz, "rows"),
            (xc, "rows"),
            (bc, "rows"),
            (cum, "rows"),
            (pre_step, "rows"),
            (hb, "block"),
            (w2, wz_spec),
            (par, "whole"),
            (spread, "whole"),
        ],
        [
            row_out(inner, F32),
            row_out(LANES, F32),
            row_out(LANES, F32),
            row_out(LANES, F32),
            row_out(LANES, F32),
            row_out(width, F32),
        ],
        [pltpu.VMEM((LANES, BLOCK), F32)],
        micros=17,
    )
    partial, halo_grad, *g1 = call(
        functools.partial(state_back_kernel, counts, heads, dp_count, len(packets), parts),
        steps,
        info,
        packets
        + [
            (exits, "block"),
            (h, "block"),
            (xc, "rows"),
            (bc, "rows"),
            (cum, "rows"),
            (pre_step, "rows"),
            (de, "rows"),
            (dxc, "rows"),
            (dcq, "rows"),
            (dbq, "rows"),
            (row_sums, "rows"),
            (col_sums, "rows"),
            (decay, "block"),
            (v, "rows"),
            (v, "tail"),
            (halo_v, "whole"),
            (halo_normed, "whole"),
            (halo, "whole"),
            (tokens, "rows"),
            (normed, "rows"),
            (dnz, "rows"),
            (small_gate, "whole"),
            (w1, "whole"),
            (par, "whole"),
            (dtp, "whole"),
            (spread, "whole"),
        ],
        [
            row_out(width, BF16),
            out((8, width), F32, "whole"),
        ]
        + [out((width // parts, channels + LANES), BF16, "whole")] * parts,
        [
            pltpu.VMEM((inner, LANES), F32),
            pltpu.VMEM((8, LANES), F32),
            pltpu.VMEM((8 + BLOCK, channels), F32),
            pltpu.VMEM((8 + BLOCK, channels), F32),
            pltpu.VMEM((width, channels + LANES), F32),
            pltpu.VMEM((8, channels), F32),
        ],
        reverse=True,
        micros=28,
    )
    other = swapped(partial)
    size = ctx_count * 2
    back = [(s, s - 2) for s in range(2, size)]
    cross = [(s, (s - 2) ^ 1) for s in range(2, size)]
    halo_a = lax.ppermute(halo_grad, ("ctx", "tp"), back)
    halo_b = lax.ppermute(halo_grad, ("ctx", "tp"), cross)
    with jax.named_scope("reduce_input_weights"):
        total1 = reduce_rows(g1)
        across = swapped(total1[:, inner:])
        lane = jnp.arange(3 * LANES) - 2 * LANES
        both = (lane < 0) | (lane == NORM) | ((lane >= STATE_TAPS) & (lane < BY_HEAD))
        summed = total1[:, inner:] + jnp.where(both[None, :], across, 0)
        total1 = jnp.concatenate([total1[:, :inner], summed], axis=1)
        total1 = exchanged(total1, "ctx") if parts > 1 else [total1]
    (grad_tokens,) = call(
        functools.partial(finish_kernel, counts),
        steps,
        info,
        [
            (partial, "rows"),
            (other, "rows"),
            (halo_a, "whole"),
            (halo_b, "whole"),
            (tokens, "rows"),
            (cotangent, "rows"),
            (par, "whole"),
        ],
        [row_out(width, F32)],
        micros=5,
    )
    each = HEAD // dp_count
    part_bc = bias_bc.shape[0]
    tall = -(-shard // LANES) * LANES

    def final(*sizes):
        return out(sizes, F32, "whole")

    (
        grad_wx, grad_wbc, grad_wdt, grad_norm, grad_taps, grad_bias, grad_state_taps, grad_state_bias,
        grad_dt_bias, grad_a_log, grad_skip, grad_gate,
    ) = call(
        functools.partial(unpack_input_kernel, counts, heads, parts),
        1,
        info,
        [(value, "whole") for value in total1],
        [
            final(shard, inner),
            final(shard, 2 * LANES),
            final(heads, shard),
            final(1, shard),
            final(heads, CONV, each),
            final(heads, each),
            final(CONV, part_bc),
            final(1, part_bc),
            final(1, heads),
            final(1, heads),
            final(1, heads),
            final(heads, each),
        ],
        [pltpu.VMEM((tall, channels + LANES), F32)],
        micros=2,
    )
    return (
        layer_out,
        grad_tokens,
        grad_norm[0],
        total2[:, :inner],
        grad_wx,
        grad_wbc,
        grad_wdt.T,
        grad_taps.transpose(1, 0, 2),
        grad_bias,
        grad_state_taps,
        grad_state_bias[0],
        grad_dt_bias[0],
        grad_a_log[0],
        grad_skip[0],
        grad_gate,
        total2[:, inner:].T,
    )


def solution(mesh):
    shards = P(("dp", "ctx"), None)
    return jax.shard_map(
        body,
        mesh=mesh,
        in_specs=(
            shards,
            shards,
            P("dp", None),
            P("dp", None),
            P("dp"),
            P("dp", "tp"),
            P("dp", "tp"),
            P("dp", None),
            P("dp", "tp"),
            P(None, "tp", "dp"),
            P("tp", "dp"),
            P(None, "dp"),
            P("dp"),
            P("tp"),
            P("tp"),
            P("tp"),
            P("tp", "dp"),
            P("tp", "dp"),
        ),
        out_specs=(
            P(("dp", "ctx"), "tp"),
            shards,
            P("dp"),
            P("dp", "tp"),
            P("dp", "tp"),
            P("dp", None),
            P("dp", "tp"),
            P(None, "tp", "dp"),
            P("tp", "dp"),
            P(None, "dp"),
            P("dp"),
            P("tp"),
            P("tp"),
            P("tp"),
            P("tp", "dp"),
            P("tp", "dp"),
        ),
        check_vma=False,
    )
```

```python
import functools

import jax
import jax.numpy as jnp
from jax import lax
from jax.experimental import pallas as pl
from jax.experimental.pallas import tpu as pltpu
from jax.sharding import PartitionSpec as P

CONV = 4
BLOCK = 256
HEAD = 64
LANES = 128
EPS = 1e-05
VMEM = 56 * 1024 * 1024
F32 = jnp.float32
BF16 = jnp.bfloat16


def dot(left, right):
    return jnp.dot(left, right, preferred_element_type=F32)


def dot_tn(left, right):
    return lax.dot_general(left, right, (((0,), (0,)), ((), ())), preferred_element_type=F32)


def dot_nt(left, right):
    return lax.dot_general(left, right, (((1,), (1,)), ((), ())), preferred_element_type=F32)


def dot_exact(left, right):
    return jnp.dot(left, right, preferred_element_type=F32, precision=lax.Precision.HIGHEST)


def iota(shape, dim):
    return lax.broadcasted_iota(jnp.int32, shape, dim)


def sigmoid(value):
    return 1.0 / (1.0 + jnp.exp(-value))


def softplus(value):
    return jnp.maximum(value, 0.0) + jnp.log1p(jnp.exp(-jnp.abs(value)))


def split(value):
    high = value.astype(BF16)
    return high, (value - high.astype(F32)).astype(BF16)


def expand(value, spread):
    return dot(jnp.concatenate(split(value), axis=1), spread[...])


def reduce_heads(value, spread):
    high, low = split(value)
    pick = spread[:LANES, :]
    return dot_nt(high, pick) + dot_nt(low, pick)


def head_column(row, channels):
    shape = (channels, LANES)
    return jnp.sum(jnp.where(iota(shape, 0) // HEAD == iota(shape, 1), row, 0.0), axis=1, keepdims=True)


def xor(value, mask):
    return jnp.bitwise_xor(value, jnp.int32(mask))


class Place:
    def __init__(self, info, counts):
        devices, sequences = counts
        own = info[devices + sequences]
        self.ctx = own
        self.tp = info[devices + sequences + 1]
        self.dp = info[devices + sequences + 2]
        self.fill = jnp.int32(0)
        self.first = jnp.int32(0)
        for device in range(devices):
            rows = info[device] * BLOCK
            self.fill = self.fill + jnp.where(own == device, rows, 0)
            self.first = self.first + jnp.where(own > device, rows, 0)
        self.ends = []
        total = jnp.int32(0)
        for sequence in range(sequences - 1):
            total = total + info[devices + sequence]
            self.ends.append(total)

    def of(self, position):
        found = (position >= self.ends[0]).astype(jnp.int32)
        for end in self.ends[1:]:
            found = found + (position >= end).astype(jnp.int32)
        return jnp.where(position < 0, -1, found)

    def rows(self, index):
        return self.of(self.first + jnp.minimum(index, self.fill - 1))

    def before(self, block):
        position = self.first + jnp.minimum(block * BLOCK, self.fill) - 1
        found = jnp.int32(0)
        for end in self.ends:
            found = found + jnp.where(position >= end, 1, 0)
        return jnp.where(position < 0, -1, found)

    def last(self, block):
        position = self.first + jnp.minimum(block * BLOCK + BLOCK - 1, self.fill - 1)
        found = jnp.int32(0)
        for end in self.ends:
            found = found + jnp.where(position >= end, 1, 0)
        return found

    def column(self, block, shift=0):
        return self.rows(block * BLOCK + shift + iota((BLOCK, 1), 0))

    def valid(self, block):
        return (block * BLOCK + iota((BLOCK, 1), 0) < self.fill).astype(F32)

    def keep(self, block):
        across = self.rows(block * BLOCK + iota((1, BLOCK), 1))
        return (self.column(block) == across) & (iota((BLOCK, BLOCK), 0) >= iota((BLOCK, BLOCK), 1))


def step_sizes(place, block, pre_step, heads):
    lane = iota((BLOCK, LANES), 1)
    return jnp.where(lane < heads, softplus(pre_step), 0.0) * place.valid(block)


def end_weights(place, block, cum):
    same = (place.column(block) == place.last(block)).astype(F32)
    return jnp.exp(cum[BLOCK - 1 :, :] - cum) * same


def enter_weights(place, block, cum):
    return jnp.exp(cum) * (place.column(block) == place.before(block)).astype(F32)


def block_decay(place, block, cum):
    return jnp.exp(cum[BLOCK - 1 :, :]) * jnp.where(place.last(block) == place.before(block), 1.0, 0.0)


def decay_kernel(keep, cum, cum_rows, head):
    return jnp.exp(jnp.where(keep, cum[:, head : head + 1] - cum_rows[head : head + 1, :], -1e30))


def both_halves(pair):
    lane = iota(pair.shape, 1)
    zero = jnp.zeros_like(pair)
    return [jnp.where(lane < HEAD, pair, zero), jnp.where(lane >= HEAD, pair, zero)]


def same_mask(place, block, tap):
    return (place.column(block, tap - (CONV - 1)) == place.column(block)).astype(F32)


def conv_pre(place, block, ext, par, channels):
    total = par[4:5, :channels]
    for tap in range(CONV):
        first = 8 - (CONV - 1) + tap
        total = total + par[tap : tap + 1, :channels] * ext[first : first + BLOCK, :] * same_mask(
            place, block, tap
        )
    return total


def state_packet(state, decay):
    high, low = split(decay)
    row = iota((16, LANES), 0)
    tail = jnp.where(row == 0, high.astype(F32), jnp.where(row == 1, low.astype(F32), 0.0))
    return jnp.concatenate([state.astype(BF16), tail.astype(BF16)], axis=0)


def merge_packets(packets, inner):
    total = jnp.zeros((inner, LANES), F32)
    for packet in reversed(packets):
        tail = packet[inner : inner + 16, :].astype(F32)
        decay = tail[0:1, :] + tail[1:2, :]
        total = packet[:inner, :].astype(F32) + head_column(decay, inner) * total
    return total


def normalise(rows, gain):
    inv = lax.rsqrt(jnp.mean(rows * rows, axis=1, keepdims=True) + EPS)
    return rows * inv, inv, (rows * inv * gain).astype(BF16)


def piece_rows(place, dp_count, parts, rows):
    for part in range(parts):
        for block in range(dp_count):
            owner = xor(place.dp, block) * parts + (xor(place.ctx, part) if parts > 1 else 0)
            yield part, block, pl.multiple_of(owner * rows, rows)


def join_pieces(place, dp_count, parts, whole):
    columns = parts[0].shape[1]
    if len(parts) == 1:
        whole[:, :columns] = parts[0][...]
        return
    rows = parts[0].shape[0] // dp_count
    for part, block, first in piece_rows(place, dp_count, len(parts), rows):
        whole[pl.ds(first, rows), :columns] = parts[part][block * rows : (block + 1) * rows, :]


def cut_pieces(place, dp_count, whole, parts, lanes):
    if len(parts) == 1:
        parts[0][:, lanes] = whole[...].astype(BF16)
        return
    rows = parts[0].shape[0] // dp_count
    for part, block, first in piece_rows(place, dp_count, len(parts), rows):
        parts[part][block * rows : (block + 1) * rows, lanes] = whole[pl.ds(first, rows), :].astype(BF16)


def join_parameters(place, vectors, skip, heads, par, w1):
    shard = vectors[0].shape[1] // 2
    each = HEAD // len(vectors)
    inner = heads * HEAD
    by_channel = jnp.zeros((16, inner), F32)
    in_order = jnp.zeros((16, shard * len(vectors)), F32)
    by_state = jnp.zeros((16, 2 * LANES), F32)
    states = 2 * LANES // len(vectors)
    eye = (iota((16, LANES), 0) == iota((16, LANES), 1)).astype(BF16)
    for block, vector in enumerate(vectors):
        owner = xor(place.dp, block)
        first = pl.multiple_of(owner * shard, shard)
        w1[pl.ds(first, shard), inner + 2 * LANES :] = dot_tn(vector[:, shard:], eye).astype(BF16)
        source, target = iota((shard, inner), 0), iota((shard, inner), 1)
        pick = target == source // each * HEAD + owner * each + source % each
        by_channel = by_channel + dot(vector[:, :shard], pick.astype(BF16))
        source, target = iota((shard, in_order.shape[1]), 0), iota((shard, in_order.shape[1]), 1)
        in_order = in_order + dot(vector[:, :shard], (target == owner * shard + source).astype(BF16))
        source, target = iota((shard, 2 * LANES), 0), iota((shard, 2 * LANES), 1)
        pick = (target == owner * states + source) & (source < states)
        by_state = by_state + dot(vector[:, :shard], pick.astype(BF16))
    par[...] = jnp.zeros_like(par)
    par[0:5, :inner] = by_channel[0:5, :]
    par[0:5, inner:] = by_state[8:13, :]
    par[5:6, : in_order.shape[1]] = in_order[5:6, :]
    par[6:7, :inner] = by_channel[6:7, :]
    par[7:8, :inner] = skip


TAPS, GATE, STATE_TAPS, BY_HEAD, NORM = 12, 18, 20, 25, 26


def lanes(pieces, columns):
    rows, at = [], 0
    for first, value in pieces:
        if first > at:
            rows.append(jnp.zeros((first - at, columns), F32))
        rows.append(value)
        at = first + value.shape[0]
    rows.append(jnp.zeros((LANES - at, columns), F32))
    return jnp.concatenate(rows, axis=0)


def pack_norm(place, dp_count, part_count, row, rows):
    columns = row.shape[1]
    shard = columns // dp_count
    size = shard // rows
    total = jnp.zeros((dp_count * rows, LANES), F32)
    source, target = iota((dp_count * rows, columns), 0), iota((dp_count * rows, columns), 1)
    owner = source // rows
    if part_count > 1:
        owner = jnp.bitwise_xor(owner, place.dp)
    for lane in range(size):
        pick = target == owner * shard + lane * rows + source % rows
        total = total + dot_nt(pick.astype(BF16), lanes([(NORM + lane, row)], columns).astype(BF16))
    return total


def pack_parameters(dp_count, heads, small, gate, skip):
    inner = heads * HEAD
    each = HEAD // dp_count
    shard = inner // dp_count
    states = 2 * LANES // dp_count

    source, target = iota((inner, inner), 0), iota((inner, inner), 1)
    inside = source % shard
    pick = target == inside // each * HEAD + source // shard * each + inside % each
    by_channel = lanes([(TAPS, small[0:5, :inner]), (GATE, gate)], inner)
    total = dot_nt(pick.astype(BF16), by_channel.astype(BF16))
    source, target = iota((inner, 2 * LANES), 0), iota((inner, 2 * LANES), 1)
    inside = source % shard
    pick = (target == source // shard * states + inside) & (inside < states)
    by_state = lanes([(STATE_TAPS, small[0:5, inner : inner + 2 * LANES])], 2 * LANES)
    total = total + dot_nt(pick.astype(BF16), by_state.astype(BF16))
    source, target = iota((inner, LANES), 0) % shard, iota((inner, LANES), 1)
    for index, row in enumerate((small[6:7, :LANES], small[7:8, :LANES], skip)):
        pick = (source == target + index * heads) & (target < heads)
        total = total + dot_nt(pick.astype(BF16), lanes([(BY_HEAD, row)], LANES).astype(BF16))
    return total


def forward_kernel(
    counts, heads, dp_count, part_count, info, *refs
):
    vectors = refs[:dp_count]
    parts = refs[dp_count : dp_count + part_count]
    (
        tok, halo, dtp, spread,
        w1, par, normed_o, halo_normed_o, halo_v_o, v_o, xc_o, bc_o, ypart_o, pre_o, cum_o, entry_o, decay_o,
        packet_o, ext, run, factor,
    ) = refs[dp_count + part_count :]
    forward_block(
        counts, heads, info, vectors, parts, tok, halo, w1, par, dtp, spread,
        normed_o, halo_normed_o, halo_v_o, v_o, xc_o, bc_o, ypart_o, pre_o, cum_o, entry_o, decay_o, packet_o,
        ext, run, factor,
    )


def forward_block(
    counts, heads, info, vectors, parts, tok, halo, w1, par, dtp, spread,
    normed_o, halo_normed_o, halo_v_o, v_o, xc_o, bc_o, ypart_o, pre_o, cum_o, entry_o, decay_o, packet_o,
    ext, run, factor,
):
    block = pl.program_id(0)
    place = Place(info, counts)
    inner = heads * HEAD
    state = LANES
    channels = inner + 2 * state
    width = tok.shape[1]

    @pl.when(block == 0)
    def _():
        join_pieces(place, len(vectors), parts, w1)
        join_parameters(place, vectors, expand(dtp[...], spread)[2:3, :], heads, par, w1)

    gain = par[5:6, :width]
    _, _, normed = normalise(tok[...].astype(F32), gain)
    normed_o[...] = normed

    @pl.when(block == 0)
    def _():
        _, _, before = normalise(halo[...].astype(F32), gain)
        halo_normed_o[...] = before
        raw = dot(before, w1[:, :channels]).astype(BF16).astype(F32)
        ext[0:8, :] = raw[8:16, :]
        halo_v_o[...] = raw[8:16, :]
        run[...] = jnp.zeros_like(run)
        factor[...] = jnp.ones_like(factor)

    @pl.when(block > 0)
    def _():
        ext[0:8, :] = ext[BLOCK : BLOCK + 8, :]

    raw = dot(normed, w1[...])
    v = raw[:, :channels].astype(BF16)
    v_o[...] = v
    ext[8 : 8 + BLOCK, :] = v.astype(F32)
    pre = conv_pre(place, block, ext, par, channels)
    act = (pre * sigmoid(pre)).astype(BF16)
    xc = act[:, :inner]
    bq = act[:, inner : inner + state]
    cq = act[:, inner + state :]
    xc_o[...] = xc
    bc_o[...] = act[:, inner:]
    pre_step = raw[:, channels:].astype(BF16).astype(F32) + dtp[0:1, :]
    pre_o[...] = pre_step
    step = step_sizes(place, block, pre_step, heads)
    tri = (iota((BLOCK, BLOCK), 0) >= iota((BLOCK, BLOCK), 1)).astype(F32)
    cum = dot_exact(tri, -dtp[1:2, :] * step)
    cum_o[...] = cum
    cum_rows = cum.T
    step_rows = step.T
    gram = dot_nt(cq, bq)
    keep = place.keep(block)
    for pair in range(heads // 2):
        lanes = slice(pair * LANES, (pair + 1) * LANES)
        mixing = []
        for head in (2 * pair, 2 * pair + 1):
            weight = decay_kernel(keep, cum, cum_rows, head) * step_rows[head : head + 1, :]
            mixing.append((gram * weight).astype(BF16))
        x_pair = xc[:, lanes]
        y_pair = dot(jnp.concatenate(mixing, axis=1), jnp.concatenate(both_halves(x_pair), axis=0))
        ypart_o[:, lanes] = y_pair + par[7:8, lanes] * x_pair.astype(F32)
    weighted = (expand(end_weights(place, block, cum) * step, spread) * xc.astype(F32)).astype(BF16)
    block_state = dot_tn(weighted, bq)
    decay = block_decay(place, block, cum)
    entry_o[0] = run[...]
    total = head_column(decay, inner) * run[...] + block_state
    run[...] = total
    before = factor[0:1, :]
    row = iota((8, LANES), 0)
    decay_o[0] = jnp.where(row == 0, decay, jnp.where(row == 1, before, 0.0))
    after = before * decay
    factor[...] = jnp.broadcast_to(after, factor.shape)

    @pl.when(block == pl.num_programs(0) - 1)
    def _():
        packet_o[...] = state_packet(total, after)


def gate_matmul_kernel(counts, dp_count, part_count, info, *refs):
    parts = refs[:part_count]
    normed, cot, w2, z_o, dn_o = refs[part_count:]
    block = pl.program_id(0)
    place = Place(info, counts)
    inner = z_o.shape[1]

    @pl.when(block == 0)
    def _():
        join_pieces(place, dp_count, parts, w2)

    z_o[...] = dot(normed[...], w2[:, :inner]).astype(BF16)
    grad = (cot[...].astype(F32) * place.valid(block)).astype(BF16)
    dn_o[...] = dot(grad, w2[:, inner:])


def apply_kernel(counts, packet_count, info, *refs):
    packets = refs[:packet_count]
    entry, decay, cum, bc, ypart, z, dn, par, spread, y_o, hb_o, h_o, stat_o, start = refs[packet_count:]
    block = pl.program_id(0)
    place = Place(info, counts)
    inner = z.shape[1]

    @pl.when(block == 0)
    def _():
        start[...] = merge_packets([packet[...] for packet in packets], inner)

    state = entry[0] + head_column(decay[0, 1:2, :], inner) * start[...]
    h_o[0] = state
    low = state.astype(BF16)
    hb_o[0] = low
    cq = bc[:, LANES:]
    y = ypart[...] + expand(enter_weights(place, block, cum[...]), spread) * dot_nt(cq, low)
    y_o[...] = y
    gate = z[...].astype(F32)
    gated = y * gate * sigmoid(gate)
    squares = jnp.sum(gated * gated, axis=1, keepdims=True)
    cross = jnp.sum(par[6:7, :inner] * dn[...] * gated, axis=1, keepdims=True)
    lane = iota((BLOCK, LANES), 1)
    both = jnp.where(lane == 0, squares, jnp.where(lane == 1, cross, 0.0))
    stat_o[...] = both.T[0:8, :]


def gate_back_kernel(
    counts, inner_all, info, stat, y, z, dn, cot, cum, bc, xc, hb, decay, wo, par, spread,
    keep_o, send_o, gwo_o, small_o, dy_o, dz_o, de_o, exit_o, packet_o,
    acc, run, factor,
):
    step = pl.program_id(0)
    block = pl.num_programs(0) - 1 - step
    place = Place(info, counts)
    inner = z.shape[1]
    width = cot.shape[1]
    half = width // 2

    @pl.when(step == 0)
    def _():
        acc[...] = jnp.zeros_like(acc)
        run[...] = jnp.zeros_like(run)
        factor[...] = jnp.ones_like(factor)
        small_o[...] = jnp.zeros_like(small_o)

    column = jnp.concatenate([stat[...], jnp.zeros((LANES - 8, BLOCK), F32)], axis=0).T
    inv = lax.rsqrt(column[:, 0:1] / inner_all + EPS)
    cross = column[:, 1:2]
    gain = par[6:7, :inner]
    gate = z[...].astype(F32)
    sig = sigmoid(gate)
    silu = gate * sig
    mixed = y[...]
    gated = mixed * silu
    normal = (gated * inv * gain).astype(BF16)
    own = pl.multiple_of(place.tp * half, half)
    other = pl.multiple_of((1 - place.tp) * half, half)
    keep_o[...] = dot_nt(normal, wo[pl.ds(own, half), :]).astype(BF16)
    send_o[...] = dot_nt(normal, wo[pl.ds(other, half), :]).astype(BF16)
    grad = (cot[...].astype(F32) * place.valid(block)).astype(BF16)
    acc[...] += dot_tn(grad, normal)
    back = dn[...]
    grad_gated = inv * (gain * back) - gated * (inv * inv * inv) * (cross / inner_all)
    dy = (grad_gated * silu).astype(BF16)
    dy_o[...] = dy
    dz_o[...] = (grad_gated * mixed * sig * (1.0 + gate * (1.0 - sig))).astype(BF16)
    dy_float = dy.astype(F32)
    cq = bc[:, LANES:]
    read = dot_nt(cq, hb[0])
    de_o[...] = reduce_heads(dy_float * read, spread)
    small_o[0:1, :] += jnp.sum(back * gated * inv, axis=0, keepdims=True)
    small_o[1:2, :] += jnp.sum(dy_float * xc[...].astype(F32), axis=0, keepdims=True)
    dq = (expand(enter_weights(place, block, cum[...]), spread) * dy_float).astype(BF16)
    exit_o[0] = run[...]
    here = decay[0, 0:1, :]
    total = head_column(here, inner) * run[...] + dot_tn(dq, cq)
    run[...] = total
    after = factor[0:1, :] * here
    factor[...] = jnp.broadcast_to(after, factor.shape)

    @pl.when(step == pl.num_programs(0) - 1)
    def _():
        packet_o[...] = state_packet(total, after)
        gwo_o[...] = acc[...].astype(BF16)


def intra_back_kernel(counts, heads, dp_count, info, *refs):
    dy, dz, xc, bc, cum, pre_step, hb, normed, wz, gwo, par, spread = refs[:12]
    dxc_o, dcq_o, dbq_o, rows_o, cols_o, dnz_o = refs[12:18]
    parts = refs[18:-2]
    acc, columns = refs[-2:]
    block = pl.program_id(0)
    place = Place(info, counts)
    inner = heads * HEAD

    @pl.when(block == 0)
    def _():
        acc[...] = jnp.zeros_like(acc)
        columns[...] = jnp.zeros_like(columns)

    bq = bc[:, :LANES]
    cq = bc[:, LANES:]
    cums = cum[...]
    step = step_sizes(place, block, pre_step[...], heads)
    cum_rows = cums.T
    step_rows = step.T
    gram = dot_nt(cq, bq)
    keep = place.keep(block)
    lane = iota((BLOCK, LANES), 1)
    grad_gram = jnp.zeros((BLOCK, BLOCK), F32)
    sums = jnp.zeros((BLOCK, LANES), F32)
    for pair in range(heads // 2):
        lanes = slice(pair * LANES, (pair + 1) * LANES)
        dy_pair = dy[:, lanes]
        x_pair = xc[:, lanes]
        halves = jnp.concatenate(both_halves(dy_pair), axis=0)
        grad_mixing = dot_nt(halves, x_pair)
        mixing = []
        for side in range(2):
            head = 2 * pair + side
            grad_m = grad_mixing[side * BLOCK : (side + 1) * BLOCK, :]
            kernel = decay_kernel(keep, cums, cum_rows, head)
            step_row = step_rows[head : head + 1, :]
            weight = kernel * step_row
            mixing.append((gram * weight).astype(BF16))
            grad_gram = grad_gram + grad_m * weight
            part = grad_m * gram * kernel
            columns[head : head + 1, :] = jnp.sum(part, axis=0, keepdims=True)
            sums = sums + jnp.where(lane == head, jnp.sum(part * step_row, axis=1, keepdims=True), 0.0)
        dx_pair = dot_tn(jnp.concatenate(mixing, axis=0), halves)
        dxc_o[:, lanes] = dx_pair + par[7:8, lanes] * dy_pair.astype(F32)
    grad_low = grad_gram.astype(BF16)
    dq = (expand(enter_weights(place, block, cums), spread) * dy[...].astype(F32)).astype(BF16)
    dcq_o[...] = dot(grad_low, bq) + dot(dq, hb[0])
    dbq_o[...] = dot_tn(grad_low, cq)
    rows_o[...] = sums
    cols_o[...] = columns[...].T
    dnz_o[...] = dot_nt(dz[...], wz[...])
    acc[...] += dot_tn(normed[...], dz[...])

    @pl.when(block == pl.num_programs(0) - 1)
    def _():
        cut_pieces(place, dp_count, acc, parts, slice(0, inner))
        cut_pieces(place, dp_count, gwo, parts, slice(inner, 2 * inner))


def state_back_kernel(counts, heads, packet_count, info, *refs):
    packets = refs[:packet_count]
    (
        exits, h, xc, bc, cum, pre_step, de, dxc, dcq, dbq, rows, cols, decay, dtp, spread,
        act_o, ddt_o, small_o,
        start, factor,
    ) = refs[packet_count:]
    step_id = pl.program_id(0)
    block = pl.num_programs(0) - 1 - step_id
    place = Place(info, counts)
    inner = heads * HEAD

    @pl.when(step_id == 0)
    def _():
        start[...] = merge_packets([packet[...] for packet in packets], inner)
        factor[...] = jnp.ones_like(factor)
        small_o[...] = jnp.zeros_like(small_o)

    here = decay[0, 0:1, :]
    before = factor[0:1, :]
    grad_state = exits[0] + head_column(before, inner) * start[...]
    factor[...] = jnp.broadcast_to(before * here, factor.shape)
    shape = (inner, LANES)
    overlap = jnp.sum(grad_state * h[0], axis=1, keepdims=True)
    grad_decay = jnp.sum(
        jnp.where(iota(shape, 0) // HEAD == iota(shape, 1), overlap, 0.0), axis=0, keepdims=True
    )
    low = grad_state.astype(BF16)
    bq = bc[:, :LANES]
    cums = cum[...]
    x_float = xc[...].astype(F32)
    pre_dt = pre_step[...]
    valid = place.valid(block)
    step = step_sizes(place, block, pre_dt, heads)
    end_kernel = end_weights(place, block, cums)
    end_weight = end_kernel * step
    end_wide = expand(end_weight, spread)
    spread_b = dot_nt(bq, low)
    act_o[:, :inner] = dxc[...] + end_wide * spread_b
    grad_end = reduce_heads(x_float * spread_b, spread)
    act_o[:, inner : inner + LANES] = dbq[...] + dot((x_float * end_wide).astype(BF16), low)
    act_o[:, inner + LANES :] = dcq[...]
    end_part = grad_end * end_weight
    last = iota((BLOCK, LANES), 0) == BLOCK - 1
    grad_cum = rows[...] - cols[...] * step - end_part + de[...] * enter_weights(place, block, cums)
    grad_cum = grad_cum + jnp.where(
        last, jnp.sum(end_part, axis=0, keepdims=True) + grad_decay * here, 0.0
    )
    upper = (iota((BLOCK, BLOCK), 0) <= iota((BLOCK, BLOCK), 1)).astype(F32)
    grad_log = dot_exact(upper, grad_cum)
    rates = dtp[1:2, :]
    grad_step = cols[...] + grad_end * end_kernel - rates * grad_log
    heads_lane = iota((BLOCK, LANES), 1) < heads
    grad_pre_dt = jnp.where(heads_lane, grad_step * sigmoid(pre_dt), 0.0) * valid
    ddt_o[...] = grad_pre_dt.astype(BF16)
    small_o[0:1, :] += jnp.sum(grad_pre_dt, axis=0, keepdims=True)
    small_o[1:2, :] += jnp.sum(grad_log * (-rates * step), axis=0, keepdims=True)


def conv_back_kernel(counts, heads, dp_count, part_count, info, *refs):
    act, ddt, v, v_tail, halo_v, halo_normed, normed, small_gate, small_state, par, spread = refs[:11]
    packed_o, back_o = refs[11:13]
    parts = refs[13 : 13 + part_count]
    ext, grad_ext, acc, small_o = refs[13 + part_count :]
    step_id = pl.program_id(0)
    block = pl.num_programs(0) - 1 - step_id
    place = Place(info, counts)
    inner = heads * HEAD
    channels = inner + 2 * LANES

    @pl.when(step_id == 0)
    def _():
        acc[...] = jnp.zeros_like(acc)
        grad_ext[...] = jnp.zeros_like(grad_ext)
        small_o[...] = jnp.zeros_like(small_o)

    ext[8 : 8 + BLOCK, :] = v[...].astype(F32)

    @pl.when(block == 0)
    def _():
        ext[0:8, :] = halo_v[...]

    @pl.when(block > 0)
    def _():
        ext[0:8, :] = v_tail[...].astype(F32)[8:16, :]

    pre = conv_pre(place, block, ext, par, channels)
    sig = sigmoid(pre)
    slope = sig * (1.0 + pre * (1.0 - sig))
    grad_pre = act[...] * slope
    small_o[4:5, :] += jnp.sum(grad_pre, axis=0, keepdims=True)
    carry = grad_ext[0:8, :]
    grad_ext[0:BLOCK, :] = jnp.zeros((BLOCK, channels), F32)
    grad_ext[BLOCK : BLOCK + 8, :] = carry
    for tap in range(CONV):
        first = 8 - (CONV - 1) + tap
        masked = grad_pre * same_mask(place, block, tap)
        small_o[tap : tap + 1, :] += jnp.sum(masked * ext[first : first + BLOCK, :], axis=0, keepdims=True)
        grad_ext[first : first + BLOCK, :] += par[tap : tap + 1, :channels] * masked
    packed = jnp.concatenate([grad_ext[8 : 8 + BLOCK, :].astype(BF16), ddt[...]], axis=1)
    packed_o[...] = packed
    acc[...] += dot_tn(normed[...], packed)

    @pl.when(block == 0)
    def _():
        back = jnp.concatenate([jnp.zeros((8, channels), F32), grad_ext[0:8, :]], axis=0).astype(BF16)
        back_o[...] = back
        acc[:, :channels] += dot_tn(halo_normed[...], back)
        small_o[6:7, :LANES] = small_state[0:1, :]
        small_o[7:8, :LANES] = small_state[1:2, :]
        skip = reduce_heads(jnp.broadcast_to(small_gate[1:2, :], (8, inner)), spread)[0:1, :]
        acc[:, channels:] += pack_parameters(dp_count, heads, small_o, small_gate[0:1, :], skip)
        cut_pieces(place, dp_count, acc, parts, slice(0, channels + LANES))


def input_back_kernel(
    counts, dp_count, part_count, info, packed, back, dnz, tok, halo, w1, par,
    dn_o, dnh_o, norm_o, total,
):
    block = pl.program_id(0)
    place = Place(info, counts)
    width = tok.shape[1]
    channels = back.shape[1]
    gain = par[5:6, :width]

    @pl.when(block == 0)
    def _():
        halo_grad = dot_nt(back[...], w1[:, :channels])
        dnh_o[...] = halo_grad[8:16, :]
        halo_scaled, _, _ = normalise(halo[...].astype(F32), gain)
        total[...] = jnp.broadcast_to(
            jnp.sum(halo_grad * halo_scaled, axis=0, keepdims=True), total.shape
        )

    partial = dnz[...] + dot_nt(packed[...], w1[...])
    dn_o[...] = partial.astype(BF16)
    scaled, _, _ = normalise(tok[...].astype(F32), gain)
    total[0:1, :] += jnp.sum(partial * scaled, axis=0, keepdims=True)

    @pl.when(block == pl.num_programs(0) - 1)
    def _():
        rows = norm_o.shape[0] // dp_count
        norm_o[...] = pack_norm(place, dp_count, part_count, total[0:1, :], rows)


def finish_kernel(counts, info, own, other, halo_a, halo_b, tok, cot, par, grad_o):
    block = pl.program_id(0)
    place = Place(info, counts)
    width = tok.shape[1]
    grad = own[...].astype(F32) + other[...].astype(F32)
    is_last = jnp.where((block + 1) * BLOCK == place.fill, 1.0, 0.0)
    halo = (halo_a[...] + halo_b[...]) * is_last
    grad = jnp.concatenate([grad[: BLOCK - 8, :], grad[BLOCK - 8 :, :] + halo], axis=0)
    inputs = tok[...].astype(F32)
    inv = lax.rsqrt(jnp.mean(inputs * inputs, axis=1, keepdims=True) + EPS)
    scaled = par[5:6, :width] * grad
    inner_dot = jnp.sum(scaled * inputs, axis=1, keepdims=True)
    grad_o[...] = (
        inv * scaled - inputs * (inv * inv * inv) * (inner_dot / width) + cot[...].astype(F32)
    )


def unpack_gate_kernel(counts, part_count, info, *refs):
    parts = refs[:part_count]
    wz_o, wo_o = refs[part_count:]
    place = Place(info, counts)
    shard, inner = wz_o.shape
    rows = shard // part_count
    for part in range(part_count):
        first = pl.multiple_of(xor(place.ctx, part) * rows, rows) if part_count > 1 else 0
        wz_o[pl.ds(first, rows), :] = parts[part][:, :inner].astype(F32)
        wo_o[pl.ds(first, rows), :] = parts[part][:, inner:].astype(F32)


def unpack_input_kernel(counts, heads, part_count, info, *refs):
    parts = refs[:part_count]
    (
        wx_o, wbc_o, wdt_o, norm_o, taps_o, bias_o, state_taps_o, state_bias_o, dt_bias_o, a_log_o, skip_o,
        gate_o, wide,
    ) = refs[part_count:]
    place = Place(info, counts)
    shard, inner = wx_o.shape
    channels = inner + 2 * LANES
    rows = shard // part_count
    for part in range(part_count):
        first = pl.multiple_of(xor(place.ctx, part) * rows, rows) if part_count > 1 else 0
        wide[pl.ds(first, rows), :] = parts[part][...].astype(F32)
    wx_o[...] = wide[:shard, :inner]
    wbc_o[...] = wide[:shard, inner:channels]
    lines = wide[:, channels:].T
    wdt_o[...] = lines[:heads, :shard]
    each = gate_o.shape[1]
    size = lines.shape[1]
    source = iota((16, size), 1)
    inside = (source // each == iota((16, size), 0)) & (source < shard)
    place_in = (iota((size, LANES), 0) % each == iota((size, LANES), 1)).astype(BF16)

    def by_head(line):
        row = jnp.where(inside, lines[line : line + 1, :], 0.0).astype(BF16)
        return dot(row, place_in)[:heads, :each]

    for tap in range(CONV):
        taps_o[:, tap, :] = by_head(TAPS + tap)
    bias_o[...] = by_head(TAPS + CONV)
    gate_o[...] = by_head(GATE)
    gain = wide[:rows, channels:]
    for part in range(1, part_count):
        gain = gain + wide[part * rows : (part + 1) * rows, channels:]
    gain = jnp.concatenate([gain, jnp.zeros((LANES - rows, LANES), F32)], axis=0).T
    source, target = iota((LANES, size), 0), iota((LANES, size), 1)
    total = jnp.zeros((8, size), F32)
    for lane in range(shard // rows):
        pick = ((target == lane * rows + source) & (source < rows)).astype(F32)
        total = total + dot_exact(jnp.broadcast_to(gain[NORM + lane : NORM + lane + 1, :], (8, LANES)), pick)
    norm_o[...] = total[0:1, :shard]
    states = state_bias_o.shape[1]
    state_taps_o[...] = lines[STATE_TAPS : STATE_TAPS + CONV, :states]
    state_bias_o[...] = lines[STATE_TAPS + CONV : STATE_TAPS + CONV + 1, :states]
    row = lines[BY_HEAD : BY_HEAD + 1, :]
    dt_bias_o[...] = row[:, :heads]
    a_log_o[...] = row[:, heads : 2 * heads]
    skip_o[...] = row[:, 2 * heads : 3 * heads]


def call(body, steps, info, operands, outputs, scratch=(), reverse=False, micros=1):
    def at(index):
        return steps - 1 - index if reverse else index

    def spec(shape, kind):
        if kind == "rows":
            return pl.BlockSpec((BLOCK,) + tuple(shape[1:]), lambda i: (at(i), 0))
        if kind == "block":
            return pl.BlockSpec((1,) + tuple(shape[1:]), lambda i: (at(i), 0, 0))
        if kind == "lanes":
            return pl.BlockSpec((shape[0], BLOCK), lambda i: (0, at(i)))
        if kind == "tail":
            each = BLOCK // 16
            return pl.BlockSpec((16, shape[1]), lambda i: (jnp.maximum(at(i) * each - 1, 0), 0))
        if kind == "whole":
            return pl.BlockSpec(tuple(shape), lambda i: (0,) * len(shape))
        return kind

    return pl.pallas_call(
        body,
        grid=(steps,),
        in_specs=[pl.BlockSpec(memory_space=pltpu.SMEM)]
        + [spec(array.shape, kind) for array, kind in operands],
        out_specs=[spec(shape.shape, kind) for shape, kind in outputs],
        out_shape=[shape for shape, _ in outputs],
        scratch_shapes=list(scratch),
        compiler_params=pltpu.CompilerParams(
            dimension_semantics=("arbitrary",), vmem_limit_bytes=VMEM
        ),
        cost_estimate=pl.CostEstimate(
            flops=micros * 1_100_000_000, bytes_accessed=micros * 3_500_000, transcendentals=0
        ),
    )(info, *[array for array, _ in operands])


def shifted(value, axis, steps):
    count = lax.axis_size(axis)
    first, last = max(0, -steps), min(count, count - steps)
    return lax.ppermute(value, axis, [(source, source + steps) for source in range(first, last)])


def swapped(value):
    return lax.ppermute(value, "tp", [(0, 1), (1, 0)])


def partnered(value, axis, mask):
    return lax.ppermute(value, axis, [(one, one ^ mask) for one in range(lax.axis_size(axis))])


def exchanged(value, axis):
    return [value] + [partnered(value, axis, mask) for mask in range(1, lax.axis_size(axis))]


def own_rows(value, rows):
    return lax.dynamic_slice_in_dim(value, lax.axis_index("ctx") * rows, rows, 0)


def joined_rows(values):
    return jnp.concatenate(values, axis=0)


def ctx_sum(pieces):
    total = pieces[0].astype(F32)
    for mask in range(1, len(pieces)):
        total = total + partnered(pieces[mask], "ctx", mask).astype(F32)
    return total


def dp_sum(total):
    dp_count = lax.axis_size("dp")
    rows = total.shape[0] // dp_count
    own = total[:rows].astype(F32)
    for mask in range(1, dp_count):
        block = total[mask * rows : (mask + 1) * rows].astype(BF16)
        own = own + partnered(block, "dp", mask).astype(F32)
    return own.astype(BF16)


def whole_sum(value):
    return lax.psum(lax.psum_scatter(value, "dp", scatter_dimension=0, tiled=True), "ctx")


def body(
    tokens, cotangent, device_fill, seq_lengths, norm_gain, w_z, w_x, w_bc, w_dt,
    conv_x, conv_x_bias, conv_bc, bias_bc, dt_bias, a_log, skip_d, gate_gain, w_out,
):
    rows, width = tokens.shape
    heads = dt_bias.shape[0]
    inner = heads * HEAD
    channels = inner + 2 * LANES
    steps = rows // BLOCK
    shard = norm_gain.shape[0]
    dp_count = lax.axis_size("dp")
    ctx_count = lax.axis_size("ctx")
    tp_index = lax.axis_index("tp")
    counts = (ctx_count, seq_lengths.shape[1])

    parts = ctx_count if shard % (16 * ctx_count) == 0 else 1
    part_rows = shard // parts

    with jax.named_scope("gather_weights"):
        vector = jnp.concatenate(
            [
                jnp.concatenate(
                    [
                        conv_x.reshape(CONV, shard),
                        conv_x_bias.reshape(1, shard),
                        norm_gain[None, :],
                        gate_gain.reshape(1, shard),
                        jnp.zeros((1, shard), BF16),
                        jnp.pad(
                            jnp.concatenate([conv_bc, bias_bc[None, :]], axis=0),
                            ((0, 3), (0, shard - bias_bc.shape[0])),
                        ),
                    ],
                    axis=0,
                ),
                jnp.pad(w_dt.T, ((0, 16 - heads), (0, 0))),
            ],
            axis=1,
        )
        input_rows = jnp.concatenate([w_x, w_bc], axis=1)
        gate_rows = jnp.concatenate([w_z, w_out.T], axis=1)
        if parts > 1:
            w1_parts = joined_rows(exchanged(own_rows(input_rows, part_rows), "dp"))
            vector = jnp.pad(vector, ((0, 0), (0, 2 * inner - 2 * shard)))
            block = jnp.concatenate([own_rows(gate_rows, part_rows), vector], axis=0)
            block, _ = lax.optimization_barrier((block, w1_parts))
            vectors = exchanged(block, "dp")
            w2_parts = exchanged(joined_rows([value[:part_rows] for value in vectors]), "ctx")
            w1_parts = exchanged(w1_parts, "ctx")
        else:
            w1_parts = [lax.all_gather(input_rows, "dp", axis=0, tiled=True)]
            w2_parts = [lax.all_gather(gate_rows, "dp", axis=0, tiled=True)]
            vectors = exchanged(vector, "dp")
    first_vector = part_rows // 16 if parts > 1 else 0
    vector_spec = pl.BlockSpec((16, 2 * shard), lambda i: (first_vector, 0))

    dtp = jnp.pad(jnp.stack([dt_bias, jnp.exp(a_log), skip_d]), ((0, 5), (0, LANES - heads)))
    shape = (2 * LANES, inner)
    spread = (iota(shape, 0) % LANES == iota(shape, 1) // HEAD).astype(BF16)
    info = jnp.concatenate(
        [
            device_fill[0],
            seq_lengths[0],
            jnp.stack([lax.axis_index("ctx"), tp_index, lax.axis_index("dp")]).astype(jnp.int32),
        ]
    )
    fill = jnp.sum(jnp.where(jnp.arange(ctx_count) == lax.axis_index("ctx"), device_fill[0], 0)) * BLOCK
    halo = shifted(lax.dynamic_slice_in_dim(tokens, fill - 16, 16, 0), "ctx", 1)

    def out(shape, dtype, kind):
        return (jax.ShapeDtypeStruct(shape, dtype), kind)

    def row_out(columns, dtype):
        return out((rows, columns), dtype, "rows")

    state_out = out((steps, inner, LANES), F32, "block")
    packet_out = out((inner + 16, LANES), BF16, "whole")

    (w1, par, normed, halo_normed, halo_v, v, xc, bc, ypart, pre_step, cum, entry, decay, packet) = call(
        functools.partial(forward_kernel, counts, heads, dp_count, parts),
        steps,
        info,
        [(value, vector_spec) for value in vectors]
        + [(value, "whole") for value in w1_parts]
        + [(tokens, "rows"), (halo, "whole"), (dtp, "whole"), (spread, "whole")],
        [
            out((width, channels + LANES), BF16, "whole"),
            out((8, channels), F32, "whole"),
            row_out(width, BF16),
            out((16, width), BF16, "whole"),
            out((8, channels), F32, "whole"),
            row_out(channels, BF16),
            row_out(inner, BF16),
            row_out(2 * LANES, BF16),
            row_out(inner, F32),
            row_out(LANES, F32),
            row_out(LANES, F32),
            state_out,
            out((steps, 8, LANES), F32, "block"),
            packet_out,
        ],
        [
            pltpu.VMEM((8 + BLOCK, channels), F32),
            pltpu.VMEM((inner, LANES), F32),
            pltpu.VMEM((8, LANES), F32),
        ],
        micros=20,
    )
    packets = [(shifted(packet, "ctx", step), "whole") for step in range(1, ctx_count)]
    wz_spec = pl.BlockSpec((width, inner), lambda i: (0, 0))
    wo_spec = pl.BlockSpec((width, inner), lambda i: (0, 1))
    w2, z, dn = call(
        functools.partial(gate_matmul_kernel, counts, dp_count, parts),
        steps,
        info,
        [(value, "whole") for value in w2_parts] + [(normed, "rows"), (cotangent, "rows")],
        [out((width, 2 * inner), BF16, "whole"), row_out(inner, BF16), row_out(inner, F32)],
        micros=7,
    )
    y, hb, h, stat = call(
        functools.partial(apply_kernel, counts, len(packets)),
        steps,
        info,
        packets
        + [
            (entry, "block"),
            (decay, "block"),
            (cum, "rows"),
            (bc, "rows"),
            (ypart, "rows"),
            (z, "rows"),
            (dn, "rows"),
            (par, "whole"),
            (spread, "whole"),
        ],
        [
            row_out(inner, F32),
            out((steps, inner, LANES), BF16, "block"),
            state_out,
            out((8, rows), F32, "lanes"),
        ],
        [pltpu.VMEM((inner, LANES), F32)],
        micros=8,
    )
    stat = lax.psum(stat, "tp")
    inner_all = inner * lax.axis_size("tp")
    half = width // 2
    keep, send, gwo, small_gate, dy, dz, de, exits, packet = call(
        functools.partial(gate_back_kernel, counts, inner_all),
        steps,
        info,
        [
            (stat, "lanes"),
            (y, "rows"),
            (z, "rows"),
            (dn, "rows"),
            (cotangent, "rows"),
            (cum, "rows"),
            (bc, "rows"),
            (xc, "rows"),
            (hb, "block"),
            (decay, "block"),
            (w2, wo_spec),
            (par, "whole"),
            (spread, "whole"),
        ],
        [
            row_out(half, BF16),
            row_out(half, BF16),
            out((width, inner), BF16, "whole"),
            out((8, inner), F32, "whole"),
            row_out(inner, BF16),
            row_out(inner, BF16),
            row_out(LANES, F32),
            state_out,
            packet_out,
        ],
        [
            pltpu.VMEM((width, inner), F32),
            pltpu.VMEM((inner, LANES), F32),
            pltpu.VMEM((8, LANES), F32),
        ],
        reverse=True,
        micros=15,
    )
    packets = [(shifted(packet, "ctx", -step), "whole") for step in range(1, ctx_count)]
    with jax.named_scope("layer_out"):
        received = swapped(send)
        own_inputs = lax.dynamic_slice_in_dim(tokens, tp_index * half, half, 1).astype(F32)
        valid = (jnp.arange(rows) < fill).astype(F32)[:, None]
        layer_out = own_inputs + (keep.astype(F32) + received.astype(F32)) * valid
    dxc, dcq, dbq, row_sums, col_sums, dnz, *g2 = call(
        functools.partial(intra_back_kernel, counts, heads, dp_count),
        steps,
        info,
        [
            (dy, "rows"),
            (dz, "rows"),
            (xc, "rows"),
            (bc, "rows"),
            (cum, "rows"),
            (pre_step, "rows"),
            (hb, "block"),
            (normed, "rows"),
            (w2, wz_spec),
            (gwo, "whole"),
            (par, "whole"),
            (spread, "whole"),
        ],
        [
            row_out(inner, F32),
            row_out(LANES, F32),
            row_out(LANES, F32),
            row_out(LANES, F32),
            row_out(LANES, F32),
            row_out(width, F32),
        ]
        + [out((width // parts, 2 * inner), BF16, "whole")] * parts,
        [pltpu.VMEM((width, inner), F32), pltpu.VMEM((LANES, BLOCK), F32)],
        micros=18,
    )
    with jax.named_scope("reduce_gate_weights"):
        total2 = ctx_sum(g2) if parts > 1 else g2[0]
    grad_act, ddt, small_state = call(
        functools.partial(state_back_kernel, counts, heads, len(packets)),
        steps,
        info,
        packets
        + [
            (exits, "block"),
            (h, "block"),
            (xc, "rows"),
            (bc, "rows"),
            (cum, "rows"),
            (pre_step, "rows"),
            (de, "rows"),
            (dxc, "rows"),
            (dcq, "rows"),
            (dbq, "rows"),
            (row_sums, "rows"),
            (col_sums, "rows"),
            (decay, "block"),
            (dtp, "whole"),
            (spread, "whole"),
        ],
        [row_out(channels, F32), row_out(LANES, BF16), out((8, LANES), F32, "whole")],
        [pltpu.VMEM((inner, LANES), F32), pltpu.VMEM((8, LANES), F32)],
        reverse=True,
        micros=11,
    )
    with jax.named_scope("reduce_gate_weights"):
        if parts > 1:
            total2 = dp_sum(total2)
        else:
            total2 = whole_sum(total2)
    packed, back, *g1 = call(
        functools.partial(conv_back_kernel, counts, heads, dp_count, parts),
        steps,
        info,
        [
            (grad_act, "rows"),
            (ddt, "rows"),
            (v, "rows"),
            (v, "tail"),
            (halo_v, "whole"),
            (halo_normed, "whole"),
            (normed, "rows"),
            (small_gate, "whole"),
            (small_state, "whole"),
            (par, "whole"),
            (spread, "whole"),
        ],
        [row_out(channels + LANES, BF16), out((16, channels), BF16, "whole")]
        + [out((width // parts, channels + LANES), BF16, "whole")] * parts,
        [
            pltpu.VMEM((8 + BLOCK, channels), F32),
            pltpu.VMEM((8 + BLOCK, channels), F32),
            pltpu.VMEM((width, channels + LANES), F32),
            pltpu.VMEM((8, channels), F32),
        ],
        reverse=True,
        micros=18,
    )
    norm_rows = part_rows * dp_count
    partial, halo_grad, norm_part = call(
        functools.partial(input_back_kernel, counts, dp_count, parts),
        steps,
        info,
        [
            (packed, "rows"),
            (back, "whole"),
            (dnz, "rows"),
            (tokens, "rows"),
            (halo, "whole"),
            (w1, "whole"),
            (par, "whole"),
        ],
        [
            row_out(width, BF16),
            out((8, width), F32, "whole"),
            out((norm_rows, LANES), F32, "whole"),
        ],
        [pltpu.VMEM((8, width), F32)],
        micros=5,
    )
    other = swapped(partial)
    size = ctx_count * 2
    back = [(s, s - 2) for s in range(2, size)]
    cross = [(s, (s - 2) ^ 1) for s in range(2, size)]
    halo_a = lax.ppermute(halo_grad, ("ctx", "tp"), back)
    halo_b = lax.ppermute(halo_grad, ("ctx", "tp"), cross)
    with jax.named_scope("reduce_input_weights"):
        norm_part = jnp.pad(norm_part, ((0, 0), (channels, 0)))
        if parts > 1:
            total1 = dp_sum(ctx_sum(g1) + norm_part)
        else:
            total1 = whole_sum((g1[0].astype(F32) + norm_part).astype(BF16))
        across = swapped(total1[:, inner:])
        lane = jnp.arange(3 * LANES) - 2 * LANES
        both = (lane < 0) | ((lane >= STATE_TAPS) & (lane < BY_HEAD))
        both = both | ((lane >= NORM) & (lane < NORM + shard // part_rows))
        summed = total1[:, inner:] + jnp.where(both[None, :], across, 0)
        total1 = jnp.concatenate([total1[:, :inner], summed], axis=1)
    (grad_tokens,) = call(
        functools.partial(finish_kernel, counts),
        steps,
        info,
        [
            (partial, "rows"),
            (other, "rows"),
            (halo_a, "whole"),
            (halo_b, "whole"),
            (tokens, "rows"),
            (cotangent, "rows"),
            (par, "whole"),
        ],
        [row_out(width, F32)],
        micros=5,
    )
    with jax.named_scope("last_hop"):
        if parts > 1:
            total2 = exchanged(total2, "ctx")
            total1, grad_tokens = lax.optimization_barrier((total1, grad_tokens))
            total1 = exchanged(total1, "ctx")
        else:
            total1, total2 = [total1], [total2]
    each = HEAD // dp_count
    part_bc = bias_bc.shape[0]
    tall = -(-shard // LANES) * LANES

    def final(*sizes):
        return out(sizes, F32, "whole")

    grad_wz, grad_wo = call(
        functools.partial(unpack_gate_kernel, counts, parts),
        1,
        info,
        [(value, "whole") for value in total2],
        [final(shard, inner), final(shard, inner)],
        micros=2,
    )
    (
        grad_wx, grad_wbc, grad_wdt, grad_norm, grad_taps, grad_bias, grad_state_taps, grad_state_bias,
        grad_dt_bias, grad_a_log, grad_skip, grad_gate,
    ) = call(
        functools.partial(unpack_input_kernel, counts, heads, parts),
        1,
        info,
        [(value, "whole") for value in total1],
        [
            final(shard, inner),
            final(shard, 2 * LANES),
            final(heads, shard),
            final(1, shard),
            final(heads, CONV, each),
            final(heads, each),
            final(CONV, part_bc),
            final(1, part_bc),
            final(1, heads),
            final(1, heads),
            final(1, heads),
            final(heads, each),
        ],
        [pltpu.VMEM((tall, channels + LANES), F32)],
        micros=2,
    )
    return (
        layer_out,
        grad_tokens,
        grad_norm[0],
        grad_wz,
        grad_wx,
        grad_wbc,
        grad_wdt.T,
        grad_taps.transpose(1, 0, 2),
        grad_bias,
        grad_state_taps,
        grad_state_bias[0],
        grad_dt_bias[0],
        grad_a_log[0],
        grad_skip[0],
        grad_gate,
        grad_wo.T,
    )


def solution(mesh):
    shards = P(("dp", "ctx"), None)
    return jax.shard_map(
        body,
        mesh=mesh,
        in_specs=(
            shards,
            shards,
            P("dp", None),
            P("dp", None),
            P("dp"),
            P("dp", "tp"),
            P("dp", "tp"),
            P("dp", None),
            P("dp", "tp"),
            P(None, "tp", "dp"),
            P("tp", "dp"),
            P(None, "dp"),
            P("dp"),
            P("tp"),
            P("tp"),
            P("tp"),
            P("tp", "dp"),
            P("tp", "dp"),
        ),
        out_specs=(
            P(("dp", "ctx"), "tp"),
            shards,
            P("dp"),
            P("dp", "tp"),
            P("dp", "tp"),
            P("dp", None),
            P("dp", "tp"),
            P(None, "tp", "dp"),
            P("tp", "dp"),
            P(None, "dp"),
            P("dp"),
            P("tp"),
            P("tp"),
            P("tp"),
            P("tp", "dp"),
            P("tp", "dp"),
        ),
        check_vma=False,
    )
```

```python
import functools

import jax
import jax.numpy as jnp
from jax import lax
from jax.experimental import pallas as pl
from jax.experimental.pallas import tpu as pltpu
from jax.sharding import PartitionSpec as P

CONV = 4
BLOCK = 256
HEAD = 64
LANES = 128
EPS = 1e-05
VMEM = 56 * 1024 * 1024
F32 = jnp.float32
BF16 = jnp.bfloat16


def dot(left, right):
    return jnp.dot(left, right, preferred_element_type=F32)


def dot_tn(left, right):
    return lax.dot_general(left, right, (((0,), (0,)), ((), ())), preferred_element_type=F32)


def dot_nt(left, right):
    return lax.dot_general(left, right, (((1,), (1,)), ((), ())), preferred_element_type=F32)


def dot_exact(left, right):
    return jnp.dot(left, right, preferred_element_type=F32, precision=lax.Precision.HIGHEST)


def iota(shape, dim):
    return lax.broadcasted_iota(jnp.int32, shape, dim)


def sigmoid(value):
    return 1.0 / (1.0 + jnp.exp(-value))


def gate_sigmoid(value):
    return 0.5 * jnp.tanh(0.5 * value) + 0.5


def chunks(columns, rows=BLOCK):
    for column in range(0, columns, LANES):
        for row in range(0, rows, LANES):
            yield slice(row, row + LANES), slice(column, column + LANES)


TILES = ((0, 0), (LANES, 0), (LANES, LANES))


def tile_slices(tile):
    return slice(tile[0], tile[0] + LANES), slice(tile[1], tile[1] + LANES)


def softplus(value):
    return jnp.maximum(value, 0.0) + jnp.log1p(jnp.exp(-jnp.abs(value)))


def split(value):
    high = value.astype(BF16)
    return high, (value - high.astype(F32)).astype(BF16)


def expand(value, spread):
    return dot(jnp.concatenate(split(value), axis=1), spread[...])


def reduce_heads(value, spread):
    high, low = split(value)
    pick = spread[:LANES, :]
    return dot_nt(high, pick) + dot_nt(low, pick)


def head_column(row, channels):
    shape = (channels, LANES)
    return jnp.sum(jnp.where(iota(shape, 0) // HEAD == iota(shape, 1), row, 0.0), axis=1, keepdims=True)


def xor(value, mask):
    return jnp.bitwise_xor(value, jnp.int32(mask))


class Place:
    def __init__(self, info, counts):
        devices, sequences = counts
        own = info[devices + sequences]
        self.ctx = own
        self.tp = info[devices + sequences + 1]
        self.dp = info[devices + sequences + 2]
        self.fill = jnp.int32(0)
        self.first = jnp.int32(0)
        for device in range(devices):
            rows = info[device] * BLOCK
            self.fill = self.fill + jnp.where(own == device, rows, 0)
            self.first = self.first + jnp.where(own > device, rows, 0)
        self.ends = []
        total = jnp.int32(0)
        for sequence in range(sequences - 1):
            total = total + info[devices + sequence]
            self.ends.append(total)

    def of(self, position):
        found = (position >= self.ends[0]).astype(jnp.int32)
        for end in self.ends[1:]:
            found = found + (position >= end).astype(jnp.int32)
        return jnp.where(position < 0, -1, found)

    def rows(self, index):
        return self.of(self.first + jnp.minimum(index, self.fill - 1))

    def before(self, block):
        position = self.first + jnp.minimum(block * BLOCK, self.fill) - 1
        found = jnp.int32(0)
        for end in self.ends:
            found = found + jnp.where(position >= end, 1, 0)
        return jnp.where(position < 0, -1, found)

    def last(self, block):
        position = self.first + jnp.minimum(block * BLOCK + BLOCK - 1, self.fill - 1)
        found = jnp.int32(0)
        for end in self.ends:
            found = found + jnp.where(position >= end, 1, 0)
        return found

    def column(self, block, shift=0):
        return self.rows(block * BLOCK + shift + iota((BLOCK, 1), 0))

    def valid(self, block):
        return (block * BLOCK + iota((BLOCK, 1), 0) < self.fill).astype(F32)

    def keep(self, block):
        across = self.rows(block * BLOCK + iota((1, BLOCK), 1))
        return (self.column(block) == across) & (iota((BLOCK, BLOCK), 0) >= iota((BLOCK, BLOCK), 1))


def step_sizes(place, block, pre_step, heads):
    lane = iota((BLOCK, LANES), 1)
    return jnp.where(lane < heads, softplus(pre_step), 0.0) * place.valid(block)


def end_weights(place, block, cum):
    same = (place.column(block) == place.last(block)).astype(F32)
    return jnp.exp(cum[BLOCK - 1 :, :] - cum) * same


def enter_weights(place, block, cum):
    return jnp.exp(cum) * (place.column(block) == place.before(block)).astype(F32)


def block_decay(place, block, cum):
    return jnp.exp(cum[BLOCK - 1 :, :]) * jnp.where(place.last(block) == place.before(block), 1.0, 0.0)


def decay_tile(neg, cum, cum_rows, head, tile):
    rows, columns = tile_slices(tile)
    diff = cum[rows, head : head + 1] - cum_rows[head : head + 1, columns]
    return jnp.exp(diff + neg[rows, columns])


def both_halves(pair):
    lane = iota(pair.shape, 1)
    zero = jnp.zeros_like(pair)
    return [jnp.where(lane < HEAD, pair, zero), jnp.where(lane >= HEAD, pair, zero)]


def same_mask(place, block, tap):
    return (place.column(block, tap - (CONV - 1)) == place.column(block)).astype(F32)


def fill_masks(place, block, masks):
    for tap in range(CONV - 1):
        masks[tap] = jnp.broadcast_to(same_mask(place, block, tap), (BLOCK, LANES))


def shifted_rows(ext, masks, tap, rows, columns):
    first = 8 - (CONV - 1) + tap + rows.start
    value = ext[first : first + LANES, columns]
    return value if tap == CONV - 1 else value * masks[tap, rows, :]


def conv_chunk(shifts, par, columns):
    total = par[CONV : CONV + 1, columns]
    for tap in range(CONV):
        total = total + par[tap : tap + 1, columns] * shifts[tap]
    return total


def state_packet(state, decay):
    high, low = split(decay)
    row = iota((16, LANES), 0)
    tail = jnp.where(row == 0, high.astype(F32), jnp.where(row == 1, low.astype(F32), 0.0))
    return jnp.concatenate([state.astype(BF16), tail.astype(BF16)], axis=0)


def merge_packets(packets, inner):
    total = jnp.zeros((inner, LANES), F32)
    for packet in reversed(packets):
        tail = packet[inner : inner + 16, :].astype(F32)
        decay = tail[0:1, :] + tail[1:2, :]
        total = packet[:inner, :].astype(F32) + head_column(decay, inner) * total
    return total


def normalise(rows, gain):
    inv = lax.rsqrt(jnp.mean(rows * rows, axis=1, keepdims=True) + EPS)
    return rows * inv, inv, (rows * inv * gain).astype(BF16)


def piece_rows(place, dp_count, parts, rows):
    for part in range(parts):
        for block in range(dp_count):
            owner = xor(place.dp, block) * parts + (xor(place.ctx, part) if parts > 1 else 0)
            yield part, block, pl.multiple_of(owner * rows, rows)


def join_pieces(place, dp_count, parts, whole):
    columns = parts[0].shape[1]
    if len(parts) == 1:
        whole[:, :columns] = parts[0][...]
        return
    rows = parts[0].shape[0] // dp_count
    for part, block, first in piece_rows(place, dp_count, len(parts), rows):
        whole[pl.ds(first, rows), :columns] = parts[part][block * rows : (block + 1) * rows, :]


def cut_pieces(place, dp_count, whole, parts, lanes):
    if len(parts) == 1:
        parts[0][:, lanes] = whole[...].astype(BF16)
        return
    rows = parts[0].shape[0] // dp_count
    for part, block, first in piece_rows(place, dp_count, len(parts), rows):
        parts[part][block * rows : (block + 1) * rows, lanes] = whole[pl.ds(first, rows), :].astype(BF16)


def join_parameters(place, vectors, skip, heads, par, w1):
    shard = vectors[0].shape[1] // 2
    each = HEAD // len(vectors)
    inner = heads * HEAD
    by_channel = jnp.zeros((16, inner), F32)
    in_order = jnp.zeros((16, shard * len(vectors)), F32)
    by_state = jnp.zeros((16, 2 * LANES), F32)
    states = 2 * LANES // len(vectors)
    eye = (iota((16, LANES), 0) == iota((16, LANES), 1)).astype(BF16)
    for block, vector in enumerate(vectors):
        owner = xor(place.dp, block)
        first = pl.multiple_of(owner * shard, shard)
        w1[pl.ds(first, shard), inner + 2 * LANES :] = dot_tn(vector[:, shard:], eye).astype(BF16)
        source, target = iota((shard, inner), 0), iota((shard, inner), 1)
        pick = target == source // each * HEAD + owner * each + source % each
        by_channel = by_channel + dot(vector[:, :shard], pick.astype(BF16))
        source, target = iota((shard, in_order.shape[1]), 0), iota((shard, in_order.shape[1]), 1)
        in_order = in_order + dot(vector[:, :shard], (target == owner * shard + source).astype(BF16))
        source, target = iota((shard, 2 * LANES), 0), iota((shard, 2 * LANES), 1)
        pick = (target == owner * states + source) & (source < states)
        by_state = by_state + dot(vector[:, :shard], pick.astype(BF16))
    par[...] = jnp.zeros_like(par)
    par[0:5, :inner] = by_channel[0:5, :]
    par[0:5, inner:] = by_state[8:13, :]
    par[5:6, : in_order.shape[1]] = in_order[5:6, :]
    par[6:7, :inner] = by_channel[6:7, :]
    par[7:8, :inner] = skip


TAPS, GATE, STATE_TAPS, BY_HEAD, NORM = 12, 18, 20, 25, 26


def lanes(pieces, columns):
    rows, at = [], 0
    for first, value in pieces:
        if first > at:
            rows.append(jnp.zeros((first - at, columns), F32))
        rows.append(value)
        at = first + value.shape[0]
    rows.append(jnp.zeros((LANES - at, columns), F32))
    return jnp.concatenate(rows, axis=0)


def pack_norm(place, dp_count, part_count, row, rows):
    columns = row.shape[1]
    shard = columns // dp_count
    size = shard // rows
    total = jnp.zeros((dp_count * rows, LANES), F32)
    source, target = iota((dp_count * rows, columns), 0), iota((dp_count * rows, columns), 1)
    owner = source // rows
    if part_count > 1:
        owner = jnp.bitwise_xor(owner, place.dp)
    for lane in range(size):
        pick = target == owner * shard + lane * rows + source % rows
        total = total + dot_nt(pick.astype(BF16), lanes([(NORM + lane, row)], columns).astype(BF16))
    return total


def pack_parameters(dp_count, heads, small, gate, skip):
    inner = heads * HEAD
    each = HEAD // dp_count
    shard = inner // dp_count
    states = 2 * LANES // dp_count

    source, target = iota((inner, inner), 0), iota((inner, inner), 1)
    inside = source % shard
    pick = target == inside // each * HEAD + source // shard * each + inside % each
    by_channel = lanes([(TAPS, small[0:5, :inner]), (GATE, gate)], inner)
    total = dot_nt(pick.astype(BF16), by_channel.astype(BF16))
    source, target = iota((inner, 2 * LANES), 0), iota((inner, 2 * LANES), 1)
    inside = source % shard
    pick = (target == source // shard * states + inside) & (inside < states)
    by_state = lanes([(STATE_TAPS, small[0:5, inner : inner + 2 * LANES])], 2 * LANES)
    total = total + dot_nt(pick.astype(BF16), by_state.astype(BF16))
    source, target = iota((inner, LANES), 0) % shard, iota((inner, LANES), 1)
    for index, row in enumerate((small[6:7, :LANES], small[7:8, :LANES], skip)):
        pick = (source == target + index * heads) & (target < heads)
        total = total + dot_nt(pick.astype(BF16), lanes([(BY_HEAD, row)], LANES).astype(BF16))
    return total


def forward_kernel(
    counts, heads, dp_count, part_count, info, *refs
):
    vectors = refs[:dp_count]
    parts = refs[dp_count : dp_count + part_count]
    (
        tok, halo, dtp, spread,
        w1, par, normed_o, halo_normed_o, halo_v_o, v_o, xc_o, bc_o, ypart_o, pre_o, cum_o, entry_o, decay_o,
        packet_o, ext, run, factor, masks, gram, neg, mix,
    ) = refs[dp_count + part_count :]
    forward_block(
        counts, heads, info, vectors, parts, tok, halo, w1, par, dtp, spread,
        normed_o, halo_normed_o, halo_v_o, v_o, xc_o, bc_o, ypart_o, pre_o, cum_o, entry_o, decay_o, packet_o,
        ext, run, factor, masks, gram, neg, mix,
    )


def forward_block(
    counts, heads, info, vectors, parts, tok, halo, w1, par, dtp, spread,
    normed_o, halo_normed_o, halo_v_o, v_o, xc_o, bc_o, ypart_o, pre_o, cum_o, entry_o, decay_o, packet_o,
    ext, run, factor, masks, gram, neg, mix,
):
    block = pl.program_id(0)
    place = Place(info, counts)
    inner = heads * HEAD
    state = LANES
    channels = inner + 2 * state
    width = tok.shape[1]

    @pl.when(block == 0)
    def _():
        join_pieces(place, len(vectors), parts, w1)
        join_parameters(place, vectors, expand(dtp[...], spread)[2:3, :], heads, par, w1)

    gain = par[5:6, :width]
    _, _, normed = normalise(tok[...].astype(F32), gain)
    normed_o[...] = normed

    @pl.when(block == 0)
    def _():
        _, _, before = normalise(halo[...].astype(F32), gain)
        halo_normed_o[...] = before
        raw = dot(before, w1[:, :channels]).astype(BF16).astype(F32)
        ext[0:8, :] = raw[8:16, :]
        halo_v_o[...] = raw[8:16, :]
        run[...] = jnp.zeros_like(run)
        factor[...] = jnp.ones_like(factor)

    @pl.when(block > 0)
    def _():
        ext[0:8, :] = ext[BLOCK : BLOCK + 8, :]

    raw = dot(normed, w1[...])
    v = raw[:, :channels].astype(BF16)
    v_o[...] = v
    ext[8 : 8 + BLOCK, :] = v.astype(F32)
    fill_masks(place, block, masks)
    for rows, columns in chunks(channels):
        pre = conv_chunk([shifted_rows(ext, masks, tap, rows, columns) for tap in range(CONV)], par, columns)
        act = (pre * gate_sigmoid(pre)).astype(BF16)
        if columns.start < inner:
            xc_o[rows, columns] = act
        else:
            bc_o[rows, columns.start - inner : columns.stop - inner] = act
    xc = xc_o[...]
    bq = bc_o[:, :state]
    cq = bc_o[:, state:]
    pre_step = raw[:, channels:].astype(BF16).astype(F32) + dtp[0:1, :]
    pre_o[...] = pre_step
    step = step_sizes(place, block, pre_step, heads)
    tri = (iota((BLOCK, BLOCK), 0) >= iota((BLOCK, BLOCK), 1)).astype(F32)
    cum = dot_exact(tri, -dtp[1:2, :] * step)
    cum_o[...] = cum
    cum_rows = cum.T
    step_rows = step.T
    gram[...] = dot_nt(cq, bq)
    neg[...] = jnp.where(place.keep(block), 0.0, -1e30)

    @pl.when(block == 0)
    def _():
        mix[...] = jnp.zeros_like(mix)

    for pair in range(heads // 2):
        lanes = slice(pair * LANES, (pair + 1) * LANES)
        slot = pair % 2
        for side in range(2):
            head = 2 * pair + side
            for tile in TILES:
                rows, columns = tile_slices(tile)
                weight = decay_tile(neg, cum, cum_rows, head, tile) * step_rows[head : head + 1, columns]
                first = side * BLOCK + columns.start
                mix[slot, rows, first : first + LANES] = (gram[rows, columns] * weight).astype(BF16)
        x_pair = xc[:, lanes]
        y_pair = dot(mix[slot], jnp.concatenate(both_halves(x_pair), axis=0))
        ypart_o[:, lanes] = y_pair + par[7:8, lanes] * x_pair.astype(F32)
    weighted = (expand(end_weights(place, block, cum) * step, spread) * xc.astype(F32)).astype(BF16)
    block_state = dot_tn(weighted, bq)
    decay = block_decay(place, block, cum)
    entry_o[0] = run[...]
    total = head_column(decay, inner) * run[...] + block_state
    run[...] = total
    before = factor[0:1, :]
    row = iota((8, LANES), 0)
    decay_o[0] = jnp.where(row == 0, decay, jnp.where(row == 1, before, 0.0))
    after = before * decay
    factor[...] = jnp.broadcast_to(after, factor.shape)

    @pl.when(block == pl.num_programs(0) - 1)
    def _():
        packet_o[...] = state_packet(total, after)


def gate_matmul_kernel(counts, dp_count, part_count, info, *refs):
    parts = refs[:part_count]
    normed, cot, w2, z_o, dn_o = refs[part_count:]
    block = pl.program_id(0)
    place = Place(info, counts)
    inner = z_o.shape[1]

    @pl.when(block == 0)
    def _():
        join_pieces(place, dp_count, parts, w2)

    z_o[...] = dot(normed[...], w2[:, :inner]).astype(BF16)
    grad = (cot[...].astype(F32) * place.valid(block)).astype(BF16)
    dn_o[...] = dot(grad, w2[:, inner:])


def apply_kernel(counts, packet_count, info, *refs):
    packets = refs[:packet_count]
    entry, decay, cum, bc, ypart, z, dn, par, spread, y_o, hb_o, h_o, stat_o, start = refs[packet_count:]
    block = pl.program_id(0)
    place = Place(info, counts)
    inner = z.shape[1]

    @pl.when(block == 0)
    def _():
        start[...] = merge_packets([packet[...] for packet in packets], inner)

    state = entry[0] + head_column(decay[0, 1:2, :], inner) * start[...]
    h_o[0] = state
    low = state.astype(BF16)
    hb_o[0] = low
    cq = bc[:, LANES:]
    enter = jnp.concatenate(split(enter_weights(place, block, cum[...])), axis=1)
    squares, cross = [0.0, 0.0], [0.0, 0.0]
    for column in range(0, inner, LANES):
        columns = slice(column, column + LANES)
        read = dot_nt(cq, low[columns, :])
        wide = dot(enter, spread[:, columns])
        for half in range(2):
            rows = slice(half * LANES, (half + 1) * LANES)
            mixed = ypart[rows, columns] + wide[rows, :] * read[rows, :]
            y_o[rows, columns] = mixed
            gate = z[rows, columns].astype(F32)
            gated = mixed * gate * gate_sigmoid(gate)
            squares[half] = squares[half] + gated * gated
            cross[half] = cross[half] + par[6:7, columns] * dn[rows, columns] * gated
    squares = jnp.sum(jnp.concatenate(squares, axis=0), axis=1, keepdims=True)
    cross = jnp.sum(jnp.concatenate(cross, axis=0), axis=1, keepdims=True)
    lane = iota((BLOCK, LANES), 1)
    both = jnp.where(lane == 0, squares, jnp.where(lane == 1, cross, 0.0))
    stat_o[...] = both.T[0:8, :]


def gate_back_kernel(
    counts, inner_all, info, stat, y, z, dn, cot, cum, bc, xc, hb, decay, wo, par, spread,
    keep_o, send_o, gwo_o, small_o, dy_o, dz_o, de_o, exit_o, packet_o,
    normals, grads, dq, high, low, run, factor,
):
    step = pl.program_id(0)
    block = pl.num_programs(0) - 1 - step
    place = Place(info, counts)
    inner = z.shape[1]
    width = cot.shape[1]
    half = width // 2

    @pl.when(step == 0)
    def _():
        run[...] = jnp.zeros_like(run)
        factor[...] = jnp.ones_like(factor)
        small_o[...] = jnp.zeros_like(small_o)

    column = jnp.concatenate([stat[...], jnp.zeros((LANES - 8, BLOCK), F32)], axis=0).T
    inv = lax.rsqrt(column[:, 0:1] / inner_all + EPS)
    cross = column[:, 1:2] / inner_all * (inv * inv * inv)
    mine = pl.ds(pl.multiple_of(block * BLOCK, BLOCK), BLOCK)
    grads[mine, :] = (cot[...].astype(F32) * place.valid(block)).astype(BF16)
    cq = bc[:, LANES:]
    read = dot_nt(cq, hb[0])
    enter = jnp.concatenate(split(enter_weights(place, block, cum[...])), axis=1)
    wide = dot(enter, spread[...])
    for rows, columns in chunks(inner):
        gain = par[6:7, columns]
        inv_rows = inv[rows, :]
        gate = z[rows, columns].astype(F32)
        sig = gate_sigmoid(gate)
        silu = gate * sig
        mixed = y[rows, columns]
        gated = mixed * silu
        scaled = gated * inv_rows
        lines = pl.ds(pl.multiple_of(block * BLOCK + rows.start, LANES), LANES)
        normals[lines, columns] = (scaled * gain).astype(BF16)
        back = dn[rows, columns]
        grad_gated = inv_rows * (gain * back) - gated * cross[rows, :]
        dy = (grad_gated * silu).astype(BF16)
        dy_o[rows, columns] = dy
        dz_o[rows, columns] = (grad_gated * mixed * (sig + silu * (1.0 - sig))).astype(BF16)
        dy_float = dy.astype(F32)
        high[rows, columns], low[rows, columns] = split(dy_float * read[rows, columns])
        small_o[0:1, columns] += jnp.sum(back * scaled, axis=0, keepdims=True)
        small_o[1:2, columns] += jnp.sum(dy_float * xc[rows, columns].astype(F32), axis=0, keepdims=True)
        dq[rows, columns] = (wide[rows, columns] * dy_float).astype(BF16)
    normal = normals[mine, :]
    own = pl.multiple_of(place.tp * half, half)
    other = pl.multiple_of((1 - place.tp) * half, half)
    keep_o[...] = dot_nt(normal, wo[pl.ds(own, half), :]).astype(BF16)
    send_o[...] = dot_nt(normal, wo[pl.ds(other, half), :]).astype(BF16)
    pick = spread[:LANES, :]
    de_o[...] = dot_nt(high[...], pick) + dot_nt(low[...], pick)
    exit_o[0] = run[...]
    here = decay[0, 0:1, :]
    total = head_column(here, inner) * run[...] + dot_tn(dq[...], cq)
    run[...] = total
    after = factor[0:1, :] * here
    factor[...] = jnp.broadcast_to(after, factor.shape)

    @pl.when(step == pl.num_programs(0) - 1)
    def _():
        packet_o[...] = state_packet(total, after)
        gwo_o[...] = dot_tn(grads[...], normals[...]).astype(BF16)


def intra_back_kernel(counts, heads, dp_count, info, *refs):
    dy, dz, xc, bc, cum, pre_step, hb, normed, all_dz, wz, gwo, par, spread = refs[:13]
    dxc_o, dcq_o, dbq_o, rows_o, cols_o, dnz_o = refs[13:19]
    parts = refs[19:-6]
    acc, columns, neg, gram, grad_gram, mix = refs[-6:]
    block = pl.program_id(0)
    place = Place(info, counts)
    inner = heads * HEAD

    @pl.when(block == 0)
    def _():
        columns[...] = jnp.zeros_like(columns)
        mix[...] = jnp.zeros_like(mix)
        acc[...] = dot_tn(normed[...], all_dz[...])
        cut_pieces(place, dp_count, acc, parts, slice(0, inner))
        cut_pieces(place, dp_count, gwo, parts, slice(inner, 2 * inner))

    bq = bc[:, :LANES]
    cq = bc[:, LANES:]
    cums = cum[...]
    step = step_sizes(place, block, pre_step[...], heads)
    cum_rows = cums.T
    step_rows = step.T
    gram[...] = dot_nt(cq, bq)
    neg[...] = jnp.where(place.keep(block), 0.0, -1e30)
    lane = iota((LANES, LANES), 1)
    grad_gram[...] = jnp.zeros_like(grad_gram)
    rows_o[...] = jnp.zeros_like(rows_o)
    for pair in range(heads // 2):
        lanes_here = slice(pair * LANES, (pair + 1) * LANES)
        slot = pair % 2
        dy_pair = dy[:, lanes_here]
        x_pair = xc[:, lanes_here]
        halves = jnp.concatenate(both_halves(dy_pair), axis=0)
        grad_mixing = dot_nt(halves, x_pair)
        for side in range(2):
            head = 2 * pair + side
            row_sums, column_sums = [0.0, 0.0], [0.0, 0.0]
            for tile in TILES:
                rows, across = tile_slices(tile)
                first = side * BLOCK + rows.start
                grad_m = grad_mixing[first : first + LANES, across]
                kernel = decay_tile(neg, cums, cum_rows, head, tile)
                step_row = step_rows[head : head + 1, across]
                weighted = gram[rows, across] * kernel
                mixing = weighted * step_row
                mix[slot, first : first + LANES, across] = mixing.astype(BF16)
                grad_gram[rows, across] += grad_m * (kernel * step_row)
                row, column = rows.start // LANES, across.start // LANES
                column_sums[column] = column_sums[column] + jnp.sum(grad_m * weighted, axis=0, keepdims=True)
                row_sums[row] = row_sums[row] + grad_m * mixing
            columns[head : head + 1, :] = jnp.concatenate(column_sums, axis=1)
            for row in range(2):
                total = jnp.sum(row_sums[row], axis=1, keepdims=True)
                rows_o[row * LANES : (row + 1) * LANES, :] += jnp.where(lane == head, total, 0.0)
        dx_pair = dot_tn(mix[slot], halves)
        dxc_o[:, lanes_here] = dx_pair + par[7:8, lanes_here] * dy_pair.astype(F32)
    grad_low = grad_gram[...].astype(BF16)
    dq = (expand(enter_weights(place, block, cums), spread) * dy[...].astype(F32)).astype(BF16)
    dcq_o[...] = dot(grad_low, bq) + dot(dq, hb[0])
    dbq_o[...] = dot_tn(grad_low, cq)
    cols_o[...] = columns[...].T
    dnz_o[...] = dot_nt(dz[...], wz[...])


def state_back_kernel(counts, heads, packet_count, info, *refs):
    packets = refs[:packet_count]
    (
        exits, h, xc, bc, cum, pre_step, de, dxc, dcq, dbq, rows, cols, decay, dtp, spread,
        act_o, ddt_o, small_o,
        start, factor,
    ) = refs[packet_count:]
    step_id = pl.program_id(0)
    block = pl.num_programs(0) - 1 - step_id
    place = Place(info, counts)
    inner = heads * HEAD

    @pl.when(step_id == 0)
    def _():
        start[...] = merge_packets([packet[...] for packet in packets], inner)
        factor[...] = jnp.ones_like(factor)
        small_o[...] = jnp.zeros_like(small_o)

    here = decay[0, 0:1, :]
    before = factor[0:1, :]
    grad_state = exits[0] + head_column(before, inner) * start[...]
    factor[...] = jnp.broadcast_to(before * here, factor.shape)
    shape = (inner, LANES)
    overlap = jnp.sum(grad_state * h[0], axis=1, keepdims=True)
    grad_decay = jnp.sum(
        jnp.where(iota(shape, 0) // HEAD == iota(shape, 1), overlap, 0.0), axis=0, keepdims=True
    )
    low = grad_state.astype(BF16)
    bq = bc[:, :LANES]
    cums = cum[...]
    pre_dt = pre_step[...]
    valid = place.valid(block)
    step = step_sizes(place, block, pre_dt, heads)
    end_kernel = end_weights(place, block, cums)
    end_weight = end_kernel * step
    end_split = jnp.concatenate(split(end_weight), axis=1)
    grad_end = jnp.zeros((BLOCK, LANES), F32)
    grad_b = dbq[...]
    for column in range(0, inner, LANES):
        columns = slice(column, column + LANES)
        low_part = low[columns, :]
        spread_b = dot_nt(bq, low_part)
        wide = dot(end_split, spread[:, columns])
        x_part = xc[:, columns].astype(F32)
        act_o[:, columns] = dxc[:, columns] + wide * spread_b
        high, rest = split(x_part * spread_b)
        pick = spread[:LANES, columns]
        grad_end = grad_end + dot_nt(high, pick) + dot_nt(rest, pick)
        grad_b = grad_b + dot((x_part * wide).astype(BF16), low_part)
    act_o[:, inner : inner + LANES] = grad_b
    act_o[:, inner + LANES :] = dcq[...]
    end_part = grad_end * end_weight
    last = iota((BLOCK, LANES), 0) == BLOCK - 1
    grad_cum = rows[...] - cols[...] * step - end_part + de[...] * enter_weights(place, block, cums)
    grad_cum = grad_cum + jnp.where(
        last, jnp.sum(end_part, axis=0, keepdims=True) + grad_decay * here, 0.0
    )
    upper = (iota((BLOCK, BLOCK), 0) <= iota((BLOCK, BLOCK), 1)).astype(F32)
    grad_log = dot_exact(upper, grad_cum)
    rates = dtp[1:2, :]
    grad_step = cols[...] + grad_end * end_kernel - rates * grad_log
    heads_lane = iota((BLOCK, LANES), 1) < heads
    grad_pre_dt = jnp.where(heads_lane, grad_step * sigmoid(pre_dt), 0.0) * valid
    ddt_o[...] = grad_pre_dt.astype(BF16)
    small_o[0:1, :] += jnp.sum(grad_pre_dt, axis=0, keepdims=True)
    small_o[1:2, :] += jnp.sum(grad_log * (-rates * step), axis=0, keepdims=True)


def conv_back_kernel(counts, heads, dp_count, part_count, info, *refs):
    act, ddt, v, v_tail, halo_v, halo_normed, normed, small_gate, small_state, par, spread = refs[:11]
    packed_o, back_o = refs[11:13]
    parts = refs[13 : 13 + part_count]
    ext, grads, masks, ahead, acc, small_o = refs[13 + part_count :]
    step_id = pl.program_id(0)
    block = pl.num_programs(0) - 1 - step_id
    place = Place(info, counts)
    inner = heads * HEAD
    channels = inner + 2 * LANES

    @pl.when(step_id == 0)
    def _():
        grads[...] = jnp.zeros_like(grads)
        small_o[...] = jnp.zeros_like(small_o)

    ext[8 : 8 + BLOCK, :] = v[...].astype(F32)
    grads[8 + BLOCK :, :] = grads[8:16, :]

    @pl.when(block == 0)
    def _():
        ext[0:8, :] = halo_v[...]

    @pl.when(block > 0)
    def _():
        ext[0:8, :] = v_tail[...].astype(F32)[8:16, :]

    fill_masks(place, block, masks)
    here = place.rows(block * BLOCK - 8 + iota((8 + BLOCK, 1), 0))
    for step in range(1, CONV):
        later = place.rows(block * BLOCK - 8 + step + iota((8 + BLOCK, 1), 0))
        ahead[step - 1] = jnp.broadcast_to((here == later).astype(F32), (8 + BLOCK, LANES))
    for rows, columns in chunks(channels):
        shifts = [shifted_rows(ext, masks, tap, rows, columns) for tap in range(CONV)]
        pre = conv_chunk(shifts, par, columns)
        sig = gate_sigmoid(pre)
        grad_pre = act[rows, columns] * (sig * (1.0 + pre * (1.0 - sig)))
        grads[8 + rows.start : 8 + rows.stop, columns] = grad_pre
        small_o[4:5, columns] += jnp.sum(grad_pre, axis=0, keepdims=True)
        for tap in range(CONV):
            small_o[tap : tap + 1, columns] += jnp.sum(grad_pre * shifts[tap], axis=0, keepdims=True)

    def behind(first, size, columns):
        total = par[CONV - 1 : CONV, columns] * grads[first : first + size, columns]
        for step in range(1, CONV):
            value = grads[first + step : first + step + size, columns] * ahead[step - 1, first : first + size, :]
            total = total + par[CONV - 1 - step : CONV - step, columns] * value
        return total

    first_line = pl.multiple_of(block * BLOCK, BLOCK)
    for rows, columns in chunks(channels):
        lines = pl.ds(pl.multiple_of(first_line + rows.start, LANES), LANES)
        packed_o[lines, columns] = behind(8 + rows.start, LANES, columns).astype(BF16)
    packed_o[pl.ds(first_line, BLOCK), channels:] = ddt[...]

    @pl.when(block == 0)
    def _():
        grads[0:8, :] = jnp.zeros((8, channels), F32)
        halo_part = jnp.concatenate(
            [behind(0, 8, slice(column, column + LANES)) for column in range(0, channels, LANES)], axis=1
        )
        back = jnp.concatenate([jnp.zeros((8, channels), F32), halo_part], axis=0).astype(BF16)
        back_o[...] = back
        acc[...] = dot_tn(normed[...], packed_o[...])
        acc[:, :channels] += dot_tn(halo_normed[...], back)
        small_o[6:7, :LANES] = small_state[0:1, :]
        small_o[7:8, :LANES] = small_state[1:2, :]
        skip = reduce_heads(jnp.broadcast_to(small_gate[1:2, :], (8, inner)), spread)[0:1, :]
        acc[:, channels:] += pack_parameters(dp_count, heads, small_o, small_gate[0:1, :], skip)
        cut_pieces(place, dp_count, acc, parts, slice(0, channels + LANES))


def input_back_kernel(
    counts, dp_count, part_count, info, packed, back, dnz, tok, halo, w1, par,
    dn_o, dnh_o, norm_o, total, turned,
):
    block = pl.program_id(0)
    place = Place(info, counts)
    width = tok.shape[1]
    channels = back.shape[1]
    gain = par[5:6, :width]

    @pl.when(block == 0)
    def _():
        turned[...] = w1[...].T
        halo_grad = dot(back[...], turned[:channels, :])
        dnh_o[...] = halo_grad[8:16, :]
        halo_scaled, _, _ = normalise(halo[...].astype(F32), gain)
        total[...] = jnp.broadcast_to(
            jnp.sum(halo_grad * halo_scaled, axis=0, keepdims=True), total.shape
        )

    partial = dnz[...] + dot(packed[...], turned[...])
    dn_o[...] = partial.astype(BF16)
    scaled, _, _ = normalise(tok[...].astype(F32), gain)
    total[0:1, :] += jnp.sum(partial * scaled, axis=0, keepdims=True)

    @pl.when(block == pl.num_programs(0) - 1)
    def _():
        rows = norm_o.shape[0] // dp_count
        norm_o[...] = pack_norm(place, dp_count, part_count, total[0:1, :], rows)


def finish_kernel(counts, info, own, other, halo_a, halo_b, tok, cot, par, grad_o):
    block = pl.program_id(0)
    place = Place(info, counts)
    width = tok.shape[1]
    grad = own[...].astype(F32) + other[...].astype(F32)
    is_last = jnp.where((block + 1) * BLOCK == place.fill, 1.0, 0.0)
    halo = (halo_a[...] + halo_b[...]) * is_last
    grad = jnp.concatenate([grad[: BLOCK - 8, :], grad[BLOCK - 8 :, :] + halo], axis=0)
    inputs = tok[...].astype(F32)
    inv = lax.rsqrt(jnp.mean(inputs * inputs, axis=1, keepdims=True) + EPS)
    scaled = par[5:6, :width] * grad
    inner_dot = jnp.sum(scaled * inputs, axis=1, keepdims=True)
    grad_o[...] = (
        inv * scaled - inputs * (inv * inv * inv) * (inner_dot / width) + cot[...].astype(F32)
    )


def unpack_gate_kernel(counts, part_count, info, *refs):
    parts = refs[:part_count]
    wz_o, wo_o = refs[part_count:]
    place = Place(info, counts)
    shard, inner = wz_o.shape
    rows = shard // part_count
    for part in range(part_count):
        first = pl.multiple_of(xor(place.ctx, part) * rows, rows) if part_count > 1 else 0
        wz_o[pl.ds(first, rows), :] = parts[part][:, :inner].astype(F32)
        wo_o[pl.ds(first, rows), :] = parts[part][:, inner:].astype(F32)


def unpack_input_kernel(counts, heads, part_count, info, *refs):
    parts = refs[:part_count]
    (
        wx_o, wbc_o, wdt_o, norm_o, taps_o, bias_o, state_taps_o, state_bias_o, dt_bias_o, a_log_o, skip_o,
        gate_o, wide,
    ) = refs[part_count:]
    place = Place(info, counts)
    shard, inner = wx_o.shape
    channels = inner + 2 * LANES
    rows = shard // part_count
    for part in range(part_count):
        first = pl.multiple_of(xor(place.ctx, part) * rows, rows) if part_count > 1 else 0
        wide[pl.ds(first, rows), :] = parts[part][...].astype(F32)
    wx_o[...] = wide[:shard, :inner]
    wbc_o[...] = wide[:shard, inner:channels]
    lines = wide[:, channels:].T
    wdt_o[...] = lines[:heads, :shard]
    each = gate_o.shape[1]
    size = lines.shape[1]
    source = iota((16, size), 1)
    inside = (source // each == iota((16, size), 0)) & (source < shard)
    place_in = (iota((size, LANES), 0) % each == iota((size, LANES), 1)).astype(BF16)

    def by_head(line):
        row = jnp.where(inside, lines[line : line + 1, :], 0.0).astype(BF16)
        return dot(row, place_in)[:heads, :each]

    for tap in range(CONV):
        taps_o[:, tap, :] = by_head(TAPS + tap)
    bias_o[...] = by_head(TAPS + CONV)
    gate_o[...] = by_head(GATE)
    gain = wide[:rows, channels:]
    for part in range(1, part_count):
        gain = gain + wide[part * rows : (part + 1) * rows, channels:]
    gain = jnp.concatenate([gain, jnp.zeros((LANES - rows, LANES), F32)], axis=0).T
    source, target = iota((LANES, size), 0), iota((LANES, size), 1)
    total = jnp.zeros((8, size), F32)
    for lane in range(shard // rows):
        pick = ((target == lane * rows + source) & (source < rows)).astype(F32)
        total = total + dot_exact(jnp.broadcast_to(gain[NORM + lane : NORM + lane + 1, :], (8, LANES)), pick)
    norm_o[...] = total[0:1, :shard]
    states = state_bias_o.shape[1]
    state_taps_o[...] = lines[STATE_TAPS : STATE_TAPS + CONV, :states]
    state_bias_o[...] = lines[STATE_TAPS + CONV : STATE_TAPS + CONV + 1, :states]
    row = lines[BY_HEAD : BY_HEAD + 1, :]
    dt_bias_o[...] = row[:, :heads]
    a_log_o[...] = row[:, heads : 2 * heads]
    skip_o[...] = row[:, 2 * heads : 3 * heads]


def call(body, steps, info, operands, outputs, scratch=(), reverse=False, micros=1):
    def at(index):
        return steps - 1 - index if reverse else index

    def spec(shape, kind):
        if kind == "rows":
            return pl.BlockSpec((BLOCK,) + tuple(shape[1:]), lambda i: (at(i), 0))
        if kind == "block":
            return pl.BlockSpec((1,) + tuple(shape[1:]), lambda i: (at(i), 0, 0))
        if kind == "lanes":
            return pl.BlockSpec((shape[0], BLOCK), lambda i: (0, at(i)))
        if kind == "tail":
            each = BLOCK // 16
            return pl.BlockSpec((16, shape[1]), lambda i: (jnp.maximum(at(i) * each - 1, 0), 0))
        if kind == "whole":
            return pl.BlockSpec(tuple(shape), lambda i: (0,) * len(shape))
        return kind

    return pl.pallas_call(
        body,
        grid=(steps,),
        in_specs=[pl.BlockSpec(memory_space=pltpu.SMEM)]
        + [spec(array.shape, kind) for array, kind in operands],
        out_specs=[spec(shape.shape, kind) for shape, kind in outputs],
        out_shape=[shape for shape, _ in outputs],
        scratch_shapes=list(scratch),
        compiler_params=pltpu.CompilerParams(
            dimension_semantics=("arbitrary",), vmem_limit_bytes=VMEM
        ),
        cost_estimate=pl.CostEstimate(
            flops=micros * 1_100_000_000, bytes_accessed=micros * 3_500_000, transcendentals=0
        ),
    )(info, *[array for array, _ in operands])


def shifted(value, axis, steps):
    count = lax.axis_size(axis)
    first, last = max(0, -steps), min(count, count - steps)
    return lax.ppermute(value, axis, [(source, source + steps) for source in range(first, last)])


def swapped(value):
    return lax.ppermute(value, "tp", [(0, 1), (1, 0)])


def partnered(value, axis, mask):
    return lax.ppermute(value, axis, [(one, one ^ mask) for one in range(lax.axis_size(axis))])


def exchanged(value, axis):
    return [value] + [partnered(value, axis, mask) for mask in range(1, lax.axis_size(axis))]


def own_rows(value, rows):
    return lax.dynamic_slice_in_dim(value, lax.axis_index("ctx") * rows, rows, 0)


def joined_rows(values):
    return jnp.concatenate(values, axis=0)


def ctx_sum(pieces):
    total = pieces[0].astype(F32)
    for mask in range(1, len(pieces)):
        total = total + partnered(pieces[mask], "ctx", mask).astype(F32)
    return total


def dp_sum(total):
    dp_count = lax.axis_size("dp")
    rows = total.shape[0] // dp_count
    own = total[:rows].astype(F32)
    for mask in range(1, dp_count):
        block = total[mask * rows : (mask + 1) * rows].astype(BF16)
        own = own + partnered(block, "dp", mask).astype(F32)
    return own.astype(BF16)


def whole_sum(value):
    return lax.psum(lax.psum_scatter(value, "dp", scatter_dimension=0, tiled=True), "ctx")


def body(
    tokens, cotangent, device_fill, seq_lengths, norm_gain, w_z, w_x, w_bc, w_dt,
    conv_x, conv_x_bias, conv_bc, bias_bc, dt_bias, a_log, skip_d, gate_gain, w_out,
):
    rows, width = tokens.shape
    heads = dt_bias.shape[0]
    inner = heads * HEAD
    channels = inner + 2 * LANES
    steps = rows // BLOCK
    shard = norm_gain.shape[0]
    dp_count = lax.axis_size("dp")
    ctx_count = lax.axis_size("ctx")
    tp_index = lax.axis_index("tp")
    counts = (ctx_count, seq_lengths.shape[1])

    parts = ctx_count if shard % (16 * ctx_count) == 0 else 1
    part_rows = shard // parts

    with jax.named_scope("gather_weights"):
        vector = jnp.concatenate(
            [
                jnp.concatenate(
                    [
                        conv_x.reshape(CONV, shard),
                        conv_x_bias.reshape(1, shard),
                        norm_gain[None, :],
                        gate_gain.reshape(1, shard),
                        jnp.zeros((1, shard), BF16),
                        jnp.pad(
                            jnp.concatenate([conv_bc, bias_bc[None, :]], axis=0),
                            ((0, 3), (0, shard - bias_bc.shape[0])),
                        ),
                    ],
                    axis=0,
                ),
                jnp.pad(w_dt.T, ((0, 16 - heads), (0, 0))),
            ],
            axis=1,
        )
        input_rows = jnp.concatenate([w_x, w_bc], axis=1)
        gate_rows = jnp.concatenate([w_z, w_out.T], axis=1)
        if parts > 1:
            w1_parts = joined_rows(exchanged(own_rows(input_rows, part_rows), "dp"))
            vector = jnp.pad(vector, ((0, 0), (0, 2 * inner - 2 * shard)))
            block = jnp.concatenate([own_rows(gate_rows, part_rows), vector], axis=0)
            block, _ = lax.optimization_barrier((block, w1_parts))
            vectors = exchanged(block, "dp")
            w2_parts = exchanged(joined_rows([value[:part_rows] for value in vectors]), "ctx")
            w1_parts = exchanged(w1_parts, "ctx")
        else:
            w1_parts = [lax.all_gather(input_rows, "dp", axis=0, tiled=True)]
            w2_parts = [lax.all_gather(gate_rows, "dp", axis=0, tiled=True)]
            vectors = exchanged(vector, "dp")
    first_vector = part_rows // 16 if parts > 1 else 0
    vector_spec = pl.BlockSpec((16, 2 * shard), lambda i: (first_vector, 0))

    dtp = jnp.pad(jnp.stack([dt_bias, jnp.exp(a_log), skip_d]), ((0, 5), (0, LANES - heads)))
    shape = (2 * LANES, inner)
    spread = (iota(shape, 0) % LANES == iota(shape, 1) // HEAD).astype(BF16)
    info = jnp.concatenate(
        [
            device_fill[0],
            seq_lengths[0],
            jnp.stack([lax.axis_index("ctx"), tp_index, lax.axis_index("dp")]).astype(jnp.int32),
        ]
    )
    fill = jnp.sum(jnp.where(jnp.arange(ctx_count) == lax.axis_index("ctx"), device_fill[0], 0)) * BLOCK
    halo = shifted(lax.dynamic_slice_in_dim(tokens, fill - 16, 16, 0), "ctx", 1)

    def out(shape, dtype, kind):
        return (jax.ShapeDtypeStruct(shape, dtype), kind)

    def row_out(columns, dtype):
        return out((rows, columns), dtype, "rows")

    state_out = out((steps, inner, LANES), F32, "block")
    packet_out = out((inner + 16, LANES), BF16, "whole")

    (w1, par, normed, halo_normed, halo_v, v, xc, bc, ypart, pre_step, cum, entry, decay, packet) = call(
        functools.partial(forward_kernel, counts, heads, dp_count, parts),
        steps,
        info,
        [(value, vector_spec) for value in vectors]
        + [(value, "whole") for value in w1_parts]
        + [(tokens, "rows"), (halo, "whole"), (dtp, "whole"), (spread, "whole")],
        [
            out((width, channels + LANES), BF16, "whole"),
            out((8, channels), F32, "whole"),
            row_out(width, BF16),
            out((16, width), BF16, "whole"),
            out((8, channels), F32, "whole"),
            row_out(channels, BF16),
            row_out(inner, BF16),
            row_out(2 * LANES, BF16),
            row_out(inner, F32),
            row_out(LANES, F32),
            row_out(LANES, F32),
            state_out,
            out((steps, 8, LANES), F32, "block"),
            packet_out,
        ],
        [
            pltpu.VMEM((8 + BLOCK, channels), F32),
            pltpu.VMEM((inner, LANES), F32),
            pltpu.VMEM((8, LANES), F32),
            pltpu.VMEM((CONV - 1, BLOCK, LANES), F32),
            pltpu.VMEM((BLOCK, BLOCK), F32),
            pltpu.VMEM((BLOCK, BLOCK), F32),
            pltpu.VMEM((2, BLOCK, 2 * BLOCK), BF16),
        ],
        micros=20,
    )
    packets = [(shifted(packet, "ctx", step), "whole") for step in range(1, ctx_count)]
    wz_spec = pl.BlockSpec((width, inner), lambda i: (0, 0))
    wo_spec = pl.BlockSpec((width, inner), lambda i: (0, 1))
    w2, z, dn = call(
        functools.partial(gate_matmul_kernel, counts, dp_count, parts),
        steps,
        info,
        [(value, "whole") for value in w2_parts] + [(normed, "rows"), (cotangent, "rows")],
        [out((width, 2 * inner), BF16, "whole"), row_out(inner, BF16), row_out(inner, F32)],
        micros=7,
    )
    y, hb, h, stat = call(
        functools.partial(apply_kernel, counts, len(packets)),
        steps,
        info,
        packets
        + [
            (entry, "block"),
            (decay, "block"),
            (cum, "rows"),
            (bc, "rows"),
            (ypart, "rows"),
            (z, "rows"),
            (dn, "rows"),
            (par, "whole"),
            (spread, "whole"),
        ],
        [
            row_out(inner, F32),
            out((steps, inner, LANES), BF16, "block"),
            state_out,
            out((8, rows), F32, "lanes"),
        ],
        [pltpu.VMEM((inner, LANES), F32)],
        micros=8,
    )
    stat = lax.psum(stat, "tp")
    inner_all = inner * lax.axis_size("tp")
    half = width // 2
    keep, send, gwo, small_gate, dy, dz, de, exits, packet = call(
        functools.partial(gate_back_kernel, counts, inner_all),
        steps,
        info,
        [
            (stat, "lanes"),
            (y, "rows"),
            (z, "rows"),
            (dn, "rows"),
            (cotangent, "rows"),
            (cum, "rows"),
            (bc, "rows"),
            (xc, "rows"),
            (hb, "block"),
            (decay, "block"),
            (w2, wo_spec),
            (par, "whole"),
            (spread, "whole"),
        ],
        [
            row_out(half, BF16),
            row_out(half, BF16),
            out((width, inner), BF16, "whole"),
            out((8, inner), F32, "whole"),
            row_out(inner, BF16),
            row_out(inner, BF16),
            row_out(LANES, F32),
            state_out,
            packet_out,
        ],
        [
            pltpu.VMEM((rows, inner), BF16),
            pltpu.VMEM((rows, width), BF16),
            pltpu.VMEM((BLOCK, inner), BF16),
            pltpu.VMEM((BLOCK, inner), BF16),
            pltpu.VMEM((BLOCK, inner), BF16),
            pltpu.VMEM((inner, LANES), F32),
            pltpu.VMEM((8, LANES), F32),
        ],
        reverse=True,
        micros=15,
    )
    packets = [(shifted(packet, "ctx", -step), "whole") for step in range(1, ctx_count)]
    with jax.named_scope("layer_out"):
        received = swapped(send)
        own_inputs = lax.dynamic_slice_in_dim(tokens, tp_index * half, half, 1).astype(F32)
        valid = (jnp.arange(rows) < fill).astype(F32)[:, None]
        layer_out = own_inputs + (keep.astype(F32) + received.astype(F32)) * valid
    dxc, dcq, dbq, row_sums, col_sums, dnz, *g2 = call(
        functools.partial(intra_back_kernel, counts, heads, dp_count),
        steps,
        info,
        [
            (dy, "rows"),
            (dz, "rows"),
            (xc, "rows"),
            (bc, "rows"),
            (cum, "rows"),
            (pre_step, "rows"),
            (hb, "block"),
            (normed, "whole"),
            (dz, "whole"),
            (w2, wz_spec),
            (gwo, "whole"),
            (par, "whole"),
            (spread, "whole"),
        ],
        [
            row_out(inner, F32),
            row_out(LANES, F32),
            row_out(LANES, F32),
            row_out(LANES, F32),
            row_out(LANES, F32),
            row_out(width, F32),
        ]
        + [out((width // parts, 2 * inner), BF16, "whole")] * parts,
        [
            pltpu.VMEM((width, inner), F32),
            pltpu.VMEM((LANES, BLOCK), F32),
            pltpu.VMEM((BLOCK, BLOCK), F32),
            pltpu.VMEM((BLOCK, BLOCK), F32),
            pltpu.VMEM((BLOCK, BLOCK), F32),
            pltpu.VMEM((2, 2 * BLOCK, BLOCK), BF16),
        ],
        micros=18,
    )
    with jax.named_scope("reduce_gate_weights"):
        total2 = ctx_sum(g2) if parts > 1 else g2[0]
    grad_act, ddt, small_state = call(
        functools.partial(state_back_kernel, counts, heads, len(packets)),
        steps,
        info,
        packets
        + [
            (exits, "block"),
            (h, "block"),
            (xc, "rows"),
            (bc, "rows"),
            (cum, "rows"),
            (pre_step, "rows"),
            (de, "rows"),
            (dxc, "rows"),
            (dcq, "rows"),
            (dbq, "rows"),
            (row_sums, "rows"),
            (col_sums, "rows"),
            (decay, "block"),
            (dtp, "whole"),
            (spread, "whole"),
        ],
        [row_out(channels, F32), row_out(LANES, BF16), out((8, LANES), F32, "whole")],
        [pltpu.VMEM((inner, LANES), F32), pltpu.VMEM((8, LANES), F32)],
        reverse=True,
        micros=11,
    )
    with jax.named_scope("reduce_gate_weights"):
        if parts > 1:
            total2 = dp_sum(total2)
        else:
            total2 = whole_sum(total2)
    packed, back, *g1 = call(
        functools.partial(conv_back_kernel, counts, heads, dp_count, parts),
        steps,
        info,
        [
            (grad_act, "rows"),
            (ddt, "rows"),
            (v, "rows"),
            (v, "tail"),
            (halo_v, "whole"),
            (halo_normed, "whole"),
            (normed, "whole"),
            (small_gate, "whole"),
            (small_state, "whole"),
            (par, "whole"),
            (spread, "whole"),
        ],
        [out((rows, channels + LANES), BF16, "whole"), out((16, channels), BF16, "whole")]
        + [out((width // parts, channels + LANES), BF16, "whole")] * parts,
        [
            pltpu.VMEM((8 + BLOCK, channels), F32),
            pltpu.VMEM((16 + BLOCK, channels), F32),
            pltpu.VMEM((CONV - 1, BLOCK, LANES), F32),
            pltpu.VMEM((CONV - 1, 8 + BLOCK, LANES), F32),
            pltpu.VMEM((width, channels + LANES), F32),
            pltpu.VMEM((8, channels), F32),
        ],
        reverse=True,
        micros=18,
    )
    norm_rows = part_rows * dp_count
    if parts > 1:
        g1 = [g1[0]] + [partnered(g1[mask], "ctx", mask) for mask in range(1, parts)]
        packed, g1[1] = lax.optimization_barrier((packed, g1[1]))
    partial, halo_grad, norm_part = call(
        functools.partial(input_back_kernel, counts, dp_count, parts),
        steps,
        info,
        [
            (packed, "rows"),
            (back, "whole"),
            (dnz, "rows"),
            (tokens, "rows"),
            (halo, "whole"),
            (w1, "whole"),
            (par, "whole"),
        ],
        [
            row_out(width, BF16),
            out((8, width), F32, "whole"),
            out((norm_rows, LANES), F32, "whole"),
        ],
        [pltpu.VMEM((8, width), F32), pltpu.VMEM((channels + LANES, width), BF16)],
        micros=8,
    )
    other = swapped(partial)
    size = ctx_count * 2
    back = [(s, s - 2) for s in range(2, size)]
    cross = [(s, (s - 2) ^ 1) for s in range(2, size)]
    halo_a = lax.ppermute(halo_grad, ("ctx", "tp"), back)
    halo_b = lax.ppermute(halo_grad, ("ctx", "tp"), cross)
    with jax.named_scope("reduce_input_weights"):
        norm_part = jnp.pad(norm_part, ((0, 0), (channels, 0)))
        if parts > 1:
            total1 = dp_sum(sum(piece.astype(F32) for piece in g1) + norm_part)
        else:
            total1 = whole_sum((g1[0].astype(F32) + norm_part).astype(BF16))
        across = swapped(total1[:, inner:])
        lane = jnp.arange(3 * LANES) - 2 * LANES
        both = (lane < 0) | ((lane >= STATE_TAPS) & (lane < BY_HEAD))
        both = both | ((lane >= NORM) & (lane < NORM + shard // part_rows))
        summed = total1[:, inner:] + jnp.where(both[None, :], across, 0)
        total1 = jnp.concatenate([total1[:, :inner], summed], axis=1)
    (grad_tokens,) = call(
        functools.partial(finish_kernel, counts),
        steps,
        info,
        [
            (partial, "rows"),
            (other, "rows"),
            (halo_a, "whole"),
            (halo_b, "whole"),
            (tokens, "rows"),
            (cotangent, "rows"),
            (par, "whole"),
        ],
        [row_out(width, F32)],
        micros=5,
    )
    with jax.named_scope("last_hop"):
        if parts > 1:
            total2 = exchanged(total2, "ctx")
            total1, grad_tokens = lax.optimization_barrier((total1, grad_tokens))
            total1 = exchanged(total1, "ctx")
        else:
            total1, total2 = [total1], [total2]
    each = HEAD // dp_count
    part_bc = bias_bc.shape[0]
    tall = -(-shard // LANES) * LANES

    def final(*sizes):
        return out(sizes, F32, "whole")

    grad_wz, grad_wo = call(
        functools.partial(unpack_gate_kernel, counts, parts),
        1,
        info,
        [(value, "whole") for value in total2],
        [final(shard, inner), final(shard, inner)],
        micros=2,
    )
    (
        grad_wx, grad_wbc, grad_wdt, grad_norm, grad_taps, grad_bias, grad_state_taps, grad_state_bias,
        grad_dt_bias, grad_a_log, grad_skip, grad_gate,
    ) = call(
        functools.partial(unpack_input_kernel, counts, heads, parts),
        1,
        info,
        [(value, "whole") for value in total1],
        [
            final(shard, inner),
            final(shard, 2 * LANES),
            final(heads, shard),
            final(1, shard),
            final(heads, CONV, each),
            final(heads, each),
            final(CONV, part_bc),
            final(1, part_bc),
            final(1, heads),
            final(1, heads),
            final(1, heads),
            final(heads, each),
        ],
        [pltpu.VMEM((tall, channels + LANES), F32)],
        micros=2,
    )
    return (
        layer_out,
        grad_tokens,
        grad_norm[0],
        grad_wz,
        grad_wx,
        grad_wbc,
        grad_wdt.T,
        grad_taps.transpose(1, 0, 2),
        grad_bias,
        grad_state_taps,
        grad_state_bias[0],
        grad_dt_bias[0],
        grad_a_log[0],
        grad_skip[0],
        grad_gate,
        grad_wo.T,
    )


def solution(mesh):
    shards = P(("dp", "ctx"), None)
    return jax.shard_map(
        body,
        mesh=mesh,
        in_specs=(
            shards,
            shards,
            P("dp", None),
            P("dp", None),
            P("dp"),
            P("dp", "tp"),
            P("dp", "tp"),
            P("dp", None),
            P("dp", "tp"),
            P(None, "tp", "dp"),
            P("tp", "dp"),
            P(None, "dp"),
            P("dp"),
            P("tp"),
            P("tp"),
            P("tp"),
            P("tp", "dp"),
            P("tp", "dp"),
        ),
        out_specs=(
            P(("dp", "ctx"), "tp"),
            shards,
            P("dp"),
            P("dp", "tp"),
            P("dp", "tp"),
            P("dp", None),
            P("dp", "tp"),
            P(None, "tp", "dp"),
            P("tp", "dp"),
            P(None, "dp"),
            P("dp"),
            P("tp"),
            P("tp"),
            P("tp"),
            P("tp", "dp"),
            P("tp", "dp"),
        ),
        check_vma=False,
    )
```

```python
import functools

import jax
import jax.numpy as jnp
from jax import lax
from jax.experimental import pallas as pl
from jax.experimental.pallas import tpu as pltpu
from jax.sharding import PartitionSpec as P

CONV = 4
BLOCK = 256
HEAD = 64
LANES = 128
EPS = 1e-05
MEGA = 1024 * 1024
F32 = jnp.float32
BF16 = jnp.bfloat16


def dot(left, right):
    return jnp.dot(left, right, preferred_element_type=F32)


def dot_tn(left, right):
    return lax.dot_general(left, right, (((0,), (0,)), ((), ())), preferred_element_type=F32)


def dot_nt(left, right):
    return lax.dot_general(left, right, (((1,), (1,)), ((), ())), preferred_element_type=F32)


def dot_exact(left, right):
    return jnp.dot(left, right, preferred_element_type=F32, precision=lax.Precision.HIGHEST)


def iota(shape, dim):
    return lax.broadcasted_iota(jnp.int32, shape, dim)


def sigmoid(value):
    return 1.0 / (1.0 + jnp.exp(-value))


def gate_sigmoid(value):
    return 0.5 * jnp.tanh(0.5 * value) + 0.5


def softplus(value):
    return jnp.maximum(value, 0.0) + jnp.log1p(jnp.exp(-jnp.abs(value)))


def split(value):
    high = value.astype(BF16)
    return high, (value - high.astype(F32)).astype(BF16)


def expand(value, spread):
    return dot(jnp.concatenate(split(value), axis=1), spread[...])


def reduce_heads(value, spread):
    high, low = split(value)
    pick = spread[:LANES, :]
    return dot_nt(high, pick) + dot_nt(low, pick)


def head_column(row, channels):
    shape = (channels, LANES)
    return jnp.sum(jnp.where(iota(shape, 0) // HEAD == iota(shape, 1), row, 0.0), axis=1, keepdims=True)


def xor(value, mask):
    return jnp.bitwise_xor(value, jnp.int32(mask))


class Place:
    def __init__(self, info, counts):
        devices, sequences = counts
        own = info[devices + sequences]
        self.ctx = own
        self.tp = info[devices + sequences + 1]
        self.dp = info[devices + sequences + 2]
        self.fill = jnp.int32(0)
        self.first = jnp.int32(0)
        for device in range(devices):
            rows = info[device] * BLOCK
            self.fill = self.fill + jnp.where(own == device, rows, 0)
            self.first = self.first + jnp.where(own > device, rows, 0)
        self.ends = []
        total = jnp.int32(0)
        for sequence in range(sequences - 1):
            total = total + info[devices + sequence]
            self.ends.append(total)

    def of(self, position):
        found = (position >= self.ends[0]).astype(jnp.int32)
        for end in self.ends[1:]:
            found = found + (position >= end).astype(jnp.int32)
        return jnp.where(position < 0, -1, found)

    def rows(self, index):
        return self.of(self.first + jnp.minimum(index, self.fill - 1))

    def before(self, block):
        position = self.first + jnp.minimum(block * BLOCK, self.fill) - 1
        found = jnp.int32(0)
        for end in self.ends:
            found = found + jnp.where(position >= end, 1, 0)
        return jnp.where(position < 0, -1, found)

    def last(self, block):
        position = self.first + jnp.minimum(block * BLOCK + BLOCK - 1, self.fill - 1)
        found = jnp.int32(0)
        for end in self.ends:
            found = found + jnp.where(position >= end, 1, 0)
        return found

    def column(self, block, shift=0):
        return self.rows(block * BLOCK + shift + iota((BLOCK, 1), 0))

    def valid(self, block):
        return (block * BLOCK + iota((BLOCK, 1), 0) < self.fill).astype(F32)

    def keep(self, block):
        across = self.rows(block * BLOCK + iota((1, BLOCK), 1))
        return (self.column(block) == across) & (iota((BLOCK, BLOCK), 0) >= iota((BLOCK, BLOCK), 1))


def step_sizes(place, block, pre_step, heads):
    lane = iota((BLOCK, LANES), 1)
    return jnp.where(lane < heads, softplus(pre_step), 0.0) * place.valid(block)


def end_weights(place, block, cum):
    same = (place.column(block) == place.last(block)).astype(F32)
    return jnp.exp(cum[BLOCK - 1 :, :] - cum) * same


def enter_weights(place, block, cum):
    return jnp.exp(cum) * (place.column(block) == place.before(block)).astype(F32)


def block_decay(place, block, cum):
    return jnp.exp(cum[BLOCK - 1 :, :]) * jnp.where(place.last(block) == place.before(block), 1.0, 0.0)


def decay_kernel(keep, cum, cum_rows, head):
    return jnp.exp(jnp.where(keep, cum[:, head : head + 1] - cum_rows[head : head + 1, :], -1e30))


def both_halves(pair):
    lane = iota(pair.shape, 1)
    zero = jnp.zeros_like(pair)
    return [jnp.where(lane < HEAD, pair, zero), jnp.where(lane >= HEAD, pair, zero)]


def same_mask(place, block, tap):
    return (place.column(block, tap - (CONV - 1)) == place.column(block)).astype(F32)


def conv_pre(place, block, ext, par, channels):
    total = par[4:5, :channels]
    for tap in range(CONV):
        first = 8 - (CONV - 1) + tap
        total = total + par[tap : tap + 1, :channels] * ext[first : first + BLOCK, :] * same_mask(
            place, block, tap
        )
    return total


def state_packet(state, decay):
    high, low = split(decay)
    row = iota((16, LANES), 0)
    tail = jnp.where(row == 0, high.astype(F32), jnp.where(row == 1, low.astype(F32), 0.0))
    return jnp.concatenate([state.astype(BF16), tail.astype(BF16)], axis=0)


def merge_packets(packets, inner):
    total = jnp.zeros((inner, LANES), F32)
    for packet in reversed(packets):
        tail = packet[inner : inner + 16, :].astype(F32)
        decay = tail[0:1, :] + tail[1:2, :]
        total = packet[:inner, :].astype(F32) + head_column(decay, inner) * total
    return total


def normalise(rows, gain):
    inv = lax.rsqrt(jnp.mean(rows * rows, axis=1, keepdims=True) + EPS)
    return rows * inv, inv, (rows * inv * gain).astype(BF16)


def piece_rows(place, dp_count, parts, rows):
    for part in range(parts):
        for block in range(dp_count):
            owner = xor(place.dp, block) * parts + (xor(place.ctx, part) if parts > 1 else 0)
            yield part, block, pl.multiple_of(owner * rows, rows)


def join_pieces(place, dp_count, parts, whole):
    columns = parts[0].shape[1]
    if len(parts) == 1:
        whole[:, :columns] = parts[0][...]
        return
    rows = parts[0].shape[0] // dp_count
    for part, block, first in piece_rows(place, dp_count, len(parts), rows):
        whole[pl.ds(first, rows), :columns] = parts[part][block * rows : (block + 1) * rows, :]


def cut_pieces(place, dp_count, whole, parts, lanes):
    if len(parts) == 1:
        parts[0][:, lanes] = whole[...].astype(BF16)
        return
    rows = parts[0].shape[0] // dp_count
    for part, block, first in piece_rows(place, dp_count, len(parts), rows):
        parts[part][block * rows : (block + 1) * rows, lanes] = whole[pl.ds(first, rows), :].astype(BF16)


def join_parameters(place, vectors, skip, heads, par, w1):
    shard = vectors[0].shape[1] // 2
    each = HEAD // len(vectors)
    inner = heads * HEAD
    by_channel = jnp.zeros((16, inner), F32)
    in_order = jnp.zeros((16, shard * len(vectors)), F32)
    by_state = jnp.zeros((16, 2 * LANES), F32)
    states = 2 * LANES // len(vectors)
    eye = (iota((16, LANES), 0) == iota((16, LANES), 1)).astype(BF16)
    for block, vector in enumerate(vectors):
        owner = xor(place.dp, block)
        first = pl.multiple_of(owner * shard, shard)
        w1[pl.ds(first, shard), inner + 2 * LANES :] = dot_tn(vector[:, shard:], eye).astype(BF16)
        source, target = iota((shard, inner), 0), iota((shard, inner), 1)
        pick = target == source // each * HEAD + owner * each + source % each
        by_channel = by_channel + dot(vector[:, :shard], pick.astype(BF16))
        source, target = iota((shard, in_order.shape[1]), 0), iota((shard, in_order.shape[1]), 1)
        in_order = in_order + dot(vector[:, :shard], (target == owner * shard + source).astype(BF16))
        source, target = iota((shard, 2 * LANES), 0), iota((shard, 2 * LANES), 1)
        pick = (target == owner * states + source) & (source < states)
        by_state = by_state + dot(vector[:, :shard], pick.astype(BF16))
    par[...] = jnp.zeros_like(par)
    par[0:5, :inner] = by_channel[0:5, :]
    par[0:5, inner:] = by_state[8:13, :]
    par[5:6, : in_order.shape[1]] = in_order[5:6, :]
    par[6:7, :inner] = by_channel[6:7, :]
    par[7:8, :inner] = skip


TAPS, GATE, STATE_TAPS, BY_HEAD, NORM = 12, 18, 20, 25, 26


def lanes(pieces, columns):
    rows, at = [], 0
    for first, value in pieces:
        if first > at:
            rows.append(jnp.zeros((first - at, columns), F32))
        rows.append(value)
        at = first + value.shape[0]
    rows.append(jnp.zeros((LANES - at, columns), F32))
    return jnp.concatenate(rows, axis=0)


def pack_norm(place, dp_count, part_count, row, rows):
    columns = row.shape[1]
    shard = columns // dp_count
    size = shard // rows
    total = jnp.zeros((dp_count * rows, LANES), F32)
    source, target = iota((dp_count * rows, columns), 0), iota((dp_count * rows, columns), 1)
    owner = source // rows
    if part_count > 1:
        owner = jnp.bitwise_xor(owner, place.dp)
    for lane in range(size):
        pick = target == owner * shard + lane * rows + source % rows
        total = total + dot_nt(pick.astype(BF16), lanes([(NORM + lane, row)], columns).astype(BF16))
    return total


def pack_parameters(dp_count, heads, small, gate, skip):
    inner = heads * HEAD
    each = HEAD // dp_count
    shard = inner // dp_count
    states = 2 * LANES // dp_count

    source, target = iota((inner, inner), 0), iota((inner, inner), 1)
    inside = source % shard
    pick = target == inside // each * HEAD + source // shard * each + inside % each
    by_channel = lanes([(TAPS, small[0:5, :inner]), (GATE, gate)], inner)
    total = dot_nt(pick.astype(BF16), by_channel.astype(BF16))
    source, target = iota((inner, 2 * LANES), 0), iota((inner, 2 * LANES), 1)
    inside = source % shard
    pick = (target == source // shard * states + inside) & (inside < states)
    by_state = lanes([(STATE_TAPS, small[0:5, inner : inner + 2 * LANES])], 2 * LANES)
    total = total + dot_nt(pick.astype(BF16), by_state.astype(BF16))
    source, target = iota((inner, LANES), 0) % shard, iota((inner, LANES), 1)
    for index, row in enumerate((small[6:7, :LANES], small[7:8, :LANES], skip)):
        pick = (source == target + index * heads) & (target < heads)
        total = total + dot_nt(pick.astype(BF16), lanes([(BY_HEAD, row)], LANES).astype(BF16))
    return total


def forward_kernel(
    counts, heads, dp_count, part_count, info, *refs
):
    vectors = refs[:dp_count]
    parts = refs[dp_count : dp_count + part_count]
    (
        tok, halo, dtp, spread,
        w1, par, normed_o, halo_normed_o, halo_v_o, v_o, xc_o, bc_o, ypart_o, pre_o, cum_o, entry_o, decay_o,
        packet_o, ext, run, factor,
    ) = refs[dp_count + part_count :]
    forward_block(
        counts, heads, info, vectors, parts, tok, halo, w1, par, dtp, spread,
        normed_o, halo_normed_o, halo_v_o, v_o, xc_o, bc_o, ypart_o, pre_o, cum_o, entry_o, decay_o, packet_o,
        ext, run, factor,
    )


def forward_block(
    counts, heads, info, vectors, parts, tok, halo, w1, par, dtp, spread,
    normed_o, halo_normed_o, halo_v_o, v_o, xc_o, bc_o, ypart_o, pre_o, cum_o, entry_o, decay_o, packet_o,
    ext, run, factor,
):
    block = pl.program_id(0)
    place = Place(info, counts)
    inner = heads * HEAD
    state = LANES
    channels = inner + 2 * state
    width = tok.shape[1]

    @pl.when(block == 0)
    def _():
        join_pieces(place, len(vectors), parts, w1)
        join_parameters(place, vectors, expand(dtp[...], spread)[2:3, :], heads, par, w1)

    gain = par[5:6, :width]
    _, _, normed = normalise(tok[...].astype(F32), gain)
    normed_o[...] = normed

    @pl.when(block == 0)
    def _():
        _, _, before = normalise(halo[...].astype(F32), gain)
        halo_normed_o[...] = before
        raw = dot(before, w1[:, :channels]).astype(BF16).astype(F32)
        ext[0:8, :] = raw[8:16, :]
        halo_v_o[...] = raw[8:16, :]
        run[...] = jnp.zeros_like(run)
        factor[...] = jnp.ones_like(factor)

    @pl.when(block > 0)
    def _():
        ext[0:8, :] = ext[BLOCK : BLOCK + 8, :]

    raw = dot(normed, w1[...])
    v = raw[:, :channels].astype(BF16)
    v_o[...] = v
    ext[8 : 8 + BLOCK, :] = v.astype(F32)
    pre = conv_pre(place, block, ext, par, channels)
    act = (pre * gate_sigmoid(pre)).astype(BF16)
    xc = act[:, :inner]
    bq = act[:, inner : inner + state]
    cq = act[:, inner + state :]
    xc_o[...] = xc
    bc_o[...] = act[:, inner:]
    pre_step = raw[:, channels:].astype(BF16).astype(F32) + dtp[0:1, :]
    pre_o[...] = pre_step
    step = step_sizes(place, block, pre_step, heads)
    tri = (iota((BLOCK, BLOCK), 0) >= iota((BLOCK, BLOCK), 1)).astype(F32)
    cum = dot_exact(tri, -dtp[1:2, :] * step)
    cum_o[...] = cum
    cum_rows = cum.T
    step_rows = step.T
    gram = dot_nt(cq, bq)
    keep = place.keep(block)
    for pair in range(heads // 2):
        lanes = slice(pair * LANES, (pair + 1) * LANES)
        mixing = []
        for head in (2 * pair, 2 * pair + 1):
            weight = decay_kernel(keep, cum, cum_rows, head) * step_rows[head : head + 1, :]
            mixing.append((gram * weight).astype(BF16))
        x_pair = xc[:, lanes]
        y_pair = dot(jnp.concatenate(mixing, axis=1), jnp.concatenate(both_halves(x_pair), axis=0))
        ypart_o[:, lanes] = y_pair + par[7:8, lanes] * x_pair.astype(F32)
    weighted = (expand(end_weights(place, block, cum) * step, spread) * xc.astype(F32)).astype(BF16)
    block_state = dot_tn(weighted, bq)
    decay = block_decay(place, block, cum)
    entry_o[0] = run[...]
    total = head_column(decay, inner) * run[...] + block_state
    run[...] = total
    before = factor[0:1, :]
    row = iota((8, LANES), 0)
    decay_o[0] = jnp.where(row == 0, decay, jnp.where(row == 1, before, 0.0))
    after = before * decay
    factor[...] = jnp.broadcast_to(after, factor.shape)

    @pl.when(block == pl.num_programs(0) - 1)
    def _():
        packet_o[...] = state_packet(total, after)


def gate_matmul_kernel(counts, dp_count, part_count, info, *refs):
    parts = refs[:part_count]
    normed, cot, w2, z_o, dn_o = refs[part_count:]
    block = pl.program_id(0)
    place = Place(info, counts)
    inner = z_o.shape[1]

    @pl.when(block == 0)
    def _():
        join_pieces(place, dp_count, parts, w2)

    z_o[...] = dot(normed[...], w2[:, :inner]).astype(BF16)
    grad = (cot[...].astype(F32) * place.valid(block)).astype(BF16)
    dn_o[...] = dot(grad, w2[:, inner:])


def apply_kernel(counts, packet_count, info, *refs):
    packets = refs[:packet_count]
    entry, decay, cum, bc, ypart, z, dn, par, spread, y_o, hb_o, h_o, stat_o, start = refs[packet_count:]
    block = pl.program_id(0)
    place = Place(info, counts)
    inner = z.shape[1]

    @pl.when(block == 0)
    def _():
        start[...] = merge_packets([packet[...] for packet in packets], inner)

    state = entry[0] + head_column(decay[0, 1:2, :], inner) * start[...]
    h_o[0] = state
    low = state.astype(BF16)
    hb_o[0] = low
    cq = bc[:, LANES:]
    y = ypart[...] + expand(enter_weights(place, block, cum[...]), spread) * dot_nt(cq, low)
    y_o[...] = y
    gate = z[...].astype(F32)
    gated = y * gate * gate_sigmoid(gate)
    squares = jnp.sum(gated * gated, axis=1, keepdims=True)
    cross = jnp.sum(par[6:7, :inner] * dn[...] * gated, axis=1, keepdims=True)
    lane = iota((BLOCK, LANES), 1)
    both = jnp.where(lane == 0, squares, jnp.where(lane == 1, cross, 0.0))
    stat_o[...] = both.T[0:8, :]


def gate_back_kernel(
    counts, inner_all, info, stat, y, z, dn, cot, cum, bc, xc, hb, decay, wo, par, spread,
    keep_o, send_o, gwo_o, small_o, dy_o, dz_o, de_o, exit_o, packet_o,
    acc, run, factor,
):
    step = pl.program_id(0)
    block = pl.num_programs(0) - 1 - step
    place = Place(info, counts)
    inner = z.shape[1]
    width = cot.shape[1]
    half = width // 2

    @pl.when(step == 0)
    def _():
        acc[...] = jnp.zeros_like(acc)
        run[...] = jnp.zeros_like(run)
        factor[...] = jnp.ones_like(factor)
        small_o[...] = jnp.zeros_like(small_o)

    column = jnp.concatenate([stat[...], jnp.zeros((LANES - 8, BLOCK), F32)], axis=0).T
    inv = lax.rsqrt(column[:, 0:1] / inner_all + EPS)
    cross = column[:, 1:2]
    gain = par[6:7, :inner]
    gate = z[...].astype(F32)
    sig = gate_sigmoid(gate)
    silu = gate * sig
    mixed = y[...]
    gated = mixed * silu
    normal = (gated * inv * gain).astype(BF16)
    own = pl.multiple_of(place.tp * half, half)
    other = pl.multiple_of((1 - place.tp) * half, half)
    keep_o[...] = dot_nt(normal, wo[pl.ds(own, half), :]).astype(BF16)
    send_o[...] = dot_nt(normal, wo[pl.ds(other, half), :]).astype(BF16)
    grad = (cot[...].astype(F32) * place.valid(block)).astype(BF16)
    acc[...] += dot_tn(grad, normal)
    back = dn[...]
    grad_gated = inv * (gain * back) - gated * (inv * inv * inv) * (cross / inner_all)
    dy = (grad_gated * silu).astype(BF16)
    dy_o[...] = dy
    dz_o[...] = (grad_gated * mixed * sig * (1.0 + gate * (1.0 - sig))).astype(BF16)
    dy_float = dy.astype(F32)
    cq = bc[:, LANES:]
    read = dot_nt(cq, hb[0])
    de_o[...] = reduce_heads(dy_float * read, spread)
    small_o[0:1, :] += jnp.sum(back * gated * inv, axis=0, keepdims=True)
    small_o[1:2, :] += jnp.sum(dy_float * xc[...].astype(F32), axis=0, keepdims=True)
    dq = (expand(enter_weights(place, block, cum[...]), spread) * dy_float).astype(BF16)
    exit_o[0] = run[...]
    here = decay[0, 0:1, :]
    total = head_column(here, inner) * run[...] + dot_tn(dq, cq)
    run[...] = total
    after = factor[0:1, :] * here
    factor[...] = jnp.broadcast_to(after, factor.shape)

    @pl.when(step == pl.num_programs(0) - 1)
    def _():
        packet_o[...] = state_packet(total, after)
        gwo_o[...] = acc[...].astype(BF16)


def intra_back_kernel(counts, heads, dp_count, info, *refs):
    dy, dz, xc, bc, cum, pre_step, hb, normed, wz, gwo, par, spread = refs[:12]
    dxc_o, dcq_o, dbq_o, rows_o, cols_o, dnz_o = refs[12:18]
    parts = refs[18:-2]
    acc, columns = refs[-2:]
    block = pl.program_id(0)
    place = Place(info, counts)
    inner = heads * HEAD

    @pl.when(block == 0)
    def _():
        acc[...] = jnp.zeros_like(acc)
        columns[...] = jnp.zeros_like(columns)

    bq = bc[:, :LANES]
    cq = bc[:, LANES:]
    cums = cum[...]
    step = step_sizes(place, block, pre_step[...], heads)
    cum_rows = cums.T
    step_rows = step.T
    gram = dot_nt(cq, bq)
    keep = place.keep(block)
    lane = iota((BLOCK, LANES), 1)
    grad_gram = jnp.zeros((BLOCK, BLOCK), F32)
    sums = jnp.zeros((BLOCK, LANES), F32)
    for pair in range(heads // 2):
        lanes = slice(pair * LANES, (pair + 1) * LANES)
        dy_pair = dy[:, lanes]
        x_pair = xc[:, lanes]
        halves = jnp.concatenate(both_halves(dy_pair), axis=0)
        grad_mixing = dot_nt(halves, x_pair)
        mixing = []
        for side in range(2):
            head = 2 * pair + side
            grad_m = grad_mixing[side * BLOCK : (side + 1) * BLOCK, :]
            kernel = decay_kernel(keep, cums, cum_rows, head)
            step_row = step_rows[head : head + 1, :]
            weight = kernel * step_row
            mixing.append((gram * weight).astype(BF16))
            grad_gram = grad_gram + grad_m * weight
            part = grad_m * gram * kernel
            columns[head : head + 1, :] = jnp.sum(part, axis=0, keepdims=True)
            sums = sums + jnp.where(lane == head, jnp.sum(part * step_row, axis=1, keepdims=True), 0.0)
        dx_pair = dot_tn(jnp.concatenate(mixing, axis=0), halves)
        dxc_o[:, lanes] = dx_pair + par[7:8, lanes] * dy_pair.astype(F32)
    grad_low = grad_gram.astype(BF16)
    dq = (expand(enter_weights(place, block, cums), spread) * dy[...].astype(F32)).astype(BF16)
    dcq_o[...] = dot(grad_low, bq) + dot(dq, hb[0])
    dbq_o[...] = dot_tn(grad_low, cq)
    rows_o[...] = sums
    cols_o[...] = columns[...].T
    dnz_o[...] = dot_nt(dz[...], wz[...])
    acc[...] += dot_tn(normed[...], dz[...])

    @pl.when(block == pl.num_programs(0) - 1)
    def _():
        cut_pieces(place, dp_count, acc, parts, slice(0, inner))
        cut_pieces(place, dp_count, gwo, parts, slice(inner, 2 * inner))


def state_back_kernel(counts, heads, dp_count, packet_count, part_count, info, *refs):
    packets = refs[:packet_count]
    (
        exits, h, xc, bc, cum, pre_step, de, dxc, dcq, dbq, rows, cols, decay, v, v_tail, halo_v, halo_normed,
        normed, small_gate, par, dtp, spread,
        packed_o, back_o,
    ) = refs[packet_count : -6 - part_count]
    parts = refs[-6 - part_count : -6]
    start, factor, ext, grad_ext, acc, small_o = refs[-6:]
    step_id = pl.program_id(0)
    block = pl.num_programs(0) - 1 - step_id
    place = Place(info, counts)
    inner = heads * HEAD
    channels = inner + 2 * LANES

    @pl.when(step_id == 0)
    def _():
        start[...] = merge_packets([packet[...] for packet in packets], inner)
        factor[...] = jnp.ones_like(factor)
        acc[...] = jnp.zeros_like(acc)
        grad_ext[...] = jnp.zeros_like(grad_ext)
        small_o[...] = jnp.zeros_like(small_o)

    here = decay[0, 0:1, :]
    before = factor[0:1, :]
    grad_state = exits[0] + head_column(before, inner) * start[...]
    factor[...] = jnp.broadcast_to(before * here, factor.shape)
    shape = (inner, LANES)
    overlap = jnp.sum(grad_state * h[0], axis=1, keepdims=True)
    grad_decay = jnp.sum(
        jnp.where(iota(shape, 0) // HEAD == iota(shape, 1), overlap, 0.0), axis=0, keepdims=True
    )
    low = grad_state.astype(BF16)
    bq = bc[:, :LANES]
    cums = cum[...]
    x_float = xc[...].astype(F32)
    pre_dt = pre_step[...]
    valid = place.valid(block)
    step = step_sizes(place, block, pre_dt, heads)
    end_kernel = end_weights(place, block, cums)
    end_weight = end_kernel * step
    end_wide = expand(end_weight, spread)
    spread_b = dot_nt(bq, low)
    grad_x = dxc[...] + end_wide * spread_b
    grad_end = reduce_heads(x_float * spread_b, spread)
    grad_b = dbq[...] + dot((x_float * end_wide).astype(BF16), low)
    end_part = grad_end * end_weight
    last = iota((BLOCK, LANES), 0) == BLOCK - 1
    grad_cum = rows[...] - cols[...] * step - end_part + de[...] * enter_weights(place, block, cums)
    grad_cum = grad_cum + jnp.where(
        last, jnp.sum(end_part, axis=0, keepdims=True) + grad_decay * here, 0.0
    )
    upper = (iota((BLOCK, BLOCK), 0) <= iota((BLOCK, BLOCK), 1)).astype(F32)
    grad_log = dot_exact(upper, grad_cum)
    rates = dtp[1:2, :]
    grad_step = cols[...] + grad_end * end_kernel - rates * grad_log
    heads_lane = iota((BLOCK, LANES), 1) < heads
    grad_pre_dt = jnp.where(heads_lane, grad_step * sigmoid(pre_dt), 0.0) * valid
    small_o[6:7, :LANES] += jnp.sum(grad_pre_dt, axis=0, keepdims=True)
    small_o[7:8, :LANES] += jnp.sum(grad_log * (-rates * step), axis=0, keepdims=True)

    ext[8 : 8 + BLOCK, :] = v[...].astype(F32)

    @pl.when(block == 0)
    def _():
        ext[0:8, :] = halo_v[...]

    @pl.when(block > 0)
    def _():
        ext[0:8, :] = v_tail[...].astype(F32)[8:16, :]

    pre = conv_pre(place, block, ext, par, channels)
    sig = gate_sigmoid(pre)
    slope = sig * (1.0 + pre * (1.0 - sig))
    grad_pre = jnp.concatenate([grad_x, grad_b, dcq[...]], axis=1) * slope
    small_o[4:5, :] += jnp.sum(grad_pre, axis=0, keepdims=True)
    carry = grad_ext[0:8, :]
    grad_ext[0:BLOCK, :] = jnp.zeros((BLOCK, channels), F32)
    grad_ext[BLOCK : BLOCK + 8, :] = carry
    for tap in range(CONV):
        first = 8 - (CONV - 1) + tap
        masked = grad_pre * same_mask(place, block, tap)
        small_o[tap : tap + 1, :] += jnp.sum(masked * ext[first : first + BLOCK, :], axis=0, keepdims=True)
        grad_ext[first : first + BLOCK, :] += par[tap : tap + 1, :channels] * masked
    packed = jnp.concatenate([grad_ext[8 : 8 + BLOCK, :].astype(BF16), grad_pre_dt.astype(BF16)], axis=1)
    packed_o[...] = packed
    acc[...] += dot_tn(normed[...], packed)

    @pl.when(block == 0)
    def _():
        back = jnp.concatenate([jnp.zeros((8, channels), F32), grad_ext[0:8, :]], axis=0).astype(BF16)
        back_o[...] = back
        acc[:, :channels] += dot_tn(halo_normed[...], back)
        skip = reduce_heads(jnp.broadcast_to(small_gate[1:2, :], (8, inner)), spread)[0:1, :]
        acc[:, channels:] += pack_parameters(dp_count, heads, small_o, small_gate[0:1, :], skip)
        cut_pieces(place, dp_count, acc, parts, slice(0, channels + LANES))


def input_back_kernel(
    counts, dp_count, part_count, info, packed, back, dnz, tok, halo, w1, par,
    dn_o, dnh_o, norm_o, total,
):
    block = pl.program_id(0)
    place = Place(info, counts)
    width = tok.shape[1]
    channels = back.shape[1]
    gain = par[5:6, :width]

    @pl.when(block == 0)
    def _():
        halo_grad = dot_nt(back[...], w1[:, :channels])
        dnh_o[...] = halo_grad[8:16, :]
        halo_scaled, _, _ = normalise(halo[...].astype(F32), gain)
        total[...] = jnp.broadcast_to(
            jnp.sum(halo_grad * halo_scaled, axis=0, keepdims=True), total.shape
        )

    partial = dnz[...] + dot_nt(packed[...], w1[...])
    dn_o[...] = partial.astype(BF16)
    scaled, _, _ = normalise(tok[...].astype(F32), gain)
    total[0:1, :] += jnp.sum(partial * scaled, axis=0, keepdims=True)

    @pl.when(block == pl.num_programs(0) - 1)
    def _():
        rows = norm_o.shape[0] // dp_count
        norm_o[...] = pack_norm(place, dp_count, part_count, total[0:1, :], rows)


def finish_kernel(counts, info, own, other, halo_a, halo_b, tok, cot, par, grad_o):
    block = pl.program_id(0)
    place = Place(info, counts)
    width = tok.shape[1]
    grad = own[...].astype(F32) + other[...].astype(F32)
    is_last = jnp.where((block + 1) * BLOCK == place.fill, 1.0, 0.0)
    halo = (halo_a[...] + halo_b[...]) * is_last
    grad = jnp.concatenate([grad[: BLOCK - 8, :], grad[BLOCK - 8 :, :] + halo], axis=0)
    inputs = tok[...].astype(F32)
    inv = lax.rsqrt(jnp.mean(inputs * inputs, axis=1, keepdims=True) + EPS)
    scaled = par[5:6, :width] * grad
    inner_dot = jnp.sum(scaled * inputs, axis=1, keepdims=True)
    grad_o[...] = (
        inv * scaled - inputs * (inv * inv * inv) * (inner_dot / width) + cot[...].astype(F32)
    )


def unpack_gate_kernel(counts, part_count, info, *refs):
    parts = refs[:part_count]
    wz_o, wo_o = refs[part_count:]
    place = Place(info, counts)
    shard, inner = wz_o.shape
    rows = shard // part_count
    for part in range(part_count):
        first = pl.multiple_of(xor(place.ctx, part) * rows, rows) if part_count > 1 else 0
        wz_o[pl.ds(first, rows), :] = parts[part][:, :inner].astype(F32)
        wo_o[pl.ds(first, rows), :] = parts[part][:, inner:].astype(F32)


def unpack_input_kernel(counts, heads, part_count, info, *refs):
    parts = refs[:part_count]
    (
        wx_o, wbc_o, wdt_o, norm_o, taps_o, bias_o, state_taps_o, state_bias_o, dt_bias_o, a_log_o, skip_o,
        gate_o, wide,
    ) = refs[part_count:]
    place = Place(info, counts)
    shard, inner = wx_o.shape
    channels = inner + 2 * LANES
    rows = shard // part_count
    for part in range(part_count):
        first = pl.multiple_of(xor(place.ctx, part) * rows, rows) if part_count > 1 else 0
        wide[pl.ds(first, rows), :] = parts[part][...].astype(F32)
    wx_o[...] = wide[:shard, :inner]
    wbc_o[...] = wide[:shard, inner:channels]
    lines = wide[:, channels:].T
    wdt_o[...] = lines[:heads, :shard]
    each = gate_o.shape[1]
    size = lines.shape[1]
    source = iota((16, size), 1)
    inside = (source // each == iota((16, size), 0)) & (source < shard)
    place_in = (iota((size, LANES), 0) % each == iota((size, LANES), 1)).astype(BF16)

    def by_head(line):
        row = jnp.where(inside, lines[line : line + 1, :], 0.0).astype(BF16)
        return dot(row, place_in)[:heads, :each]

    for tap in range(CONV):
        taps_o[:, tap, :] = by_head(TAPS + tap)
    bias_o[...] = by_head(TAPS + CONV)
    gate_o[...] = by_head(GATE)
    gain = wide[:rows, channels:]
    for part in range(1, part_count):
        gain = gain + wide[part * rows : (part + 1) * rows, channels:]
    gain = jnp.concatenate([gain, jnp.zeros((LANES - rows, LANES), F32)], axis=0).T
    source, target = iota((LANES, size), 0), iota((LANES, size), 1)
    total = jnp.zeros((8, size), F32)
    for lane in range(shard // rows):
        pick = ((target == lane * rows + source) & (source < rows)).astype(F32)
        total = total + dot_exact(jnp.broadcast_to(gain[NORM + lane : NORM + lane + 1, :], (8, LANES)), pick)
    norm_o[...] = total[0:1, :shard]
    states = state_bias_o.shape[1]
    state_taps_o[...] = lines[STATE_TAPS : STATE_TAPS + CONV, :states]
    state_bias_o[...] = lines[STATE_TAPS + CONV : STATE_TAPS + CONV + 1, :states]
    row = lines[BY_HEAD : BY_HEAD + 1, :]
    dt_bias_o[...] = row[:, :heads]
    a_log_o[...] = row[:, heads : 2 * heads]
    skip_o[...] = row[:, 2 * heads : 3 * heads]


def call(body, steps, info, operands, outputs, scratch=(), reverse=False, micros=1, mega=20):
    def at(index):
        return steps - 1 - index if reverse else index

    def spec(shape, kind):
        if kind == "rows":
            return pl.BlockSpec((BLOCK,) + tuple(shape[1:]), lambda i: (at(i), 0))
        if kind == "block":
            return pl.BlockSpec((1,) + tuple(shape[1:]), lambda i: (at(i), 0, 0))
        if kind == "lanes":
            return pl.BlockSpec((shape[0], BLOCK), lambda i: (0, at(i)))
        if kind == "tail":
            each = BLOCK // 16
            return pl.BlockSpec((16, shape[1]), lambda i: (jnp.maximum(at(i) * each - 1, 0), 0))
        if kind == "whole":
            return pl.BlockSpec(tuple(shape), lambda i: (0,) * len(shape))
        return kind

    return pl.pallas_call(
        body,
        grid=(steps,),
        in_specs=[pl.BlockSpec(memory_space=pltpu.SMEM)]
        + [spec(array.shape, kind) for array, kind in operands],
        out_specs=[spec(shape.shape, kind) for shape, kind in outputs],
        out_shape=[shape for shape, _ in outputs],
        scratch_shapes=list(scratch),
        compiler_params=pltpu.CompilerParams(
            dimension_semantics=("arbitrary",), vmem_limit_bytes=mega * MEGA
        ),
        cost_estimate=pl.CostEstimate(
            flops=micros * 1_100_000_000, bytes_accessed=micros * 3_500_000, transcendentals=0
        ),
    )(info, *[array for array, _ in operands])


def shifted(value, axis, steps):
    count = lax.axis_size(axis)
    first, last = max(0, -steps), min(count, count - steps)
    return lax.ppermute(value, axis, [(source, source + steps) for source in range(first, last)])


def swapped(value):
    return lax.ppermute(value, "tp", [(0, 1), (1, 0)])


def partnered(value, axis, mask):
    return lax.ppermute(value, axis, [(one, one ^ mask) for one in range(lax.axis_size(axis))])


def exchanged(value, axis):
    return [value] + [partnered(value, axis, mask) for mask in range(1, lax.axis_size(axis))]


def own_rows(value, rows):
    return lax.dynamic_slice_in_dim(value, lax.axis_index("ctx") * rows, rows, 0)


def joined_rows(values):
    return jnp.concatenate(values, axis=0)


def ctx_sum(pieces):
    total = pieces[0].astype(F32)
    for mask in range(1, len(pieces)):
        total = total + partnered(pieces[mask], "ctx", mask).astype(F32)
    return total


def dp_sum(total):
    dp_count = lax.axis_size("dp")
    rows = total.shape[0] // dp_count
    own = total[:rows].astype(F32)
    for mask in range(1, dp_count):
        block = total[mask * rows : (mask + 1) * rows].astype(BF16)
        own = own + partnered(block, "dp", mask).astype(F32)
    return own.astype(BF16)


def whole_sum(value):
    return lax.psum(lax.psum_scatter(value, "dp", scatter_dimension=0, tiled=True), "ctx")


def body(
    tokens, cotangent, device_fill, seq_lengths, norm_gain, w_z, w_x, w_bc, w_dt,
    conv_x, conv_x_bias, conv_bc, bias_bc, dt_bias, a_log, skip_d, gate_gain, w_out,
):
    rows, width = tokens.shape
    heads = dt_bias.shape[0]
    inner = heads * HEAD
    channels = inner + 2 * LANES
    steps = rows // BLOCK
    shard = norm_gain.shape[0]
    dp_count = lax.axis_size("dp")
    ctx_count = lax.axis_size("ctx")
    tp_index = lax.axis_index("tp")
    counts = (ctx_count, seq_lengths.shape[1])

    parts = ctx_count if shard % (16 * ctx_count) == 0 else 1
    part_rows = shard // parts

    with jax.named_scope("gather_weights"):
        vector = jnp.concatenate(
            [
                jnp.concatenate(
                    [
                        conv_x.reshape(CONV, shard),
                        conv_x_bias.reshape(1, shard),
                        norm_gain[None, :],
                        gate_gain.reshape(1, shard),
                        jnp.zeros((1, shard), BF16),
                        jnp.pad(
                            jnp.concatenate([conv_bc, bias_bc[None, :]], axis=0),
                            ((0, 3), (0, shard - bias_bc.shape[0])),
                        ),
                    ],
                    axis=0,
                ),
                jnp.pad(w_dt.T, ((0, 16 - heads), (0, 0))),
            ],
            axis=1,
        )
        input_rows = jnp.concatenate([w_x, w_bc], axis=1)
        gate_rows = jnp.concatenate([w_z, w_out.T], axis=1)
        if parts > 1:
            w1_parts = joined_rows(exchanged(own_rows(input_rows, part_rows), "dp"))
            vector = jnp.pad(vector, ((0, 0), (0, 2 * inner - 2 * shard)))
            block = jnp.concatenate([own_rows(gate_rows, part_rows), vector], axis=0)
            block, _ = lax.optimization_barrier((block, w1_parts))
            vectors = exchanged(block, "dp")
            w2_parts = exchanged(joined_rows([value[:part_rows] for value in vectors]), "ctx")
            w1_parts = exchanged(w1_parts, "ctx")
        else:
            w1_parts = [lax.all_gather(input_rows, "dp", axis=0, tiled=True)]
            w2_parts = [lax.all_gather(gate_rows, "dp", axis=0, tiled=True)]
            vectors = exchanged(vector, "dp")
    first_vector = part_rows // 16 if parts > 1 else 0
    vector_spec = pl.BlockSpec((16, 2 * shard), lambda i: (first_vector, 0))

    dtp = jnp.pad(jnp.stack([dt_bias, jnp.exp(a_log), skip_d]), ((0, 5), (0, LANES - heads)))
    shape = (2 * LANES, inner)
    spread = (iota(shape, 0) % LANES == iota(shape, 1) // HEAD).astype(BF16)
    info = jnp.concatenate(
        [
            device_fill[0],
            seq_lengths[0],
            jnp.stack([lax.axis_index("ctx"), tp_index, lax.axis_index("dp")]).astype(jnp.int32),
        ]
    )
    fill = jnp.sum(jnp.where(jnp.arange(ctx_count) == lax.axis_index("ctx"), device_fill[0], 0)) * BLOCK
    halo = shifted(lax.dynamic_slice_in_dim(tokens, fill - 16, 16, 0), "ctx", 1)

    def out(shape, dtype, kind):
        return (jax.ShapeDtypeStruct(shape, dtype), kind)

    def row_out(columns, dtype):
        return out((rows, columns), dtype, "rows")

    state_out = out((steps, inner, LANES), F32, "block")
    packet_out = out((inner + 16, LANES), BF16, "whole")

    (w1, par, normed, halo_normed, halo_v, v, xc, bc, ypart, pre_step, cum, entry, decay, packet) = call(
        functools.partial(forward_kernel, counts, heads, dp_count, parts),
        steps,
        info,
        [(value, vector_spec) for value in vectors]
        + [(value, "whole") for value in w1_parts]
        + [(tokens, "rows"), (halo, "whole"), (dtp, "whole"), (spread, "whole")],
        [
            out((width, channels + LANES), BF16, "whole"),
            out((8, channels), F32, "whole"),
            row_out(width, BF16),
            out((16, width), BF16, "whole"),
            out((8, channels), F32, "whole"),
            row_out(channels, BF16),
            row_out(inner, BF16),
            row_out(2 * LANES, BF16),
            row_out(inner, F32),
            row_out(LANES, F32),
            row_out(LANES, F32),
            state_out,
            out((steps, 8, LANES), F32, "block"),
            packet_out,
        ],
        [
            pltpu.VMEM((8 + BLOCK, channels), F32),
            pltpu.VMEM((inner, LANES), F32),
            pltpu.VMEM((8, LANES), F32),
        ],
        micros=20,
        mega=28,
    )
    packets = [(shifted(packet, "ctx", step), "whole") for step in range(1, ctx_count)]
    wz_spec = pl.BlockSpec((width, inner), lambda i: (0, 0))
    wo_spec = pl.BlockSpec((width, inner), lambda i: (0, 1))
    w2, z, dn = call(
        functools.partial(gate_matmul_kernel, counts, dp_count, parts),
        steps,
        info,
        [(value, "whole") for value in w2_parts] + [(normed, "rows"), (cotangent, "rows")],
        [out((width, 2 * inner), BF16, "whole"), row_out(inner, BF16), row_out(inner, F32)],
        micros=7,
        mega=20,
    )
    y, hb, h, stat = call(
        functools.partial(apply_kernel, counts, len(packets)),
        steps,
        info,
        packets
        + [
            (entry, "block"),
            (decay, "block"),
            (cum, "rows"),
            (bc, "rows"),
            (ypart, "rows"),
            (z, "rows"),
            (dn, "rows"),
            (par, "whole"),
            (spread, "whole"),
        ],
        [
            row_out(inner, F32),
            out((steps, inner, LANES), BF16, "block"),
            state_out,
            out((8, rows), F32, "lanes"),
        ],
        [pltpu.VMEM((inner, LANES), F32)],
        micros=8,
    )
    stat = lax.psum(stat, "tp")
    inner_all = inner * lax.axis_size("tp")
    half = width // 2
    keep, send, gwo, small_gate, dy, dz, de, exits, packet = call(
        functools.partial(gate_back_kernel, counts, inner_all),
        steps,
        info,
        [
            (stat, "lanes"),
            (y, "rows"),
            (z, "rows"),
            (dn, "rows"),
            (cotangent, "rows"),
            (cum, "rows"),
            (bc, "rows"),
            (xc, "rows"),
            (hb, "block"),
            (decay, "block"),
            (w2, wo_spec),
            (par, "whole"),
            (spread, "whole"),
        ],
        [
            row_out(half, BF16),
            row_out(half, BF16),
            out((width, inner), BF16, "whole"),
            out((8, inner), F32, "whole"),
            row_out(inner, BF16),
            row_out(inner, BF16),
            row_out(LANES, F32),
            state_out,
            packet_out,
        ],
        [
            pltpu.VMEM((width, inner), F32),
            pltpu.VMEM((inner, LANES), F32),
            pltpu.VMEM((8, LANES), F32),
        ],
        reverse=True,
        micros=15,
        mega=24,
    )
    packets = [(shifted(packet, "ctx", -step), "whole") for step in range(1, ctx_count)]
    with jax.named_scope("layer_out"):
        received = swapped(send)
        own_inputs = lax.dynamic_slice_in_dim(tokens, tp_index * half, half, 1).astype(F32)
        valid = (jnp.arange(rows) < fill).astype(F32)[:, None]
        layer_out = own_inputs + (keep.astype(F32) + received.astype(F32)) * valid
    dxc, dcq, dbq, row_sums, col_sums, dnz, *g2 = call(
        functools.partial(intra_back_kernel, counts, heads, dp_count),
        steps,
        info,
        [
            (dy, "rows"),
            (dz, "rows"),
            (xc, "rows"),
            (bc, "rows"),
            (cum, "rows"),
            (pre_step, "rows"),
            (hb, "block"),
            (normed, "rows"),
            (w2, wz_spec),
            (gwo, "whole"),
            (par, "whole"),
            (spread, "whole"),
        ],
        [
            row_out(inner, F32),
            row_out(LANES, F32),
            row_out(LANES, F32),
            row_out(LANES, F32),
            row_out(LANES, F32),
            row_out(width, F32),
        ]
        + [out((width // parts, 2 * inner), BF16, "whole")] * parts,
        [pltpu.VMEM((width, inner), F32), pltpu.VMEM((LANES, BLOCK), F32)],
        micros=18,
        mega=24,
    )
    with jax.named_scope("reduce_gate_weights"):
        total2 = ctx_sum(g2) if parts > 1 else g2[0]
    packed, back, *g1 = call(
        functools.partial(state_back_kernel, counts, heads, dp_count, len(packets), parts),
        steps,
        info,
        packets
        + [
            (exits, "block"),
            (h, "block"),
            (xc, "rows"),
            (bc, "rows"),
            (cum, "rows"),
            (pre_step, "rows"),
            (de, "rows"),
            (dxc, "rows"),
            (dcq, "rows"),
            (dbq, "rows"),
            (row_sums, "rows"),
            (col_sums, "rows"),
            (decay, "block"),
            (v, "rows"),
            (v, "tail"),
            (halo_v, "whole"),
            (halo_normed, "whole"),
            (normed, "rows"),
            (small_gate, "whole"),
            (par, "whole"),
            (dtp, "whole"),
            (spread, "whole"),
        ],
        [row_out(channels + LANES, BF16), out((16, channels), BF16, "whole")]
        + [out((width // parts, channels + LANES), BF16, "whole")] * parts,
        [
            pltpu.VMEM((inner, LANES), F32),
            pltpu.VMEM((8, LANES), F32),
            pltpu.VMEM((8 + BLOCK, channels), F32),
            pltpu.VMEM((8 + BLOCK, channels), F32),
            pltpu.VMEM((width, channels + LANES), F32),
            pltpu.VMEM((8, channels), F32),
        ],
        reverse=True,
        micros=25,
        mega=32,
    )
    with jax.named_scope("reduce_gate_weights"):
        total2 = dp_sum(total2) if parts > 1 else whole_sum(total2)
    norm_rows = part_rows * dp_count
    if parts > 1:
        g1 = [g1[0]] + [partnered(g1[mask], "ctx", mask) for mask in range(1, parts)]
        packed, g1[1] = lax.optimization_barrier((packed, g1[1]))
    partial, halo_grad, norm_part = call(
        functools.partial(input_back_kernel, counts, dp_count, parts),
        steps,
        info,
        [
            (packed, "rows"),
            (back, "whole"),
            (dnz, "rows"),
            (tokens, "rows"),
            (halo, "whole"),
            (w1, "whole"),
            (par, "whole"),
        ],
        [
            row_out(width, BF16),
            out((8, width), F32, "whole"),
            out((norm_rows, LANES), F32, "whole"),
        ],
        [pltpu.VMEM((8, width), F32)],
        micros=5,
    )
    other = swapped(partial)
    size = ctx_count * 2
    back = [(s, s - 2) for s in range(2, size)]
    cross = [(s, (s - 2) ^ 1) for s in range(2, size)]
    halo_a = lax.ppermute(halo_grad, ("ctx", "tp"), back)
    halo_b = lax.ppermute(halo_grad, ("ctx", "tp"), cross)
    with jax.named_scope("reduce_input_weights"):
        norm_part = jnp.pad(norm_part, ((0, 0), (channels, 0)))
        if parts > 1:
            total1 = dp_sum(sum(piece.astype(F32) for piece in g1) + norm_part)
        else:
            total1 = whole_sum((g1[0].astype(F32) + norm_part).astype(BF16))
        across = swapped(total1[:, inner:])
        lane = jnp.arange(3 * LANES) - 2 * LANES
        both = (lane < 0) | ((lane >= STATE_TAPS) & (lane < BY_HEAD))
        both = both | ((lane >= NORM) & (lane < NORM + shard // part_rows))
        summed = total1[:, inner:] + jnp.where(both[None, :], across, 0)
        total1 = jnp.concatenate([total1[:, :inner], summed], axis=1)
    (grad_tokens,) = call(
        functools.partial(finish_kernel, counts),
        steps,
        info,
        [
            (partial, "rows"),
            (other, "rows"),
            (halo_a, "whole"),
            (halo_b, "whole"),
            (tokens, "rows"),
            (cotangent, "rows"),
            (par, "whole"),
        ],
        [row_out(width, F32)],
        micros=5,
    )
    with jax.named_scope("last_hop"):
        if parts > 1:
            total2 = exchanged(total2, "ctx")
            total1, grad_tokens = lax.optimization_barrier((total1, grad_tokens))
            total1 = exchanged(total1, "ctx")
        else:
            total1, total2 = [total1], [total2]
    each = HEAD // dp_count
    part_bc = bias_bc.shape[0]
    tall = -(-shard // LANES) * LANES

    def final(*sizes):
        return out(sizes, F32, "whole")

    grad_wz, grad_wo = call(
        functools.partial(unpack_gate_kernel, counts, parts),
        1,
        info,
        [(value, "whole") for value in total2],
        [final(shard, inner), final(shard, inner)],
        micros=2,
    )
    (
        grad_wx, grad_wbc, grad_wdt, grad_norm, grad_taps, grad_bias, grad_state_taps, grad_state_bias,
        grad_dt_bias, grad_a_log, grad_skip, grad_gate,
    ) = call(
        functools.partial(unpack_input_kernel, counts, heads, parts),
        1,
        info,
        [(value, "whole") for value in total1],
        [
            final(shard, inner),
            final(shard, 2 * LANES),
            final(heads, shard),
            final(1, shard),
            final(heads, CONV, each),
            final(heads, each),
            final(CONV, part_bc),
            final(1, part_bc),
            final(1, heads),
            final(1, heads),
            final(1, heads),
            final(heads, each),
        ],
        [pltpu.VMEM((tall, channels + LANES), F32)],
        micros=2,
    )
    return (
        layer_out,
        grad_tokens,
        grad_norm[0],
        grad_wz,
        grad_wx,
        grad_wbc,
        grad_wdt.T,
        grad_taps.transpose(1, 0, 2),
        grad_bias,
        grad_state_taps,
        grad_state_bias[0],
        grad_dt_bias[0],
        grad_a_log[0],
        grad_skip[0],
        grad_gate,
        grad_wo.T,
    )


def solution(mesh):
    shards = P(("dp", "ctx"), None)
    return jax.shard_map(
        body,
        mesh=mesh,
        in_specs=(
            shards,
            shards,
            P("dp", None),
            P("dp", None),
            P("dp"),
            P("dp", "tp"),
            P("dp", "tp"),
            P("dp", None),
            P("dp", "tp"),
            P(None, "tp", "dp"),
            P("tp", "dp"),
            P(None, "dp"),
            P("dp"),
            P("tp"),
            P("tp"),
            P("tp"),
            P("tp", "dp"),
            P("tp", "dp"),
        ),
        out_specs=(
            P(("dp", "ctx"), "tp"),
            shards,
            P("dp"),
            P("dp", "tp"),
            P("dp", "tp"),
            P("dp", None),
            P("dp", "tp"),
            P(None, "tp", "dp"),
            P("tp", "dp"),
            P(None, "dp"),
            P("dp"),
            P("tp"),
            P("tp"),
            P("tp"),
            P("tp", "dp"),
            P("tp", "dp"),
        ),
        check_vma=False,
    )
```

```python
import functools

import jax
import jax.numpy as jnp
from jax import lax
from jax.experimental import pallas as pl
from jax.experimental.pallas import tpu as pltpu
from jax.sharding import PartitionSpec as P

CONV = 4
BLOCK = 256
HEAD = 64
LANES = 128
EPS = 1e-05
MEGA = 1024 * 1024
F32 = jnp.float32
BF16 = jnp.bfloat16


def dot(left, right):
    return jnp.dot(left, right, preferred_element_type=F32)


def dot_tn(left, right):
    return lax.dot_general(left, right, (((0,), (0,)), ((), ())), preferred_element_type=F32)


def dot_nt(left, right):
    return lax.dot_general(left, right, (((1,), (1,)), ((), ())), preferred_element_type=F32)


def dot_exact(left, right):
    return jnp.dot(left, right, preferred_element_type=F32, precision=lax.Precision.HIGHEST)


def iota(shape, dim):
    return lax.broadcasted_iota(jnp.int32, shape, dim)


def sigmoid(value):
    return 1.0 / (1.0 + jnp.exp(-value))


def gate_sigmoid(value):
    return 0.5 * jnp.tanh(0.5 * value) + 0.5


def softplus(value):
    return jnp.maximum(value, 0.0) + jnp.log1p(jnp.exp(-jnp.abs(value)))


def split(value):
    high = value.astype(BF16)
    return high, (value - high.astype(F32)).astype(BF16)


def expand(value, spread):
    return dot(jnp.concatenate(split(value), axis=1), spread[...])


def reduce_heads(value, spread):
    high, low = split(value)
    pick = spread[:LANES, :]
    return dot_nt(high, pick) + dot_nt(low, pick)


def head_column(row, channels):
    shape = (channels, LANES)
    return jnp.sum(jnp.where(iota(shape, 0) // HEAD == iota(shape, 1), row, 0.0), axis=1, keepdims=True)


def xor(value, mask):
    return jnp.bitwise_xor(value, jnp.int32(mask))


class Place:
    def __init__(self, info, counts):
        devices, sequences = counts
        own = info[devices + sequences]
        self.ctx = own
        self.tp = info[devices + sequences + 1]
        self.dp = info[devices + sequences + 2]
        self.fill = jnp.int32(0)
        self.first = jnp.int32(0)
        for device in range(devices):
            rows = info[device] * BLOCK
            self.fill = self.fill + jnp.where(own == device, rows, 0)
            self.first = self.first + jnp.where(own > device, rows, 0)
        self.ends = []
        total = jnp.int32(0)
        for sequence in range(sequences - 1):
            total = total + info[devices + sequence]
            self.ends.append(total)

    def of(self, position):
        found = (position >= self.ends[0]).astype(jnp.int32)
        for end in self.ends[1:]:
            found = found + (position >= end).astype(jnp.int32)
        return jnp.where(position < 0, -1, found)

    def rows(self, index):
        return self.of(self.first + jnp.minimum(index, self.fill - 1))

    def before(self, block):
        position = self.first + jnp.minimum(block * BLOCK, self.fill) - 1
        found = jnp.int32(0)
        for end in self.ends:
            found = found + jnp.where(position >= end, 1, 0)
        return jnp.where(position < 0, -1, found)

    def last(self, block):
        position = self.first + jnp.minimum(block * BLOCK + BLOCK - 1, self.fill - 1)
        found = jnp.int32(0)
        for end in self.ends:
            found = found + jnp.where(position >= end, 1, 0)
        return found

    def column(self, block, shift=0):
        return self.rows(block * BLOCK + shift + iota((BLOCK, 1), 0))

    def valid(self, block):
        return (block * BLOCK + iota((BLOCK, 1), 0) < self.fill).astype(F32)

    def keep(self, block):
        across = self.rows(block * BLOCK + iota((1, BLOCK), 1))
        return (self.column(block) == across) & (iota((BLOCK, BLOCK), 0) >= iota((BLOCK, BLOCK), 1))


def step_sizes(place, block, pre_step, heads):
    lane = iota((BLOCK, LANES), 1)
    return jnp.where(lane < heads, softplus(pre_step), 0.0) * place.valid(block)


def end_weights(place, block, cum):
    same = (place.column(block) == place.last(block)).astype(F32)
    return jnp.exp(cum[BLOCK - 1 :, :] - cum) * same


def enter_weights(place, block, cum):
    return jnp.exp(cum) * (place.column(block) == place.before(block)).astype(F32)


def block_decay(place, block, cum):
    return jnp.exp(cum[BLOCK - 1 :, :]) * jnp.where(place.last(block) == place.before(block), 1.0, 0.0)


def decay_kernel(keep, cum, cum_rows, head):
    return jnp.exp(jnp.where(keep, cum[:, head : head + 1] - cum_rows[head : head + 1, :], -1e30))


def both_halves(pair):
    lane = iota(pair.shape, 1)
    zero = jnp.zeros_like(pair)
    return [jnp.where(lane < HEAD, pair, zero), jnp.where(lane >= HEAD, pair, zero)]


def same_mask(place, block, tap):
    return (place.column(block, tap - (CONV - 1)) == place.column(block)).astype(F32)


def conv_pre(place, block, ext, par, channels):
    total = par[4:5, :channels]
    for tap in range(CONV):
        first = 8 - (CONV - 1) + tap
        total = total + par[tap : tap + 1, :channels] * ext[first : first + BLOCK, :] * same_mask(
            place, block, tap
        )
    return total


def state_packet(state, decay):
    high, low = split(decay)
    row = iota((16, LANES), 0)
    tail = jnp.where(row == 0, high.astype(F32), jnp.where(row == 1, low.astype(F32), 0.0))
    return jnp.concatenate([state.astype(BF16), tail.astype(BF16)], axis=0)


def merge_packets(packets, inner):
    total = jnp.zeros((inner, LANES), F32)
    for packet in reversed(packets):
        tail = packet[inner : inner + 16, :].astype(F32)
        decay = tail[0:1, :] + tail[1:2, :]
        total = packet[:inner, :].astype(F32) + head_column(decay, inner) * total
    return total


def normalise(rows, gain):
    inv = lax.rsqrt(jnp.mean(rows * rows, axis=1, keepdims=True) + EPS)
    return rows * inv, inv, (rows * inv * gain).astype(BF16)


def piece_rows(place, dp_count, parts, rows):
    for part in range(parts):
        for block in range(dp_count):
            owner = xor(place.dp, block) * parts + (xor(place.ctx, part) if parts > 1 else 0)
            yield part, block, pl.multiple_of(owner * rows, rows)


def join_pieces(place, dp_count, parts, whole):
    columns = parts[0].shape[1]
    if len(parts) == 1:
        whole[:, :columns] = parts[0][...]
        return
    rows = parts[0].shape[0] // dp_count
    for part, block, first in piece_rows(place, dp_count, len(parts), rows):
        whole[pl.ds(first, rows), :columns] = parts[part][block * rows : (block + 1) * rows, :]


def cut_pieces(place, dp_count, whole, parts, lanes):
    if len(parts) == 1:
        parts[0][:, lanes] = whole[...].astype(BF16)
        return
    rows = parts[0].shape[0] // dp_count
    for part, block, first in piece_rows(place, dp_count, len(parts), rows):
        parts[part][block * rows : (block + 1) * rows, lanes] = whole[pl.ds(first, rows), :].astype(BF16)


def join_parameters(place, vectors, skip, heads, par, w1):
    shard = vectors[0].shape[1] // 2
    each = HEAD // len(vectors)
    inner = heads * HEAD
    by_channel = jnp.zeros((16, inner), F32)
    in_order = jnp.zeros((16, shard * len(vectors)), F32)
    by_state = jnp.zeros((16, 2 * LANES), F32)
    states = 2 * LANES // len(vectors)
    eye = (iota((16, LANES), 0) == iota((16, LANES), 1)).astype(BF16)
    for block, vector in enumerate(vectors):
        owner = xor(place.dp, block)
        first = pl.multiple_of(owner * shard, shard)
        w1[pl.ds(first, shard), inner + 2 * LANES :] = dot_tn(vector[:, shard:], eye).astype(BF16)
        source, target = iota((shard, inner), 0), iota((shard, inner), 1)
        pick = target == source // each * HEAD + owner * each + source % each
        by_channel = by_channel + dot(vector[:, :shard], pick.astype(BF16))
        source, target = iota((shard, in_order.shape[1]), 0), iota((shard, in_order.shape[1]), 1)
        in_order = in_order + dot(vector[:, :shard], (target == owner * shard + source).astype(BF16))
        source, target = iota((shard, 2 * LANES), 0), iota((shard, 2 * LANES), 1)
        pick = (target == owner * states + source) & (source < states)
        by_state = by_state + dot(vector[:, :shard], pick.astype(BF16))
    par[...] = jnp.zeros_like(par)
    par[0:5, :inner] = by_channel[0:5, :]
    par[0:5, inner:] = by_state[8:13, :]
    par[5:6, : in_order.shape[1]] = in_order[5:6, :]
    par[6:7, :inner] = by_channel[6:7, :]
    par[7:8, :inner] = skip


TAPS, GATE, STATE_TAPS, BY_HEAD, NORM = 12, 18, 20, 25, 26


def lanes(pieces, columns):
    rows, at = [], 0
    for first, value in pieces:
        if first > at:
            rows.append(jnp.zeros((first - at, columns), F32))
        rows.append(value)
        at = first + value.shape[0]
    rows.append(jnp.zeros((LANES - at, columns), F32))
    return jnp.concatenate(rows, axis=0)


def pack_norm(place, dp_count, part_count, row, rows):
    columns = row.shape[1]
    shard = columns // dp_count
    size = shard // rows
    total = jnp.zeros((dp_count * rows, LANES), F32)
    source, target = iota((dp_count * rows, columns), 0), iota((dp_count * rows, columns), 1)
    owner = source // rows
    if part_count > 1:
        owner = jnp.bitwise_xor(owner, place.dp)
    for lane in range(size):
        pick = target == owner * shard + lane * rows + source % rows
        total = total + dot_nt(pick.astype(BF16), lanes([(NORM + lane, row)], columns).astype(BF16))
    return total


def pack_parameters(dp_count, heads, small, gate, skip):
    inner = heads * HEAD
    each = HEAD // dp_count
    shard = inner // dp_count
    states = 2 * LANES // dp_count

    source, target = iota((inner, inner), 0), iota((inner, inner), 1)
    inside = source % shard
    pick = target == inside // each * HEAD + source // shard * each + inside % each
    by_channel = lanes([(TAPS, small[0:5, :inner]), (GATE, gate)], inner)
    total = dot_nt(pick.astype(BF16), by_channel.astype(BF16))
    source, target = iota((inner, 2 * LANES), 0), iota((inner, 2 * LANES), 1)
    inside = source % shard
    pick = (target == source // shard * states + inside) & (inside < states)
    by_state = lanes([(STATE_TAPS, small[0:5, inner : inner + 2 * LANES])], 2 * LANES)
    total = total + dot_nt(pick.astype(BF16), by_state.astype(BF16))
    source, target = iota((inner, LANES), 0) % shard, iota((inner, LANES), 1)
    for index, row in enumerate((small[6:7, :LANES], small[7:8, :LANES], skip)):
        pick = (source == target + index * heads) & (target < heads)
        total = total + dot_nt(pick.astype(BF16), lanes([(BY_HEAD, row)], LANES).astype(BF16))
    return total


def forward_kernel(
    counts, heads, dp_count, part_count, info, *refs
):
    vectors = refs[:dp_count]
    parts = refs[dp_count : dp_count + part_count]
    (
        tok, halo, dtp, spread,
        w1, par, normed_o, halo_normed_o, halo_v_o, v_o, xc_o, bc_o, ypart_o, pre_o, cum_o, entry_o, decay_o,
        packet_o, ext, run, factor,
    ) = refs[dp_count + part_count :]
    forward_block(
        counts, heads, info, vectors, parts, tok, halo, w1, par, dtp, spread,
        normed_o, halo_normed_o, halo_v_o, v_o, xc_o, bc_o, ypart_o, pre_o, cum_o, entry_o, decay_o, packet_o,
        ext, run, factor,
    )


def forward_block(
    counts, heads, info, vectors, parts, tok, halo, w1, par, dtp, spread,
    normed_o, halo_normed_o, halo_v_o, v_o, xc_o, bc_o, ypart_o, pre_o, cum_o, entry_o, decay_o, packet_o,
    ext, run, factor,
):
    block = pl.program_id(0)
    place = Place(info, counts)
    inner = heads * HEAD
    state = LANES
    channels = inner + 2 * state
    width = tok.shape[1]

    @pl.when(block == 0)
    def _():
        join_pieces(place, len(vectors), parts, w1)
        join_parameters(place, vectors, expand(dtp[...], spread)[2:3, :], heads, par, w1)

    gain = par[5:6, :width]
    _, _, normed = normalise(tok[...].astype(F32), gain)
    normed_o[...] = normed

    @pl.when(block == 0)
    def _():
        _, _, before = normalise(halo[...].astype(F32), gain)
        halo_normed_o[...] = before
        raw = dot(before, w1[:, :channels]).astype(BF16).astype(F32)
        ext[0:8, :] = raw[8:16, :]
        halo_v_o[...] = raw[8:16, :]
        run[...] = jnp.zeros_like(run)
        factor[...] = jnp.ones_like(factor)

    @pl.when(block > 0)
    def _():
        ext[0:8, :] = ext[BLOCK : BLOCK + 8, :]

    raw = dot(normed, w1[...])
    v = raw[:, :channels].astype(BF16)
    v_o[...] = v
    ext[8 : 8 + BLOCK, :] = v.astype(F32)
    pre = conv_pre(place, block, ext, par, channels)
    act = (pre * gate_sigmoid(pre)).astype(BF16)
    xc = act[:, :inner]
    bq = act[:, inner : inner + state]
    cq = act[:, inner + state :]
    xc_o[...] = xc
    bc_o[...] = act[:, inner:]
    pre_step = raw[:, channels:].astype(BF16).astype(F32) + dtp[0:1, :]
    pre_o[...] = pre_step
    step = step_sizes(place, block, pre_step, heads)
    tri = (iota((BLOCK, BLOCK), 0) >= iota((BLOCK, BLOCK), 1)).astype(F32)
    cum = dot_exact(tri, -dtp[1:2, :] * step)
    cum_o[...] = cum
    cum_rows = cum.T
    step_rows = step.T
    gram = dot_nt(cq, bq)
    keep = place.keep(block)
    for pair in range(heads // 2):
        lanes = slice(pair * LANES, (pair + 1) * LANES)
        mixing = []
        for head in (2 * pair, 2 * pair + 1):
            weight = decay_kernel(keep, cum, cum_rows, head) * step_rows[head : head + 1, :]
            mixing.append((gram * weight).astype(BF16))
        x_pair = xc[:, lanes]
        y_pair = dot(jnp.concatenate(mixing, axis=1), jnp.concatenate(both_halves(x_pair), axis=0))
        ypart_o[:, lanes] = y_pair + par[7:8, lanes] * x_pair.astype(F32)
    weighted = (expand(end_weights(place, block, cum) * step, spread) * xc.astype(F32)).astype(BF16)
    block_state = dot_tn(weighted, bq)
    decay = block_decay(place, block, cum)
    entry_o[0] = run[...]
    total = head_column(decay, inner) * run[...] + block_state
    run[...] = total
    before = factor[0:1, :]
    row = iota((8, LANES), 0)
    decay_o[0] = jnp.where(row == 0, decay, jnp.where(row == 1, before, 0.0))
    after = before * decay
    factor[...] = jnp.broadcast_to(after, factor.shape)

    @pl.when(block == pl.num_programs(0) - 1)
    def _():
        packet_o[...] = state_packet(total, after)


def gate_matmul_kernel(counts, dp_count, part_count, info, *refs):
    parts = refs[:part_count]
    normed, cot, w2, z_o, dn_o = refs[part_count:]
    block = pl.program_id(0)
    place = Place(info, counts)
    inner = z_o.shape[1]

    @pl.when(block == 0)
    def _():
        join_pieces(place, dp_count, parts, w2)

    z_o[...] = dot(normed[...], w2[:, :inner]).astype(BF16)
    grad = (cot[...].astype(F32) * place.valid(block)).astype(BF16)
    dn_o[...] = dot(grad, w2[:, inner:]).astype(BF16)


def apply_kernel(counts, packet_count, info, *refs):
    packets = refs[:packet_count]
    entry, decay, cum, bc, ypart, z, dn, par, spread, y_o, hb_o, h_o, stat_o, start = refs[packet_count:]
    block = pl.program_id(0)
    place = Place(info, counts)
    inner = z.shape[1]

    @pl.when(block == 0)
    def _():
        start[...] = merge_packets([packet[...] for packet in packets], inner)

    state = entry[0] + head_column(decay[0, 1:2, :], inner) * start[...]
    h_o[0] = state
    low = state.astype(BF16)
    hb_o[0] = low
    cq = bc[:, LANES:]
    y = ypart[...] + expand(enter_weights(place, block, cum[...]), spread) * dot_nt(cq, low)
    y_o[...] = y
    gate = z[...].astype(F32)
    gated = y * gate * gate_sigmoid(gate)
    squares = jnp.sum(gated * gated, axis=1, keepdims=True)
    cross = jnp.sum(par[6:7, :inner] * dn[...].astype(F32) * gated, axis=1, keepdims=True)
    lane = iota((BLOCK, LANES), 1)
    both = jnp.where(lane == 0, squares, jnp.where(lane == 1, cross, 0.0))
    stat_o[...] = both.T[0:8, :]


def gate_back_kernel(
    counts, inner_all, info, stat, y, z, dn, cot, cum, bc, xc, hb, decay, wo, par, spread,
    keep_o, send_o, gwo_o, small_o, dy_o, dz_o, de_o, exit_o, packet_o,
    acc, run, factor,
):
    step = pl.program_id(0)
    block = pl.num_programs(0) - 1 - step
    place = Place(info, counts)
    inner = z.shape[1]
    width = cot.shape[1]
    half = width // 2

    @pl.when(step == 0)
    def _():
        acc[...] = jnp.zeros_like(acc)
        run[...] = jnp.zeros_like(run)
        factor[...] = jnp.ones_like(factor)
        small_o[...] = jnp.zeros_like(small_o)

    column = jnp.concatenate([stat[...], jnp.zeros((LANES - 8, BLOCK), F32)], axis=0).T
    inv = lax.rsqrt(column[:, 0:1] / inner_all + EPS)
    cross = column[:, 1:2]
    gain = par[6:7, :inner]
    gate = z[...].astype(F32)
    sig = gate_sigmoid(gate)
    silu = gate * sig
    mixed = y[...]
    gated = mixed * silu
    normal = (gated * inv * gain).astype(BF16)
    own = pl.multiple_of(place.tp * half, half)
    other = pl.multiple_of((1 - place.tp) * half, half)
    keep_o[...] = dot_nt(normal, wo[pl.ds(own, half), :]).astype(BF16)
    send_o[...] = dot_nt(normal, wo[pl.ds(other, half), :]).astype(BF16)
    grad = (cot[...].astype(F32) * place.valid(block)).astype(BF16)
    acc[...] += dot_tn(grad, normal)
    back = dn[...].astype(F32)
    grad_gated = inv * (gain * back) - gated * (inv * inv * inv) * (cross / inner_all)
    dy = (grad_gated * silu).astype(BF16)
    dy_o[...] = dy
    dz_o[...] = (grad_gated * mixed * sig * (1.0 + gate * (1.0 - sig))).astype(BF16)
    dy_float = dy.astype(F32)
    cq = bc[:, LANES:]
    read = dot_nt(cq, hb[0])
    de_o[...] = reduce_heads(dy_float * read, spread)
    small_o[0:1, :] += jnp.sum(back * gated * inv, axis=0, keepdims=True)
    small_o[1:2, :] += jnp.sum(dy_float * xc[...].astype(F32), axis=0, keepdims=True)
    dq = (expand(enter_weights(place, block, cum[...]), spread) * dy_float).astype(BF16)
    exit_o[0] = run[...]
    here = decay[0, 0:1, :]
    total = head_column(here, inner) * run[...] + dot_tn(dq, cq)
    run[...] = total
    after = factor[0:1, :] * here
    factor[...] = jnp.broadcast_to(after, factor.shape)

    @pl.when(step == pl.num_programs(0) - 1)
    def _():
        packet_o[...] = state_packet(total, after)
        gwo_o[...] = acc[...].astype(BF16)


def intra_back_kernel(counts, heads, dp_count, info, *refs):
    dy, dz, xc, bc, cum, pre_step, hb, normed, gwo, par, spread = refs[:11]
    dxc_o, dcq_o, dbq_o, rows_o, cols_o = refs[11:16]
    parts = refs[16:-2]
    acc, columns = refs[-2:]
    block = pl.program_id(0)
    place = Place(info, counts)
    inner = heads * HEAD

    @pl.when(block == 0)
    def _():
        acc[...] = jnp.zeros_like(acc)
        columns[...] = jnp.zeros_like(columns)

    bq = bc[:, :LANES]
    cq = bc[:, LANES:]
    cums = cum[...]
    step = step_sizes(place, block, pre_step[...], heads)
    cum_rows = cums.T
    step_rows = step.T
    gram = dot_nt(cq, bq)
    keep = place.keep(block)
    lane = iota((BLOCK, LANES), 1)
    grad_gram = jnp.zeros((BLOCK, BLOCK), F32)
    sums = jnp.zeros((BLOCK, LANES), F32)
    for pair in range(heads // 2):
        lanes = slice(pair * LANES, (pair + 1) * LANES)
        dy_pair = dy[:, lanes]
        x_pair = xc[:, lanes]
        halves = jnp.concatenate(both_halves(dy_pair), axis=0)
        grad_mixing = dot_nt(halves, x_pair)
        mixing = []
        for side in range(2):
            head = 2 * pair + side
            grad_m = grad_mixing[side * BLOCK : (side + 1) * BLOCK, :]
            kernel = decay_kernel(keep, cums, cum_rows, head)
            step_row = step_rows[head : head + 1, :]
            weight = kernel * step_row
            mixing.append((gram * weight).astype(BF16))
            grad_gram = grad_gram + grad_m * weight
            part = grad_m * gram * kernel
            columns[head : head + 1, :] = jnp.sum(part, axis=0, keepdims=True)
            sums = sums + jnp.where(lane == head, jnp.sum(part * step_row, axis=1, keepdims=True), 0.0)
        dx_pair = dot_tn(jnp.concatenate(mixing, axis=0), halves)
        dxc_o[:, lanes] = (dx_pair + par[7:8, lanes] * dy_pair.astype(F32)).astype(BF16)
    grad_low = grad_gram.astype(BF16)
    dq = (expand(enter_weights(place, block, cums), spread) * dy[...].astype(F32)).astype(BF16)
    dcq_o[...] = dot(grad_low, bq) + dot(dq, hb[0])
    dbq_o[...] = dot_tn(grad_low, cq)
    rows_o[...] = sums
    cols_o[...] = columns[...].T
    acc[...] += dot_tn(normed[...], dz[...])

    @pl.when(block == pl.num_programs(0) - 1)
    def _():
        cut_pieces(place, dp_count, acc, parts, slice(0, inner))
        cut_pieces(place, dp_count, gwo, parts, slice(inner, 2 * inner))


def state_back_kernel(counts, heads, dp_count, packet_count, part_count, info, *refs):
    packets = refs[:packet_count]
    (
        exits, h, xc, bc, cum, pre_step, de, dxc, dcq, dbq, rows, cols, decay, v, v_tail, halo_v, halo_normed,
        normed, small_gate, par, dtp, spread,
        packed_o, back_o,
    ) = refs[packet_count : -6 - part_count]
    parts = refs[-6 - part_count : -6]
    start, factor, ext, grad_ext, acc, small_o = refs[-6:]
    step_id = pl.program_id(0)
    block = pl.num_programs(0) - 1 - step_id
    place = Place(info, counts)
    inner = heads * HEAD
    channels = inner + 2 * LANES

    @pl.when(step_id == 0)
    def _():
        start[...] = merge_packets([packet[...] for packet in packets], inner)
        factor[...] = jnp.ones_like(factor)
        acc[...] = jnp.zeros_like(acc)
        grad_ext[...] = jnp.zeros_like(grad_ext)
        small_o[...] = jnp.zeros_like(small_o)

    here = decay[0, 0:1, :]
    before = factor[0:1, :]
    grad_state = exits[0] + head_column(before, inner) * start[...]
    factor[...] = jnp.broadcast_to(before * here, factor.shape)
    shape = (inner, LANES)
    overlap = jnp.sum(grad_state * h[0], axis=1, keepdims=True)
    grad_decay = jnp.sum(
        jnp.where(iota(shape, 0) // HEAD == iota(shape, 1), overlap, 0.0), axis=0, keepdims=True
    )
    low = grad_state.astype(BF16)
    bq = bc[:, :LANES]
    cums = cum[...]
    x_float = xc[...].astype(F32)
    pre_dt = pre_step[...]
    valid = place.valid(block)
    step = step_sizes(place, block, pre_dt, heads)
    end_kernel = end_weights(place, block, cums)
    end_weight = end_kernel * step
    end_wide = expand(end_weight, spread)
    spread_b = dot_nt(bq, low)
    grad_x = dxc[...].astype(F32) + end_wide * spread_b
    grad_end = reduce_heads(x_float * spread_b, spread)
    grad_b = dbq[...] + dot((x_float * end_wide).astype(BF16), low)
    end_part = grad_end * end_weight
    last = iota((BLOCK, LANES), 0) == BLOCK - 1
    grad_cum = rows[...] - cols[...] * step - end_part + de[...] * enter_weights(place, block, cums)
    grad_cum = grad_cum + jnp.where(
        last, jnp.sum(end_part, axis=0, keepdims=True) + grad_decay * here, 0.0
    )
    upper = (iota((BLOCK, BLOCK), 0) <= iota((BLOCK, BLOCK), 1)).astype(F32)
    grad_log = dot_exact(upper, grad_cum)
    rates = dtp[1:2, :]
    grad_step = cols[...] + grad_end * end_kernel - rates * grad_log
    heads_lane = iota((BLOCK, LANES), 1) < heads
    grad_pre_dt = jnp.where(heads_lane, grad_step * sigmoid(pre_dt), 0.0) * valid
    small_o[6:7, :LANES] += jnp.sum(grad_pre_dt, axis=0, keepdims=True)
    small_o[7:8, :LANES] += jnp.sum(grad_log * (-rates * step), axis=0, keepdims=True)

    ext[8 : 8 + BLOCK, :] = v[...].astype(F32)

    @pl.when(block == 0)
    def _():
        ext[0:8, :] = halo_v[...]

    @pl.when(block > 0)
    def _():
        ext[0:8, :] = v_tail[...].astype(F32)[8:16, :]

    pre = conv_pre(place, block, ext, par, channels)
    sig = gate_sigmoid(pre)
    slope = sig * (1.0 + pre * (1.0 - sig))
    grad_pre = jnp.concatenate([grad_x, grad_b, dcq[...]], axis=1) * slope
    small_o[4:5, :] += jnp.sum(grad_pre, axis=0, keepdims=True)
    carry = grad_ext[0:8, :]
    grad_ext[0:BLOCK, :] = jnp.zeros((BLOCK, channels), F32)
    grad_ext[BLOCK : BLOCK + 8, :] = carry
    for tap in range(CONV):
        first = 8 - (CONV - 1) + tap
        masked = grad_pre * same_mask(place, block, tap)
        small_o[tap : tap + 1, :] += jnp.sum(masked * ext[first : first + BLOCK, :], axis=0, keepdims=True)
        grad_ext[first : first + BLOCK, :] += par[tap : tap + 1, :channels] * masked
    packed = jnp.concatenate([grad_ext[8 : 8 + BLOCK, :].astype(BF16), grad_pre_dt.astype(BF16)], axis=1)
    packed_o[...] = packed
    acc[...] += dot_tn(normed[...], packed)

    @pl.when(block == 0)
    def _():
        back = jnp.concatenate([jnp.zeros((8, channels), F32), grad_ext[0:8, :]], axis=0).astype(BF16)
        back_o[...] = back
        acc[:, :channels] += dot_tn(halo_normed[...], back)
        skip = reduce_heads(jnp.broadcast_to(small_gate[1:2, :], (8, inner)), spread)[0:1, :]
        acc[:, channels:] += pack_parameters(dp_count, heads, small_o, small_gate[0:1, :], skip)
        cut_pieces(place, dp_count, acc, parts, slice(0, channels + LANES))


def input_back_kernel(
    counts, dp_count, part_count, info, packed, back, dz, wz, tok, halo, w1, par,
    dn_o, dnh_o, norm_o, total,
):
    block = pl.program_id(0)
    place = Place(info, counts)
    width = tok.shape[1]
    channels = back.shape[1]
    gain = par[5:6, :width]

    @pl.when(block == 0)
    def _():
        halo_grad = dot_nt(back[...], w1[:, :channels])
        dnh_o[...] = halo_grad[8:16, :]
        halo_scaled, _, _ = normalise(halo[...].astype(F32), gain)
        total[...] = jnp.broadcast_to(
            jnp.sum(halo_grad * halo_scaled, axis=0, keepdims=True), total.shape
        )

    partial = dot_nt(dz[...], wz[...]) + dot_nt(packed[...], w1[...])
    dn_o[...] = partial.astype(BF16)
    scaled, _, _ = normalise(tok[...].astype(F32), gain)
    total[0:1, :] += jnp.sum(partial * scaled, axis=0, keepdims=True)

    @pl.when(block == pl.num_programs(0) - 1)
    def _():
        rows = norm_o.shape[0] // dp_count
        norm_o[...] = pack_norm(place, dp_count, part_count, total[0:1, :], rows)


def finish_kernel(counts, info, own, other, halo_a, halo_b, tok, cot, par, grad_o):
    block = pl.program_id(0)
    place = Place(info, counts)
    width = tok.shape[1]
    grad = own[...].astype(F32) + other[...].astype(F32)
    is_last = jnp.where((block + 1) * BLOCK == place.fill, 1.0, 0.0)
    halo = (halo_a[...] + halo_b[...]) * is_last
    grad = jnp.concatenate([grad[: BLOCK - 8, :], grad[BLOCK - 8 :, :] + halo], axis=0)
    inputs = tok[...].astype(F32)
    inv = lax.rsqrt(jnp.mean(inputs * inputs, axis=1, keepdims=True) + EPS)
    scaled = par[5:6, :width] * grad
    inner_dot = jnp.sum(scaled * inputs, axis=1, keepdims=True)
    grad_o[...] = (
        inv * scaled - inputs * (inv * inv * inv) * (inner_dot / width) + cot[...].astype(F32)
    )


def unpack_gate_kernel(counts, part_count, info, *refs):
    whole, wz_o, wo_o = refs
    place = Place(info, counts)
    shard, inner = wz_o.shape
    rows = shard // part_count
    for part in range(part_count):
        first = pl.multiple_of(xor(place.ctx, part) * rows, rows) if part_count > 1 else 0
        lines = slice(part * rows, (part + 1) * rows)
        wz_o[pl.ds(first, rows), :] = whole[lines, :inner].astype(F32)
        wo_o[pl.ds(first, rows), :] = whole[lines, inner:].astype(F32)


def unpack_input_kernel(counts, heads, part_count, info, *refs):
    parts = refs[:part_count]
    (
        wx_o, wbc_o, wdt_o, norm_o, taps_o, bias_o, state_taps_o, state_bias_o, dt_bias_o, a_log_o, skip_o,
        gate_o, wide,
    ) = refs[part_count:]
    place = Place(info, counts)
    shard, inner = wx_o.shape
    channels = inner + 2 * LANES
    rows = shard // part_count
    for part in range(part_count):
        first = pl.multiple_of(xor(place.ctx, part) * rows, rows) if part_count > 1 else 0
        wide[pl.ds(first, rows), :] = parts[part][...].astype(F32)
    wx_o[...] = wide[:shard, :inner]
    wbc_o[...] = wide[:shard, inner:channels]
    lines = wide[:, channels:].T
    wdt_o[...] = lines[:heads, :shard]
    each = gate_o.shape[1]
    size = lines.shape[1]
    source = iota((16, size), 1)
    inside = (source // each == iota((16, size), 0)) & (source < shard)
    place_in = (iota((size, LANES), 0) % each == iota((size, LANES), 1)).astype(BF16)

    def by_head(line):
        row = jnp.where(inside, lines[line : line + 1, :], 0.0).astype(BF16)
        return dot(row, place_in)[:heads, :each]

    for tap in range(CONV):
        taps_o[:, tap, :] = by_head(TAPS + tap)
    bias_o[...] = by_head(TAPS + CONV)
    gate_o[...] = by_head(GATE)
    gain = wide[:rows, channels:]
    for part in range(1, part_count):
        gain = gain + wide[part * rows : (part + 1) * rows, channels:]
    gain = jnp.concatenate([gain, jnp.zeros((LANES - rows, LANES), F32)], axis=0).T
    source, target = iota((LANES, size), 0), iota((LANES, size), 1)
    total = jnp.zeros((8, size), F32)
    for lane in range(shard // rows):
        pick = ((target == lane * rows + source) & (source < rows)).astype(F32)
        total = total + dot_exact(jnp.broadcast_to(gain[NORM + lane : NORM + lane + 1, :], (8, LANES)), pick)
    norm_o[...] = total[0:1, :shard]
    states = state_bias_o.shape[1]
    state_taps_o[...] = lines[STATE_TAPS : STATE_TAPS + CONV, :states]
    state_bias_o[...] = lines[STATE_TAPS + CONV : STATE_TAPS + CONV + 1, :states]
    row = lines[BY_HEAD : BY_HEAD + 1, :]
    dt_bias_o[...] = row[:, :heads]
    a_log_o[...] = row[:, heads : 2 * heads]
    skip_o[...] = row[:, 2 * heads : 3 * heads]


def call(body, steps, info, operands, outputs, scratch=(), reverse=False, micros=1, mega=20):
    def at(index):
        return steps - 1 - index if reverse else index

    def spec(shape, kind):
        if kind == "rows":
            return pl.BlockSpec((BLOCK,) + tuple(shape[1:]), lambda i: (at(i), 0))
        if kind == "block":
            return pl.BlockSpec((1,) + tuple(shape[1:]), lambda i: (at(i), 0, 0))
        if kind == "lanes":
            return pl.BlockSpec((shape[0], BLOCK), lambda i: (0, at(i)))
        if kind == "tail":
            each = BLOCK // 16
            return pl.BlockSpec((16, shape[1]), lambda i: (jnp.maximum(at(i) * each - 1, 0), 0))
        if kind == "whole":
            return pl.BlockSpec(tuple(shape), lambda i: (0,) * len(shape))
        if kind == "once":
            return pl.BlockSpec(tuple(shape), lambda i: (0,) * len(shape), pipeline_mode=pl.Buffered(1))
        return kind

    return pl.pallas_call(
        body,
        grid=(steps,),
        in_specs=[pl.BlockSpec(memory_space=pltpu.SMEM)]
        + [spec(array.shape, "once" if kind == "whole" else kind) for array, kind in operands],
        out_specs=[spec(shape.shape, kind) for shape, kind in outputs],
        out_shape=[shape for shape, _ in outputs],
        scratch_shapes=list(scratch),
        compiler_params=pltpu.CompilerParams(
            dimension_semantics=("arbitrary",), vmem_limit_bytes=mega * MEGA
        ),
        cost_estimate=pl.CostEstimate(
            flops=micros * 1_100_000_000, bytes_accessed=micros * 3_500_000, transcendentals=0
        ),
    )(info, *[array for array, _ in operands])


def shifted(value, axis, steps):
    count = lax.axis_size(axis)
    first, last = max(0, -steps), min(count, count - steps)
    return lax.ppermute(value, axis, [(source, source + steps) for source in range(first, last)])


def swapped(value):
    return lax.ppermute(value, "tp", [(0, 1), (1, 0)])


def partnered(value, axis, mask):
    return lax.ppermute(value, axis, [(one, one ^ mask) for one in range(lax.axis_size(axis))])


def exchanged(value, axis):
    return [value] + [partnered(value, axis, mask) for mask in range(1, lax.axis_size(axis))]


def own_rows(value, rows):
    return lax.dynamic_slice_in_dim(value, lax.axis_index("ctx") * rows, rows, 0)


def joined_rows(values):
    return jnp.concatenate(values, axis=0)


def ctx_sum(pieces):
    total = pieces[0].astype(F32)
    for mask in range(1, len(pieces)):
        total = total + partnered(pieces[mask], "ctx", mask).astype(F32)
    return total


def dp_sum(total):
    dp_count = lax.axis_size("dp")
    rows = total.shape[0] // dp_count
    own = total[:rows].astype(F32)
    for mask in range(1, dp_count):
        block = total[mask * rows : (mask + 1) * rows].astype(BF16)
        own = own + partnered(block, "dp", mask).astype(F32)
    return own.astype(BF16)


def halved_sum(total):
    blocks = lax.axis_size("dp")
    rows = total.shape[0] // blocks
    total = total.reshape(blocks, rows, -1).astype(F32)
    mask = 1
    while mask < blocks:
        kept = [total[block] for block in range(total.shape[0]) if block % 2 == 0]
        sent = [total[block] for block in range(total.shape[0]) if block % 2 == 1]
        received = partnered(jnp.concatenate(sent, axis=0).astype(BF16), "dp", mask)
        received = received.reshape(len(sent), rows, -1).astype(F32)
        total = jnp.stack(kept) + received
        mask *= 2
    return total[0].astype(BF16)


def doubled(value):
    mask = 1
    while mask < lax.axis_size("ctx"):
        value = jnp.concatenate([value, partnered(value, "ctx", mask)], axis=0)
        mask *= 2
    return value


def whole_sum(value):
    return lax.psum(lax.psum_scatter(value, "dp", scatter_dimension=0, tiled=True), "ctx")


def body(
    tokens, cotangent, device_fill, seq_lengths, norm_gain, w_z, w_x, w_bc, w_dt,
    conv_x, conv_x_bias, conv_bc, bias_bc, dt_bias, a_log, skip_d, gate_gain, w_out,
):
    rows, width = tokens.shape
    heads = dt_bias.shape[0]
    inner = heads * HEAD
    channels = inner + 2 * LANES
    steps = rows // BLOCK
    shard = norm_gain.shape[0]
    dp_count = lax.axis_size("dp")
    ctx_count = lax.axis_size("ctx")
    tp_index = lax.axis_index("tp")
    counts = (ctx_count, seq_lengths.shape[1])

    parts = ctx_count if shard % (16 * ctx_count) == 0 else 1
    part_rows = shard // parts

    with jax.named_scope("gather_weights"):
        vector = jnp.concatenate(
            [
                jnp.concatenate(
                    [
                        conv_x.reshape(CONV, shard),
                        conv_x_bias.reshape(1, shard),
                        norm_gain[None, :],
                        gate_gain.reshape(1, shard),
                        jnp.zeros((1, shard), BF16),
                        jnp.pad(
                            jnp.concatenate([conv_bc, bias_bc[None, :]], axis=0),
                            ((0, 3), (0, shard - bias_bc.shape[0])),
                        ),
                    ],
                    axis=0,
                ),
                jnp.pad(w_dt.T, ((0, 16 - heads), (0, 0))),
            ],
            axis=1,
        )
        input_rows = jnp.concatenate([w_x, w_bc], axis=1)
        gate_rows = jnp.concatenate([w_z, w_out.T], axis=1)
        if parts > 1:
            w1_parts = joined_rows(exchanged(own_rows(input_rows, part_rows), "dp"))
            vector = jnp.pad(vector, ((0, 0), (0, 2 * inner - 2 * shard)))
            block = jnp.concatenate([own_rows(gate_rows, part_rows), vector], axis=0)
            block, _ = lax.optimization_barrier((block, w1_parts))
            vectors = exchanged(block, "dp")
            w2_parts = exchanged(joined_rows([value[:part_rows] for value in vectors]), "ctx")
            w1_parts = exchanged(w1_parts, "ctx")
        else:
            w1_parts = [lax.all_gather(input_rows, "dp", axis=0, tiled=True)]
            w2_parts = [lax.all_gather(gate_rows, "dp", axis=0, tiled=True)]
            vectors = exchanged(vector, "dp")
    first_vector = part_rows // 16 if parts > 1 else 0
    vector_spec = pl.BlockSpec(
        (16, 2 * shard), lambda i: (first_vector, 0), pipeline_mode=pl.Buffered(1)
    )

    dtp = jnp.pad(jnp.stack([dt_bias, jnp.exp(a_log), skip_d]), ((0, 5), (0, LANES - heads)))
    shape = (2 * LANES, inner)
    spread = (iota(shape, 0) % LANES == iota(shape, 1) // HEAD).astype(BF16)
    info = jnp.concatenate(
        [
            device_fill[0],
            seq_lengths[0],
            jnp.stack([lax.axis_index("ctx"), tp_index, lax.axis_index("dp")]).astype(jnp.int32),
        ]
    )
    fill = jnp.sum(jnp.where(jnp.arange(ctx_count) == lax.axis_index("ctx"), device_fill[0], 0)) * BLOCK
    halo = shifted(lax.dynamic_slice_in_dim(tokens, fill - 16, 16, 0), "ctx", 1)

    def out(shape, dtype, kind):
        return (jax.ShapeDtypeStruct(shape, dtype), kind)

    def row_out(columns, dtype):
        return out((rows, columns), dtype, "rows")

    state_out = out((steps, inner, LANES), F32, "block")
    packet_out = out((inner + 16, LANES), BF16, "whole")

    (w1, par, normed, halo_normed, halo_v, v, xc, bc, ypart, pre_step, cum, entry, decay, packet) = call(
        functools.partial(forward_kernel, counts, heads, dp_count, parts),
        steps,
        info,
        [(value, vector_spec) for value in vectors]
        + [(value, "whole") for value in w1_parts]
        + [(tokens, "rows"), (halo, "whole"), (dtp, "whole"), (spread, "whole")],
        [
            out((width, channels + LANES), BF16, "whole"),
            out((8, channels), F32, "whole"),
            row_out(width, BF16),
            out((16, width), BF16, "whole"),
            out((8, channels), F32, "whole"),
            row_out(channels, BF16),
            row_out(inner, BF16),
            row_out(2 * LANES, BF16),
            row_out(inner, F32),
            row_out(LANES, F32),
            row_out(LANES, F32),
            state_out,
            out((steps, 8, LANES), F32, "block"),
            packet_out,
        ],
        [
            pltpu.VMEM((8 + BLOCK, channels), F32),
            pltpu.VMEM((inner, LANES), F32),
            pltpu.VMEM((8, LANES), F32),
        ],
        micros=20,
        mega=16,
    )
    packets = [(shifted(packet, "ctx", step), "whole") for step in range(1, ctx_count)]
    wz_spec = pl.BlockSpec((width, inner), lambda i: (0, 0), pipeline_mode=pl.Buffered(1))
    wo_spec = pl.BlockSpec((width, inner), lambda i: (0, 1), pipeline_mode=pl.Buffered(1))
    w2, z, dn = call(
        functools.partial(gate_matmul_kernel, counts, dp_count, parts),
        steps,
        info,
        [(value, "whole") for value in w2_parts] + [(normed, "rows"), (cotangent, "rows")],
        [out((width, 2 * inner), BF16, "whole"), row_out(inner, BF16), row_out(inner, BF16)],
        micros=7,
        mega=12,
    )
    y, hb, h, stat = call(
        functools.partial(apply_kernel, counts, len(packets)),
        steps,
        info,
        packets
        + [
            (entry, "block"),
            (decay, "block"),
            (cum, "rows"),
            (bc, "rows"),
            (ypart, "rows"),
            (z, "rows"),
            (dn, "rows"),
            (par, "whole"),
            (spread, "whole"),
        ],
        [
            row_out(inner, F32),
            out((steps, inner, LANES), BF16, "block"),
            state_out,
            out((8, rows), F32, "lanes"),
        ],
        [pltpu.VMEM((inner, LANES), F32)],
        micros=8,
        mega=12,
    )
    stat = lax.psum(stat, "tp")
    inner_all = inner * lax.axis_size("tp")
    half = width // 2
    keep, send, gwo, small_gate, dy, dz, de, exits, packet = call(
        functools.partial(gate_back_kernel, counts, inner_all),
        steps,
        info,
        [
            (stat, "lanes"),
            (y, "rows"),
            (z, "rows"),
            (dn, "rows"),
            (cotangent, "rows"),
            (cum, "rows"),
            (bc, "rows"),
            (xc, "rows"),
            (hb, "block"),
            (decay, "block"),
            (w2, wo_spec),
            (par, "whole"),
            (spread, "whole"),
        ],
        [
            row_out(half, BF16),
            row_out(half, BF16),
            out((width, inner), BF16, "whole"),
            out((8, inner), F32, "whole"),
            row_out(inner, BF16),
            row_out(inner, BF16),
            row_out(LANES, F32),
            state_out,
            packet_out,
        ],
        [
            pltpu.VMEM((width, inner), F32),
            pltpu.VMEM((inner, LANES), F32),
            pltpu.VMEM((8, LANES), F32),
        ],
        reverse=True,
        micros=15,
        mega=14,
    )
    packets = [(shifted(packet, "ctx", -step), "whole") for step in range(1, ctx_count)]
    with jax.named_scope("layer_out"):
        received = swapped(send)
        own_inputs = lax.dynamic_slice_in_dim(tokens, tp_index * half, half, 1).astype(F32)
        valid = (jnp.arange(rows) < fill).astype(F32)[:, None]
        layer_out = own_inputs + (keep.astype(F32) + received.astype(F32)) * valid
    dxc, dcq, dbq, row_sums, col_sums, *g2 = call(
        functools.partial(intra_back_kernel, counts, heads, dp_count),
        steps,
        info,
        [
            (dy, "rows"),
            (dz, "rows"),
            (xc, "rows"),
            (bc, "rows"),
            (cum, "rows"),
            (pre_step, "rows"),
            (hb, "block"),
            (normed, "rows"),
            (gwo, "whole"),
            (par, "whole"),
            (spread, "whole"),
        ],
        [
            row_out(inner, BF16),
            row_out(LANES, F32),
            row_out(LANES, F32),
            row_out(LANES, F32),
            row_out(LANES, F32),
        ]
        + [out((width // parts, 2 * inner), BF16, "whole")] * parts,
        [pltpu.VMEM((width, inner), F32), pltpu.VMEM((LANES, BLOCK), F32)],
        micros=18,
        mega=14,
    )
    with jax.named_scope("reduce_gate_weights"):
        total2 = ctx_sum(g2) if parts > 1 else g2[0]
    packed, back, *g1 = call(
        functools.partial(state_back_kernel, counts, heads, dp_count, len(packets), parts),
        steps,
        info,
        packets
        + [
            (exits, "block"),
            (h, "block"),
            (xc, "rows"),
            (bc, "rows"),
            (cum, "rows"),
            (pre_step, "rows"),
            (de, "rows"),
            (dxc, "rows"),
            (dcq, "rows"),
            (dbq, "rows"),
            (row_sums, "rows"),
            (col_sums, "rows"),
            (decay, "block"),
            (v, "rows"),
            (v, "tail"),
            (halo_v, "whole"),
            (halo_normed, "whole"),
            (normed, "rows"),
            (small_gate, "whole"),
            (par, "whole"),
            (dtp, "whole"),
            (spread, "whole"),
        ],
        [row_out(channels + LANES, BF16), out((16, channels), BF16, "whole")]
        + [out((width // parts, channels + LANES), BF16, "whole")] * parts,
        [
            pltpu.VMEM((inner, LANES), F32),
            pltpu.VMEM((8, LANES), F32),
            pltpu.VMEM((8 + BLOCK, channels), F32),
            pltpu.VMEM((8 + BLOCK, channels), F32),
            pltpu.VMEM((width, channels + LANES), F32),
            pltpu.VMEM((8, channels), F32),
        ],
        reverse=True,
        micros=25,
        mega=20,
    )
    with jax.named_scope("reduce_gate_weights"):
        total2 = halved_sum(total2) if parts > 1 else whole_sum(total2)
    norm_rows = part_rows * dp_count
    if parts > 1:
        g1 = [g1[0]] + [partnered(g1[mask], "ctx", mask) for mask in range(1, parts)]
        packed, g1[1] = lax.optimization_barrier((packed, g1[1]))
    partial, halo_grad, norm_part = call(
        functools.partial(input_back_kernel, counts, dp_count, parts),
        steps,
        info,
        [
            (packed, "rows"),
            (back, "whole"),
            (dz, "rows"),
            (w2, wz_spec),
            (tokens, "rows"),
            (halo, "whole"),
            (w1, "whole"),
            (par, "whole"),
        ],
        [
            row_out(width, BF16),
            out((8, width), F32, "whole"),
            out((norm_rows, LANES), F32, "whole"),
        ],
        [pltpu.VMEM((8, width), F32)],
        micros=5,
        mega=12,
    )
    other = swapped(partial)
    size = ctx_count * 2
    back = [(s, s - 2) for s in range(2, size)]
    cross = [(s, (s - 2) ^ 1) for s in range(2, size)]
    halo_a = lax.ppermute(halo_grad, ("ctx", "tp"), back)
    halo_b = lax.ppermute(halo_grad, ("ctx", "tp"), cross)
    with jax.named_scope("reduce_input_weights"):
        norm_part = jnp.pad(norm_part, ((0, 0), (channels, 0)))
        if parts > 1:
            total1 = dp_sum(sum(piece.astype(F32) for piece in g1) + norm_part)
        else:
            total1 = whole_sum((g1[0].astype(F32) + norm_part).astype(BF16))
        across = swapped(total1[:, inner:])
        lane = jnp.arange(3 * LANES) - 2 * LANES
        both = (lane < 0) | ((lane >= STATE_TAPS) & (lane < BY_HEAD))
        both = both | ((lane >= NORM) & (lane < NORM + shard // part_rows))
        summed = total1[:, inner:] + jnp.where(both[None, :], across, 0)
        total1 = jnp.concatenate([total1[:, :inner], summed], axis=1)
    (grad_tokens,) = call(
        functools.partial(finish_kernel, counts),
        steps,
        info,
        [
            (partial, "rows"),
            (other, "rows"),
            (halo_a, "whole"),
            (halo_b, "whole"),
            (tokens, "rows"),
            (cotangent, "rows"),
            (par, "whole"),
        ],
        [row_out(width, F32)],
        micros=5,
        mega=10,
    )
    with jax.named_scope("last_hop"):
        if parts > 1:
            total2 = doubled(total2)
            total1, grad_tokens = lax.optimization_barrier((total1, grad_tokens))
            total1 = exchanged(total1, "ctx")
        else:
            total1 = [total1]
    each = HEAD // dp_count
    part_bc = bias_bc.shape[0]
    tall = -(-shard // LANES) * LANES

    def final(*sizes):
        return out(sizes, F32, "whole")

    grad_wz, grad_wo = call(
        functools.partial(unpack_gate_kernel, counts, parts),
        1,
        info,
        [(total2, "whole")],
        [final(shard, inner), final(shard, inner)],
        micros=2,
        mega=8,
    )
    (
        grad_wx, grad_wbc, grad_wdt, grad_norm, grad_taps, grad_bias, grad_state_taps, grad_state_bias,
        grad_dt_bias, grad_a_log, grad_skip, grad_gate,
    ) = call(
        functools.partial(unpack_input_kernel, counts, heads, parts),
        1,
        info,
        [(value, "whole") for value in total1],
        [
            final(shard, inner),
            final(shard, 2 * LANES),
            final(heads, shard),
            final(1, shard),
            final(heads, CONV, each),
            final(heads, each),
            final(CONV, part_bc),
            final(1, part_bc),
            final(1, heads),
            final(1, heads),
            final(1, heads),
            final(heads, each),
        ],
        [pltpu.VMEM((tall, channels + LANES), F32)],
        micros=2,
        mega=8,
    )
    return (
        layer_out,
        grad_tokens,
        grad_norm[0],
        grad_wz,
        grad_wx,
        grad_wbc,
        grad_wdt.T,
        grad_taps.transpose(1, 0, 2),
        grad_bias,
        grad_state_taps,
        grad_state_bias[0],
        grad_dt_bias[0],
        grad_a_log[0],
        grad_skip[0],
        grad_gate,
        grad_wo.T,
    )


def solution(mesh):
    shards = P(("dp", "ctx"), None)
    return jax.shard_map(
        body,
        mesh=mesh,
        in_specs=(
            shards,
            shards,
            P("dp", None),
            P("dp", None),
            P("dp"),
            P("dp", "tp"),
            P("dp", "tp"),
            P("dp", None),
            P("dp", "tp"),
            P(None, "tp", "dp"),
            P("tp", "dp"),
            P(None, "dp"),
            P("dp"),
            P("tp"),
            P("tp"),
            P("tp"),
            P("tp", "dp"),
            P("tp", "dp"),
        ),
        out_specs=(
            P(("dp", "ctx"), "tp"),
            shards,
            P("dp"),
            P("dp", "tp"),
            P("dp", "tp"),
            P("dp", None),
            P("dp", "tp"),
            P(None, "tp", "dp"),
            P("tp", "dp"),
            P(None, "dp"),
            P("dp"),
            P("tp"),
            P("tp"),
            P("tp"),
            P("tp", "dp"),
            P("tp", "dp"),
        ),
        check_vma=False,
    )
```

```python
import functools

import jax
import jax.numpy as jnp
from jax import lax
from jax.experimental import pallas as pl
from jax.experimental.pallas import tpu as pltpu
from jax.sharding import PartitionSpec as P

CONV = 4
BLOCK = 256
HEAD = 64
LANES = 128
EPS = 1e-05
MEGA = 1024 * 1024
F32 = jnp.float32
BF16 = jnp.bfloat16


def dot(left, right):
    return jnp.dot(left, right, preferred_element_type=F32)


def dot_tn(left, right):
    return lax.dot_general(left, right, (((0,), (0,)), ((), ())), preferred_element_type=F32)


def dot_nt(left, right):
    return lax.dot_general(left, right, (((1,), (1,)), ((), ())), preferred_element_type=F32)


def dot_exact(left, right):
    return jnp.dot(left, right, preferred_element_type=F32, precision=lax.Precision.HIGHEST)


def iota(shape, dim):
    return lax.broadcasted_iota(jnp.int32, shape, dim)


def sigmoid(value):
    return 1.0 / (1.0 + jnp.exp(-value))


def gate_sigmoid(value):
    return 0.5 * jnp.tanh(0.5 * value) + 0.5


def softplus(value):
    return jnp.maximum(value, 0.0) + jnp.log1p(jnp.exp(-jnp.abs(value)))


def split(value):
    high = value.astype(BF16)
    return high, (value - high.astype(F32)).astype(BF16)


def expand(value, spread):
    return dot(jnp.concatenate(split(value), axis=1), spread[...])


def reduce_heads(value, spread):
    high, low = split(value)
    pick = spread[:LANES, :]
    return dot_nt(high, pick) + dot_nt(low, pick)


def head_column(row, channels):
    shape = (channels, LANES)
    return jnp.sum(jnp.where(iota(shape, 0) // HEAD == iota(shape, 1), row, 0.0), axis=1, keepdims=True)


def xor(value, mask):
    return jnp.bitwise_xor(value, jnp.int32(mask))


class Place:
    def __init__(self, info, counts):
        devices, sequences = counts
        own = info[devices + sequences]
        self.ctx = own
        self.tp = info[devices + sequences + 1]
        self.dp = info[devices + sequences + 2]
        self.fill = jnp.int32(0)
        self.first = jnp.int32(0)
        for device in range(devices):
            rows = info[device] * BLOCK
            self.fill = self.fill + jnp.where(own == device, rows, 0)
            self.first = self.first + jnp.where(own > device, rows, 0)
        self.ends = []
        total = jnp.int32(0)
        for sequence in range(sequences - 1):
            total = total + info[devices + sequence]
            self.ends.append(total)

    def of(self, position):
        found = (position >= self.ends[0]).astype(jnp.int32)
        for end in self.ends[1:]:
            found = found + (position >= end).astype(jnp.int32)
        return jnp.where(position < 0, -1, found)

    def rows(self, index):
        return self.of(self.first + jnp.minimum(index, self.fill - 1))

    def before(self, block):
        position = self.first + jnp.minimum(block * BLOCK, self.fill) - 1
        found = jnp.int32(0)
        for end in self.ends:
            found = found + jnp.where(position >= end, 1, 0)
        return jnp.where(position < 0, -1, found)

    def last(self, block):
        position = self.first + jnp.minimum(block * BLOCK + BLOCK - 1, self.fill - 1)
        found = jnp.int32(0)
        for end in self.ends:
            found = found + jnp.where(position >= end, 1, 0)
        return found

    def column(self, block, shift=0):
        return self.rows(block * BLOCK + shift + iota((BLOCK, 1), 0))

    def valid(self, block):
        return (block * BLOCK + iota((BLOCK, 1), 0) < self.fill).astype(F32)

    def keep(self, block):
        across = self.rows(block * BLOCK + iota((1, BLOCK), 1))
        return (self.column(block) == across) & (iota((BLOCK, BLOCK), 0) >= iota((BLOCK, BLOCK), 1))


def step_sizes(place, block, pre_step, heads):
    lane = iota((BLOCK, LANES), 1)
    return jnp.where(lane < heads, softplus(pre_step), 0.0) * place.valid(block)


def end_weights(place, block, cum):
    same = (place.column(block) == place.last(block)).astype(F32)
    return jnp.exp(cum[BLOCK - 1 :, :] - cum) * same


def enter_weights(place, block, cum):
    return jnp.exp(cum) * (place.column(block) == place.before(block)).astype(F32)


def block_decay(place, block, cum):
    return jnp.exp(cum[BLOCK - 1 :, :]) * jnp.where(place.last(block) == place.before(block), 1.0, 0.0)


def decay_kernel(keep, cum, cum_rows, head):
    return jnp.exp(jnp.where(keep, cum[:, head : head + 1] - cum_rows[head : head + 1, :], -1e30))


def both_halves(pair):
    lane = iota(pair.shape, 1)
    zero = jnp.zeros_like(pair)
    return [jnp.where(lane < HEAD, pair, zero), jnp.where(lane >= HEAD, pair, zero)]


def same_mask(place, block, tap):
    return (place.column(block, tap - (CONV - 1)) == place.column(block)).astype(F32)


def conv_pre(place, block, ext, par, channels):
    total = par[4:5, :channels]
    for tap in range(CONV):
        first = 8 - (CONV - 1) + tap
        total = total + par[tap : tap + 1, :channels] * ext[first : first + BLOCK, :] * same_mask(
            place, block, tap
        )
    return total


def state_packet(state, decay):
    high, low = split(decay)
    row = iota((16, LANES), 0)
    tail = jnp.where(row == 0, high.astype(F32), jnp.where(row == 1, low.astype(F32), 0.0))
    return jnp.concatenate([state.astype(BF16), tail.astype(BF16)], axis=0)


def merge_packets(packets, inner):
    total = jnp.zeros((inner, LANES), F32)
    for packet in reversed(packets):
        tail = packet[inner : inner + 16, :].astype(F32)
        decay = tail[0:1, :] + tail[1:2, :]
        total = packet[:inner, :].astype(F32) + head_column(decay, inner) * total
    return total


def normalise(rows, gain):
    inv = lax.rsqrt(jnp.mean(rows * rows, axis=1, keepdims=True) + EPS)
    return rows * inv, inv, (rows * inv * gain).astype(BF16)


def piece_rows(place, dp_count, parts, rows):
    for part in range(parts):
        for block in range(dp_count):
            owner = xor(place.dp, block) * parts + (xor(place.ctx, part) if parts > 1 else 0)
            yield part, block, pl.multiple_of(owner * rows, rows)


def join_pieces(place, dp_count, parts, whole):
    columns = parts[0].shape[1]
    if len(parts) == 1:
        whole[:, :columns] = parts[0][...]
        return
    rows = parts[0].shape[0] // dp_count
    for part, block, first in piece_rows(place, dp_count, len(parts), rows):
        whole[pl.ds(first, rows), :columns] = parts[part][block * rows : (block + 1) * rows, :]


def cut_pieces(place, dp_count, whole, parts, lanes):
    if len(parts) == 1:
        parts[0][:, lanes] = whole[...].astype(BF16)
        return
    rows = parts[0].shape[0] // dp_count
    for part, block, first in piece_rows(place, dp_count, len(parts), rows):
        parts[part][block * rows : (block + 1) * rows, lanes] = whole[pl.ds(first, rows), :].astype(BF16)


def join_parameters(place, vectors, skip, heads, par, w1):
    shard = vectors[0].shape[1] // 2
    each = HEAD // len(vectors)
    inner = heads * HEAD
    by_channel = jnp.zeros((16, inner), F32)
    in_order = jnp.zeros((16, shard * len(vectors)), F32)
    by_state = jnp.zeros((16, 2 * LANES), F32)
    states = 2 * LANES // len(vectors)
    eye = (iota((16, LANES), 0) == iota((16, LANES), 1)).astype(BF16)
    for block, vector in enumerate(vectors):
        owner = xor(place.dp, block)
        first = pl.multiple_of(owner * shard, shard)
        w1[pl.ds(first, shard), inner + 2 * LANES :] = dot_tn(vector[:, shard:], eye).astype(BF16)
        source, target = iota((shard, inner), 0), iota((shard, inner), 1)
        pick = target == source // each * HEAD + owner * each + source % each
        by_channel = by_channel + dot(vector[:, :shard], pick.astype(BF16))
        source, target = iota((shard, in_order.shape[1]), 0), iota((shard, in_order.shape[1]), 1)
        in_order = in_order + dot(vector[:, :shard], (target == owner * shard + source).astype(BF16))
        source, target = iota((shard, 2 * LANES), 0), iota((shard, 2 * LANES), 1)
        pick = (target == owner * states + source) & (source < states)
        by_state = by_state + dot(vector[:, :shard], pick.astype(BF16))
    par[...] = jnp.zeros_like(par)
    par[0:5, :inner] = by_channel[0:5, :]
    par[0:5, inner:] = by_state[8:13, :]
    par[5:6, : in_order.shape[1]] = in_order[5:6, :]
    par[6:7, :inner] = by_channel[6:7, :]
    par[7:8, :inner] = skip


TAPS, GATE, STATE_TAPS, BY_HEAD, NORM = 12, 18, 20, 25, 26


def lanes(pieces, columns):
    rows, at = [], 0
    for first, value in pieces:
        if first > at:
            rows.append(jnp.zeros((first - at, columns), F32))
        rows.append(value)
        at = first + value.shape[0]
    rows.append(jnp.zeros((LANES - at, columns), F32))
    return jnp.concatenate(rows, axis=0)


def pack_norm(place, dp_count, part_count, row, rows):
    columns = row.shape[1]
    shard = columns // dp_count
    size = shard // rows
    total = jnp.zeros((dp_count * rows, LANES), F32)
    source, target = iota((dp_count * rows, columns), 0), iota((dp_count * rows, columns), 1)
    owner = source // rows
    if part_count > 1:
        owner = jnp.bitwise_xor(owner, place.dp)
    for lane in range(size):
        pick = target == owner * shard + lane * rows + source % rows
        total = total + dot_nt(pick.astype(BF16), lanes([(NORM + lane, row)], columns).astype(BF16))
    return total


def pack_parameters(dp_count, heads, small, gate, skip):
    inner = heads * HEAD
    each = HEAD // dp_count
    shard = inner // dp_count
    states = 2 * LANES // dp_count

    source, target = iota((inner, inner), 0), iota((inner, inner), 1)
    inside = source % shard
    pick = target == inside // each * HEAD + source // shard * each + inside % each
    by_channel = lanes([(TAPS, small[0:5, :inner]), (GATE, gate)], inner)
    total = dot_nt(pick.astype(BF16), by_channel.astype(BF16))
    source, target = iota((inner, 2 * LANES), 0), iota((inner, 2 * LANES), 1)
    inside = source % shard
    pick = (target == source // shard * states + inside) & (inside < states)
    by_state = lanes([(STATE_TAPS, small[0:5, inner : inner + 2 * LANES])], 2 * LANES)
    total = total + dot_nt(pick.astype(BF16), by_state.astype(BF16))
    source, target = iota((inner, LANES), 0) % shard, iota((inner, LANES), 1)
    for index, row in enumerate((small[6:7, :LANES], small[7:8, :LANES], skip)):
        pick = (source == target + index * heads) & (target < heads)
        total = total + dot_nt(pick.astype(BF16), lanes([(BY_HEAD, row)], LANES).astype(BF16))
    return total


def forward_kernel(
    counts, heads, dp_count, part_count, info, *refs
):
    vectors = refs[:dp_count]
    parts = refs[dp_count : dp_count + part_count]
    (
        tok, halo, dtp, spread,
        w1, par, normed_o, halo_normed_o, halo_v_o, v_o, xc_o, bc_o, ypart_o, pre_o, cum_o, entry_o, decay_o,
        packet_o, ext, run, factor,
    ) = refs[dp_count + part_count :]
    forward_block(
        counts, heads, info, vectors, parts, tok, halo, w1, par, dtp, spread,
        normed_o, halo_normed_o, halo_v_o, v_o, xc_o, bc_o, ypart_o, pre_o, cum_o, entry_o, decay_o, packet_o,
        ext, run, factor,
    )


def forward_block(
    counts, heads, info, vectors, parts, tok, halo, w1, par, dtp, spread,
    normed_o, halo_normed_o, halo_v_o, v_o, xc_o, bc_o, ypart_o, pre_o, cum_o, entry_o, decay_o, packet_o,
    ext, run, factor,
):
    block = pl.program_id(0)
    place = Place(info, counts)
    inner = heads * HEAD
    state = LANES
    channels = inner + 2 * state
    width = tok.shape[1]

    @pl.when(block == 0)
    def _():
        join_pieces(place, len(vectors), parts, w1)
        join_parameters(place, vectors, expand(dtp[...], spread)[2:3, :], heads, par, w1)

    gain = par[5:6, :width]
    _, _, normed = normalise(tok[...].astype(F32), gain)
    normed_o[...] = normed

    @pl.when(block == 0)
    def _():
        _, _, before = normalise(halo[...].astype(F32), gain)
        halo_normed_o[...] = before
        raw = dot(before, w1[:, :channels]).astype(BF16).astype(F32)
        ext[0:8, :] = raw[8:16, :]
        halo_v_o[...] = raw[8:16, :]
        run[...] = jnp.zeros_like(run)
        factor[...] = jnp.ones_like(factor)

    @pl.when(block > 0)
    def _():
        ext[0:8, :] = ext[BLOCK : BLOCK + 8, :]

    raw = dot(normed, w1[...])
    v = raw[:, :channels].astype(BF16)
    v_o[...] = v
    ext[8 : 8 + BLOCK, :] = v.astype(F32)
    pre = conv_pre(place, block, ext, par, channels)
    act = (pre * gate_sigmoid(pre)).astype(BF16)
    xc = act[:, :inner]
    bq = act[:, inner : inner + state]
    cq = act[:, inner + state :]
    xc_o[...] = xc
    bc_o[...] = act[:, inner:]
    pre_step = raw[:, channels:].astype(BF16).astype(F32) + dtp[0:1, :]
    pre_o[...] = pre_step
    step = step_sizes(place, block, pre_step, heads)
    tri = (iota((BLOCK, BLOCK), 0) >= iota((BLOCK, BLOCK), 1)).astype(F32)
    cum = dot_exact(tri, -dtp[1:2, :] * step)
    cum_o[...] = cum
    cum_rows = cum.T
    step_rows = step.T
    gram = dot_nt(cq, bq)
    keep = place.keep(block)
    for pair in range(heads // 2):
        lanes = slice(pair * LANES, (pair + 1) * LANES)
        mixing = []
        for head in (2 * pair, 2 * pair + 1):
            weight = decay_kernel(keep, cum, cum_rows, head) * step_rows[head : head + 1, :]
            mixing.append((gram * weight).astype(BF16))
        x_pair = xc[:, lanes]
        y_pair = dot(jnp.concatenate(mixing, axis=1), jnp.concatenate(both_halves(x_pair), axis=0))
        ypart_o[:, lanes] = y_pair + par[7:8, lanes] * x_pair.astype(F32)
    weighted = (expand(end_weights(place, block, cum) * step, spread) * xc.astype(F32)).astype(BF16)
    block_state = dot_tn(weighted, bq)
    decay = block_decay(place, block, cum)
    entry_o[0] = run[...]
    total = head_column(decay, inner) * run[...] + block_state
    run[...] = total
    before = factor[0:1, :]
    row = iota((8, LANES), 0)
    decay_o[0] = jnp.where(row == 0, decay, jnp.where(row == 1, before, 0.0))
    after = before * decay
    factor[...] = jnp.broadcast_to(after, factor.shape)

    @pl.when(block == pl.num_programs(0) - 1)
    def _():
        packet_o[...] = state_packet(total, after)


def gate_matmul_kernel(counts, dp_count, part_count, info, *refs):
    parts = refs[:part_count]
    normed, cot, w2, z_o, dn_o = refs[part_count:]
    block = pl.program_id(0)
    place = Place(info, counts)
    inner = z_o.shape[1]

    @pl.when(block == 0)
    def _():
        join_pieces(place, dp_count, parts, w2)

    z_o[...] = dot(normed[...], w2[:, :inner]).astype(BF16)
    grad = (cot[...].astype(F32) * place.valid(block)).astype(BF16)
    dn_o[...] = dot(grad, w2[:, inner:]).astype(BF16)


def apply_kernel(counts, packet_count, info, *refs):
    packets = refs[:packet_count]
    entry, decay, cum, bc, ypart, z, dn, par, spread, y_o, hb_o, h_o, stat_o, start = refs[packet_count:]
    block = pl.program_id(0)
    place = Place(info, counts)
    inner = z.shape[1]

    @pl.when(block == 0)
    def _():
        start[...] = merge_packets([packet[...] for packet in packets], inner)

    state = entry[0] + head_column(decay[0, 1:2, :], inner) * start[...]
    h_o[0] = state
    low = state.astype(BF16)
    hb_o[0] = low
    cq = bc[:, LANES:]
    y = ypart[...] + expand(enter_weights(place, block, cum[...]), spread) * dot_nt(cq, low)
    y_o[...] = y
    gate = z[...].astype(F32)
    gated = y * gate * gate_sigmoid(gate)
    squares = jnp.sum(gated * gated, axis=1, keepdims=True)
    cross = jnp.sum(par[6:7, :inner] * dn[...].astype(F32) * gated, axis=1, keepdims=True)
    lane = iota((BLOCK, LANES), 1)
    both = jnp.where(lane == 0, squares, jnp.where(lane == 1, cross, 0.0))
    stat_o[...] = both.T[0:8, :]


def gate_back_kernel(
    counts, inner_all, info, stat, other_stat, y, z, dn, cot, cum, bc, xc, hb, decay, wo, par, spread,
    keep_o, send_o, gwo_o, small_o, dy_o, dz_o, de_o, exit_o, packet_o,
    acc, run, factor,
):
    step = pl.program_id(0)
    block = pl.num_programs(0) - 1 - step
    place = Place(info, counts)
    inner = z.shape[1]
    width = cot.shape[1]
    half = width // 2

    @pl.when(step == 0)
    def _():
        acc[...] = jnp.zeros_like(acc)
        run[...] = jnp.zeros_like(run)
        factor[...] = jnp.ones_like(factor)
        small_o[...] = jnp.zeros_like(small_o)

    column = jnp.concatenate([stat[...] + other_stat[...], jnp.zeros((LANES - 8, BLOCK), F32)], axis=0).T
    inv = lax.rsqrt(column[:, 0:1] / inner_all + EPS)
    cross = column[:, 1:2]
    gain = par[6:7, :inner]
    gate = z[...].astype(F32)
    sig = gate_sigmoid(gate)
    silu = gate * sig
    mixed = y[...]
    gated = mixed * silu
    normal = (gated * inv * gain).astype(BF16)
    own = pl.multiple_of(place.tp * half, half)
    other = pl.multiple_of((1 - place.tp) * half, half)
    keep_o[...] = dot_nt(normal, wo[pl.ds(own, half), :]).astype(BF16)
    send_o[...] = dot_nt(normal, wo[pl.ds(other, half), :]).astype(BF16)
    grad = (cot[...].astype(F32) * place.valid(block)).astype(BF16)
    acc[...] += dot_tn(grad, normal)
    back = dn[...].astype(F32)
    grad_gated = inv * (gain * back) - gated * (inv * inv * inv) * (cross / inner_all)
    dy = (grad_gated * silu).astype(BF16)
    dy_o[...] = dy
    dz_o[...] = (grad_gated * mixed * sig * (1.0 + gate * (1.0 - sig))).astype(BF16)
    dy_float = dy.astype(F32)
    cq = bc[:, LANES:]
    read = dot_nt(cq, hb[0])
    de_o[...] = reduce_heads(dy_float * read, spread)
    small_o[0:1, :] += jnp.sum(back * gated * inv, axis=0, keepdims=True)
    small_o[1:2, :] += jnp.sum(dy_float * xc[...].astype(F32), axis=0, keepdims=True)
    dq = (expand(enter_weights(place, block, cum[...]), spread) * dy_float).astype(BF16)
    exit_o[0] = run[...]
    here = decay[0, 0:1, :]
    total = head_column(here, inner) * run[...] + dot_tn(dq, cq)
    run[...] = total
    after = factor[0:1, :] * here
    factor[...] = jnp.broadcast_to(after, factor.shape)

    @pl.when(step == pl.num_programs(0) - 1)
    def _():
        packet_o[...] = state_packet(total, after)
        gwo_o[...] = acc[...].astype(BF16)


def intra_back_kernel(counts, heads, dp_count, info, *refs):
    dy, dz, xc, bc, cum, pre_step, hb, normed, gwo, par, spread = refs[:11]
    dxc_o, dcq_o, dbq_o, rows_o, cols_o = refs[11:16]
    parts = refs[16:-2]
    acc, columns = refs[-2:]
    block = pl.program_id(0)
    place = Place(info, counts)
    inner = heads * HEAD

    @pl.when(block == 0)
    def _():
        acc[...] = jnp.zeros_like(acc)
        columns[...] = jnp.zeros_like(columns)

    bq = bc[:, :LANES]
    cq = bc[:, LANES:]
    cums = cum[...]
    step = step_sizes(place, block, pre_step[...], heads)
    cum_rows = cums.T
    step_rows = step.T
    gram = dot_nt(cq, bq)
    keep = place.keep(block)
    lane = iota((BLOCK, LANES), 1)
    grad_gram = jnp.zeros((BLOCK, BLOCK), F32)
    sums = jnp.zeros((BLOCK, LANES), F32)
    for pair in range(heads // 2):
        lanes = slice(pair * LANES, (pair + 1) * LANES)
        dy_pair = dy[:, lanes]
        x_pair = xc[:, lanes]
        halves = jnp.concatenate(both_halves(dy_pair), axis=0)
        grad_mixing = dot_nt(halves, x_pair)
        mixing = []
        for side in range(2):
            head = 2 * pair + side
            grad_m = grad_mixing[side * BLOCK : (side + 1) * BLOCK, :]
            kernel = decay_kernel(keep, cums, cum_rows, head)
            step_row = step_rows[head : head + 1, :]
            weight = kernel * step_row
            mixing.append((gram * weight).astype(BF16))
            grad_gram = grad_gram + grad_m * weight
            part = grad_m * gram * kernel
            columns[head : head + 1, :] = jnp.sum(part, axis=0, keepdims=True)
            sums = sums + jnp.where(lane == head, jnp.sum(part * step_row, axis=1, keepdims=True), 0.0)
        dx_pair = dot_tn(jnp.concatenate(mixing, axis=0), halves)
        dxc_o[:, lanes] = (dx_pair + par[7:8, lanes] * dy_pair.astype(F32)).astype(BF16)
    grad_low = grad_gram.astype(BF16)
    dq = (expand(enter_weights(place, block, cums), spread) * dy[...].astype(F32)).astype(BF16)
    dcq_o[...] = dot(grad_low, bq) + dot(dq, hb[0])
    dbq_o[...] = dot_tn(grad_low, cq)
    rows_o[...] = sums
    cols_o[...] = columns[...].T
    acc[...] += dot_tn(normed[...], dz[...])

    @pl.when(block == pl.num_programs(0) - 1)
    def _():
        cut_pieces(place, dp_count, acc, parts, slice(0, inner))
        cut_pieces(place, dp_count, gwo, parts, slice(inner, 2 * inner))


def state_back_kernel(counts, heads, dp_count, packet_count, part_count, info, *refs):
    packets = refs[:packet_count]
    (
        exits, h, xc, bc, cum, pre_step, de, dxc, dcq, dbq, rows, cols, decay, v, v_tail, halo_v, halo_normed,
        normed, small_gate, par, dtp, spread,
        packed_o, back_o,
    ) = refs[packet_count : -6 - part_count]
    parts = refs[-6 - part_count : -6]
    start, factor, ext, grad_ext, acc, small_o = refs[-6:]
    step_id = pl.program_id(0)
    block = pl.num_programs(0) - 1 - step_id
    place = Place(info, counts)
    inner = heads * HEAD
    channels = inner + 2 * LANES

    @pl.when(step_id == 0)
    def _():
        start[...] = merge_packets([packet[...] for packet in packets], inner)
        factor[...] = jnp.ones_like(factor)
        acc[...] = jnp.zeros_like(acc)
        grad_ext[...] = jnp.zeros_like(grad_ext)
        small_o[...] = jnp.zeros_like(small_o)

    here = decay[0, 0:1, :]
    before = factor[0:1, :]
    grad_state = exits[0] + head_column(before, inner) * start[...]
    factor[...] = jnp.broadcast_to(before * here, factor.shape)
    shape = (inner, LANES)
    overlap = jnp.sum(grad_state * h[0], axis=1, keepdims=True)
    grad_decay = jnp.sum(
        jnp.where(iota(shape, 0) // HEAD == iota(shape, 1), overlap, 0.0), axis=0, keepdims=True
    )
    low = grad_state.astype(BF16)
    bq = bc[:, :LANES]
    cums = cum[...]
    x_float = xc[...].astype(F32)
    pre_dt = pre_step[...]
    valid = place.valid(block)
    step = step_sizes(place, block, pre_dt, heads)
    end_kernel = end_weights(place, block, cums)
    end_weight = end_kernel * step
    end_wide = expand(end_weight, spread)
    spread_b = dot_nt(bq, low)
    grad_x = dxc[...].astype(F32) + end_wide * spread_b
    grad_end = reduce_heads(x_float * spread_b, spread)
    grad_b = dbq[...] + dot((x_float * end_wide).astype(BF16), low)
    end_part = grad_end * end_weight
    last = iota((BLOCK, LANES), 0) == BLOCK - 1
    grad_cum = rows[...] - cols[...] * step - end_part + de[...] * enter_weights(place, block, cums)
    grad_cum = grad_cum + jnp.where(
        last, jnp.sum(end_part, axis=0, keepdims=True) + grad_decay * here, 0.0
    )
    upper = (iota((BLOCK, BLOCK), 0) <= iota((BLOCK, BLOCK), 1)).astype(F32)
    grad_log = dot_exact(upper, grad_cum)
    rates = dtp[1:2, :]
    grad_step = cols[...] + grad_end * end_kernel - rates * grad_log
    heads_lane = iota((BLOCK, LANES), 1) < heads
    grad_pre_dt = jnp.where(heads_lane, grad_step * sigmoid(pre_dt), 0.0) * valid
    small_o[6:7, :LANES] += jnp.sum(grad_pre_dt, axis=0, keepdims=True)
    small_o[7:8, :LANES] += jnp.sum(grad_log * (-rates * step), axis=0, keepdims=True)

    ext[8 : 8 + BLOCK, :] = v[...].astype(F32)

    @pl.when(block == 0)
    def _():
        ext[0:8, :] = halo_v[...]

    @pl.when(block > 0)
    def _():
        ext[0:8, :] = v_tail[...].astype(F32)[8:16, :]

    pre = conv_pre(place, block, ext, par, channels)
    sig = gate_sigmoid(pre)
    slope = sig * (1.0 + pre * (1.0 - sig))
    grad_pre = jnp.concatenate([grad_x, grad_b, dcq[...]], axis=1) * slope
    small_o[4:5, :] += jnp.sum(grad_pre, axis=0, keepdims=True)
    carry = grad_ext[0:8, :]
    grad_ext[0:BLOCK, :] = jnp.zeros((BLOCK, channels), F32)
    grad_ext[BLOCK : BLOCK + 8, :] = carry
    for tap in range(CONV):
        first = 8 - (CONV - 1) + tap
        masked = grad_pre * same_mask(place, block, tap)
        small_o[tap : tap + 1, :] += jnp.sum(masked * ext[first : first + BLOCK, :], axis=0, keepdims=True)
        grad_ext[first : first + BLOCK, :] += par[tap : tap + 1, :channels] * masked
    packed = jnp.concatenate([grad_ext[8 : 8 + BLOCK, :].astype(BF16), grad_pre_dt.astype(BF16)], axis=1)
    packed_o[...] = packed
    acc[...] += dot_tn(normed[...], packed)

    @pl.when(block == 0)
    def _():
        back = jnp.concatenate([jnp.zeros((8, channels), F32), grad_ext[0:8, :]], axis=0).astype(BF16)
        back_o[...] = back
        acc[:, :channels] += dot_tn(halo_normed[...], back)
        skip = reduce_heads(jnp.broadcast_to(small_gate[1:2, :], (8, inner)), spread)[0:1, :]
        acc[:, channels:] += pack_parameters(dp_count, heads, small_o, small_gate[0:1, :], skip)
        cut_pieces(place, dp_count, acc, parts, slice(0, channels + LANES))


def input_back_kernel(
    counts, dp_count, part_count, info, packed, back, dz, wz, tok, halo, w1, par,
    dn_o, dnh_o, norm_o, total,
):
    block = pl.program_id(0)
    place = Place(info, counts)
    width = tok.shape[1]
    channels = back.shape[1]
    gain = par[5:6, :width]

    @pl.when(block == 0)
    def _():
        halo_grad = dot_nt(back[...], w1[:, :channels])
        dnh_o[...] = halo_grad[8:16, :]
        halo_scaled, _, _ = normalise(halo[...].astype(F32), gain)
        total[...] = jnp.broadcast_to(
            jnp.sum(halo_grad * halo_scaled, axis=0, keepdims=True), total.shape
        )

    partial = dot_nt(dz[...], wz[...]) + dot_nt(packed[...], w1[...])
    dn_o[...] = partial.astype(BF16)
    scaled, _, _ = normalise(tok[...].astype(F32), gain)
    total[0:1, :] += jnp.sum(partial * scaled, axis=0, keepdims=True)

    @pl.when(block == pl.num_programs(0) - 1)
    def _():
        rows = norm_o.shape[0] // dp_count
        norm_o[...] = pack_norm(place, dp_count, part_count, total[0:1, :], rows)


def finish_kernel(counts, info, own, other, halo_a, halo_b, tok, cot, par, grad_o):
    block = pl.program_id(0)
    place = Place(info, counts)
    width = tok.shape[1]
    grad = own[...].astype(F32) + other[...].astype(F32)
    is_last = jnp.where((block + 1) * BLOCK == place.fill, 1.0, 0.0)
    halo = (halo_a[...] + halo_b[...]) * is_last
    grad = jnp.concatenate([grad[: BLOCK - 8, :], grad[BLOCK - 8 :, :] + halo], axis=0)
    inputs = tok[...].astype(F32)
    inv = lax.rsqrt(jnp.mean(inputs * inputs, axis=1, keepdims=True) + EPS)
    scaled = par[5:6, :width] * grad
    inner_dot = jnp.sum(scaled * inputs, axis=1, keepdims=True)
    grad_o[...] = (
        inv * scaled - inputs * (inv * inv * inv) * (inner_dot / width) + cot[...].astype(F32)
    )


def unpack_gate_kernel(counts, part_count, info, *refs):
    whole, wz_o, wo_o = refs
    place = Place(info, counts)
    shard, inner = wz_o.shape
    rows = shard // part_count
    for part in range(part_count):
        first = pl.multiple_of(xor(place.ctx, part) * rows, rows) if part_count > 1 else 0
        lines = slice(part * rows, (part + 1) * rows)
        wz_o[pl.ds(first, rows), :] = whole[lines, :inner].astype(F32)
        wo_o[pl.ds(first, rows), :] = whole[lines, inner:].astype(F32)


def unpack_input_kernel(counts, heads, part_count, info, *refs):
    parts = refs[:part_count]
    (
        wx_o, wbc_o, wdt_o, norm_o, taps_o, bias_o, state_taps_o, state_bias_o, dt_bias_o, a_log_o, skip_o,
        gate_o, wide,
    ) = refs[part_count:]
    place = Place(info, counts)
    shard, inner = wx_o.shape
    channels = inner + 2 * LANES
    rows = shard // part_count
    for part in range(part_count):
        first = pl.multiple_of(xor(place.ctx, part) * rows, rows) if part_count > 1 else 0
        wide[pl.ds(first, rows), :] = parts[part][...].astype(F32)
    wx_o[...] = wide[:shard, :inner]
    wbc_o[...] = wide[:shard, inner:channels]
    lines = wide[:, channels:].T
    wdt_o[...] = lines[:heads, :shard]
    each = gate_o.shape[1]
    size = lines.shape[1]
    source = iota((16, size), 1)
    inside = (source // each == iota((16, size), 0)) & (source < shard)
    place_in = (iota((size, LANES), 0) % each == iota((size, LANES), 1)).astype(BF16)

    def by_head(line):
        row = jnp.where(inside, lines[line : line + 1, :], 0.0).astype(BF16)
        return dot(row, place_in)[:heads, :each]

    for tap in range(CONV):
        taps_o[:, tap, :] = by_head(TAPS + tap)
    bias_o[...] = by_head(TAPS + CONV)
    gate_o[...] = by_head(GATE)
    gain = wide[:rows, channels:]
    for part in range(1, part_count):
        gain = gain + wide[part * rows : (part + 1) * rows, channels:]
    gain = jnp.concatenate([gain, jnp.zeros((LANES - rows, LANES), F32)], axis=0).T
    source, target = iota((LANES, size), 0), iota((LANES, size), 1)
    total = jnp.zeros((8, size), F32)
    for lane in range(shard // rows):
        pick = ((target == lane * rows + source) & (source < rows)).astype(F32)
        total = total + dot_exact(jnp.broadcast_to(gain[NORM + lane : NORM + lane + 1, :], (8, LANES)), pick)
    norm_o[...] = total[0:1, :shard]
    states = state_bias_o.shape[1]
    state_taps_o[...] = lines[STATE_TAPS : STATE_TAPS + CONV, :states]
    state_bias_o[...] = lines[STATE_TAPS + CONV : STATE_TAPS + CONV + 1, :states]
    row = lines[BY_HEAD : BY_HEAD + 1, :]
    dt_bias_o[...] = row[:, :heads]
    a_log_o[...] = row[:, heads : 2 * heads]
    skip_o[...] = row[:, 2 * heads : 3 * heads]


def call(body, steps, info, operands, outputs, scratch=(), reverse=False, micros=1, mega=20):
    def at(index):
        return steps - 1 - index if reverse else index

    def spec(shape, kind):
        if kind == "rows":
            return pl.BlockSpec((BLOCK,) + tuple(shape[1:]), lambda i: (at(i), 0))
        if kind == "block":
            return pl.BlockSpec((1,) + tuple(shape[1:]), lambda i: (at(i), 0, 0))
        if kind == "lanes":
            return pl.BlockSpec((shape[0], BLOCK), lambda i: (0, at(i)))
        if kind == "tail":
            each = BLOCK // 16
            return pl.BlockSpec((16, shape[1]), lambda i: (jnp.maximum(at(i) * each - 1, 0), 0))
        if kind == "whole":
            return pl.BlockSpec(tuple(shape), lambda i: (0,) * len(shape))
        if kind == "once":
            return pl.BlockSpec(tuple(shape), lambda i: (0,) * len(shape), pipeline_mode=pl.Buffered(1))
        return kind

    return pl.pallas_call(
        body,
        grid=(steps,),
        in_specs=[pl.BlockSpec(memory_space=pltpu.SMEM)]
        + [spec(array.shape, "once" if kind == "whole" else kind) for array, kind in operands],
        out_specs=[spec(shape.shape, kind) for shape, kind in outputs],
        out_shape=[shape for shape, _ in outputs],
        scratch_shapes=list(scratch),
        compiler_params=pltpu.CompilerParams(
            dimension_semantics=("arbitrary",), vmem_limit_bytes=mega * MEGA
        ),
        cost_estimate=pl.CostEstimate(
            flops=micros * 1_100_000_000, bytes_accessed=micros * 3_500_000, transcendentals=0
        ),
    )(info, *[array for array, _ in operands])


def shifted(value, axis, steps):
    count = lax.axis_size(axis)
    first, last = max(0, -steps), min(count, count - steps)
    return lax.ppermute(value, axis, [(source, source + steps) for source in range(first, last)])


def swapped(value):
    return lax.ppermute(value, "tp", [(0, 1), (1, 0)])


def partnered(value, axis, mask):
    return lax.ppermute(value, axis, [(one, one ^ mask) for one in range(lax.axis_size(axis))])


def exchanged(value, axis):
    return [value] + [partnered(value, axis, mask) for mask in range(1, lax.axis_size(axis))]


def own_rows(value, rows):
    return lax.dynamic_slice_in_dim(value, lax.axis_index("ctx") * rows, rows, 0)


def joined_rows(values):
    return jnp.concatenate(values, axis=0)


def ctx_sum(pieces):
    total = pieces[0].astype(F32)
    for mask in range(1, len(pieces)):
        total = total + partnered(pieces[mask], "ctx", mask).astype(F32)
    return total


def dp_sum(total):
    dp_count = lax.axis_size("dp")
    rows = total.shape[0] // dp_count
    own = total[:rows].astype(F32)
    for mask in range(1, dp_count):
        block = total[mask * rows : (mask + 1) * rows].astype(BF16)
        own = own + partnered(block, "dp", mask).astype(F32)
    return own.astype(BF16)


def halved_sum(total):
    blocks = lax.axis_size("dp")
    rows = total.shape[0] // blocks
    total = total.reshape(blocks, rows, -1).astype(F32)
    mask = 1
    while mask < blocks:
        kept = [total[block] for block in range(total.shape[0]) if block % 2 == 0]
        sent = [total[block] for block in range(total.shape[0]) if block % 2 == 1]
        received = partnered(jnp.concatenate(sent, axis=0).astype(BF16), "dp", mask)
        received = received.reshape(len(sent), rows, -1).astype(F32)
        total = jnp.stack(kept) + received
        mask *= 2
    return total[0].astype(BF16)


def doubled(value):
    mask = 1
    while mask < lax.axis_size("ctx"):
        value = jnp.concatenate([value, partnered(value, "ctx", mask)], axis=0)
        mask *= 2
    return value


def whole_sum(value):
    return lax.psum(lax.psum_scatter(value, "dp", scatter_dimension=0, tiled=True), "ctx")


def body(
    tokens, cotangent, device_fill, seq_lengths, norm_gain, w_z, w_x, w_bc, w_dt,
    conv_x, conv_x_bias, conv_bc, bias_bc, dt_bias, a_log, skip_d, gate_gain, w_out,
):
    rows, width = tokens.shape
    heads = dt_bias.shape[0]
    inner = heads * HEAD
    channels = inner + 2 * LANES
    steps = rows // BLOCK
    shard = norm_gain.shape[0]
    dp_count = lax.axis_size("dp")
    ctx_count = lax.axis_size("ctx")
    tp_index = lax.axis_index("tp")
    counts = (ctx_count, seq_lengths.shape[1])

    parts = ctx_count if shard % (16 * ctx_count) == 0 else 1
    part_rows = shard // parts

    with jax.named_scope("gather_weights"):
        vector = jnp.concatenate(
            [
                jnp.concatenate(
                    [
                        conv_x.reshape(CONV, shard),
                        conv_x_bias.reshape(1, shard),
                        norm_gain[None, :],
                        gate_gain.reshape(1, shard),
                        jnp.zeros((1, shard), BF16),
                        jnp.pad(
                            jnp.concatenate([conv_bc, bias_bc[None, :]], axis=0),
                            ((0, 3), (0, shard - bias_bc.shape[0])),
                        ),
                    ],
                    axis=0,
                ),
                jnp.pad(w_dt.T, ((0, 16 - heads), (0, 0))),
            ],
            axis=1,
        )
        input_rows = jnp.concatenate([w_x, w_bc], axis=1)
        gate_rows = jnp.concatenate([w_z, w_out.T], axis=1)
        if parts > 1:
            w1_parts = joined_rows(exchanged(own_rows(input_rows, part_rows), "dp"))
            vector = jnp.pad(vector, ((0, 0), (0, 2 * inner - 2 * shard)))
            block = jnp.concatenate([own_rows(gate_rows, part_rows), vector], axis=0)
            block, _ = lax.optimization_barrier((block, w1_parts))
            vectors = exchanged(block, "dp")
            w2_parts = exchanged(joined_rows([value[:part_rows] for value in vectors]), "ctx")
            w1_parts = exchanged(w1_parts, "ctx")
        else:
            w1_parts = [lax.all_gather(input_rows, "dp", axis=0, tiled=True)]
            w2_parts = [lax.all_gather(gate_rows, "dp", axis=0, tiled=True)]
            vectors = exchanged(vector, "dp")
    first_vector = part_rows // 16 if parts > 1 else 0
    vector_spec = pl.BlockSpec(
        (16, 2 * shard), lambda i: (first_vector, 0), pipeline_mode=pl.Buffered(1)
    )

    dtp = jnp.pad(jnp.stack([dt_bias, jnp.exp(a_log), skip_d]), ((0, 5), (0, LANES - heads)))
    shape = (2 * LANES, inner)
    spread = (iota(shape, 0) % LANES == iota(shape, 1) // HEAD).astype(BF16)
    info = jnp.concatenate(
        [
            device_fill[0],
            seq_lengths[0],
            jnp.stack([lax.axis_index("ctx"), tp_index, lax.axis_index("dp")]).astype(jnp.int32),
        ]
    )
    fill = jnp.sum(jnp.where(jnp.arange(ctx_count) == lax.axis_index("ctx"), device_fill[0], 0)) * BLOCK
    halo = shifted(lax.dynamic_slice_in_dim(tokens, fill - 16, 16, 0), "ctx", 1)

    def out(shape, dtype, kind):
        return (jax.ShapeDtypeStruct(shape, dtype), kind)

    def row_out(columns, dtype):
        return out((rows, columns), dtype, "rows")

    state_out = out((steps, inner, LANES), F32, "block")
    packet_out = out((inner + 16, LANES), BF16, "whole")

    (w1, par, normed, halo_normed, halo_v, v, xc, bc, ypart, pre_step, cum, entry, decay, packet) = call(
        functools.partial(forward_kernel, counts, heads, dp_count, parts),
        steps,
        info,
        [(value, vector_spec) for value in vectors]
        + [(value, "whole") for value in w1_parts]
        + [(tokens, "rows"), (halo, "whole"), (dtp, "whole"), (spread, "whole")],
        [
            out((width, channels + LANES), BF16, "whole"),
            out((8, channels), F32, "whole"),
            row_out(width, BF16),
            out((16, width), BF16, "whole"),
            out((8, channels), F32, "whole"),
            row_out(channels, BF16),
            row_out(inner, BF16),
            row_out(2 * LANES, BF16),
            row_out(inner, F32),
            row_out(LANES, F32),
            row_out(LANES, F32),
            state_out,
            out((steps, 8, LANES), F32, "block"),
            packet_out,
        ],
        [
            pltpu.VMEM((8 + BLOCK, channels), F32),
            pltpu.VMEM((inner, LANES), F32),
            pltpu.VMEM((8, LANES), F32),
        ],
        micros=40,
        mega=16,
    )
    packets = [(shifted(packet, "ctx", step), "whole") for step in range(1, ctx_count)]
    wz_spec = pl.BlockSpec((width, inner), lambda i: (0, 0), pipeline_mode=pl.Buffered(1))
    wo_spec = pl.BlockSpec((width, inner), lambda i: (0, 1), pipeline_mode=pl.Buffered(1))
    w2, z, dn = call(
        functools.partial(gate_matmul_kernel, counts, dp_count, parts),
        steps,
        info,
        [(value, "whole") for value in w2_parts] + [(normed, "rows"), (cotangent, "rows")],
        [out((width, 2 * inner), BF16, "whole"), row_out(inner, BF16), row_out(inner, BF16)],
        micros=7,
        mega=12,
    )
    y, hb, h, stat = call(
        functools.partial(apply_kernel, counts, len(packets)),
        steps,
        info,
        packets
        + [
            (entry, "block"),
            (decay, "block"),
            (cum, "rows"),
            (bc, "rows"),
            (ypart, "rows"),
            (z, "rows"),
            (dn, "rows"),
            (par, "whole"),
            (spread, "whole"),
        ],
        [
            row_out(inner, F32),
            out((steps, inner, LANES), BF16, "block"),
            state_out,
            out((8, rows), F32, "lanes"),
        ],
        [pltpu.VMEM((inner, LANES), F32)],
        micros=8,
        mega=12,
    )
    other_stat = swapped(stat)
    inner_all = inner * lax.axis_size("tp")
    half = width // 2
    keep, send, gwo, small_gate, dy, dz, de, exits, packet = call(
        functools.partial(gate_back_kernel, counts, inner_all),
        steps,
        info,
        [
            (stat, "lanes"),
            (other_stat, "lanes"),
            (y, "rows"),
            (z, "rows"),
            (dn, "rows"),
            (cotangent, "rows"),
            (cum, "rows"),
            (bc, "rows"),
            (xc, "rows"),
            (hb, "block"),
            (decay, "block"),
            (w2, wo_spec),
            (par, "whole"),
            (spread, "whole"),
        ],
        [
            row_out(half, BF16),
            row_out(half, BF16),
            out((width, inner), BF16, "whole"),
            out((8, inner), F32, "whole"),
            row_out(inner, BF16),
            row_out(inner, BF16),
            row_out(LANES, F32),
            state_out,
            packet_out,
        ],
        [
            pltpu.VMEM((width, inner), F32),
            pltpu.VMEM((inner, LANES), F32),
            pltpu.VMEM((8, LANES), F32),
        ],
        reverse=True,
        micros=15,
        mega=14,
    )
    packets = [(shifted(packet, "ctx", -step), "whole") for step in range(1, ctx_count)]
    with jax.named_scope("layer_out"):
        received = swapped(send)
        own_inputs = lax.dynamic_slice_in_dim(tokens, tp_index * half, half, 1).astype(F32)
        valid = (jnp.arange(rows) < fill).astype(F32)[:, None]
        layer_out = own_inputs + (keep.astype(F32) + received.astype(F32)) * valid
    dxc, dcq, dbq, row_sums, col_sums, *g2 = call(
        functools.partial(intra_back_kernel, counts, heads, dp_count),
        steps,
        info,
        [
            (dy, "rows"),
            (dz, "rows"),
            (xc, "rows"),
            (bc, "rows"),
            (cum, "rows"),
            (pre_step, "rows"),
            (hb, "block"),
            (normed, "rows"),
            (gwo, "whole"),
            (par, "whole"),
            (spread, "whole"),
        ],
        [
            row_out(inner, BF16),
            row_out(LANES, F32),
            row_out(LANES, F32),
            row_out(LANES, F32),
            row_out(LANES, F32),
        ]
        + [out((width // parts, 2 * inner), BF16, "whole")] * parts,
        [pltpu.VMEM((width, inner), F32), pltpu.VMEM((LANES, BLOCK), F32)],
        micros=18,
        mega=14,
    )
    with jax.named_scope("reduce_gate_weights"):
        total2 = ctx_sum(g2) if parts > 1 else g2[0]
    packed, back, *g1 = call(
        functools.partial(state_back_kernel, counts, heads, dp_count, len(packets), parts),
        steps,
        info,
        packets
        + [
            (exits, "block"),
            (h, "block"),
            (xc, "rows"),
            (bc, "rows"),
            (cum, "rows"),
            (pre_step, "rows"),
            (de, "rows"),
            (dxc, "rows"),
            (dcq, "rows"),
            (dbq, "rows"),
            (row_sums, "rows"),
            (col_sums, "rows"),
            (decay, "block"),
            (v, "rows"),
            (v, "tail"),
            (halo_v, "whole"),
            (halo_normed, "whole"),
            (normed, "rows"),
            (small_gate, "whole"),
            (par, "whole"),
            (dtp, "whole"),
            (spread, "whole"),
        ],
        [row_out(channels + LANES, BF16), out((16, channels), BF16, "whole")]
        + [out((width // parts, channels + LANES), BF16, "whole")] * parts,
        [
            pltpu.VMEM((inner, LANES), F32),
            pltpu.VMEM((8, LANES), F32),
            pltpu.VMEM((8 + BLOCK, channels), F32),
            pltpu.VMEM((8 + BLOCK, channels), F32),
            pltpu.VMEM((width, channels + LANES), F32),
            pltpu.VMEM((8, channels), F32),
        ],
        reverse=True,
        micros=25,
        mega=20,
    )
    with jax.named_scope("reduce_gate_weights"):
        total2 = halved_sum(total2) if parts > 1 else whole_sum(total2)
    norm_rows = part_rows * dp_count
    if parts > 1:
        g1 = [g1[0]] + [partnered(g1[mask], "ctx", mask) for mask in range(1, parts)]
        packed, g1[1] = lax.optimization_barrier((packed, g1[1]))
    partial, halo_grad, norm_part = call(
        functools.partial(input_back_kernel, counts, dp_count, parts),
        steps,
        info,
        [
            (packed, "rows"),
            (back, "whole"),
            (dz, "rows"),
            (w2, wz_spec),
            (tokens, "rows"),
            (halo, "whole"),
            (w1, "whole"),
            (par, "whole"),
        ],
        [
            row_out(width, BF16),
            out((8, width), F32, "whole"),
            out((norm_rows, LANES), F32, "whole"),
        ],
        [pltpu.VMEM((8, width), F32)],
        micros=5,
        mega=12,
    )
    other = swapped(partial)
    size = ctx_count * 2
    back = [(s, s - 2) for s in range(2, size)]
    cross = [(s, (s - 2) ^ 1) for s in range(2, size)]
    halo_a = lax.ppermute(halo_grad, ("ctx", "tp"), back)
    halo_b = lax.ppermute(halo_grad, ("ctx", "tp"), cross)
    with jax.named_scope("reduce_input_weights"):
        norm_part = jnp.pad(norm_part, ((0, 0), (channels, 0)))
        if parts > 1:
            total1 = sum(piece.astype(F32) for piece in g1) + norm_part
            total1, total2 = lax.optimization_barrier((total1, total2))
            total1 = dp_sum(total1)
            total2 = doubled(total2)
            total1, total2 = lax.optimization_barrier((total1, total2))
        else:
            total1 = whole_sum((g1[0].astype(F32) + norm_part).astype(BF16))
        across = swapped(total1[:, inner:])
        lane = jnp.arange(3 * LANES) - 2 * LANES
        both = (lane < 0) | ((lane >= STATE_TAPS) & (lane < BY_HEAD))
        both = both | ((lane >= NORM) & (lane < NORM + shard // part_rows))
        summed = total1[:, inner:] + jnp.where(both[None, :], across, 0)
        total1 = jnp.concatenate([total1[:, :inner], summed], axis=1)
    (grad_tokens,) = call(
        functools.partial(finish_kernel, counts),
        steps,
        info,
        [
            (partial, "rows"),
            (other, "rows"),
            (halo_a, "whole"),
            (halo_b, "whole"),
            (tokens, "rows"),
            (cotangent, "rows"),
            (par, "whole"),
        ],
        [row_out(width, F32)],
        micros=5,
        mega=10,
    )
    with jax.named_scope("last_hop"):
        if parts > 1:
            total1 = exchanged(total1, "ctx")
            total1[-1], grad_tokens = lax.optimization_barrier((total1[-1], grad_tokens))
        else:
            total1 = [total1]
    each = HEAD // dp_count
    part_bc = bias_bc.shape[0]
    tall = -(-shard // LANES) * LANES

    def final(*sizes):
        return out(sizes, F32, "whole")

    grad_wz, grad_wo = call(
        functools.partial(unpack_gate_kernel, counts, parts),
        1,
        info,
        [(total2, "whole")],
        [final(shard, inner), final(shard, inner)],
        micros=2,
        mega=8,
    )
    (
        grad_wx, grad_wbc, grad_wdt, grad_norm, grad_taps, grad_bias, grad_state_taps, grad_state_bias,
        grad_dt_bias, grad_a_log, grad_skip, grad_gate,
    ) = call(
        functools.partial(unpack_input_kernel, counts, heads, parts),
        1,
        info,
        [(value, "whole") for value in total1],
        [
            final(shard, inner),
            final(shard, 2 * LANES),
            final(heads, shard),
            final(1, shard),
            final(heads, CONV, each),
            final(heads, each),
            final(CONV, part_bc),
            final(1, part_bc),
            final(1, heads),
            final(1, heads),
            final(1, heads),
            final(heads, each),
        ],
        [pltpu.VMEM((tall, channels + LANES), F32)],
        micros=2,
        mega=8,
    )
    return (
        layer_out,
        grad_tokens,
        grad_norm[0],
        grad_wz,
        grad_wx,
        grad_wbc,
        grad_wdt.T,
        grad_taps.transpose(1, 0, 2),
        grad_bias,
        grad_state_taps,
        grad_state_bias[0],
        grad_dt_bias[0],
        grad_a_log[0],
        grad_skip[0],
        grad_gate,
        grad_wo.T,
    )


def solution(mesh):
    shards = P(("dp", "ctx"), None)
    return jax.shard_map(
        body,
        mesh=mesh,
        in_specs=(
            shards,
            shards,
            P("dp", None),
            P("dp", None),
            P("dp"),
            P("dp", "tp"),
            P("dp", "tp"),
            P("dp", None),
            P("dp", "tp"),
            P(None, "tp", "dp"),
            P("tp", "dp"),
            P(None, "dp"),
            P("dp"),
            P("tp"),
            P("tp"),
            P("tp"),
            P("tp", "dp"),
            P("tp", "dp"),
        ),
        out_specs=(
            P(("dp", "ctx"), "tp"),
            shards,
            P("dp"),
            P("dp", "tp"),
            P("dp", "tp"),
            P("dp", None),
            P("dp", "tp"),
            P(None, "tp", "dp"),
            P("tp", "dp"),
            P(None, "dp"),
            P("dp"),
            P("tp"),
            P("tp"),
            P("tp"),
            P("tp", "dp"),
            P("tp", "dp"),
        ),
        check_vma=False,
    )
```

```python
import functools

import jax
import jax.numpy as jnp
import numpy as np
from jax import lax
from jax.experimental import pallas as pl
from jax.experimental.pallas import tpu as pltpu
from jax.sharding import PartitionSpec as P

CONV = 4
BLOCK = 256
HEAD = 64
LANES = 128
EPS = 1e-05
MEGA = 1024 * 1024
F32 = jnp.float32
BF16 = jnp.bfloat16


def dot(left, right):
    return jnp.dot(left, right, preferred_element_type=F32)


def dot_tn(left, right):
    return lax.dot_general(left, right, (((0,), (0,)), ((), ())), preferred_element_type=F32)


def dot_nt(left, right):
    return lax.dot_general(left, right, (((1,), (1,)), ((), ())), preferred_element_type=F32)


def dot_exact(left, right):
    return jnp.dot(left, right, preferred_element_type=F32, precision=lax.Precision.HIGHEST)


def iota(shape, dim):
    return lax.broadcasted_iota(jnp.int32, shape, dim)


def sigmoid(value):
    return 1.0 / (1.0 + jnp.exp(-value))


def gate_sigmoid(value):
    return 0.5 * jnp.tanh(0.5 * value) + 0.5


def softplus(value):
    return jnp.maximum(value, 0.0) + jnp.log1p(jnp.exp(-jnp.abs(value)))


def split(value):
    high = value.astype(BF16)
    return high, (value - high.astype(F32)).astype(BF16)


def expand(value, spread):
    return dot(jnp.concatenate(split(value), axis=1), spread[...])


def reduce_heads(value, spread):
    high, low = split(value)
    pick = spread[:LANES, :]
    return dot_nt(high, pick) + dot_nt(low, pick)


def head_column(row, channels):
    shape = (channels, LANES)
    return jnp.sum(jnp.where(iota(shape, 0) // HEAD == iota(shape, 1), row, 0.0), axis=1, keepdims=True)


def xor(value, mask):
    return jnp.bitwise_xor(value, jnp.int32(mask))


class Place:
    def __init__(self, info, counts):
        devices, sequences = counts
        own = info[devices + sequences]
        self.ctx = own
        self.tp = info[devices + sequences + 1]
        self.dp = info[devices + sequences + 2]
        self.fill = jnp.int32(0)
        self.first = jnp.int32(0)
        for device in range(devices):
            rows = info[device] * BLOCK
            self.fill = self.fill + jnp.where(own == device, rows, 0)
            self.first = self.first + jnp.where(own > device, rows, 0)
        self.ends = []
        total = jnp.int32(0)
        for sequence in range(sequences - 1):
            total = total + info[devices + sequence]
            self.ends.append(total)

    def of(self, position):
        found = (position >= self.ends[0]).astype(jnp.int32)
        for end in self.ends[1:]:
            found = found + (position >= end).astype(jnp.int32)
        return jnp.where(position < 0, -1, found)

    def rows(self, index):
        return self.of(self.first + jnp.minimum(index, self.fill - 1))

    def before(self, block):
        position = self.first + jnp.minimum(block * BLOCK, self.fill) - 1
        found = jnp.int32(0)
        for end in self.ends:
            found = found + jnp.where(position >= end, 1, 0)
        return jnp.where(position < 0, -1, found)

    def last(self, block):
        position = self.first + jnp.minimum(block * BLOCK + BLOCK - 1, self.fill - 1)
        found = jnp.int32(0)
        for end in self.ends:
            found = found + jnp.where(position >= end, 1, 0)
        return found

    def column(self, block, shift=0):
        return self.rows(block * BLOCK + shift + iota((BLOCK, 1), 0))

    def valid(self, block):
        return (block * BLOCK + iota((BLOCK, 1), 0) < self.fill).astype(F32)

    def keep(self, block):
        across = self.rows(block * BLOCK + iota((1, BLOCK), 1))
        return (self.column(block) == across) & (iota((BLOCK, BLOCK), 0) >= iota((BLOCK, BLOCK), 1))


def step_sizes(place, block, pre_step, heads):
    lane = iota((BLOCK, LANES), 1)
    return jnp.where(lane < heads, softplus(pre_step), 0.0) * place.valid(block)


def end_weights(place, block, cum):
    same = (place.column(block) == place.last(block)).astype(F32)
    return jnp.exp(cum[BLOCK - 1 :, :] - cum) * same


def enter_weights(place, block, cum):
    return jnp.exp(cum) * (place.column(block) == place.before(block)).astype(F32)


def block_decay(place, block, cum):
    return jnp.exp(cum[BLOCK - 1 :, :]) * jnp.where(place.last(block) == place.before(block), 1.0, 0.0)


def decay_kernel(keep, cum, cum_rows, head):
    return jnp.exp(jnp.where(keep, cum[:, head : head + 1] - cum_rows[head : head + 1, :], -1e30))


def both_halves(pair):
    lane = iota(pair.shape, 1)
    zero = jnp.zeros_like(pair)
    return [jnp.where(lane < HEAD, pair, zero), jnp.where(lane >= HEAD, pair, zero)]


def same_mask(place, block, tap):
    return (place.column(block, tap - (CONV - 1)) == place.column(block)).astype(F32)


def conv_pre(place, block, ext, par, channels):
    total = par[4:5, :channels]
    for tap in range(CONV):
        first = 8 - (CONV - 1) + tap
        total = total + par[tap : tap + 1, :channels] * ext[first : first + BLOCK, :] * same_mask(
            place, block, tap
        )
    return total


def state_packet(state, decay):
    high, low = split(decay)
    row = iota((16, LANES), 0)
    tail = jnp.where(row == 0, high.astype(F32), jnp.where(row == 1, low.astype(F32), 0.0))
    return jnp.concatenate([state.astype(BF16), tail.astype(BF16)], axis=0)


def merge_packets(packets, inner):
    total = jnp.zeros((inner, LANES), F32)
    for packet in reversed(packets):
        tail = packet[inner : inner + 16, :].astype(F32)
        decay = tail[0:1, :] + tail[1:2, :]
        total = packet[:inner, :].astype(F32) + head_column(decay, inner) * total
    return total


def normalise(rows, gain):
    inv = lax.rsqrt(jnp.mean(rows * rows, axis=1, keepdims=True) + EPS)
    return rows * inv, inv, (rows * inv * gain).astype(BF16)


def piece_rows(place, dp_count, parts, rows):
    for part in range(parts):
        for block in range(dp_count):
            owner = xor(place.dp, block) * parts + (xor(place.ctx, part) if parts > 1 else 0)
            yield part, block, pl.multiple_of(owner * rows, rows)


def join_pieces(place, dp_count, parts, whole):
    columns = parts[0].shape[1]
    if len(parts) == 1:
        whole[:, :columns] = parts[0][...]
        return
    rows = parts[0].shape[0] // dp_count
    for part, block, first in piece_rows(place, dp_count, len(parts), rows):
        whole[pl.ds(first, rows), :columns] = parts[part][block * rows : (block + 1) * rows, :]


def cut_pieces(place, dp_count, whole, parts, lanes):
    if len(parts) == 1:
        parts[0][:, lanes] = whole[...].astype(BF16)
        return
    rows = parts[0].shape[0] // dp_count
    for part, block, first in piece_rows(place, dp_count, len(parts), rows):
        parts[part][block * rows : (block + 1) * rows, lanes] = whole[pl.ds(first, rows), :].astype(BF16)


def join_parameters(place, vectors, skip, heads, par, w1):
    shard = vectors[0].shape[1] // 2
    each = HEAD // len(vectors)
    inner = heads * HEAD
    by_channel = jnp.zeros((16, inner), F32)
    in_order = jnp.zeros((16, shard * len(vectors)), F32)
    by_state = jnp.zeros((16, 2 * LANES), F32)
    states = 2 * LANES // len(vectors)
    eye = (iota((16, LANES), 0) == iota((16, LANES), 1)).astype(BF16)
    for block, vector in enumerate(vectors):
        owner = xor(place.dp, block)
        first = pl.multiple_of(owner * shard, shard)
        w1[pl.ds(first, shard), inner + 2 * LANES :] = dot_tn(vector[:, shard:], eye).astype(BF16)
        source, target = iota((shard, inner), 0), iota((shard, inner), 1)
        pick = target == source // each * HEAD + owner * each + source % each
        by_channel = by_channel + dot(vector[:, :shard], pick.astype(BF16))
        source, target = iota((shard, in_order.shape[1]), 0), iota((shard, in_order.shape[1]), 1)
        in_order = in_order + dot(vector[:, :shard], (target == owner * shard + source).astype(BF16))
        source, target = iota((shard, 2 * LANES), 0), iota((shard, 2 * LANES), 1)
        pick = (target == owner * states + source) & (source < states)
        by_state = by_state + dot(vector[:, :shard], pick.astype(BF16))
    par[...] = jnp.zeros_like(par)
    par[0:5, :inner] = by_channel[0:5, :]
    par[0:5, inner:] = by_state[8:13, :]
    par[5:6, : in_order.shape[1]] = in_order[5:6, :]
    par[6:7, :inner] = by_channel[6:7, :]
    par[7:8, :inner] = skip


TAPS, GATE, STATE_TAPS, BY_HEAD, NORM = 12, 18, 20, 25, 26


def lanes(pieces, columns):
    rows, at = [], 0
    for first, value in pieces:
        if first > at:
            rows.append(jnp.zeros((first - at, columns), F32))
        rows.append(value)
        at = first + value.shape[0]
    rows.append(jnp.zeros((LANES - at, columns), F32))
    return jnp.concatenate(rows, axis=0)


def pack_norm(place, dp_count, part_count, row, rows):
    columns = row.shape[1]
    shard = columns // dp_count
    size = shard // rows
    total = jnp.zeros((dp_count * rows, LANES), F32)
    source, target = iota((dp_count * rows, columns), 0), iota((dp_count * rows, columns), 1)
    owner = source // rows
    if part_count > 1:
        owner = jnp.bitwise_xor(owner, place.dp)
    for lane in range(size):
        pick = target == owner * shard + lane * rows + source % rows
        total = total + dot_nt(pick.astype(BF16), lanes([(NORM + lane, row)], columns).astype(BF16))
    return total


def pack_parameters(dp_count, heads, small, gate, skip):
    inner = heads * HEAD
    each = HEAD // dp_count
    shard = inner // dp_count
    states = 2 * LANES // dp_count

    source, target = iota((inner, inner), 0), iota((inner, inner), 1)
    inside = source % shard
    pick = target == inside // each * HEAD + source // shard * each + inside % each
    by_channel = lanes([(TAPS, small[0:5, :inner]), (GATE, gate)], inner)
    total = dot_nt(pick.astype(BF16), by_channel.astype(BF16))
    source, target = iota((inner, 2 * LANES), 0), iota((inner, 2 * LANES), 1)
    inside = source % shard
    pick = (target == source // shard * states + inside) & (inside < states)
    by_state = lanes([(STATE_TAPS, small[0:5, inner : inner + 2 * LANES])], 2 * LANES)
    total = total + dot_nt(pick.astype(BF16), by_state.astype(BF16))
    source, target = iota((inner, LANES), 0) % shard, iota((inner, LANES), 1)
    for index, row in enumerate((small[6:7, :LANES], small[7:8, :LANES], skip)):
        pick = (source == target + index * heads) & (target < heads)
        total = total + dot_nt(pick.astype(BF16), lanes([(BY_HEAD, row)], LANES).astype(BF16))
    return total


def forward_kernel(
    counts, heads, dp_count, part_count, info, *refs
):
    vectors = refs[:dp_count]
    parts = refs[dp_count : dp_count + part_count]
    (
        tok, halo, dtp, spread,
        w1, par, normed_o, halo_normed_o, halo_v_o, v_o, xc_o, bc_o, ypart_o, pre_o, cum_o, entry_o, decay_o,
        packet_o, ext, run, factor,
    ) = refs[dp_count + part_count :]
    forward_block(
        counts, heads, info, vectors, parts, tok, halo, w1, par, dtp, spread,
        normed_o, halo_normed_o, halo_v_o, v_o, xc_o, bc_o, ypart_o, pre_o, cum_o, entry_o, decay_o, packet_o,
        ext, run, factor,
    )


def forward_block(
    counts, heads, info, vectors, parts, tok, halo, w1, par, dtp, spread,
    normed_o, halo_normed_o, halo_v_o, v_o, xc_o, bc_o, ypart_o, pre_o, cum_o, entry_o, decay_o, packet_o,
    ext, run, factor,
):
    block = pl.program_id(0)
    place = Place(info, counts)
    inner = heads * HEAD
    state = LANES
    channels = inner + 2 * state
    width = tok.shape[1]

    @pl.when(block == 0)
    def _():
        join_pieces(place, len(vectors), parts, w1)
        join_parameters(place, vectors, expand(dtp[...], spread)[2:3, :], heads, par, w1)

    gain = par[5:6, :width]
    _, _, normed = normalise(tok[...].astype(F32), gain)
    normed_o[...] = normed

    @pl.when(block == 0)
    def _():
        _, _, before = normalise(halo[...].astype(F32), gain)
        halo_normed_o[...] = before
        raw = dot(before, w1[:, :channels]).astype(BF16).astype(F32)
        ext[0:8, :] = raw[8:16, :]
        halo_v_o[...] = raw[8:16, :]
        run[...] = jnp.zeros_like(run)
        factor[...] = jnp.ones_like(factor)

    @pl.when(block > 0)
    def _():
        ext[0:8, :] = ext[BLOCK : BLOCK + 8, :]

    raw = dot(normed, w1[...])
    v = raw[:, :channels].astype(BF16)
    v_o[...] = v
    ext[8 : 8 + BLOCK, :] = v.astype(F32)
    pre = conv_pre(place, block, ext, par, channels)
    act = (pre * gate_sigmoid(pre)).astype(BF16)
    xc = act[:, :inner]
    bq = act[:, inner : inner + state]
    cq = act[:, inner + state :]
    xc_o[...] = xc
    bc_o[...] = act[:, inner:]
    pre_step = raw[:, channels:].astype(BF16).astype(F32) + dtp[0:1, :]
    pre_o[...] = pre_step
    step = step_sizes(place, block, pre_step, heads)
    tri = (iota((BLOCK, BLOCK), 0) >= iota((BLOCK, BLOCK), 1)).astype(F32)
    cum = dot_exact(tri, -dtp[1:2, :] * step)
    cum_o[...] = cum
    cum_rows = cum.T
    step_rows = step.T
    gram = dot_nt(cq, bq)
    keep = place.keep(block)
    for pair in range(heads // 2):
        lanes = slice(pair * LANES, (pair + 1) * LANES)
        mixing = []
        for head in (2 * pair, 2 * pair + 1):
            weight = decay_kernel(keep, cum, cum_rows, head) * step_rows[head : head + 1, :]
            mixing.append((gram * weight).astype(BF16))
        x_pair = xc[:, lanes]
        y_pair = dot(jnp.concatenate(mixing, axis=1), jnp.concatenate(both_halves(x_pair), axis=0))
        ypart_o[:, lanes] = y_pair + par[7:8, lanes] * x_pair.astype(F32)
    weighted = (expand(end_weights(place, block, cum) * step, spread) * xc.astype(F32)).astype(BF16)
    block_state = dot_tn(weighted, bq)
    decay = block_decay(place, block, cum)
    entry_o[0] = run[...]
    total = head_column(decay, inner) * run[...] + block_state
    run[...] = total
    before = factor[0:1, :]
    row = iota((8, LANES), 0)
    decay_o[0] = jnp.where(row == 0, decay, jnp.where(row == 1, before, 0.0))
    after = before * decay
    factor[...] = jnp.broadcast_to(after, factor.shape)

    @pl.when(block == pl.num_programs(0) - 1)
    def _():
        packet_o[...] = state_packet(total, after)


def gate_matmul_kernel(counts, dp_count, part_count, info, *refs):
    parts = refs[:part_count]
    normed, cot, w2, z_o, dn_o = refs[part_count:]
    block = pl.program_id(0)
    place = Place(info, counts)
    inner = z_o.shape[1]

    @pl.when(block == 0)
    def _():
        join_pieces(place, dp_count, parts, w2)

    z_o[...] = dot(normed[...], w2[:, :inner]).astype(BF16)
    grad = (cot[...].astype(F32) * place.valid(block)).astype(BF16)
    dn_o[...] = dot(grad, w2[:, inner:]).astype(BF16)


def apply_kernel(counts, packet_count, info, *refs):
    packets = refs[:packet_count]
    entry, decay, cum, bc, ypart, z, dn, par, spread, y_o, hb_o, h_o, stat_o, start = refs[packet_count:]
    block = pl.program_id(0)
    place = Place(info, counts)
    inner = z.shape[1]

    @pl.when(block == 0)
    def _():
        start[...] = merge_packets([packet[...] for packet in packets], inner)

    state = entry[0] + head_column(decay[0, 1:2, :], inner) * start[...]
    h_o[0] = state
    low = state.astype(BF16)
    hb_o[0] = low
    cq = bc[:, LANES:]
    y = ypart[...] + expand(enter_weights(place, block, cum[...]), spread) * dot_nt(cq, low)
    y_o[...] = y
    gate = z[...].astype(F32)
    gated = y * gate * gate_sigmoid(gate)
    squares = jnp.sum(gated * gated, axis=1, keepdims=True)
    cross = jnp.sum(par[6:7, :inner] * dn[...].astype(F32) * gated, axis=1, keepdims=True)
    lane = iota((BLOCK, LANES), 1)
    both = jnp.where(lane == 0, squares, jnp.where(lane == 1, cross, 0.0))
    stat_o[...] = both.T[0:8, :]


def gate_back_kernel(
    counts, inner_all, info, stat, other_stat, y, z, dn, cot, cum, bc, xc, hb, decay, wo, par, spread,
    keep_o, send_o, gwo_o, small_o, dy_o, dz_o, de_o, exit_o, packet_o,
    acc, run, factor,
):
    step = pl.program_id(0)
    block = pl.num_programs(0) - 1 - step
    place = Place(info, counts)
    inner = z.shape[1]
    width = cot.shape[1]
    half = width // 2

    @pl.when(step == 0)
    def _():
        acc[...] = jnp.zeros_like(acc)
        run[...] = jnp.zeros_like(run)
        factor[...] = jnp.ones_like(factor)
        small_o[...] = jnp.zeros_like(small_o)

    column = jnp.concatenate([stat[...] + other_stat[...], jnp.zeros((LANES - 8, BLOCK), F32)], axis=0).T
    inv = lax.rsqrt(column[:, 0:1] / inner_all + EPS)
    cross = column[:, 1:2]
    gain = par[6:7, :inner]
    gate = z[...].astype(F32)
    sig = gate_sigmoid(gate)
    silu = gate * sig
    mixed = y[...]
    gated = mixed * silu
    normal = (gated * inv * gain).astype(BF16)
    own = pl.multiple_of(place.tp * half, half)
    other = pl.multiple_of((1 - place.tp) * half, half)
    keep_o[...] = dot_nt(normal, wo[pl.ds(own, half), :]).astype(BF16)
    send_o[...] = dot_nt(normal, wo[pl.ds(other, half), :]).astype(BF16)
    grad = (cot[...].astype(F32) * place.valid(block)).astype(BF16)
    acc[...] += dot_tn(grad, normal)
    back = dn[...].astype(F32)
    grad_gated = inv * (gain * back) - gated * (inv * inv * inv) * (cross / inner_all)
    dy = (grad_gated * silu).astype(BF16)
    dy_o[...] = dy
    dz_o[...] = (grad_gated * mixed * sig * (1.0 + gate * (1.0 - sig))).astype(BF16)
    dy_float = dy.astype(F32)
    cq = bc[:, LANES:]
    read = dot_nt(cq, hb[0])
    de_o[...] = reduce_heads(dy_float * read, spread)
    small_o[0:1, :] += jnp.sum(back * gated * inv, axis=0, keepdims=True)
    small_o[1:2, :] += jnp.sum(dy_float * xc[...].astype(F32), axis=0, keepdims=True)
    dq = (expand(enter_weights(place, block, cum[...]), spread) * dy_float).astype(BF16)
    exit_o[0] = run[...]
    here = decay[0, 0:1, :]
    total = head_column(here, inner) * run[...] + dot_tn(dq, cq)
    run[...] = total
    after = factor[0:1, :] * here
    factor[...] = jnp.broadcast_to(after, factor.shape)

    @pl.when(step == pl.num_programs(0) - 1)
    def _():
        packet_o[...] = state_packet(total, after)
        gwo_o[...] = acc[...].astype(BF16)


def intra_back_kernel(counts, heads, dp_count, info, *refs):
    dy, dz, xc, bc, cum, pre_step, hb, normed, gwo, par, spread = refs[:11]
    dxc_o, dcq_o, dbq_o, rows_o, cols_o = refs[11:16]
    parts = refs[16:-2]
    acc, columns = refs[-2:]
    block = pl.program_id(0)
    place = Place(info, counts)
    inner = heads * HEAD

    @pl.when(block == 0)
    def _():
        acc[...] = jnp.zeros_like(acc)
        columns[...] = jnp.zeros_like(columns)

    bq = bc[:, :LANES]
    cq = bc[:, LANES:]
    cums = cum[...]
    step = step_sizes(place, block, pre_step[...], heads)
    cum_rows = cums.T
    step_rows = step.T
    gram = dot_nt(cq, bq)
    keep = place.keep(block)
    lane = iota((BLOCK, LANES), 1)
    grad_gram = jnp.zeros((BLOCK, BLOCK), F32)
    sums = jnp.zeros((BLOCK, LANES), F32)
    for pair in range(heads // 2):
        lanes = slice(pair * LANES, (pair + 1) * LANES)
        dy_pair = dy[:, lanes]
        x_pair = xc[:, lanes]
        halves = jnp.concatenate(both_halves(dy_pair), axis=0)
        grad_mixing = dot_nt(halves, x_pair)
        mixing = []
        for side in range(2):
            head = 2 * pair + side
            grad_m = grad_mixing[side * BLOCK : (side + 1) * BLOCK, :]
            kernel = decay_kernel(keep, cums, cum_rows, head)
            step_row = step_rows[head : head + 1, :]
            weight = kernel * step_row
            mixing.append((gram * weight).astype(BF16))
            grad_gram = grad_gram + grad_m * weight
            part = grad_m * gram * kernel
            columns[head : head + 1, :] = jnp.sum(part, axis=0, keepdims=True)
            sums = sums + jnp.where(lane == head, jnp.sum(part * step_row, axis=1, keepdims=True), 0.0)
        dx_pair = dot_tn(jnp.concatenate(mixing, axis=0), halves)
        dxc_o[:, lanes] = (dx_pair + par[7:8, lanes] * dy_pair.astype(F32)).astype(BF16)
    grad_low = grad_gram.astype(BF16)
    dq = (expand(enter_weights(place, block, cums), spread) * dy[...].astype(F32)).astype(BF16)
    dcq_o[...] = dot(grad_low, bq) + dot(dq, hb[0])
    dbq_o[...] = dot_tn(grad_low, cq)
    rows_o[...] = sums
    cols_o[...] = columns[...].T
    acc[...] += dot_tn(normed[...], dz[...])

    @pl.when(block == pl.num_programs(0) - 1)
    def _():
        cut_pieces(place, dp_count, acc, parts, slice(0, inner))
        cut_pieces(place, dp_count, gwo, parts, slice(inner, 2 * inner))


def state_back_kernel(counts, heads, dp_count, packet_count, part_count, info, *refs):
    packets = refs[:packet_count]
    (
        exits, h, xc, bc, cum, pre_step, de, dxc, dcq, dbq, rows, cols, decay, v, v_tail, halo_v, halo_normed,
        normed, small_gate, par, dtp, spread,
        packed_o, back_o,
    ) = refs[packet_count : -6 - part_count]
    parts = refs[-6 - part_count : -6]
    start, factor, ext, grad_ext, acc, small_o = refs[-6:]
    step_id = pl.program_id(0)
    block = pl.num_programs(0) - 1 - step_id
    place = Place(info, counts)
    inner = heads * HEAD
    channels = inner + 2 * LANES

    @pl.when(step_id == 0)
    def _():
        start[...] = merge_packets([packet[...] for packet in packets], inner)
        factor[...] = jnp.ones_like(factor)
        acc[...] = jnp.zeros_like(acc)
        grad_ext[...] = jnp.zeros_like(grad_ext)
        small_o[...] = jnp.zeros_like(small_o)

    here = decay[0, 0:1, :]
    before = factor[0:1, :]
    grad_state = exits[0] + head_column(before, inner) * start[...]
    factor[...] = jnp.broadcast_to(before * here, factor.shape)
    shape = (inner, LANES)
    overlap = jnp.sum(grad_state * h[0], axis=1, keepdims=True)
    grad_decay = jnp.sum(
        jnp.where(iota(shape, 0) // HEAD == iota(shape, 1), overlap, 0.0), axis=0, keepdims=True
    )
    low = grad_state.astype(BF16)
    bq = bc[:, :LANES]
    cums = cum[...]
    x_float = xc[...].astype(F32)
    pre_dt = pre_step[...]
    valid = place.valid(block)
    step = step_sizes(place, block, pre_dt, heads)
    end_kernel = end_weights(place, block, cums)
    end_weight = end_kernel * step
    end_wide = expand(end_weight, spread)
    spread_b = dot_nt(bq, low)
    grad_x = dxc[...].astype(F32) + end_wide * spread_b
    grad_end = reduce_heads(x_float * spread_b, spread)
    grad_b = dbq[...] + dot((x_float * end_wide).astype(BF16), low)
    end_part = grad_end * end_weight
    last = iota((BLOCK, LANES), 0) == BLOCK - 1
    grad_cum = rows[...] - cols[...] * step - end_part + de[...] * enter_weights(place, block, cums)
    grad_cum = grad_cum + jnp.where(
        last, jnp.sum(end_part, axis=0, keepdims=True) + grad_decay * here, 0.0
    )
    upper = (iota((BLOCK, BLOCK), 0) <= iota((BLOCK, BLOCK), 1)).astype(F32)
    grad_log = dot_exact(upper, grad_cum)
    rates = dtp[1:2, :]
    grad_step = cols[...] + grad_end * end_kernel - rates * grad_log
    heads_lane = iota((BLOCK, LANES), 1) < heads
    grad_pre_dt = jnp.where(heads_lane, grad_step * sigmoid(pre_dt), 0.0) * valid
    small_o[6:7, :LANES] += jnp.sum(grad_pre_dt, axis=0, keepdims=True)
    small_o[7:8, :LANES] += jnp.sum(grad_log * (-rates * step), axis=0, keepdims=True)

    ext[8 : 8 + BLOCK, :] = v[...].astype(F32)

    @pl.when(block == 0)
    def _():
        ext[0:8, :] = halo_v[...]

    @pl.when(block > 0)
    def _():
        ext[0:8, :] = v_tail[...].astype(F32)[8:16, :]

    pre = conv_pre(place, block, ext, par, channels)
    sig = gate_sigmoid(pre)
    slope = sig * (1.0 + pre * (1.0 - sig))
    grad_pre = jnp.concatenate([grad_x, grad_b, dcq[...]], axis=1) * slope
    small_o[4:5, :] += jnp.sum(grad_pre, axis=0, keepdims=True)
    carry = grad_ext[0:8, :]
    grad_ext[0:BLOCK, :] = jnp.zeros((BLOCK, channels), F32)
    grad_ext[BLOCK : BLOCK + 8, :] = carry
    for tap in range(CONV):
        first = 8 - (CONV - 1) + tap
        masked = grad_pre * same_mask(place, block, tap)
        small_o[tap : tap + 1, :] += jnp.sum(masked * ext[first : first + BLOCK, :], axis=0, keepdims=True)
        grad_ext[first : first + BLOCK, :] += par[tap : tap + 1, :channels] * masked
    packed = jnp.concatenate([grad_ext[8 : 8 + BLOCK, :].astype(BF16), grad_pre_dt.astype(BF16)], axis=1)
    packed_o[...] = packed
    acc[...] += dot_tn(normed[...], packed)

    @pl.when(block == 0)
    def _():
        back = jnp.concatenate([jnp.zeros((8, channels), F32), grad_ext[0:8, :]], axis=0).astype(BF16)
        back_o[...] = back
        acc[:, :channels] += dot_tn(halo_normed[...], back)
        skip = reduce_heads(jnp.broadcast_to(small_gate[1:2, :], (8, inner)), spread)[0:1, :]
        acc[:, channels:] += pack_parameters(dp_count, heads, small_o, small_gate[0:1, :], skip)
        cut_pieces(place, dp_count, acc, parts, slice(0, channels + LANES))


def input_back_kernel(
    counts, dp_count, part_count, info, packed, back, dz, wz, tok, halo, w1, par,
    dn_o, dnh_o, norm_o, total,
):
    block = pl.program_id(0)
    place = Place(info, counts)
    width = tok.shape[1]
    channels = back.shape[1]
    gain = par[5:6, :width]

    @pl.when(block == 0)
    def _():
        halo_grad = dot_nt(back[...], w1[:, :channels])
        dnh_o[...] = halo_grad[8:16, :]
        halo_scaled, _, _ = normalise(halo[...].astype(F32), gain)
        total[...] = jnp.broadcast_to(
            jnp.sum(halo_grad * halo_scaled, axis=0, keepdims=True), total.shape
        )

    partial = dot_nt(dz[...], wz[...]) + dot_nt(packed[...], w1[...])
    dn_o[...] = partial.astype(BF16)
    scaled, _, _ = normalise(tok[...].astype(F32), gain)
    total[0:1, :] += jnp.sum(partial * scaled, axis=0, keepdims=True)

    @pl.when(block == pl.num_programs(0) - 1)
    def _():
        rows = norm_o.shape[0] // dp_count
        norm_o[...] = pack_norm(place, dp_count, part_count, total[0:1, :], rows)


def finish_kernel(counts, info, own, other, halo_a, halo_b, keep, received, tok, cot, par, grad_o, out_o):
    block = pl.program_id(0)
    place = Place(info, counts)
    width = tok.shape[1]
    grad = own[...].astype(F32) + other[...].astype(F32)
    is_last = jnp.where((block + 1) * BLOCK == place.fill, 1.0, 0.0)
    halo = (halo_a[...] + halo_b[...]) * is_last
    grad = jnp.concatenate([grad[: BLOCK - 8, :], grad[BLOCK - 8 :, :] + halo], axis=0)
    inputs = tok[...].astype(F32)
    inv = lax.rsqrt(jnp.mean(inputs * inputs, axis=1, keepdims=True) + EPS)
    scaled = par[5:6, :width] * grad
    inner_dot = jnp.sum(scaled * inputs, axis=1, keepdims=True)
    half = width // 2
    branch = (keep[...].astype(F32) + received[...].astype(F32)) * place.valid(block)
    out_o[...] = jnp.where(place.tp == 0, inputs[:, :half], inputs[:, half:]) + branch
    grad_o[...] = (
        inv * scaled - inputs * (inv * inv * inv) * (inner_dot / width) + cot[...].astype(F32)
    )


def unpack_gate_kernel(counts, part_count, info, *refs):
    whole, wz_o, wo_o = refs
    place = Place(info, counts)
    shard, inner = wz_o.shape
    rows = shard // part_count
    for part in range(part_count):
        first = pl.multiple_of(xor(place.ctx, part) * rows, rows) if part_count > 1 else 0
        lines = slice(part * rows, (part + 1) * rows)
        wz_o[pl.ds(first, rows), :] = whole[lines, :inner].astype(F32)
        wo_o[pl.ds(first, rows), :] = whole[lines, inner:].astype(F32)


def unpack_input_kernel(counts, heads, part_count, info, *refs):
    parts = refs[:part_count]
    (
        wx_o, wbc_o, wdt_o, norm_o, taps_o, bias_o, state_taps_o, state_bias_o, dt_bias_o, a_log_o, skip_o,
        gate_o, wide,
    ) = refs[part_count:]
    place = Place(info, counts)
    shard, inner = wx_o.shape
    channels = inner + 2 * LANES
    rows = shard // part_count
    for part in range(part_count):
        first = pl.multiple_of(xor(place.ctx, part) * rows, rows) if part_count > 1 else 0
        wide[pl.ds(first, rows), :] = parts[part][...].astype(F32)
    wx_o[...] = wide[:shard, :inner]
    wbc_o[...] = wide[:shard, inner:channels]
    lines = wide[:, channels:].T
    wdt_o[...] = lines[:heads, :shard]
    each = gate_o.shape[1]
    size = lines.shape[1]
    source = iota((16, size), 1)
    inside = (source // each == iota((16, size), 0)) & (source < shard)
    place_in = (iota((size, LANES), 0) % each == iota((size, LANES), 1)).astype(BF16)

    def by_head(line):
        row = jnp.where(inside, lines[line : line + 1, :], 0.0).astype(BF16)
        return dot(row, place_in)[:heads, :each]

    for tap in range(CONV):
        taps_o[:, tap, :] = by_head(TAPS + tap)
    bias_o[...] = by_head(TAPS + CONV)
    gate_o[...] = by_head(GATE)
    gain = wide[:rows, channels:]
    for part in range(1, part_count):
        gain = gain + wide[part * rows : (part + 1) * rows, channels:]
    gain = jnp.concatenate([gain, jnp.zeros((LANES - rows, LANES), F32)], axis=0).T
    source, target = iota((LANES, size), 0), iota((LANES, size), 1)
    total = jnp.zeros((8, size), F32)
    for lane in range(shard // rows):
        pick = ((target == lane * rows + source) & (source < rows)).astype(F32)
        total = total + dot_exact(jnp.broadcast_to(gain[NORM + lane : NORM + lane + 1, :], (8, LANES)), pick)
    norm_o[...] = total[0:1, :shard]
    states = state_bias_o.shape[1]
    state_taps_o[...] = lines[STATE_TAPS : STATE_TAPS + CONV, :states]
    state_bias_o[...] = lines[STATE_TAPS + CONV : STATE_TAPS + CONV + 1, :states]
    row = lines[BY_HEAD : BY_HEAD + 1, :]
    dt_bias_o[...] = row[:, :heads]
    a_log_o[...] = row[:, heads : 2 * heads]
    skip_o[...] = row[:, 2 * heads : 3 * heads]


def call(body, steps, info, operands, outputs, scratch=(), reverse=False, micros=1, mega=20):
    def at(index):
        return steps - 1 - index if reverse else index

    def spec(shape, kind):
        if kind == "rows":
            return pl.BlockSpec((BLOCK,) + tuple(shape[1:]), lambda i: (at(i), 0))
        if kind == "block":
            return pl.BlockSpec((1,) + tuple(shape[1:]), lambda i: (at(i), 0, 0))
        if kind == "lanes":
            return pl.BlockSpec((shape[0], BLOCK), lambda i: (0, at(i)))
        if kind == "tail":
            each = BLOCK // 16
            return pl.BlockSpec((16, shape[1]), lambda i: (jnp.maximum(at(i) * each - 1, 0), 0))
        if kind == "whole":
            return pl.BlockSpec(tuple(shape), lambda i: (0,) * len(shape))
        if kind == "once":
            return pl.BlockSpec(tuple(shape), lambda i: (0,) * len(shape), pipeline_mode=pl.Buffered(1))
        return kind

    return pl.pallas_call(
        body,
        grid=(steps,),
        in_specs=[pl.BlockSpec(memory_space=pltpu.SMEM)]
        + [spec(array.shape, "once" if kind == "whole" else kind) for array, kind in operands],
        out_specs=[spec(shape.shape, kind) for shape, kind in outputs],
        out_shape=[shape for shape, _ in outputs],
        scratch_shapes=list(scratch),
        compiler_params=pltpu.CompilerParams(
            dimension_semantics=("arbitrary",), vmem_limit_bytes=mega * MEGA
        ),
        cost_estimate=pl.CostEstimate(
            flops=micros * 1_100_000_000, bytes_accessed=micros * 3_500_000, transcendentals=0
        ),
    )(info, *[array for array, _ in operands])


def shifted(value, axis, steps):
    count = lax.axis_size(axis)
    first, last = max(0, -steps), min(count, count - steps)
    return lax.ppermute(value, axis, [(source, source + steps) for source in range(first, last)])


def swapped(value):
    return lax.ppermute(value, "tp", [(0, 1), (1, 0)])


def partnered(value, axis, mask):
    return lax.ppermute(value, axis, [(one, one ^ mask) for one in range(lax.axis_size(axis))])


def exchanged(value, axis):
    return [value] + [partnered(value, axis, mask) for mask in range(1, lax.axis_size(axis))]


def own_rows(value, rows):
    return lax.dynamic_slice_in_dim(value, lax.axis_index("ctx") * rows, rows, 0)


def joined_rows(values):
    return jnp.concatenate(values, axis=0)


def ctx_sum(pieces):
    total = pieces[0].astype(F32)
    for mask in range(1, len(pieces)):
        total = total + partnered(pieces[mask], "ctx", mask).astype(F32)
    return total


def dp_sum(total):
    dp_count = lax.axis_size("dp")
    rows = total.shape[0] // dp_count
    own = total[:rows].astype(F32)
    for mask in range(1, dp_count):
        block = total[mask * rows : (mask + 1) * rows].astype(BF16)
        own = own + partnered(block, "dp", mask).astype(F32)
    return own.astype(BF16)


def halved(blocks, mask):
    count, rows = blocks.shape[:2]
    sent = jnp.concatenate([blocks[block] for block in range(1, count, 2)], axis=0).astype(BF16)
    received = partnered(sent, "dp", mask).reshape(count // 2, rows, -1).astype(F32)
    return jnp.stack([blocks[block] for block in range(0, count, 2)]) + received


def doubled(value, mask):
    return jnp.concatenate([value, partnered(value, "ctx", mask)], axis=0)


def whole_sum(value):
    return lax.psum(lax.psum_scatter(value, "dp", scatter_dimension=0, tiled=True), "ctx")


def body(
    tokens, cotangent, device_fill, seq_lengths, norm_gain, w_z, w_x, w_bc, w_dt,
    conv_x, conv_x_bias, conv_bc, bias_bc, dt_bias, a_log, skip_d, gate_gain, w_out,
):
    rows, width = tokens.shape
    heads = dt_bias.shape[0]
    inner = heads * HEAD
    channels = inner + 2 * LANES
    steps = rows // BLOCK
    shard = norm_gain.shape[0]
    dp_count = lax.axis_size("dp")
    ctx_count = lax.axis_size("ctx")
    tp_index = lax.axis_index("tp")
    counts = (ctx_count, seq_lengths.shape[1])

    parts = ctx_count if shard % (16 * ctx_count) == 0 else 1
    part_rows = shard // parts

    with jax.named_scope("gather_weights"):
        vector = jnp.concatenate(
            [
                jnp.concatenate(
                    [
                        conv_x.reshape(CONV, shard),
                        conv_x_bias.reshape(1, shard),
                        norm_gain[None, :],
                        gate_gain.reshape(1, shard),
                        jnp.zeros((1, shard), BF16),
                        jnp.pad(
                            jnp.concatenate([conv_bc, bias_bc[None, :]], axis=0),
                            ((0, 3), (0, shard - bias_bc.shape[0])),
                        ),
                    ],
                    axis=0,
                ),
                jnp.pad(w_dt.T, ((0, 16 - heads), (0, 0))),
            ],
            axis=1,
        )
        input_rows = jnp.concatenate([w_x, w_bc], axis=1)
        gate_rows = jnp.concatenate([w_z, w_out.T], axis=1)
        if parts > 1:
            w1_parts = joined_rows(exchanged(own_rows(input_rows, part_rows), "dp"))
            vector = jnp.pad(vector, ((0, 0), (0, 2 * inner - 2 * shard)))
            block = jnp.concatenate([own_rows(gate_rows, part_rows), vector], axis=0)
            block, _ = lax.optimization_barrier((block, w1_parts))
            vectors = exchanged(block, "dp")
            w2_parts = exchanged(joined_rows([value[:part_rows] for value in vectors]), "ctx")
            w1_parts = exchanged(w1_parts, "ctx")
        else:
            w1_parts = [lax.all_gather(input_rows, "dp", axis=0, tiled=True)]
            w2_parts = [lax.all_gather(gate_rows, "dp", axis=0, tiled=True)]
            vectors = exchanged(vector, "dp")
    first_vector = part_rows // 16 if parts > 1 else 0
    vector_spec = pl.BlockSpec(
        (16, 2 * shard), lambda i: (first_vector, 0), pipeline_mode=pl.Buffered(1)
    )

    dtp = jnp.pad(jnp.stack([dt_bias, jnp.exp(a_log), skip_d]), ((0, 5), (0, LANES - heads)))
    shape = (2 * LANES, inner)
    spread = (iota(shape, 0) % LANES == iota(shape, 1) // HEAD).astype(BF16)
    info = jnp.concatenate(
        [
            device_fill[0],
            seq_lengths[0],
            jnp.stack([lax.axis_index("ctx"), tp_index, lax.axis_index("dp")]).astype(jnp.int32),
        ]
    )
    fill = jnp.sum(jnp.where(jnp.arange(ctx_count) == lax.axis_index("ctx"), device_fill[0], 0)) * BLOCK
    halo = shifted(lax.dynamic_slice_in_dim(tokens, fill - 16, 16, 0), "ctx", 1)

    def out(shape, dtype, kind):
        return (jax.ShapeDtypeStruct(shape, dtype), kind)

    def row_out(columns, dtype):
        return out((rows, columns), dtype, "rows")

    state_out = out((steps, inner, LANES), F32, "block")
    packet_out = out((inner + 16, LANES), BF16, "whole")

    (w1, par, normed, halo_normed, halo_v, v, xc, bc, ypart, pre_step, cum, entry, decay, packet) = call(
        functools.partial(forward_kernel, counts, heads, dp_count, parts),
        steps,
        info,
        [(value, vector_spec) for value in vectors]
        + [(value, "whole") for value in w1_parts]
        + [(tokens, "rows"), (halo, "whole"), (dtp, "whole"), (spread, "whole")],
        [
            out((width, channels + LANES), BF16, "whole"),
            out((8, channels), F32, "whole"),
            row_out(width, BF16),
            out((16, width), BF16, "whole"),
            out((8, channels), F32, "whole"),
            row_out(channels, BF16),
            row_out(inner, BF16),
            row_out(2 * LANES, BF16),
            row_out(inner, F32),
            row_out(LANES, F32),
            row_out(LANES, F32),
            state_out,
            out((steps, 8, LANES), F32, "block"),
            packet_out,
        ],
        [
            pltpu.VMEM((8 + BLOCK, channels), F32),
            pltpu.VMEM((inner, LANES), F32),
            pltpu.VMEM((8, LANES), F32),
        ],
        micros=20,
        mega=16,
    )
    packets = [(shifted(packet, "ctx", step), "whole") for step in range(1, ctx_count)]
    wz_spec = pl.BlockSpec((width, inner), lambda i: (0, 0), pipeline_mode=pl.Buffered(1))
    wo_spec = pl.BlockSpec((width, inner), lambda i: (0, 1), pipeline_mode=pl.Buffered(1))
    w2, z, dn = call(
        functools.partial(gate_matmul_kernel, counts, dp_count, parts),
        steps,
        info,
        [(value, "whole") for value in w2_parts] + [(normed, "rows"), (cotangent, "rows")],
        [out((width, 2 * inner), BF16, "whole"), row_out(inner, BF16), row_out(inner, BF16)],
        micros=7,
        mega=12,
    )
    y, hb, h, stat = call(
        functools.partial(apply_kernel, counts, len(packets)),
        steps,
        info,
        packets
        + [
            (entry, "block"),
            (decay, "block"),
            (cum, "rows"),
            (bc, "rows"),
            (ypart, "rows"),
            (z, "rows"),
            (dn, "rows"),
            (par, "whole"),
            (spread, "whole"),
        ],
        [
            row_out(inner, F32),
            out((steps, inner, LANES), BF16, "block"),
            state_out,
            out((8, rows), F32, "lanes"),
        ],
        [pltpu.VMEM((inner, LANES), F32)],
        micros=8,
        mega=12,
    )
    other_stat = swapped(stat)
    inner_all = inner * lax.axis_size("tp")
    half = width // 2
    keep, send, gwo, small_gate, dy, dz, de, exits, packet = call(
        functools.partial(gate_back_kernel, counts, inner_all),
        steps,
        info,
        [
            (stat, "lanes"),
            (other_stat, "lanes"),
            (y, "rows"),
            (z, "rows"),
            (dn, "rows"),
            (cotangent, "rows"),
            (cum, "rows"),
            (bc, "rows"),
            (xc, "rows"),
            (hb, "block"),
            (decay, "block"),
            (w2, wo_spec),
            (par, "whole"),
            (spread, "whole"),
        ],
        [
            row_out(half, BF16),
            row_out(half, BF16),
            out((width, inner), BF16, "whole"),
            out((8, inner), F32, "whole"),
            row_out(inner, BF16),
            row_out(inner, BF16),
            row_out(LANES, F32),
            state_out,
            packet_out,
        ],
        [
            pltpu.VMEM((width, inner), F32),
            pltpu.VMEM((inner, LANES), F32),
            pltpu.VMEM((8, LANES), F32),
        ],
        reverse=True,
        micros=15,
        mega=14,
    )
    packets = [(shifted(packet, "ctx", -step), "whole") for step in range(1, ctx_count)]
    received = swapped(send)
    dxc, dcq, dbq, row_sums, col_sums, *g2 = call(
        functools.partial(intra_back_kernel, counts, heads, dp_count),
        steps,
        info,
        [
            (dy, "rows"),
            (dz, "rows"),
            (xc, "rows"),
            (bc, "rows"),
            (cum, "rows"),
            (pre_step, "rows"),
            (hb, "block"),
            (normed, "rows"),
            (gwo, "whole"),
            (par, "whole"),
            (spread, "whole"),
        ],
        [
            row_out(inner, BF16),
            row_out(LANES, F32),
            row_out(LANES, F32),
            row_out(LANES, F32),
            row_out(LANES, F32),
        ]
        + [out((width // parts, 2 * inner), BF16, "whole")] * parts,
        [pltpu.VMEM((width, inner), F32), pltpu.VMEM((LANES, BLOCK), F32)],
        micros=18,
        mega=14,
    )
    with jax.named_scope("reduce_gate_weights"):
        total2 = ctx_sum(g2) if parts > 1 else g2[0]
    packed, back, *g1 = call(
        functools.partial(state_back_kernel, counts, heads, dp_count, len(packets), parts),
        steps,
        info,
        packets
        + [
            (exits, "block"),
            (h, "block"),
            (xc, "rows"),
            (bc, "rows"),
            (cum, "rows"),
            (pre_step, "rows"),
            (de, "rows"),
            (dxc, "rows"),
            (dcq, "rows"),
            (dbq, "rows"),
            (row_sums, "rows"),
            (col_sums, "rows"),
            (decay, "block"),
            (v, "rows"),
            (v, "tail"),
            (halo_v, "whole"),
            (halo_normed, "whole"),
            (normed, "rows"),
            (small_gate, "whole"),
            (par, "whole"),
            (dtp, "whole"),
            (spread, "whole"),
        ],
        [row_out(channels + LANES, BF16), out((16, channels), BF16, "whole")]
        + [out((width // parts, channels + LANES), BF16, "whole")] * parts,
        [
            pltpu.VMEM((inner, LANES), F32),
            pltpu.VMEM((8, LANES), F32),
            pltpu.VMEM((8 + BLOCK, channels), F32),
            pltpu.VMEM((8 + BLOCK, channels), F32),
            pltpu.VMEM((width, channels + LANES), F32),
            pltpu.VMEM((8, channels), F32),
        ],
        reverse=True,
        micros=25,
        mega=20,
    )
    with jax.named_scope("reduce_gate_weights"):
        if parts > 1:
            total2 = total2.reshape(dp_count, part_rows, 2 * inner)
            total2 = halved(total2, 1) if dp_count > 1 else total2
        else:
            total2 = whole_sum(total2)
    norm_rows = part_rows * dp_count
    if parts > 1:
        g1 = [g1[0]] + [partnered(g1[mask], "ctx", mask) for mask in range(1, parts)]
        packed, g1[1], total2 = lax.optimization_barrier((packed, g1[1], total2))
        mask = 2
        while mask < dp_count:
            total2 = halved(total2, mask)
            mask *= 2
        total2 = total2[0].astype(BF16)
    partial, halo_grad, norm_part = call(
        functools.partial(input_back_kernel, counts, dp_count, parts),
        steps,
        info,
        [
            (packed, "rows"),
            (back, "whole"),
            (dz, "rows"),
            (w2, wz_spec),
            (tokens, "rows"),
            (halo, "whole"),
            (w1, "whole"),
            (par, "whole"),
        ],
        [
            row_out(width, BF16),
            out((8, width), F32, "whole"),
            out((norm_rows, LANES), F32, "whole"),
        ],
        [pltpu.VMEM((8, width), F32)],
        micros=5,
        mega=12,
    )
    other = swapped(partial)
    size = ctx_count * 2
    back = [(s, s - 2) for s in range(2, size)]
    cross = [(s, (s - 2) ^ 1) for s in range(2, size)]
    halo_a = lax.ppermute(halo_grad, ("ctx", "tp"), back)
    halo_b = lax.ppermute(halo_grad, ("ctx", "tp"), cross)
    with jax.named_scope("reduce_input_weights"):
        norm_part = jnp.pad(norm_part, ((0, 0), (channels, 0)))
        if parts > 1:
            total1 = sum(piece.astype(F32) for piece in g1) + norm_part
            total1, total2 = lax.optimization_barrier((total1, total2))
            total1 = dp_sum(total1)
            total2 = doubled(total2, 1)
            total1, total2 = lax.optimization_barrier((total1, total2))
            mask = 2
            while mask < ctx_count:
                total2 = doubled(total2, mask)
                mask *= 2
        else:
            total1 = whole_sum((g1[0].astype(F32) + norm_part).astype(BF16))
        across = swapped(total1[:, inner:])
        lane = np.arange(3 * LANES) - 2 * LANES
        both = (lane < 0) | ((lane >= STATE_TAPS) & (lane < BY_HEAD))
        both = both | ((lane >= NORM) & (lane < NORM + shard // part_rows))
        summed = total1[:, inner:] + jnp.where(both[None, :], across, 0)
        total1 = jnp.concatenate([total1[:, :inner], summed], axis=1)
    grad_tokens, layer_out = call(
        functools.partial(finish_kernel, counts),
        steps,
        info,
        [
            (partial, "rows"),
            (other, "rows"),
            (halo_a, "whole"),
            (halo_b, "whole"),
            (keep, "rows"),
            (received, "rows"),
            (tokens, "rows"),
            (cotangent, "rows"),
            (par, "whole"),
        ],
        [row_out(width, F32), row_out(half, F32)],
        micros=5,
        mega=10,
    )
    with jax.named_scope("last_hop"):
        if parts > 1:
            total1 = exchanged(total1, "ctx")
            total1[-1], grad_tokens = lax.optimization_barrier((total1[-1], grad_tokens))
        else:
            total1 = [total1]
    each = HEAD // dp_count
    part_bc = bias_bc.shape[0]
    tall = -(-shard // LANES) * LANES

    def final(*sizes):
        return out(sizes, F32, "whole")

    grad_wz, grad_wo = call(
        functools.partial(unpack_gate_kernel, counts, parts),
        1,
        info,
        [(total2, "whole")],
        [final(shard, inner), final(shard, inner)],
        micros=2,
        mega=8,
    )
    (
        grad_wx, grad_wbc, grad_wdt, grad_norm, grad_taps, grad_bias, grad_state_taps, grad_state_bias,
        grad_dt_bias, grad_a_log, grad_skip, grad_gate,
    ) = call(
        functools.partial(unpack_input_kernel, counts, heads, parts),
        1,
        info,
        [(value, "whole") for value in total1],
        [
            final(shard, inner),
            final(shard, 2 * LANES),
            final(heads, shard),
            final(1, shard),
            final(heads, CONV, each),
            final(heads, each),
            final(CONV, part_bc),
            final(1, part_bc),
            final(1, heads),
            final(1, heads),
            final(1, heads),
            final(heads, each),
        ],
        [pltpu.VMEM((tall, channels + LANES), F32)],
        micros=2,
        mega=8,
    )
    return (
        layer_out,
        grad_tokens,
        grad_norm[0],
        grad_wz,
        grad_wx,
        grad_wbc,
        grad_wdt.T,
        grad_taps.transpose(1, 0, 2),
        grad_bias,
        grad_state_taps,
        grad_state_bias[0],
        grad_dt_bias[0],
        grad_a_log[0],
        grad_skip[0],
        grad_gate,
        grad_wo.T,
    )


def solution(mesh):
    shards = P(("dp", "ctx"), None)
    return jax.shard_map(
        body,
        mesh=mesh,
        in_specs=(
            shards,
            shards,
            P("dp", None),
            P("dp", None),
            P("dp"),
            P("dp", "tp"),
            P("dp", "tp"),
            P("dp", None),
            P("dp", "tp"),
            P(None, "tp", "dp"),
            P("tp", "dp"),
            P(None, "dp"),
            P("dp"),
            P("tp"),
            P("tp"),
            P("tp"),
            P("tp", "dp"),
            P("tp", "dp"),
        ),
        out_specs=(
            P(("dp", "ctx"), "tp"),
            shards,
            P("dp"),
            P("dp", "tp"),
            P("dp", "tp"),
            P("dp", None),
            P("dp", "tp"),
            P(None, "tp", "dp"),
            P("tp", "dp"),
            P(None, "dp"),
            P("dp"),
            P("tp"),
            P("tp"),
            P("tp"),
            P("tp", "dp"),
            P("tp", "dp"),
        ),
        check_vma=False,
    )
```

```python
import functools

import jax
import jax.numpy as jnp
import numpy as np
from jax import lax
from jax.experimental import pallas as pl
from jax.experimental.pallas import tpu as pltpu
from jax.sharding import PartitionSpec as P

CONV = 4
BLOCK = 256
HEAD = 64
LANES = 128
EPS = 1e-05
MEGA = 1024 * 1024
F32 = jnp.float32
BF16 = jnp.bfloat16


def dot(left, right):
    return jnp.dot(left, right, preferred_element_type=F32)


def dot_tn(left, right):
    return lax.dot_general(left, right, (((0,), (0,)), ((), ())), preferred_element_type=F32)


def dot_nt(left, right):
    return lax.dot_general(left, right, (((1,), (1,)), ((), ())), preferred_element_type=F32)


def dot_exact(left, right):
    return jnp.dot(left, right, preferred_element_type=F32, precision=lax.Precision.HIGHEST)


def iota(shape, dim):
    return lax.broadcasted_iota(jnp.int32, shape, dim)


def sigmoid(value):
    return 1.0 / (1.0 + jnp.exp(-value))


def gate_sigmoid(value):
    return 0.5 * jnp.tanh(0.5 * value) + 0.5


def softplus(value):
    return jnp.maximum(value, 0.0) + jnp.log1p(jnp.exp(-jnp.abs(value)))


def split(value):
    high = value.astype(BF16)
    return high, (value - high.astype(F32)).astype(BF16)


def expand(value, spread):
    return dot(jnp.concatenate(split(value), axis=1), spread[...])


def reduce_heads(value, spread):
    high, low = split(value)
    pick = spread[:LANES, :]
    return dot_nt(high, pick) + dot_nt(low, pick)


def head_column(row, channels):
    shape = (channels, LANES)
    return jnp.sum(jnp.where(iota(shape, 0) // HEAD == iota(shape, 1), row, 0.0), axis=1, keepdims=True)


def xor(value, mask):
    return jnp.bitwise_xor(value, jnp.int32(mask))


class Place:
    def __init__(self, info, counts):
        devices, sequences = counts
        own = info[devices + sequences]
        self.ctx = own
        self.tp = info[devices + sequences + 1]
        self.dp = info[devices + sequences + 2]
        self.fill = jnp.int32(0)
        self.first = jnp.int32(0)
        for device in range(devices):
            rows = info[device] * BLOCK
            self.fill = self.fill + jnp.where(own == device, rows, 0)
            self.first = self.first + jnp.where(own > device, rows, 0)
        self.ends = []
        total = jnp.int32(0)
        for sequence in range(sequences - 1):
            total = total + info[devices + sequence]
            self.ends.append(total)

    def of(self, position):
        found = (position >= self.ends[0]).astype(jnp.int32)
        for end in self.ends[1:]:
            found = found + (position >= end).astype(jnp.int32)
        return jnp.where(position < 0, -1, found)

    def rows(self, index):
        return self.of(self.first + jnp.minimum(index, self.fill - 1))

    def before(self, block):
        position = self.first + jnp.minimum(block * BLOCK, self.fill) - 1
        found = jnp.int32(0)
        for end in self.ends:
            found = found + jnp.where(position >= end, 1, 0)
        return jnp.where(position < 0, -1, found)

    def last(self, block):
        position = self.first + jnp.minimum(block * BLOCK + BLOCK - 1, self.fill - 1)
        found = jnp.int32(0)
        for end in self.ends:
            found = found + jnp.where(position >= end, 1, 0)
        return found

    def column(self, block, shift=0):
        return self.rows(block * BLOCK + shift + iota((BLOCK, 1), 0))

    def valid(self, block):
        return (block * BLOCK + iota((BLOCK, 1), 0) < self.fill).astype(F32)

    def keep(self, block):
        across = self.rows(block * BLOCK + iota((1, BLOCK), 1))
        return (self.column(block) == across) & (iota((BLOCK, BLOCK), 0) >= iota((BLOCK, BLOCK), 1))


def step_sizes(place, block, pre_step, heads):
    lane = iota((BLOCK, LANES), 1)
    return jnp.where(lane < heads, softplus(pre_step), 0.0) * place.valid(block)


def end_weights(place, block, cum):
    same = (place.column(block) == place.last(block)).astype(F32)
    return jnp.exp(cum[BLOCK - 1 :, :] - cum) * same


def enter_weights(place, block, cum):
    return jnp.exp(cum) * (place.column(block) == place.before(block)).astype(F32)


def block_decay(place, block, cum):
    return jnp.exp(cum[BLOCK - 1 :, :]) * jnp.where(place.last(block) == place.before(block), 1.0, 0.0)


def decay_kernel(keep, cum, cum_rows, head):
    return jnp.exp(jnp.where(keep, cum[:, head : head + 1] - cum_rows[head : head + 1, :], -1e30))


TILES = ((0, 0), (LANES, 0), (LANES, LANES))


def tile_slices(tile):
    return slice(tile[0], tile[0] + LANES), slice(tile[1], tile[1] + LANES)


def decay_tile(neg, cum, cum_rows, head, tile):
    rows, columns = tile_slices(tile)
    diff = cum[rows, head : head + 1] - cum_rows[head : head + 1, columns]
    return jnp.exp(diff + neg[rows, columns])


def both_halves(pair):
    lane = iota(pair.shape, 1)
    zero = jnp.zeros_like(pair)
    return [jnp.where(lane < HEAD, pair, zero), jnp.where(lane >= HEAD, pair, zero)]


def same_mask(place, block, tap):
    return (place.column(block, tap - (CONV - 1)) == place.column(block)).astype(F32)


def conv_pre(place, block, ext, par, channels):
    total = par[4:5, :channels]
    for tap in range(CONV):
        first = 8 - (CONV - 1) + tap
        total = total + par[tap : tap + 1, :channels] * ext[first : first + BLOCK, :] * same_mask(
            place, block, tap
        )
    return total


def state_packet(state, decay):
    high, low = split(decay)
    row = iota((16, LANES), 0)
    tail = jnp.where(row == 0, high.astype(F32), jnp.where(row == 1, low.astype(F32), 0.0))
    return jnp.concatenate([state.astype(BF16), tail.astype(BF16)], axis=0)


def merge_packets(packets, inner):
    total = jnp.zeros((inner, LANES), F32)
    for packet in reversed(packets):
        tail = packet[inner : inner + 16, :].astype(F32)
        decay = tail[0:1, :] + tail[1:2, :]
        total = packet[:inner, :].astype(F32) + head_column(decay, inner) * total
    return total


def normalise(rows, gain):
    inv = lax.rsqrt(jnp.mean(rows * rows, axis=1, keepdims=True) + EPS)
    return rows * inv, inv, (rows * inv * gain).astype(BF16)


def piece_rows(place, dp_count, parts, rows):
    for part in range(parts):
        for block in range(dp_count):
            owner = xor(place.dp, block) * parts + (xor(place.ctx, part) if parts > 1 else 0)
            yield part, block, pl.multiple_of(owner * rows, rows)


def join_pieces(place, dp_count, parts, whole):
    columns = parts[0].shape[1]
    if len(parts) == 1:
        whole[:, :columns] = parts[0][...]
        return
    rows = parts[0].shape[0] // dp_count
    for part, block, first in piece_rows(place, dp_count, len(parts), rows):
        whole[pl.ds(first, rows), :columns] = parts[part][block * rows : (block + 1) * rows, :]


def cut_pieces(place, dp_count, whole, parts, lanes):
    if len(parts) == 1:
        parts[0][:, lanes] = whole[...].astype(BF16)
        return
    rows = parts[0].shape[0] // dp_count
    for part, block, first in piece_rows(place, dp_count, len(parts), rows):
        parts[part][block * rows : (block + 1) * rows, lanes] = whole[pl.ds(first, rows), :].astype(BF16)


def join_parameters(place, vectors, skip, heads, par, w1):
    shard = vectors[0].shape[1] // 2
    each = HEAD // len(vectors)
    inner = heads * HEAD
    by_channel = jnp.zeros((16, inner), F32)
    in_order = jnp.zeros((16, shard * len(vectors)), F32)
    by_state = jnp.zeros((16, 2 * LANES), F32)
    states = 2 * LANES // len(vectors)
    eye = (iota((16, LANES), 0) == iota((16, LANES), 1)).astype(BF16)
    for block, vector in enumerate(vectors):
        owner = xor(place.dp, block)
        first = pl.multiple_of(owner * shard, shard)
        w1[pl.ds(first, shard), inner + 2 * LANES :] = dot_tn(vector[:, shard:], eye).astype(BF16)
        source, target = iota((shard, inner), 0), iota((shard, inner), 1)
        pick = target == source // each * HEAD + owner * each + source % each
        by_channel = by_channel + dot(vector[:, :shard], pick.astype(BF16))
        source, target = iota((shard, in_order.shape[1]), 0), iota((shard, in_order.shape[1]), 1)
        in_order = in_order + dot(vector[:, :shard], (target == owner * shard + source).astype(BF16))
        source, target = iota((shard, 2 * LANES), 0), iota((shard, 2 * LANES), 1)
        pick = (target == owner * states + source) & (source < states)
        by_state = by_state + dot(vector[:, :shard], pick.astype(BF16))
    par[...] = jnp.zeros_like(par)
    par[0:5, :inner] = by_channel[0:5, :]
    par[0:5, inner:] = by_state[8:13, :]
    par[5:6, : in_order.shape[1]] = in_order[5:6, :]
    par[6:7, :inner] = by_channel[6:7, :]
    par[7:8, :inner] = skip


TAPS, GATE, STATE_TAPS, BY_HEAD, NORM = 12, 18, 20, 25, 26


def lanes(pieces, columns):
    rows, at = [], 0
    for first, value in pieces:
        if first > at:
            rows.append(jnp.zeros((first - at, columns), F32))
        rows.append(value)
        at = first + value.shape[0]
    rows.append(jnp.zeros((LANES - at, columns), F32))
    return jnp.concatenate(rows, axis=0)


def pack_norm(place, dp_count, part_count, row, rows):
    columns = row.shape[1]
    shard = columns // dp_count
    size = shard // rows
    total = jnp.zeros((dp_count * rows, LANES), F32)
    source, target = iota((dp_count * rows, columns), 0), iota((dp_count * rows, columns), 1)
    owner = source // rows
    if part_count > 1:
        owner = jnp.bitwise_xor(owner, place.dp)
    for lane in range(size):
        pick = target == owner * shard + lane * rows + source % rows
        total = total + dot_nt(pick.astype(BF16), lanes([(NORM + lane, row)], columns).astype(BF16))
    return total


def pack_parameters(dp_count, heads, small, gate, skip):
    inner = heads * HEAD
    each = HEAD // dp_count
    shard = inner // dp_count
    states = 2 * LANES // dp_count

    source, target = iota((inner, inner), 0), iota((inner, inner), 1)
    inside = source % shard
    pick = target == inside // each * HEAD + source // shard * each + inside % each
    by_channel = lanes([(TAPS, small[0:5, :inner]), (GATE, gate)], inner)
    total = dot_nt(pick.astype(BF16), by_channel.astype(BF16))
    source, target = iota((inner, 2 * LANES), 0), iota((inner, 2 * LANES), 1)
    inside = source % shard
    pick = (target == source // shard * states + inside) & (inside < states)
    by_state = lanes([(STATE_TAPS, small[0:5, inner : inner + 2 * LANES])], 2 * LANES)
    total = total + dot_nt(pick.astype(BF16), by_state.astype(BF16))
    source, target = iota((inner, LANES), 0) % shard, iota((inner, LANES), 1)
    for index, row in enumerate((small[6:7, :LANES], small[7:8, :LANES], skip)):
        pick = (source == target + index * heads) & (target < heads)
        total = total + dot_nt(pick.astype(BF16), lanes([(BY_HEAD, row)], LANES).astype(BF16))
    return total


def forward_kernel(
    counts, heads, dp_count, part_count, info, *refs
):
    vectors = refs[:dp_count]
    parts = refs[dp_count : dp_count + part_count]
    (
        tok, halo, dtp, spread,
        w1, par, normed_o, halo_normed_o, halo_v_o, v_o, xc_o, bc_o, ypart_o, pre_o, cum_o, entry_o, decay_o,
        packet_o, ext, run, factor, gram, neg, mix,
    ) = refs[dp_count + part_count :]
    forward_block(
        counts, heads, info, vectors, parts, tok, halo, w1, par, dtp, spread,
        normed_o, halo_normed_o, halo_v_o, v_o, xc_o, bc_o, ypart_o, pre_o, cum_o, entry_o, decay_o, packet_o,
        ext, run, factor, gram, neg, mix,
    )


def forward_block(
    counts, heads, info, vectors, parts, tok, halo, w1, par, dtp, spread,
    normed_o, halo_normed_o, halo_v_o, v_o, xc_o, bc_o, ypart_o, pre_o, cum_o, entry_o, decay_o, packet_o,
    ext, run, factor, gram, neg, mix,
):
    block = pl.program_id(0)
    place = Place(info, counts)
    inner = heads * HEAD
    state = LANES
    channels = inner + 2 * state
    width = tok.shape[1]

    @pl.when(block == 0)
    def _():
        join_pieces(place, len(vectors), parts, w1)
        join_parameters(place, vectors, expand(dtp[...], spread)[2:3, :], heads, par, w1)

    gain = par[5:6, :width]
    _, _, normed = normalise(tok[...].astype(F32), gain)
    normed_o[...] = normed

    @pl.when(block == 0)
    def _():
        _, _, before = normalise(halo[...].astype(F32), gain)
        halo_normed_o[...] = before
        raw = dot(before, w1[:, :channels]).astype(BF16).astype(F32)
        ext[0:8, :] = raw[8:16, :]
        halo_v_o[...] = raw[8:16, :]
        run[...] = jnp.zeros_like(run)
        factor[...] = jnp.ones_like(factor)

    @pl.when(block > 0)
    def _():
        ext[0:8, :] = ext[BLOCK : BLOCK + 8, :]

    raw = dot(normed, w1[...])
    v = raw[:, :channels].astype(BF16)
    v_o[...] = v
    ext[8 : 8 + BLOCK, :] = v.astype(F32)
    pre = conv_pre(place, block, ext, par, channels)
    act = (pre * gate_sigmoid(pre)).astype(BF16)
    xc = act[:, :inner]
    bq = act[:, inner : inner + state]
    cq = act[:, inner + state :]
    xc_o[...] = xc
    bc_o[...] = act[:, inner:]
    pre_step = raw[:, channels:].astype(BF16).astype(F32) + dtp[0:1, :]
    pre_o[...] = pre_step
    step = step_sizes(place, block, pre_step, heads)
    tri = (iota((BLOCK, BLOCK), 0) >= iota((BLOCK, BLOCK), 1)).astype(F32)
    cum = dot_exact(tri, -dtp[1:2, :] * step)
    cum_o[...] = cum
    cum_rows = cum.T
    step_rows = step.T
    gram[...] = dot_nt(cq, bq)
    neg[...] = jnp.where(place.keep(block), 0.0, -1e30)

    @pl.when(block == 0)
    def _():
        mix[...] = jnp.zeros_like(mix)

    for pair in range(heads // 2):
        lanes = slice(pair * LANES, (pair + 1) * LANES)
        slot = pair % 2
        for side in range(2):
            head = 2 * pair + side
            for tile in TILES:
                rows, columns = tile_slices(tile)
                weight = decay_tile(neg, cum, cum_rows, head, tile) * step_rows[head : head + 1, columns]
                first = side * BLOCK + columns.start
                mix[slot, rows, first : first + LANES] = (gram[rows, columns] * weight).astype(BF16)
        x_pair = xc[:, lanes]
        y_pair = dot(mix[slot], jnp.concatenate(both_halves(x_pair), axis=0))
        ypart_o[:, lanes] = y_pair + par[7:8, lanes] * x_pair.astype(F32)
    weighted = (expand(end_weights(place, block, cum) * step, spread) * xc.astype(F32)).astype(BF16)
    block_state = dot_tn(weighted, bq)
    decay = block_decay(place, block, cum)
    entry_o[0] = run[...]
    total = head_column(decay, inner) * run[...] + block_state
    run[...] = total
    before = factor[0:1, :]
    row = iota((8, LANES), 0)
    decay_o[0] = jnp.where(row == 0, decay, jnp.where(row == 1, before, 0.0))
    after = before * decay
    factor[...] = jnp.broadcast_to(after, factor.shape)

    @pl.when(block == pl.num_programs(0) - 1)
    def _():
        packet_o[...] = state_packet(total, after)


def gate_matmul_kernel(counts, dp_count, part_count, info, *refs):
    parts = refs[:part_count]
    normed, cot, w2, z_o, dn_o = refs[part_count:]
    block = pl.program_id(0)
    place = Place(info, counts)
    inner = z_o.shape[1]

    @pl.when(block == 0)
    def _():
        join_pieces(place, dp_count, parts, w2)

    z_o[...] = dot(normed[...], w2[:, :inner]).astype(BF16)
    grad = (cot[...].astype(F32) * place.valid(block)).astype(BF16)
    dn_o[...] = dot(grad, w2[:, inner:]).astype(BF16)


def apply_kernel(counts, packet_count, info, *refs):
    packets = refs[:packet_count]
    entry, decay, cum, bc, ypart, z, dn, par, spread, y_o, hb_o, h_o, stat_o, start = refs[packet_count:]
    block = pl.program_id(0)
    place = Place(info, counts)
    inner = z.shape[1]

    @pl.when(block == 0)
    def _():
        start[...] = merge_packets([packet[...] for packet in packets], inner)

    state = entry[0] + head_column(decay[0, 1:2, :], inner) * start[...]
    h_o[0] = state
    low = state.astype(BF16)
    hb_o[0] = low
    cq = bc[:, LANES:]
    y = ypart[...] + expand(enter_weights(place, block, cum[...]), spread) * dot_nt(cq, low)
    y_o[...] = y
    gate = z[...].astype(F32)
    gated = y * gate * gate_sigmoid(gate)
    squares = jnp.sum(gated * gated, axis=1, keepdims=True)
    cross = jnp.sum(par[6:7, :inner] * dn[...].astype(F32) * gated, axis=1, keepdims=True)
    lane = iota((BLOCK, LANES), 1)
    both = jnp.where(lane == 0, squares, jnp.where(lane == 1, cross, 0.0))
    stat_o[...] = both.T[0:8, :]


def gate_back_kernel(
    counts, inner_all, info, stat, other_stat, y, z, dn, cot, cum, bc, xc, hb, decay, wo, par, spread,
    keep_o, send_o, gwo_o, small_o, dy_o, dz_o, de_o, exit_o, packet_o,
    acc, run, factor,
):
    step = pl.program_id(0)
    block = pl.num_programs(0) - 1 - step
    place = Place(info, counts)
    inner = z.shape[1]
    width = cot.shape[1]
    half = width // 2

    @pl.when(step == 0)
    def _():
        acc[...] = jnp.zeros_like(acc)
        run[...] = jnp.zeros_like(run)
        factor[...] = jnp.ones_like(factor)
        small_o[...] = jnp.zeros_like(small_o)

    column = jnp.concatenate([stat[...] + other_stat[...], jnp.zeros((LANES - 8, BLOCK), F32)], axis=0).T
    inv = lax.rsqrt(column[:, 0:1] / inner_all + EPS)
    cross = column[:, 1:2]
    gain = par[6:7, :inner]
    gate = z[...].astype(F32)
    sig = gate_sigmoid(gate)
    silu = gate * sig
    mixed = y[...]
    gated = mixed * silu
    normal = (gated * inv * gain).astype(BF16)
    own = pl.multiple_of(place.tp * half, half)
    other = pl.multiple_of((1 - place.tp) * half, half)
    keep_o[...] = dot_nt(normal, wo[pl.ds(own, half), :]).astype(BF16)
    send_o[...] = dot_nt(normal, wo[pl.ds(other, half), :]).astype(BF16)
    grad = (cot[...].astype(F32) * place.valid(block)).astype(BF16)
    acc[...] += dot_tn(grad, normal)
    back = dn[...].astype(F32)
    grad_gated = inv * (gain * back) - gated * (inv * inv * inv) * (cross / inner_all)
    dy = (grad_gated * silu).astype(BF16)
    dy_o[...] = dy
    dz_o[...] = (grad_gated * mixed * sig * (1.0 + gate * (1.0 - sig))).astype(BF16)
    dy_float = dy.astype(F32)
    cq = bc[:, LANES:]
    read = dot_nt(cq, hb[0])
    de_o[...] = reduce_heads(dy_float * read, spread)
    small_o[0:1, :] += jnp.sum(back * gated * inv, axis=0, keepdims=True)
    small_o[1:2, :] += jnp.sum(dy_float * xc[...].astype(F32), axis=0, keepdims=True)
    dq = (expand(enter_weights(place, block, cum[...]), spread) * dy_float).astype(BF16)
    exit_o[0] = run[...]
    here = decay[0, 0:1, :]
    total = head_column(here, inner) * run[...] + dot_tn(dq, cq)
    run[...] = total
    after = factor[0:1, :] * here
    factor[...] = jnp.broadcast_to(after, factor.shape)

    @pl.when(step == pl.num_programs(0) - 1)
    def _():
        packet_o[...] = state_packet(total, after)
        gwo_o[...] = acc[...].astype(BF16)


def intra_back_kernel(counts, heads, dp_count, info, *refs):
    dy, dz, xc, bc, cum, pre_step, hb, normed, gwo, par, spread = refs[:11]
    dxc_o, dcq_o, dbq_o, rows_o, cols_o = refs[11:16]
    parts = refs[16:-6]
    acc, columns, neg, gram, grad_gram, mix = refs[-6:]
    block = pl.program_id(0)
    place = Place(info, counts)
    inner = heads * HEAD

    @pl.when(block == 0)
    def _():
        acc[...] = jnp.zeros_like(acc)
        mix[...] = jnp.zeros_like(mix)
        columns[...] = jnp.zeros_like(columns)

    bq = bc[:, :LANES]
    cq = bc[:, LANES:]
    cums = cum[...]
    step = step_sizes(place, block, pre_step[...], heads)
    cum_rows = cums.T
    step_rows = step.T
    gram[...] = dot_nt(cq, bq)
    neg[...] = jnp.where(place.keep(block), 0.0, -1e30)
    lane = iota((LANES, LANES), 1)
    grad_gram[...] = jnp.zeros_like(grad_gram)
    rows_o[...] = jnp.zeros_like(rows_o)
    for pair in range(heads // 2):
        lanes_here = slice(pair * LANES, (pair + 1) * LANES)
        slot = pair % 2
        dy_pair = dy[:, lanes_here]
        x_pair = xc[:, lanes_here]
        halves = jnp.concatenate(both_halves(dy_pair), axis=0)
        grad_mixing = dot_nt(halves, x_pair)
        for side in range(2):
            head = 2 * pair + side
            row_sums, column_sums = [0.0, 0.0], [0.0, 0.0]
            for tile in TILES:
                rows, across = tile_slices(tile)
                first = side * BLOCK + rows.start
                grad_m = grad_mixing[first : first + LANES, across]
                kernel = decay_tile(neg, cums, cum_rows, head, tile)
                step_row = step_rows[head : head + 1, across]
                weighted = gram[rows, across] * kernel
                mixing = weighted * step_row
                mix[slot, first : first + LANES, across] = mixing.astype(BF16)
                grad_gram[rows, across] += grad_m * (kernel * step_row)
                row, column = rows.start // LANES, across.start // LANES
                column_sums[column] = column_sums[column] + jnp.sum(grad_m * weighted, axis=0, keepdims=True)
                row_sums[row] = row_sums[row] + grad_m * mixing
            columns[head : head + 1, :] = jnp.concatenate(column_sums, axis=1)
            for row in range(2):
                total = jnp.sum(row_sums[row], axis=1, keepdims=True)
                rows_o[row * LANES : (row + 1) * LANES, :] += jnp.where(lane == head, total, 0.0)
        dx_pair = dot_tn(mix[slot], halves)
        dxc_o[:, lanes_here] = (dx_pair + par[7:8, lanes_here] * dy_pair.astype(F32)).astype(BF16)
    grad_low = grad_gram[...].astype(BF16)
    dq = (expand(enter_weights(place, block, cums), spread) * dy[...].astype(F32)).astype(BF16)
    dcq_o[...] = dot(grad_low, bq) + dot(dq, hb[0])
    dbq_o[...] = dot_tn(grad_low, cq)
    cols_o[...] = columns[...].T
    acc[...] += dot_tn(normed[...], dz[...])

    @pl.when(block == pl.num_programs(0) - 1)
    def _():
        cut_pieces(place, dp_count, acc, parts, slice(0, inner))
        cut_pieces(place, dp_count, gwo, parts, slice(inner, 2 * inner))


def state_back_kernel(counts, heads, dp_count, packet_count, part_count, info, *refs):
    packets = refs[:packet_count]
    (
        exits, h, xc, bc, cum, pre_step, de, dxc, dcq, dbq, rows, cols, decay, v, v_tail, halo_v, halo_normed,
        normed, small_gate, par, dtp, spread,
        packed_o, back_o,
    ) = refs[packet_count : -6 - part_count]
    parts = refs[-6 - part_count : -6]
    start, factor, ext, grad_ext, acc, small_o = refs[-6:]
    step_id = pl.program_id(0)
    block = pl.num_programs(0) - 1 - step_id
    place = Place(info, counts)
    inner = heads * HEAD
    channels = inner + 2 * LANES

    @pl.when(step_id == 0)
    def _():
        start[...] = merge_packets([packet[...] for packet in packets], inner)
        factor[...] = jnp.ones_like(factor)
        acc[...] = jnp.zeros_like(acc)
        grad_ext[...] = jnp.zeros_like(grad_ext)
        small_o[...] = jnp.zeros_like(small_o)

    here = decay[0, 0:1, :]
    before = factor[0:1, :]
    grad_state = exits[0] + head_column(before, inner) * start[...]
    factor[...] = jnp.broadcast_to(before * here, factor.shape)
    shape = (inner, LANES)
    overlap = jnp.sum(grad_state * h[0], axis=1, keepdims=True)
    grad_decay = jnp.sum(
        jnp.where(iota(shape, 0) // HEAD == iota(shape, 1), overlap, 0.0), axis=0, keepdims=True
    )
    low = grad_state.astype(BF16)
    bq = bc[:, :LANES]
    cums = cum[...]
    x_float = xc[...].astype(F32)
    pre_dt = pre_step[...]
    valid = place.valid(block)
    step = step_sizes(place, block, pre_dt, heads)
    end_kernel = end_weights(place, block, cums)
    end_weight = end_kernel * step
    end_wide = expand(end_weight, spread)
    spread_b = dot_nt(bq, low)
    grad_x = dxc[...].astype(F32) + end_wide * spread_b
    grad_end = reduce_heads(x_float * spread_b, spread)
    grad_b = dbq[...] + dot((x_float * end_wide).astype(BF16), low)
    end_part = grad_end * end_weight
    last = iota((BLOCK, LANES), 0) == BLOCK - 1
    grad_cum = rows[...] - cols[...] * step - end_part + de[...] * enter_weights(place, block, cums)
    grad_cum = grad_cum + jnp.where(
        last, jnp.sum(end_part, axis=0, keepdims=True) + grad_decay * here, 0.0
    )
    upper = (iota((BLOCK, BLOCK), 0) <= iota((BLOCK, BLOCK), 1)).astype(F32)
    grad_log = dot_exact(upper, grad_cum)
    rates = dtp[1:2, :]
    grad_step = cols[...] + grad_end * end_kernel - rates * grad_log
    heads_lane = iota((BLOCK, LANES), 1) < heads
    grad_pre_dt = jnp.where(heads_lane, grad_step * sigmoid(pre_dt), 0.0) * valid
    small_o[6:7, :LANES] += jnp.sum(grad_pre_dt, axis=0, keepdims=True)
    small_o[7:8, :LANES] += jnp.sum(grad_log * (-rates * step), axis=0, keepdims=True)

    ext[8 : 8 + BLOCK, :] = v[...].astype(F32)

    @pl.when(block == 0)
    def _():
        ext[0:8, :] = halo_v[...]

    @pl.when(block > 0)
    def _():
        ext[0:8, :] = v_tail[...].astype(F32)[8:16, :]

    pre = conv_pre(place, block, ext, par, channels)
    sig = gate_sigmoid(pre)
    slope = sig * (1.0 + pre * (1.0 - sig))
    grad_pre = jnp.concatenate([grad_x, grad_b, dcq[...]], axis=1) * slope
    small_o[4:5, :] += jnp.sum(grad_pre, axis=0, keepdims=True)
    carry = grad_ext[0:8, :]
    grad_ext[0:BLOCK, :] = jnp.zeros((BLOCK, channels), F32)
    grad_ext[BLOCK : BLOCK + 8, :] = carry
    for tap in range(CONV):
        first = 8 - (CONV - 1) + tap
        masked = grad_pre * same_mask(place, block, tap)
        small_o[tap : tap + 1, :] += jnp.sum(masked * ext[first : first + BLOCK, :], axis=0, keepdims=True)
        grad_ext[first : first + BLOCK, :] += par[tap : tap + 1, :channels] * masked
    packed = jnp.concatenate([grad_ext[8 : 8 + BLOCK, :].astype(BF16), grad_pre_dt.astype(BF16)], axis=1)
    packed_o[...] = packed
    acc[...] += dot_tn(normed[...], packed)

    @pl.when(block == 0)
    def _():
        back = jnp.concatenate([jnp.zeros((8, channels), F32), grad_ext[0:8, :]], axis=0).astype(BF16)
        back_o[...] = back
        acc[:, :channels] += dot_tn(halo_normed[...], back)
        skip = reduce_heads(jnp.broadcast_to(small_gate[1:2, :], (8, inner)), spread)[0:1, :]
        acc[:, channels:] += pack_parameters(dp_count, heads, small_o, small_gate[0:1, :], skip)
        cut_pieces(place, dp_count, acc, parts, slice(0, channels + LANES))


def input_back_kernel(
    counts, dp_count, part_count, info, packed, back, dz, wz, tok, halo, w1, par,
    dn_o, dnh_o, norm_o, total,
):
    block = pl.program_id(0)
    place = Place(info, counts)
    width = tok.shape[1]
    channels = back.shape[1]
    gain = par[5:6, :width]

    @pl.when(block == 0)
    def _():
        halo_grad = dot_nt(back[...], w1[:, :channels])
        dnh_o[...] = halo_grad[8:16, :]
        halo_scaled, _, _ = normalise(halo[...].astype(F32), gain)
        total[...] = jnp.broadcast_to(
            jnp.sum(halo_grad * halo_scaled, axis=0, keepdims=True), total.shape
        )

    partial = dot_nt(dz[...], wz[...]) + dot_nt(packed[...], w1[...])
    dn_o[...] = partial.astype(BF16)
    scaled, _, _ = normalise(tok[...].astype(F32), gain)
    total[0:1, :] += jnp.sum(partial * scaled, axis=0, keepdims=True)

    @pl.when(block == pl.num_programs(0) - 1)
    def _():
        rows = norm_o.shape[0] // dp_count
        norm_o[...] = pack_norm(place, dp_count, part_count, total[0:1, :], rows)


def finish_kernel(counts, info, own, other, halo_a, halo_b, keep, received, tok, cot, par, grad_o, out_o):
    block = pl.program_id(0)
    place = Place(info, counts)
    width = tok.shape[1]
    grad = own[...].astype(F32) + other[...].astype(F32)
    is_last = jnp.where((block + 1) * BLOCK == place.fill, 1.0, 0.0)
    halo = (halo_a[...] + halo_b[...]) * is_last
    grad = jnp.concatenate([grad[: BLOCK - 8, :], grad[BLOCK - 8 :, :] + halo], axis=0)
    inputs = tok[...].astype(F32)
    inv = lax.rsqrt(jnp.mean(inputs * inputs, axis=1, keepdims=True) + EPS)
    scaled = par[5:6, :width] * grad
    inner_dot = jnp.sum(scaled * inputs, axis=1, keepdims=True)
    half = width // 2
    branch = (keep[...].astype(F32) + received[...].astype(F32)) * place.valid(block)
    out_o[...] = jnp.where(place.tp == 0, inputs[:, :half], inputs[:, half:]) + branch
    grad_o[...] = (
        inv * scaled - inputs * (inv * inv * inv) * (inner_dot / width) + cot[...].astype(F32)
    )


def unpack_gate_kernel(counts, part_count, info, *refs):
    whole, wz_o, wo_o = refs
    place = Place(info, counts)
    shard, inner = wz_o.shape
    rows = shard // part_count
    for part in range(part_count):
        first = pl.multiple_of(xor(place.ctx, part) * rows, rows) if part_count > 1 else 0
        lines = slice(part * rows, (part + 1) * rows)
        wz_o[pl.ds(first, rows), :] = whole[lines, :inner].astype(F32)
        wo_o[pl.ds(first, rows), :] = whole[lines, inner:].astype(F32)


def unpack_input_kernel(counts, heads, part_count, info, *refs):
    parts = refs[:part_count]
    (
        wx_o, wbc_o, wdt_o, norm_o, taps_o, bias_o, state_taps_o, state_bias_o, dt_bias_o, a_log_o, skip_o,
        gate_o, wide,
    ) = refs[part_count:]
    place = Place(info, counts)
    shard, inner = wx_o.shape
    channels = inner + 2 * LANES
    rows = shard // part_count
    for part in range(part_count):
        first = pl.multiple_of(xor(place.ctx, part) * rows, rows) if part_count > 1 else 0
        wide[pl.ds(first, rows), :] = parts[part][...].astype(F32)
    wx_o[...] = wide[:shard, :inner]
    wbc_o[...] = wide[:shard, inner:channels]
    lines = wide[:, channels:].T
    wdt_o[...] = lines[:heads, :shard]
    each = gate_o.shape[1]
    size = lines.shape[1]
    source = iota((16, size), 1)
    inside = (source // each == iota((16, size), 0)) & (source < shard)
    place_in = (iota((size, LANES), 0) % each == iota((size, LANES), 1)).astype(BF16)

    def by_head(line):
        row = jnp.where(inside, lines[line : line + 1, :], 0.0).astype(BF16)
        return dot(row, place_in)[:heads, :each]

    for tap in range(CONV):
        taps_o[:, tap, :] = by_head(TAPS + tap)
    bias_o[...] = by_head(TAPS + CONV)
    gate_o[...] = by_head(GATE)
    gain = wide[:rows, channels:]
    for part in range(1, part_count):
        gain = gain + wide[part * rows : (part + 1) * rows, channels:]
    gain = jnp.concatenate([gain, jnp.zeros((LANES - rows, LANES), F32)], axis=0).T
    source, target = iota((LANES, size), 0), iota((LANES, size), 1)
    total = jnp.zeros((8, size), F32)
    for lane in range(shard // rows):
        pick = ((target == lane * rows + source) & (source < rows)).astype(F32)
        total = total + dot_exact(jnp.broadcast_to(gain[NORM + lane : NORM + lane + 1, :], (8, LANES)), pick)
    norm_o[...] = total[0:1, :shard]
    states = state_bias_o.shape[1]
    state_taps_o[...] = lines[STATE_TAPS : STATE_TAPS + CONV, :states]
    state_bias_o[...] = lines[STATE_TAPS + CONV : STATE_TAPS + CONV + 1, :states]
    row = lines[BY_HEAD : BY_HEAD + 1, :]
    dt_bias_o[...] = row[:, :heads]
    a_log_o[...] = row[:, heads : 2 * heads]
    skip_o[...] = row[:, 2 * heads : 3 * heads]


def call(body, steps, info, operands, outputs, scratch=(), reverse=False, micros=1, mega=20):
    def at(index):
        return steps - 1 - index if reverse else index

    def spec(shape, kind):
        if kind == "rows":
            return pl.BlockSpec((BLOCK,) + tuple(shape[1:]), lambda i: (at(i), 0))
        if kind == "block":
            return pl.BlockSpec((1,) + tuple(shape[1:]), lambda i: (at(i), 0, 0))
        if kind == "lanes":
            return pl.BlockSpec((shape[0], BLOCK), lambda i: (0, at(i)))
        if kind == "tail":
            each = BLOCK // 16
            return pl.BlockSpec((16, shape[1]), lambda i: (jnp.maximum(at(i) * each - 1, 0), 0))
        if kind == "whole":
            return pl.BlockSpec(tuple(shape), lambda i: (0,) * len(shape))
        if kind == "once":
            return pl.BlockSpec(tuple(shape), lambda i: (0,) * len(shape), pipeline_mode=pl.Buffered(1))
        return kind

    return pl.pallas_call(
        body,
        grid=(steps,),
        in_specs=[pl.BlockSpec(memory_space=pltpu.SMEM)]
        + [spec(array.shape, "once" if kind == "whole" else kind) for array, kind in operands],
        out_specs=[spec(shape.shape, kind) for shape, kind in outputs],
        out_shape=[shape for shape, _ in outputs],
        scratch_shapes=list(scratch),
        compiler_params=pltpu.CompilerParams(
            dimension_semantics=("arbitrary",), vmem_limit_bytes=mega * MEGA
        ),
        cost_estimate=pl.CostEstimate(
            flops=micros * 1_100_000_000, bytes_accessed=micros * 3_500_000, transcendentals=0
        ),
    )(info, *[array for array, _ in operands])


def shifted(value, axis, steps):
    count = lax.axis_size(axis)
    first, last = max(0, -steps), min(count, count - steps)
    return lax.ppermute(value, axis, [(source, source + steps) for source in range(first, last)])


def swapped(value):
    return lax.ppermute(value, "tp", [(0, 1), (1, 0)])


def partnered(value, axis, mask):
    return lax.ppermute(value, axis, [(one, one ^ mask) for one in range(lax.axis_size(axis))])


def exchanged(value, axis):
    return [value] + [partnered(value, axis, mask) for mask in range(1, lax.axis_size(axis))]


def own_rows(value, rows):
    return lax.dynamic_slice_in_dim(value, lax.axis_index("ctx") * rows, rows, 0)


def joined_rows(values):
    return jnp.concatenate(values, axis=0)


def ctx_sum(pieces):
    total = pieces[0].astype(F32)
    for mask in range(1, len(pieces)):
        total = total + partnered(pieces[mask], "ctx", mask).astype(F32)
    return total


def dp_sum(total):
    dp_count = lax.axis_size("dp")
    rows = total.shape[0] // dp_count
    own = total[:rows].astype(F32)
    for mask in range(1, dp_count):
        block = total[mask * rows : (mask + 1) * rows].astype(BF16)
        own = own + partnered(block, "dp", mask).astype(F32)
    return own.astype(BF16)


def halved(blocks, mask):
    count, rows = blocks.shape[:2]
    sent = jnp.concatenate([blocks[block] for block in range(1, count, 2)], axis=0).astype(BF16)
    received = partnered(sent, "dp", mask).reshape(count // 2, rows, -1).astype(F32)
    return jnp.stack([blocks[block] for block in range(0, count, 2)]) + received


def doubled(value, mask):
    return jnp.concatenate([value, partnered(value, "ctx", mask)], axis=0)


def whole_sum(value):
    return lax.psum(lax.psum_scatter(value, "dp", scatter_dimension=0, tiled=True), "ctx")


def body(
    tokens, cotangent, device_fill, seq_lengths, norm_gain, w_z, w_x, w_bc, w_dt,
    conv_x, conv_x_bias, conv_bc, bias_bc, dt_bias, a_log, skip_d, gate_gain, w_out,
):
    rows, width = tokens.shape
    heads = dt_bias.shape[0]
    inner = heads * HEAD
    channels = inner + 2 * LANES
    steps = rows // BLOCK
    shard = norm_gain.shape[0]
    dp_count = lax.axis_size("dp")
    ctx_count = lax.axis_size("ctx")
    tp_index = lax.axis_index("tp")
    counts = (ctx_count, seq_lengths.shape[1])

    parts = ctx_count if shard % (16 * ctx_count) == 0 else 1
    part_rows = shard // parts

    fill = jnp.sum(jnp.where(jnp.arange(ctx_count) == lax.axis_index("ctx"), device_fill[0], 0)) * BLOCK
    halo = shifted(lax.dynamic_slice_in_dim(tokens, fill - 16, 16, 0), "ctx", 1)

    with jax.named_scope("gather_weights"):
        vector = jnp.concatenate(
            [
                jnp.concatenate(
                    [
                        conv_x.reshape(CONV, shard),
                        conv_x_bias.reshape(1, shard),
                        norm_gain[None, :],
                        gate_gain.reshape(1, shard),
                        jnp.zeros((1, shard), BF16),
                        jnp.pad(
                            jnp.concatenate([conv_bc, bias_bc[None, :]], axis=0),
                            ((0, 3), (0, shard - bias_bc.shape[0])),
                        ),
                    ],
                    axis=0,
                ),
                jnp.pad(w_dt.T, ((0, 16 - heads), (0, 0))),
            ],
            axis=1,
        )
        input_rows = jnp.concatenate([w_x, w_bc], axis=1)
        gate_rows = jnp.concatenate([w_z, w_out.T], axis=1)
        if parts > 1:
            w1_parts = joined_rows(exchanged(own_rows(input_rows, part_rows), "dp"))
            vector = jnp.pad(vector, ((0, 0), (0, 2 * inner - 2 * shard)))
            block = jnp.concatenate([own_rows(gate_rows, part_rows), vector], axis=0)
            block, _, halo = lax.optimization_barrier((block, w1_parts, halo))
            vectors = exchanged(block, "dp")
            w2_parts = exchanged(joined_rows([value[:part_rows] for value in vectors]), "ctx")
            w1_parts = exchanged(w1_parts, "ctx")
        else:
            w1_parts = [lax.all_gather(input_rows, "dp", axis=0, tiled=True)]
            w2_parts = [lax.all_gather(gate_rows, "dp", axis=0, tiled=True)]
            vectors = exchanged(vector, "dp")
    first_vector = part_rows // 16 if parts > 1 else 0
    vector_spec = pl.BlockSpec(
        (16, 2 * shard), lambda i: (first_vector, 0), pipeline_mode=pl.Buffered(1)
    )

    dtp = jnp.pad(jnp.stack([dt_bias, jnp.exp(a_log), skip_d]), ((0, 5), (0, LANES - heads)))
    shape = (2 * LANES, inner)
    spread = (iota(shape, 0) % LANES == iota(shape, 1) // HEAD).astype(BF16)
    info = jnp.concatenate(
        [
            device_fill[0],
            seq_lengths[0],
            jnp.stack([lax.axis_index("ctx"), tp_index, lax.axis_index("dp")]).astype(jnp.int32),
        ]
    )

    def out(shape, dtype, kind):
        return (jax.ShapeDtypeStruct(shape, dtype), kind)

    def row_out(columns, dtype):
        return out((rows, columns), dtype, "rows")

    state_out = out((steps, inner, LANES), F32, "block")
    packet_out = out((inner + 16, LANES), BF16, "whole")

    (w1, par, normed, halo_normed, halo_v, v, xc, bc, ypart, pre_step, cum, entry, decay, packet) = call(
        functools.partial(forward_kernel, counts, heads, dp_count, parts),
        steps,
        info,
        [(value, vector_spec) for value in vectors]
        + [(value, "whole") for value in w1_parts]
        + [(tokens, "rows"), (halo, "whole"), (dtp, "whole"), (spread, "whole")],
        [
            out((width, channels + LANES), BF16, "whole"),
            out((8, channels), F32, "whole"),
            row_out(width, BF16),
            out((16, width), BF16, "whole"),
            out((8, channels), F32, "whole"),
            row_out(channels, BF16),
            row_out(inner, BF16),
            row_out(2 * LANES, BF16),
            row_out(inner, F32),
            row_out(LANES, F32),
            row_out(LANES, F32),
            state_out,
            out((steps, 8, LANES), F32, "block"),
            packet_out,
        ],
        [
            pltpu.VMEM((8 + BLOCK, channels), F32),
            pltpu.VMEM((inner, LANES), F32),
            pltpu.VMEM((8, LANES), F32),
            pltpu.VMEM((BLOCK, BLOCK), F32),
            pltpu.VMEM((BLOCK, BLOCK), F32),
            pltpu.VMEM((2, BLOCK, 2 * BLOCK), BF16),
        ],
        micros=20,
        mega=16,
    )
    packets = [(shifted(packet, "ctx", step), "whole") for step in range(1, ctx_count)]
    wz_spec = pl.BlockSpec((width, inner), lambda i: (0, 0), pipeline_mode=pl.Buffered(1))
    wo_spec = pl.BlockSpec((width, inner), lambda i: (0, 1), pipeline_mode=pl.Buffered(1))
    w2, z, dn = call(
        functools.partial(gate_matmul_kernel, counts, dp_count, parts),
        steps,
        info,
        [(value, "whole") for value in w2_parts] + [(normed, "rows"), (cotangent, "rows")],
        [out((width, 2 * inner), BF16, "whole"), row_out(inner, BF16), row_out(inner, BF16)],
        micros=7,
        mega=12,
    )
    y, hb, h, stat = call(
        functools.partial(apply_kernel, counts, len(packets)),
        steps,
        info,
        packets
        + [
            (entry, "block"),
            (decay, "block"),
            (cum, "rows"),
            (bc, "rows"),
            (ypart, "rows"),
            (z, "rows"),
            (dn, "rows"),
            (par, "whole"),
            (spread, "whole"),
        ],
        [
            row_out(inner, F32),
            out((steps, inner, LANES), BF16, "block"),
            state_out,
            out((8, rows), F32, "lanes"),
        ],
        [pltpu.VMEM((inner, LANES), F32)],
        micros=8,
        mega=12,
    )
    other_stat = swapped(stat)
    inner_all = inner * lax.axis_size("tp")
    half = width // 2
    keep, send, gwo, small_gate, dy, dz, de, exits, packet = call(
        functools.partial(gate_back_kernel, counts, inner_all),
        steps,
        info,
        [
            (stat, "lanes"),
            (other_stat, "lanes"),
            (y, "rows"),
            (z, "rows"),
            (dn, "rows"),
            (cotangent, "rows"),
            (cum, "rows"),
            (bc, "rows"),
            (xc, "rows"),
            (hb, "block"),
            (decay, "block"),
            (w2, wo_spec),
            (par, "whole"),
            (spread, "whole"),
        ],
        [
            row_out(half, BF16),
            row_out(half, BF16),
            out((width, inner), BF16, "whole"),
            out((8, inner), F32, "whole"),
            row_out(inner, BF16),
            row_out(inner, BF16),
            row_out(LANES, F32),
            state_out,
            packet_out,
        ],
        [
            pltpu.VMEM((width, inner), F32),
            pltpu.VMEM((inner, LANES), F32),
            pltpu.VMEM((8, LANES), F32),
        ],
        reverse=True,
        micros=15,
        mega=14,
    )
    packets = [(shifted(packet, "ctx", -step), "whole") for step in range(1, ctx_count)]
    dxc, dcq, dbq, row_sums, col_sums, *g2 = call(
        functools.partial(intra_back_kernel, counts, heads, dp_count),
        steps,
        info,
        [
            (dy, "rows"),
            (dz, "rows"),
            (xc, "rows"),
            (bc, "rows"),
            (cum, "rows"),
            (pre_step, "rows"),
            (hb, "block"),
            (normed, "rows"),
            (gwo, "whole"),
            (par, "whole"),
            (spread, "whole"),
        ],
        [
            row_out(inner, BF16),
            row_out(LANES, F32),
            row_out(LANES, F32),
            row_out(LANES, F32),
            row_out(LANES, F32),
        ]
        + [out((width // parts, 2 * inner), BF16, "whole")] * parts,
        [
            pltpu.VMEM((width, inner), F32),
            pltpu.VMEM((LANES, BLOCK), F32),
            pltpu.VMEM((BLOCK, BLOCK), F32),
            pltpu.VMEM((BLOCK, BLOCK), F32),
            pltpu.VMEM((BLOCK, BLOCK), F32),
            pltpu.VMEM((2, 2 * BLOCK, BLOCK), BF16),
        ],
        micros=18,
        mega=16,
    )
    with jax.named_scope("reduce_gate_weights"):
        total2 = ctx_sum(g2) if parts > 1 else g2[0]
    packed, back, *g1 = call(
        functools.partial(state_back_kernel, counts, heads, dp_count, len(packets), parts),
        steps,
        info,
        packets
        + [
            (exits, "block"),
            (h, "block"),
            (xc, "rows"),
            (bc, "rows"),
            (cum, "rows"),
            (pre_step, "rows"),
            (de, "rows"),
            (dxc, "rows"),
            (dcq, "rows"),
            (dbq, "rows"),
            (row_sums, "rows"),
            (col_sums, "rows"),
            (decay, "block"),
            (v, "rows"),
            (v, "tail"),
            (halo_v, "whole"),
            (halo_normed, "whole"),
            (normed, "rows"),
            (small_gate, "whole"),
            (par, "whole"),
            (dtp, "whole"),
            (spread, "whole"),
        ],
        [row_out(channels + LANES, BF16), out((16, channels), BF16, "whole")]
        + [out((width // parts, channels + LANES), BF16, "whole")] * parts,
        [
            pltpu.VMEM((inner, LANES), F32),
            pltpu.VMEM((8, LANES), F32),
            pltpu.VMEM((8 + BLOCK, channels), F32),
            pltpu.VMEM((8 + BLOCK, channels), F32),
            pltpu.VMEM((width, channels + LANES), F32),
            pltpu.VMEM((8, channels), F32),
        ],
        reverse=True,
        micros=25,
        mega=20,
    )
    with jax.named_scope("reduce_gate_weights"):
        if parts > 1:
            total2 = total2.reshape(dp_count, part_rows, 2 * inner)
            total2 = halved(total2, 1) if dp_count > 1 else total2
        else:
            total2 = whole_sum(total2)
    norm_rows = part_rows * dp_count
    if parts > 1:
        g1 = [g1[0]] + [partnered(g1[mask], "ctx", mask) for mask in range(1, parts)]
        packed, g1[1], total2 = lax.optimization_barrier((packed, g1[1], total2))
        mask = 2
        while mask < dp_count:
            total2 = halved(total2, mask)
            mask *= 2
        total2 = total2[0].astype(BF16)
    partial, halo_grad, norm_part = call(
        functools.partial(input_back_kernel, counts, dp_count, parts),
        steps,
        info,
        [
            (packed, "rows"),
            (back, "whole"),
            (dz, "rows"),
            (w2, wz_spec),
            (tokens, "rows"),
            (halo, "whole"),
            (w1, "whole"),
            (par, "whole"),
        ],
        [
            row_out(width, BF16),
            out((8, width), F32, "whole"),
            out((norm_rows, LANES), F32, "whole"),
        ],
        [pltpu.VMEM((8, width), F32)],
        micros=5,
        mega=12,
    )
    other = swapped(partial)
    with jax.named_scope("reduce_input_weights"):
        norm_part = jnp.pad(norm_part, ((0, 0), (channels, 0)))
        if parts > 1:
            total1 = sum(piece.astype(F32) for piece in g1) + norm_part
            total1, total2 = lax.optimization_barrier((total1, total2))
            total1 = dp_sum(total1)
            total2 = doubled(total2, 1)
            total1, total2 = lax.optimization_barrier((total1, total2))
            mask = 2
            while mask < ctx_count:
                total2 = doubled(total2, mask)
                mask *= 2
        else:
            total1 = whole_sum((g1[0].astype(F32) + norm_part).astype(BF16))
        across = swapped(total1[:, inner:])
        across, halo_grad, send = lax.optimization_barrier((across, halo_grad, send))
        lane = np.arange(3 * LANES) - 2 * LANES
        both = (lane < 0) | ((lane >= STATE_TAPS) & (lane < BY_HEAD))
        both = both | ((lane >= NORM) & (lane < NORM + shard // part_rows))
        summed = total1[:, inner:] + jnp.where(both[None, :], across, 0)
        total1 = jnp.concatenate([total1[:, :inner], summed], axis=1)
    size = ctx_count * 2
    back = [(s, s - 2) for s in range(2, size)]
    cross = [(s, (s - 2) ^ 1) for s in range(2, size)]
    halo_a = lax.ppermute(halo_grad, ("ctx", "tp"), back)
    halo_b = lax.ppermute(halo_grad, ("ctx", "tp"), cross)
    received = swapped(send)
    grad_tokens, layer_out = call(
        functools.partial(finish_kernel, counts),
        steps,
        info,
        [
            (partial, "rows"),
            (other, "rows"),
            (halo_a, "whole"),
            (halo_b, "whole"),
            (keep, "rows"),
            (received, "rows"),
            (tokens, "rows"),
            (cotangent, "rows"),
            (par, "whole"),
        ],
        [row_out(width, F32), row_out(half, F32)],
        micros=5,
        mega=10,
    )
    with jax.named_scope("last_hop"):
        if parts > 1:
            total1 = exchanged(total1, "ctx")
            total1[-1], grad_tokens = lax.optimization_barrier((total1[-1], grad_tokens))
        else:
            total1 = [total1]
    each = HEAD // dp_count
    part_bc = bias_bc.shape[0]
    tall = -(-shard // LANES) * LANES

    def final(*sizes):
        return out(sizes, F32, "whole")

    grad_wz, grad_wo = call(
        functools.partial(unpack_gate_kernel, counts, parts),
        1,
        info,
        [(total2, "whole")],
        [final(shard, inner), final(shard, inner)],
        micros=2,
        mega=8,
    )
    (
        grad_wx, grad_wbc, grad_wdt, grad_norm, grad_taps, grad_bias, grad_state_taps, grad_state_bias,
        grad_dt_bias, grad_a_log, grad_skip, grad_gate,
    ) = call(
        functools.partial(unpack_input_kernel, counts, heads, parts),
        1,
        info,
        [(value, "whole") for value in total1],
        [
            final(shard, inner),
            final(shard, 2 * LANES),
            final(heads, shard),
            final(1, shard),
            final(heads, CONV, each),
            final(heads, each),
            final(CONV, part_bc),
            final(1, part_bc),
            final(1, heads),
            final(1, heads),
            final(1, heads),
            final(heads, each),
        ],
        [pltpu.VMEM((tall, channels + LANES), F32)],
        micros=2,
        mega=8,
    )
    return (
        layer_out,
        grad_tokens,
        grad_norm[0],
        grad_wz,
        grad_wx,
        grad_wbc,
        grad_wdt.T,
        grad_taps.transpose(1, 0, 2),
        grad_bias,
        grad_state_taps,
        grad_state_bias[0],
        grad_dt_bias[0],
        grad_a_log[0],
        grad_skip[0],
        grad_gate,
        grad_wo.T,
    )


def solution(mesh):
    shards = P(("dp", "ctx"), None)
    return jax.shard_map(
        body,
        mesh=mesh,
        in_specs=(
            shards,
            shards,
            P("dp", None),
            P("dp", None),
            P("dp"),
            P("dp", "tp"),
            P("dp", "tp"),
            P("dp", None),
            P("dp", "tp"),
            P(None, "tp", "dp"),
            P("tp", "dp"),
            P(None, "dp"),
            P("dp"),
            P("tp"),
            P("tp"),
            P("tp"),
            P("tp", "dp"),
            P("tp", "dp"),
        ),
        out_specs=(
            P(("dp", "ctx"), "tp"),
            shards,
            P("dp"),
            P("dp", "tp"),
            P("dp", "tp"),
            P("dp", None),
            P("dp", "tp"),
            P(None, "tp", "dp"),
            P("tp", "dp"),
            P(None, "dp"),
            P("dp"),
            P("tp"),
            P("tp"),
            P("tp"),
            P("tp", "dp"),
            P("tp", "dp"),
        ),
        check_vma=False,
    )
```

```python
import functools

import jax
import jax.numpy as jnp
import numpy as np
from jax import lax
from jax.experimental import pallas as pl
from jax.experimental.pallas import tpu as pltpu
from jax.sharding import PartitionSpec as P

CONV = 4
BLOCK = 256
HEAD = 64
LANES = 128
EPS = 1e-05
MEGA = 1024 * 1024
F32 = jnp.float32
BF16 = jnp.bfloat16


def dot(left, right):
    return jnp.dot(left, right, preferred_element_type=F32)


def dot_tn(left, right):
    return lax.dot_general(left, right, (((0,), (0,)), ((), ())), preferred_element_type=F32)


def dot_nt(left, right):
    return lax.dot_general(left, right, (((1,), (1,)), ((), ())), preferred_element_type=F32)


def dot_exact(left, right):
    return jnp.dot(left, right, preferred_element_type=F32, precision=lax.Precision.HIGHEST)


def iota(shape, dim):
    return lax.broadcasted_iota(jnp.int32, shape, dim)


def sigmoid(value):
    return 1.0 / (1.0 + jnp.exp(-value))


def gate_sigmoid(value):
    return 0.5 * jnp.tanh(0.5 * value) + 0.5


def softplus(value):
    return jnp.maximum(value, 0.0) + jnp.log1p(jnp.exp(-jnp.abs(value)))


def split(value):
    high = value.astype(BF16)
    return high, (value - high.astype(F32)).astype(BF16)


def expand(value, spread):
    return dot(jnp.concatenate(split(value), axis=1), spread[...])


def reduce_heads(value, spread):
    high, low = split(value)
    pick = spread[:LANES, :]
    return dot_nt(high, pick) + dot_nt(low, pick)


def head_column(row, channels):
    shape = (channels, LANES)
    return jnp.sum(jnp.where(iota(shape, 0) // HEAD == iota(shape, 1), row, 0.0), axis=1, keepdims=True)


def xor(value, mask):
    return jnp.bitwise_xor(value, jnp.int32(mask))


class Place:
    def __init__(self, info, counts):
        devices, sequences = counts
        own = info[devices + sequences]
        self.ctx = own
        self.tp = info[devices + sequences + 1]
        self.dp = info[devices + sequences + 2]
        self.fill = jnp.int32(0)
        self.first = jnp.int32(0)
        for device in range(devices):
            rows = info[device] * BLOCK
            self.fill = self.fill + jnp.where(own == device, rows, 0)
            self.first = self.first + jnp.where(own > device, rows, 0)
        self.ends = []
        total = jnp.int32(0)
        for sequence in range(sequences - 1):
            total = total + info[devices + sequence]
            self.ends.append(total)

    def of(self, position):
        found = (position >= self.ends[0]).astype(jnp.int32)
        for end in self.ends[1:]:
            found = found + (position >= end).astype(jnp.int32)
        return jnp.where(position < 0, -1, found)

    def rows(self, index):
        return self.of(self.first + jnp.minimum(index, self.fill - 1))

    def before(self, block):
        position = self.first + jnp.minimum(block * BLOCK, self.fill) - 1
        found = jnp.int32(0)
        for end in self.ends:
            found = found + jnp.where(position >= end, 1, 0)
        return jnp.where(position < 0, -1, found)

    def last(self, block):
        position = self.first + jnp.minimum(block * BLOCK + BLOCK - 1, self.fill - 1)
        found = jnp.int32(0)
        for end in self.ends:
            found = found + jnp.where(position >= end, 1, 0)
        return found

    def column(self, block, shift=0):
        return self.rows(block * BLOCK + shift + iota((BLOCK, 1), 0))

    def valid(self, block):
        return (block * BLOCK + iota((BLOCK, 1), 0) < self.fill).astype(F32)

    def keep(self, block):
        across = self.rows(block * BLOCK + iota((1, BLOCK), 1))
        return (self.column(block) == across) & (iota((BLOCK, BLOCK), 0) >= iota((BLOCK, BLOCK), 1))


def step_sizes(place, block, pre_step, heads):
    lane = iota((BLOCK, LANES), 1)
    return jnp.where(lane < heads, softplus(pre_step), 0.0) * place.valid(block)


def end_weights(place, block, cum):
    same = (place.column(block) == place.last(block)).astype(F32)
    return jnp.exp(cum[BLOCK - 1 :, :] - cum) * same


def enter_weights(place, block, cum):
    return jnp.exp(cum) * (place.column(block) == place.before(block)).astype(F32)


def block_decay(place, block, cum):
    return jnp.exp(cum[BLOCK - 1 :, :]) * jnp.where(place.last(block) == place.before(block), 1.0, 0.0)


def decay_kernel(keep, cum, cum_rows, head):
    return jnp.exp(jnp.where(keep, cum[:, head : head + 1] - cum_rows[head : head + 1, :], -1e30))


def both_halves(pair):
    lane = iota(pair.shape, 1)
    zero = jnp.zeros_like(pair)
    return [jnp.where(lane < HEAD, pair, zero), jnp.where(lane >= HEAD, pair, zero)]


def same_mask(place, block, tap):
    return (place.column(block, tap - (CONV - 1)) == place.column(block)).astype(F32)


def conv_pre(place, block, ext, par, channels):
    total = par[4:5, :channels]
    for tap in range(CONV):
        first = 8 - (CONV - 1) + tap
        total = total + par[tap : tap + 1, :channels] * ext[first : first + BLOCK, :] * same_mask(
            place, block, tap
        )
    return total


def state_packet(state, decay):
    high, low = split(decay)
    row = iota((16, LANES), 0)
    tail = jnp.where(row == 0, high.astype(F32), jnp.where(row == 1, low.astype(F32), 0.0))
    return jnp.concatenate([state.astype(BF16), tail.astype(BF16)], axis=0)


def merge_packets(packets, inner):
    total = jnp.zeros((inner, LANES), F32)
    for packet in reversed(packets):
        tail = packet[inner : inner + 16, :].astype(F32)
        decay = tail[0:1, :] + tail[1:2, :]
        total = packet[:inner, :].astype(F32) + head_column(decay, inner) * total
    return total


def normalise(rows, gain):
    inv = lax.rsqrt(jnp.mean(rows * rows, axis=1, keepdims=True) + EPS)
    return rows * inv, inv, (rows * inv * gain).astype(BF16)


def piece_rows(place, dp_count, parts, rows):
    for part in range(parts):
        for block in range(dp_count):
            owner = xor(place.dp, block) * parts + (xor(place.ctx, part) if parts > 1 else 0)
            yield part, block, pl.multiple_of(owner * rows, rows)


def join_pieces(place, dp_count, parts, whole):
    columns = parts[0].shape[1]
    if len(parts) == 1:
        whole[:, :columns] = parts[0][...]
        return
    rows = parts[0].shape[0] // dp_count
    for part, block, first in piece_rows(place, dp_count, len(parts), rows):
        whole[pl.ds(first, rows), :columns] = parts[part][block * rows : (block + 1) * rows, :]


def cut_pieces(place, dp_count, whole, parts, lanes):
    if len(parts) == 1:
        parts[0][:, lanes] = whole[...].astype(BF16)
        return
    rows = parts[0].shape[0] // dp_count
    for part, block, first in piece_rows(place, dp_count, len(parts), rows):
        parts[part][block * rows : (block + 1) * rows, lanes] = whole[pl.ds(first, rows), :].astype(BF16)


def join_parameters(place, vectors, skip, heads, par, w1):
    shard = vectors[0].shape[1] // 2
    each = HEAD // len(vectors)
    inner = heads * HEAD
    by_channel = jnp.zeros((16, inner), F32)
    in_order = jnp.zeros((16, shard * len(vectors)), F32)
    by_state = jnp.zeros((16, 2 * LANES), F32)
    states = 2 * LANES // len(vectors)
    eye = (iota((16, LANES), 0) == iota((16, LANES), 1)).astype(BF16)
    for block, vector in enumerate(vectors):
        owner = xor(place.dp, block)
        first = pl.multiple_of(owner * shard, shard)
        w1[pl.ds(first, shard), inner + 2 * LANES :] = dot_tn(vector[:, shard:], eye).astype(BF16)
        source, target = iota((shard, inner), 0), iota((shard, inner), 1)
        pick = target == source // each * HEAD + owner * each + source % each
        by_channel = by_channel + dot(vector[:, :shard], pick.astype(BF16))
        source, target = iota((shard, in_order.shape[1]), 0), iota((shard, in_order.shape[1]), 1)
        in_order = in_order + dot(vector[:, :shard], (target == owner * shard + source).astype(BF16))
        source, target = iota((shard, 2 * LANES), 0), iota((shard, 2 * LANES), 1)
        pick = (target == owner * states + source) & (source < states)
        by_state = by_state + dot(vector[:, :shard], pick.astype(BF16))
    par[...] = jnp.zeros_like(par)
    par[0:5, :inner] = by_channel[0:5, :]
    par[0:5, inner:] = by_state[8:13, :]
    par[5:6, : in_order.shape[1]] = in_order[5:6, :]
    par[6:7, :inner] = by_channel[6:7, :]
    par[7:8, :inner] = skip


TAPS, GATE, STATE_TAPS, BY_HEAD, NORM = 12, 18, 20, 25, 26


def lanes(pieces, columns):
    rows, at = [], 0
    for first, value in pieces:
        if first > at:
            rows.append(jnp.zeros((first - at, columns), F32))
        rows.append(value)
        at = first + value.shape[0]
    rows.append(jnp.zeros((LANES - at, columns), F32))
    return jnp.concatenate(rows, axis=0)


def pack_norm(place, dp_count, part_count, row, rows):
    columns = row.shape[1]
    shard = columns // dp_count
    size = shard // rows
    total = jnp.zeros((dp_count * rows, LANES), F32)
    source, target = iota((dp_count * rows, columns), 0), iota((dp_count * rows, columns), 1)
    owner = source // rows
    if part_count > 1:
        owner = jnp.bitwise_xor(owner, place.dp)
    for lane in range(size):
        pick = target == owner * shard + lane * rows + source % rows
        total = total + dot_nt(pick.astype(BF16), lanes([(NORM + lane, row)], columns).astype(BF16))
    return total


def pack_parameters(dp_count, heads, small, gate, skip):
    inner = heads * HEAD
    each = HEAD // dp_count
    shard = inner // dp_count
    states = 2 * LANES // dp_count

    source, target = iota((inner, inner), 0), iota((inner, inner), 1)
    inside = source % shard
    pick = target == inside // each * HEAD + source // shard * each + inside % each
    by_channel = lanes([(TAPS, small[0:5, :inner]), (GATE, gate)], inner)
    total = dot_nt(pick.astype(BF16), by_channel.astype(BF16))
    source, target = iota((inner, 2 * LANES), 0), iota((inner, 2 * LANES), 1)
    inside = source % shard
    pick = (target == source // shard * states + inside) & (inside < states)
    by_state = lanes([(STATE_TAPS, small[0:5, inner : inner + 2 * LANES])], 2 * LANES)
    total = total + dot_nt(pick.astype(BF16), by_state.astype(BF16))
    source, target = iota((inner, LANES), 0) % shard, iota((inner, LANES), 1)
    for index, row in enumerate((small[6:7, :LANES], small[7:8, :LANES], skip)):
        pick = (source == target + index * heads) & (target < heads)
        total = total + dot_nt(pick.astype(BF16), lanes([(BY_HEAD, row)], LANES).astype(BF16))
    return total


def forward_kernel(
    counts, heads, dp_count, part_count, info, *refs
):
    vectors = refs[:dp_count]
    parts = refs[dp_count : dp_count + part_count]
    (
        tok, halo, dtp, spread,
        w1, par, normed_o, halo_normed_o, halo_v_o, v_o, xc_o, bc_o, ypart_o, pre_o, cum_o, entry_o, decay_o,
        packet_o, ext, run, factor,
    ) = refs[dp_count + part_count :]
    forward_block(
        counts, heads, info, vectors, parts, tok, halo, w1, par, dtp, spread,
        normed_o, halo_normed_o, halo_v_o, v_o, xc_o, bc_o, ypart_o, pre_o, cum_o, entry_o, decay_o, packet_o,
        ext, run, factor,
    )


def forward_block(
    counts, heads, info, vectors, parts, tok, halo, w1, par, dtp, spread,
    normed_o, halo_normed_o, halo_v_o, v_o, xc_o, bc_o, ypart_o, pre_o, cum_o, entry_o, decay_o, packet_o,
    ext, run, factor,
):
    block = pl.program_id(0)
    place = Place(info, counts)
    inner = heads * HEAD
    state = LANES
    channels = inner + 2 * state
    width = tok.shape[1]

    @pl.when(block == 0)
    def _():
        join_pieces(place, len(vectors), parts, w1)
        join_parameters(place, vectors, expand(dtp[...], spread)[2:3, :], heads, par, w1)

    gain = par[5:6, :width]
    _, _, normed = normalise(tok[...].astype(F32), gain)
    normed_o[...] = normed

    @pl.when(block == 0)
    def _():
        _, _, before = normalise(halo[...].astype(F32), gain)
        halo_normed_o[...] = before
        raw = dot(before, w1[:, :channels]).astype(BF16).astype(F32)
        ext[0:8, :] = raw[8:16, :]
        halo_v_o[...] = raw[8:16, :]
        run[...] = jnp.zeros_like(run)
        factor[...] = jnp.ones_like(factor)

    @pl.when(block > 0)
    def _():
        ext[0:8, :] = ext[BLOCK : BLOCK + 8, :]

    raw = dot(normed, w1[...])
    v = raw[:, :channels].astype(BF16)
    v_o[...] = v
    ext[8 : 8 + BLOCK, :] = v.astype(F32)
    pre = conv_pre(place, block, ext, par, channels)
    act = (pre * gate_sigmoid(pre)).astype(BF16)
    xc = act[:, :inner]
    bq = act[:, inner : inner + state]
    cq = act[:, inner + state :]
    xc_o[...] = xc
    bc_o[...] = act[:, inner:]
    pre_step = raw[:, channels:].astype(BF16).astype(F32) + dtp[0:1, :]
    pre_o[...] = pre_step
    step = step_sizes(place, block, pre_step, heads)
    tri = (iota((BLOCK, BLOCK), 0) >= iota((BLOCK, BLOCK), 1)).astype(F32)
    cum = dot_exact(tri, -dtp[1:2, :] * step)
    cum_o[...] = cum
    cum_rows = cum.T
    step_rows = step.T
    gram = dot_nt(cq, bq)
    keep = place.keep(block)
    for pair in range(heads // 2):
        lanes = slice(pair * LANES, (pair + 1) * LANES)
        mixing = []
        for head in (2 * pair, 2 * pair + 1):
            weight = decay_kernel(keep, cum, cum_rows, head) * step_rows[head : head + 1, :]
            mixing.append((gram * weight).astype(BF16))
        x_pair = xc[:, lanes]
        y_pair = dot(jnp.concatenate(mixing, axis=1), jnp.concatenate(both_halves(x_pair), axis=0))
        ypart_o[:, lanes] = y_pair + par[7:8, lanes] * x_pair.astype(F32)
    weighted = (expand(end_weights(place, block, cum) * step, spread) * xc.astype(F32)).astype(BF16)
    block_state = dot_tn(weighted, bq)
    decay = block_decay(place, block, cum)
    entry_o[0] = run[...]
    total = head_column(decay, inner) * run[...] + block_state
    run[...] = total
    before = factor[0:1, :]
    row = iota((8, LANES), 0)
    decay_o[0] = jnp.where(row == 0, decay, jnp.where(row == 1, before, 0.0))
    after = before * decay
    factor[...] = jnp.broadcast_to(after, factor.shape)

    @pl.when(block == pl.num_programs(0) - 1)
    def _():
        packet_o[...] = state_packet(total, after)


def gate_matmul_kernel(counts, dp_count, part_count, info, *refs):
    parts = refs[:part_count]
    normed, cot, w2, z_o, dn_o = refs[part_count:]
    block = pl.program_id(0)
    place = Place(info, counts)
    inner = z_o.shape[1]

    @pl.when(block == 0)
    def _():
        join_pieces(place, dp_count, parts, w2)

    z_o[...] = dot(normed[...], w2[:, :inner]).astype(BF16)
    grad = (cot[...].astype(F32) * place.valid(block)).astype(BF16)
    dn_o[...] = dot(grad, w2[:, inner:]).astype(BF16)


def apply_kernel(counts, packet_count, info, *refs):
    packets = refs[:packet_count]
    entry, decay, cum, bc, ypart, z, dn, par, spread, y_o, hb_o, h_o, stat_o, start = refs[packet_count:]
    block = pl.program_id(0)
    place = Place(info, counts)
    inner = z.shape[1]

    @pl.when(block == 0)
    def _():
        start[...] = merge_packets([packet[...] for packet in packets], inner)

    state = entry[0] + head_column(decay[0, 1:2, :], inner) * start[...]
    h_o[0] = state
    low = state.astype(BF16)
    hb_o[0] = low
    cq = bc[:, LANES:]
    y = ypart[...] + expand(enter_weights(place, block, cum[...]), spread) * dot_nt(cq, low)
    y_o[...] = y
    gate = z[...].astype(F32)
    gated = y * gate * gate_sigmoid(gate)
    squares = jnp.sum(gated * gated, axis=1, keepdims=True)
    cross = jnp.sum(par[6:7, :inner] * dn[...].astype(F32) * gated, axis=1, keepdims=True)
    lane = iota((BLOCK, LANES), 1)
    both = jnp.where(lane == 0, squares, jnp.where(lane == 1, cross, 0.0))
    stat_o[...] = both.T[0:8, :]


def gate_back_kernel(
    counts, inner_all, info, stat, other_stat, y, z, dn, cot, cum, bc, xc, hb, decay, wo, par, spread,
    keep_o, send_o, gwo_o, small_o, dy_o, dz_o, de_o, exit_o, packet_o,
    acc, run, factor,
):
    step = pl.program_id(0)
    block = pl.num_programs(0) - 1 - step
    place = Place(info, counts)
    inner = z.shape[1]
    width = cot.shape[1]
    half = width // 2

    @pl.when(step == 0)
    def _():
        acc[...] = jnp.zeros_like(acc)
        run[...] = jnp.zeros_like(run)
        factor[...] = jnp.ones_like(factor)
        small_o[...] = jnp.zeros_like(small_o)

    column = jnp.concatenate([stat[...] + other_stat[...], jnp.zeros((LANES - 8, BLOCK), F32)], axis=0).T
    inv = lax.rsqrt(column[:, 0:1] / inner_all + EPS)
    cross = column[:, 1:2]
    gain = par[6:7, :inner]
    gate = z[...].astype(F32)
    sig = gate_sigmoid(gate)
    silu = gate * sig
    mixed = y[...]
    gated = mixed * silu
    normal = (gated * inv * gain).astype(BF16)
    own = pl.multiple_of(place.tp * half, half)
    other = pl.multiple_of((1 - place.tp) * half, half)
    keep_o[...] = dot_nt(normal, wo[pl.ds(own, half), :]).astype(BF16)
    send_o[...] = dot_nt(normal, wo[pl.ds(other, half), :]).astype(BF16)
    grad = (cot[...].astype(F32) * place.valid(block)).astype(BF16)
    acc[...] += dot_tn(grad, normal)
    back = dn[...].astype(F32)
    grad_gated = inv * (gain * back) - gated * (inv * inv * inv) * (cross / inner_all)
    dy = (grad_gated * silu).astype(BF16)
    dy_o[...] = dy
    dz_o[...] = (grad_gated * mixed * sig * (1.0 + gate * (1.0 - sig))).astype(BF16)
    dy_float = dy.astype(F32)
    cq = bc[:, LANES:]
    read = dot_nt(cq, hb[0])
    de_o[...] = reduce_heads(dy_float * read, spread)
    small_o[0:1, :] += jnp.sum(back * gated * inv, axis=0, keepdims=True)
    small_o[1:2, :] += jnp.sum(dy_float * xc[...].astype(F32), axis=0, keepdims=True)
    dq = (expand(enter_weights(place, block, cum[...]), spread) * dy_float).astype(BF16)
    exit_o[0] = run[...]
    here = decay[0, 0:1, :]
    total = head_column(here, inner) * run[...] + dot_tn(dq, cq)
    run[...] = total
    after = factor[0:1, :] * here
    factor[...] = jnp.broadcast_to(after, factor.shape)

    @pl.when(step == pl.num_programs(0) - 1)
    def _():
        packet_o[...] = state_packet(total, after)
        gwo_o[...] = acc[...].astype(BF16)


def intra_back_kernel(counts, heads, dp_count, info, *refs):
    dy, dz, xc, bc, cum, pre_step, hb, normed, gwo, par, spread = refs[:11]
    dxc_o, dcq_o, dbq_o, rows_o, cols_o = refs[11:16]
    parts = refs[16:-2]
    acc, columns = refs[-2:]
    block = pl.program_id(0)
    place = Place(info, counts)
    inner = heads * HEAD

    @pl.when(block == 0)
    def _():
        acc[...] = jnp.zeros_like(acc)
        columns[...] = jnp.zeros_like(columns)

    bq = bc[:, :LANES]
    cq = bc[:, LANES:]
    cums = cum[...]
    step = step_sizes(place, block, pre_step[...], heads)
    cum_rows = cums.T
    step_rows = step.T
    gram = dot_nt(cq, bq)
    keep = place.keep(block)
    lane = iota((BLOCK, LANES), 1)
    grad_gram = jnp.zeros((BLOCK, BLOCK), F32)
    sums = jnp.zeros((BLOCK, LANES), F32)
    for pair in range(heads // 2):
        lanes = slice(pair * LANES, (pair + 1) * LANES)
        dy_pair = dy[:, lanes]
        x_pair = xc[:, lanes]
        halves = jnp.concatenate(both_halves(dy_pair), axis=0)
        grad_mixing = dot_nt(halves, x_pair)
        mixing = []
        for side in range(2):
            head = 2 * pair + side
            grad_m = grad_mixing[side * BLOCK : (side + 1) * BLOCK, :]
            kernel = decay_kernel(keep, cums, cum_rows, head)
            step_row = step_rows[head : head + 1, :]
            weight = kernel * step_row
            mixing.append((gram * weight).astype(BF16))
            grad_gram = grad_gram + grad_m * weight
            part = grad_m * gram * kernel
            columns[head : head + 1, :] = jnp.sum(part, axis=0, keepdims=True)
            sums = sums + jnp.where(lane == head, jnp.sum(part * step_row, axis=1, keepdims=True), 0.0)
        dx_pair = dot_tn(jnp.concatenate(mixing, axis=0), halves)
        dxc_o[:, lanes] = (dx_pair + par[7:8, lanes] * dy_pair.astype(F32)).astype(BF16)
    grad_low = grad_gram.astype(BF16)
    dq = (expand(enter_weights(place, block, cums), spread) * dy[...].astype(F32)).astype(BF16)
    dcq_o[...] = dot(grad_low, bq) + dot(dq, hb[0])
    dbq_o[...] = dot_tn(grad_low, cq)
    rows_o[...] = sums
    cols_o[...] = columns[...].T
    acc[...] += dot_tn(normed[...], dz[...])

    @pl.when(block == pl.num_programs(0) - 1)
    def _():
        cut_pieces(place, dp_count, acc, parts, slice(0, inner))
        cut_pieces(place, dp_count, gwo, parts, slice(inner, 2 * inner))


def state_back_kernel(counts, heads, dp_count, packet_count, part_count, info, *refs):
    packets = refs[:packet_count]
    (
        exits, h, xc, bc, cum, pre_step, de, dxc, dcq, dbq, rows, cols, decay, v, v_tail, halo_v, halo_normed,
        normed, small_gate, par, dtp, spread,
        packed_o, back_o,
    ) = refs[packet_count : -6 - part_count]
    parts = refs[-6 - part_count : -6]
    start, factor, ext, grad_ext, acc, small_o = refs[-6:]
    step_id = pl.program_id(0)
    block = pl.num_programs(0) - 1 - step_id
    place = Place(info, counts)
    inner = heads * HEAD
    channels = inner + 2 * LANES

    @pl.when(step_id == 0)
    def _():
        start[...] = merge_packets([packet[...] for packet in packets], inner)
        factor[...] = jnp.ones_like(factor)
        acc[...] = jnp.zeros_like(acc)
        grad_ext[...] = jnp.zeros_like(grad_ext)
        small_o[...] = jnp.zeros_like(small_o)

    here = decay[0, 0:1, :]
    before = factor[0:1, :]
    grad_state = exits[0] + head_column(before, inner) * start[...]
    factor[...] = jnp.broadcast_to(before * here, factor.shape)
    shape = (inner, LANES)
    overlap = jnp.sum(grad_state * h[0], axis=1, keepdims=True)
    grad_decay = jnp.sum(
        jnp.where(iota(shape, 0) // HEAD == iota(shape, 1), overlap, 0.0), axis=0, keepdims=True
    )
    low = grad_state.astype(BF16)
    bq = bc[:, :LANES]
    cums = cum[...]
    x_float = xc[...].astype(F32)
    pre_dt = pre_step[...]
    valid = place.valid(block)
    step = step_sizes(place, block, pre_dt, heads)
    end_kernel = end_weights(place, block, cums)
    end_weight = end_kernel * step
    end_wide = expand(end_weight, spread)
    spread_b = dot_nt(bq, low)
    grad_x = dxc[...].astype(F32) + end_wide * spread_b
    grad_end = reduce_heads(x_float * spread_b, spread)
    grad_b = dbq[...] + dot((x_float * end_wide).astype(BF16), low)
    end_part = grad_end * end_weight
    last = iota((BLOCK, LANES), 0) == BLOCK - 1
    grad_cum = rows[...] - cols[...] * step - end_part + de[...] * enter_weights(place, block, cums)
    grad_cum = grad_cum + jnp.where(
        last, jnp.sum(end_part, axis=0, keepdims=True) + grad_decay * here, 0.0
    )
    upper = (iota((BLOCK, BLOCK), 0) <= iota((BLOCK, BLOCK), 1)).astype(F32)
    grad_log = dot_exact(upper, grad_cum)
    rates = dtp[1:2, :]
    grad_step = cols[...] + grad_end * end_kernel - rates * grad_log
    heads_lane = iota((BLOCK, LANES), 1) < heads
    grad_pre_dt = jnp.where(heads_lane, grad_step * sigmoid(pre_dt), 0.0) * valid
    small_o[6:7, :LANES] += jnp.sum(grad_pre_dt, axis=0, keepdims=True)
    small_o[7:8, :LANES] += jnp.sum(grad_log * (-rates * step), axis=0, keepdims=True)

    ext[8 : 8 + BLOCK, :] = v[...].astype(F32)

    @pl.when(block == 0)
    def _():
        ext[0:8, :] = halo_v[...]

    @pl.when(block > 0)
    def _():
        ext[0:8, :] = v_tail[...].astype(F32)[8:16, :]

    pre = conv_pre(place, block, ext, par, channels)
    sig = gate_sigmoid(pre)
    slope = sig * (1.0 + pre * (1.0 - sig))
    grad_pre = jnp.concatenate([grad_x, grad_b, dcq[...]], axis=1) * slope
    small_o[4:5, :] += jnp.sum(grad_pre, axis=0, keepdims=True)
    carry = grad_ext[0:8, :]
    grad_ext[0:BLOCK, :] = jnp.zeros((BLOCK, channels), F32)
    grad_ext[BLOCK : BLOCK + 8, :] = carry
    for tap in range(CONV):
        first = 8 - (CONV - 1) + tap
        masked = grad_pre * same_mask(place, block, tap)
        small_o[tap : tap + 1, :] += jnp.sum(masked * ext[first : first + BLOCK, :], axis=0, keepdims=True)
        grad_ext[first : first + BLOCK, :] += par[tap : tap + 1, :channels] * masked
    packed = jnp.concatenate([grad_ext[8 : 8 + BLOCK, :].astype(BF16), grad_pre_dt.astype(BF16)], axis=1)
    packed_o[...] = packed
    acc[...] += dot_tn(normed[...], packed)

    @pl.when(block == 0)
    def _():
        back = jnp.concatenate([jnp.zeros((8, channels), F32), grad_ext[0:8, :]], axis=0).astype(BF16)
        back_o[...] = back
        acc[:, :channels] += dot_tn(halo_normed[...], back)
        skip = reduce_heads(jnp.broadcast_to(small_gate[1:2, :], (8, inner)), spread)[0:1, :]
        acc[:, channels:] += pack_parameters(dp_count, heads, small_o, small_gate[0:1, :], skip)
        cut_pieces(place, dp_count, acc, parts, slice(0, channels + LANES))


def input_back_kernel(
    counts, dp_count, part_count, info, packed, back, dz, wz, tok, halo, w1, par,
    dn_o, dnh_o, norm_o, total,
):
    block = pl.program_id(0)
    place = Place(info, counts)
    width = tok.shape[1]
    channels = back.shape[1]
    gain = par[5:6, :width]

    @pl.when(block == 0)
    def _():
        halo_grad = dot_nt(back[...], w1[:, :channels])
        dnh_o[...] = halo_grad[8:16, :]
        halo_scaled, _, _ = normalise(halo[...].astype(F32), gain)
        total[...] = jnp.broadcast_to(
            jnp.sum(halo_grad * halo_scaled, axis=0, keepdims=True), total.shape
        )

    partial = dot_nt(dz[...], wz[...]) + dot_nt(packed[...], w1[...])
    dn_o[...] = partial.astype(BF16)
    scaled, _, _ = normalise(tok[...].astype(F32), gain)
    total[0:1, :] += jnp.sum(partial * scaled, axis=0, keepdims=True)

    @pl.when(block == pl.num_programs(0) - 1)
    def _():
        rows = norm_o.shape[0] // dp_count
        norm_o[...] = pack_norm(place, dp_count, part_count, total[0:1, :], rows)


def finish_kernel(counts, info, own, other, halo_a, halo_b, keep, received, tok, cot, par, grad_o, out_o):
    block = pl.program_id(0)
    place = Place(info, counts)
    width = tok.shape[1]
    grad = own[...].astype(F32) + other[...].astype(F32)
    is_last = jnp.where((block + 1) * BLOCK == place.fill, 1.0, 0.0)
    halo = (halo_a[...] + halo_b[...]) * is_last
    grad = jnp.concatenate([grad[: BLOCK - 8, :], grad[BLOCK - 8 :, :] + halo], axis=0)
    inputs = tok[...].astype(F32)
    inv = lax.rsqrt(jnp.mean(inputs * inputs, axis=1, keepdims=True) + EPS)
    scaled = par[5:6, :width] * grad
    inner_dot = jnp.sum(scaled * inputs, axis=1, keepdims=True)
    half = width // 2
    branch = (keep[...].astype(F32) + received[...].astype(F32)) * place.valid(block)
    out_o[...] = jnp.where(place.tp == 0, inputs[:, :half], inputs[:, half:]) + branch
    grad_o[...] = (
        inv * scaled - inputs * (inv * inv * inv) * (inner_dot / width) + cot[...].astype(F32)
    )


def unpack_gate_kernel(counts, part_count, info, *refs):
    whole, wz_o, wo_o = refs
    place = Place(info, counts)
    shard, inner = wz_o.shape
    rows = shard // part_count
    for part in range(part_count):
        first = pl.multiple_of(xor(place.ctx, part) * rows, rows) if part_count > 1 else 0
        lines = slice(part * rows, (part + 1) * rows)
        wz_o[pl.ds(first, rows), :] = whole[lines, :inner].astype(F32)
        wo_o[pl.ds(first, rows), :] = whole[lines, inner:].astype(F32)


def unpack_input_kernel(counts, heads, part_count, info, *refs):
    parts = refs[:part_count]
    (
        wx_o, wbc_o, wdt_o, norm_o, taps_o, bias_o, state_taps_o, state_bias_o, dt_bias_o, a_log_o, skip_o,
        gate_o, wide,
    ) = refs[part_count:]
    place = Place(info, counts)
    shard, inner = wx_o.shape
    channels = inner + 2 * LANES
    rows = shard // part_count
    for part in range(part_count):
        first = pl.multiple_of(xor(place.ctx, part) * rows, rows) if part_count > 1 else 0
        wide[pl.ds(first, rows), :] = parts[part][...].astype(F32)
    wx_o[...] = wide[:shard, :inner]
    wbc_o[...] = wide[:shard, inner:channels]
    lines = wide[:, channels:].T
    wdt_o[...] = lines[:heads, :shard]
    each = gate_o.shape[1]
    size = lines.shape[1]
    source = iota((16, size), 1)
    inside = (source // each == iota((16, size), 0)) & (source < shard)
    place_in = (iota((size, LANES), 0) % each == iota((size, LANES), 1)).astype(BF16)

    def by_head(line):
        row = jnp.where(inside, lines[line : line + 1, :], 0.0).astype(BF16)
        return dot(row, place_in)[:heads, :each]

    for tap in range(CONV):
        taps_o[:, tap, :] = by_head(TAPS + tap)
    bias_o[...] = by_head(TAPS + CONV)
    gate_o[...] = by_head(GATE)
    gain = wide[:rows, channels:]
    for part in range(1, part_count):
        gain = gain + wide[part * rows : (part + 1) * rows, channels:]
    gain = jnp.concatenate([gain, jnp.zeros((LANES - rows, LANES), F32)], axis=0).T
    source, target = iota((LANES, size), 0), iota((LANES, size), 1)
    total = jnp.zeros((8, size), F32)
    for lane in range(shard // rows):
        pick = ((target == lane * rows + source) & (source < rows)).astype(F32)
        total = total + dot_exact(jnp.broadcast_to(gain[NORM + lane : NORM + lane + 1, :], (8, LANES)), pick)
    norm_o[...] = total[0:1, :shard]
    states = state_bias_o.shape[1]
    state_taps_o[...] = lines[STATE_TAPS : STATE_TAPS + CONV, :states]
    state_bias_o[...] = lines[STATE_TAPS + CONV : STATE_TAPS + CONV + 1, :states]
    row = lines[BY_HEAD : BY_HEAD + 1, :]
    dt_bias_o[...] = row[:, :heads]
    a_log_o[...] = row[:, heads : 2 * heads]
    skip_o[...] = row[:, 2 * heads : 3 * heads]


def call(body, steps, info, operands, outputs, scratch=(), reverse=False, micros=1, mega=20):
    def at(index):
        return steps - 1 - index if reverse else index

    def spec(shape, kind):
        if kind == "rows":
            return pl.BlockSpec((BLOCK,) + tuple(shape[1:]), lambda i: (at(i), 0))
        if kind == "block":
            return pl.BlockSpec((1,) + tuple(shape[1:]), lambda i: (at(i), 0, 0))
        if kind == "lanes":
            return pl.BlockSpec((shape[0], BLOCK), lambda i: (0, at(i)))
        if kind == "tail":
            each = BLOCK // 16
            return pl.BlockSpec((16, shape[1]), lambda i: (jnp.maximum(at(i) * each - 1, 0), 0))
        if kind == "whole":
            return pl.BlockSpec(tuple(shape), lambda i: (0,) * len(shape))
        if kind == "once":
            return pl.BlockSpec(tuple(shape), lambda i: (0,) * len(shape), pipeline_mode=pl.Buffered(1))
        return kind

    return pl.pallas_call(
        body,
        grid=(steps,),
        in_specs=[pl.BlockSpec(memory_space=pltpu.SMEM)]
        + [spec(array.shape, "once" if kind == "whole" else kind) for array, kind in operands],
        out_specs=[spec(shape.shape, kind) for shape, kind in outputs],
        out_shape=[shape for shape, _ in outputs],
        scratch_shapes=list(scratch),
        compiler_params=pltpu.CompilerParams(
            dimension_semantics=("arbitrary",), vmem_limit_bytes=mega * MEGA
        ),
        cost_estimate=pl.CostEstimate(
            flops=micros * 1_100_000_000, bytes_accessed=micros * 3_500_000, transcendentals=0
        ),
    )(info, *[array for array, _ in operands])


def shifted(value, axis, steps):
    count = lax.axis_size(axis)
    first, last = max(0, -steps), min(count, count - steps)
    return lax.ppermute(value, axis, [(source, source + steps) for source in range(first, last)])


def swapped(value):
    return lax.ppermute(value, "tp", [(0, 1), (1, 0)])


def partnered(value, axis, mask):
    return lax.ppermute(value, axis, [(one, one ^ mask) for one in range(lax.axis_size(axis))])


def exchanged(value, axis):
    return [value] + [partnered(value, axis, mask) for mask in range(1, lax.axis_size(axis))]


def own_rows(value, rows):
    return lax.dynamic_slice_in_dim(value, lax.axis_index("ctx") * rows, rows, 0)


def joined_rows(values):
    return jnp.concatenate(values, axis=0)


def ctx_sum(pieces):
    total = pieces[0].astype(F32)
    for mask in range(1, len(pieces)):
        total = total + partnered(pieces[mask], "ctx", mask).astype(F32)
    return total


def dp_sum(total):
    dp_count = lax.axis_size("dp")
    rows = total.shape[0] // dp_count
    own = total[:rows].astype(F32)
    for mask in range(1, dp_count):
        block = total[mask * rows : (mask + 1) * rows].astype(BF16)
        own = own + partnered(block, "dp", mask).astype(F32)
    return own.astype(BF16)


def halved(blocks, mask):
    count, rows = blocks.shape[:2]
    sent = jnp.concatenate([blocks[block] for block in range(1, count, 2)], axis=0).astype(BF16)
    received = partnered(sent, "dp", mask).reshape(count // 2, rows, -1).astype(F32)
    return jnp.stack([blocks[block] for block in range(0, count, 2)]) + received


def doubled(value, mask):
    return jnp.concatenate([value, partnered(value, "ctx", mask)], axis=0)


def whole_sum(value):
    return lax.psum(lax.psum_scatter(value, "dp", scatter_dimension=0, tiled=True), "ctx")


def body(
    tokens, cotangent, device_fill, seq_lengths, norm_gain, w_z, w_x, w_bc, w_dt,
    conv_x, conv_x_bias, conv_bc, bias_bc, dt_bias, a_log, skip_d, gate_gain, w_out,
):
    rows, width = tokens.shape
    heads = dt_bias.shape[0]
    inner = heads * HEAD
    channels = inner + 2 * LANES
    steps = rows // BLOCK
    shard = norm_gain.shape[0]
    dp_count = lax.axis_size("dp")
    ctx_count = lax.axis_size("ctx")
    tp_index = lax.axis_index("tp")
    counts = (ctx_count, seq_lengths.shape[1])

    parts = ctx_count if shard % (16 * ctx_count) == 0 else 1
    part_rows = shard // parts

    with jax.named_scope("gather_weights"):
        vector = jnp.concatenate(
            [
                jnp.concatenate(
                    [
                        conv_x.reshape(CONV, shard),
                        conv_x_bias.reshape(1, shard),
                        norm_gain[None, :],
                        gate_gain.reshape(1, shard),
                        jnp.zeros((1, shard), BF16),
                        jnp.pad(
                            jnp.concatenate([conv_bc, bias_bc[None, :]], axis=0),
                            ((0, 3), (0, shard - bias_bc.shape[0])),
                        ),
                    ],
                    axis=0,
                ),
                jnp.pad(w_dt.T, ((0, 16 - heads), (0, 0))),
            ],
            axis=1,
        )
        input_rows = jnp.concatenate([w_x, w_bc], axis=1)
        gate_rows = jnp.concatenate([w_z, w_out.T], axis=1)
        if parts > 1:
            w1_parts = joined_rows(exchanged(own_rows(input_rows, part_rows), "dp"))
            vector = jnp.pad(vector, ((0, 0), (0, 2 * inner - 2 * shard)))
            block = jnp.concatenate([own_rows(gate_rows, part_rows), vector], axis=0)
            block, _ = lax.optimization_barrier((block, w1_parts))
            vectors = exchanged(block, "dp")
            w2_parts = exchanged(joined_rows([value[:part_rows] for value in vectors]), "ctx")
            w1_parts = exchanged(w1_parts, "ctx")
        else:
            w1_parts = [lax.all_gather(input_rows, "dp", axis=0, tiled=True)]
            w2_parts = [lax.all_gather(gate_rows, "dp", axis=0, tiled=True)]
            vectors = exchanged(vector, "dp")
    first_vector = part_rows // 16 if parts > 1 else 0
    vector_spec = pl.BlockSpec(
        (16, 2 * shard), lambda i: (first_vector, 0), pipeline_mode=pl.Buffered(1)
    )

    dtp = jnp.pad(jnp.stack([dt_bias, jnp.exp(a_log), skip_d]), ((0, 5), (0, LANES - heads)))
    shape = (2 * LANES, inner)
    spread = (iota(shape, 0) % LANES == iota(shape, 1) // HEAD).astype(BF16)
    info = jnp.concatenate(
        [
            device_fill[0],
            seq_lengths[0],
            jnp.stack([lax.axis_index("ctx"), tp_index, lax.axis_index("dp")]).astype(jnp.int32),
        ]
    )
    fill = jnp.sum(jnp.where(jnp.arange(ctx_count) == lax.axis_index("ctx"), device_fill[0], 0)) * BLOCK
    halo = shifted(lax.dynamic_slice_in_dim(tokens, fill - 16, 16, 0), "ctx", 1)

    def out(shape, dtype, kind):
        return (jax.ShapeDtypeStruct(shape, dtype), kind)

    def row_out(columns, dtype):
        return out((rows, columns), dtype, "rows")

    state_out = out((steps, inner, LANES), F32, "block")
    packet_out = out((inner + 16, LANES), BF16, "whole")

    (w1, par, normed, halo_normed, halo_v, v, xc, bc, ypart, pre_step, cum, entry, decay, packet) = call(
        functools.partial(forward_kernel, counts, heads, dp_count, parts),
        steps,
        info,
        [(value, vector_spec) for value in vectors]
        + [(value, "whole") for value in w1_parts]
        + [(tokens, "rows"), (halo, "whole"), (dtp, "whole"), (spread, "whole")],
        [
            out((width, channels + LANES), BF16, "whole"),
            out((8, channels), F32, "whole"),
            row_out(width, BF16),
            out((16, width), BF16, "whole"),
            out((8, channels), F32, "whole"),
            row_out(channels, BF16),
            row_out(inner, BF16),
            row_out(2 * LANES, BF16),
            row_out(inner, F32),
            row_out(LANES, F32),
            row_out(LANES, F32),
            state_out,
            out((steps, 8, LANES), F32, "block"),
            packet_out,
        ],
        [
            pltpu.VMEM((8 + BLOCK, channels), F32),
            pltpu.VMEM((inner, LANES), F32),
            pltpu.VMEM((8, LANES), F32),
        ],
        micros=20,
        mega=16,
    )
    packets = [(shifted(packet, "ctx", step), "whole") for step in range(1, ctx_count)]
    wz_spec = pl.BlockSpec((width, inner), lambda i: (0, 0), pipeline_mode=pl.Buffered(1))
    wo_spec = pl.BlockSpec((width, inner), lambda i: (0, 1), pipeline_mode=pl.Buffered(1))
    w2, z, dn = call(
        functools.partial(gate_matmul_kernel, counts, dp_count, parts),
        steps,
        info,
        [(value, "whole") for value in w2_parts] + [(normed, "rows"), (cotangent, "rows")],
        [out((width, 2 * inner), BF16, "whole"), row_out(inner, BF16), row_out(inner, BF16)],
        micros=7,
        mega=12,
    )
    y, hb, h, stat = call(
        functools.partial(apply_kernel, counts, len(packets)),
        steps,
        info,
        packets
        + [
            (entry, "block"),
            (decay, "block"),
            (cum, "rows"),
            (bc, "rows"),
            (ypart, "rows"),
            (z, "rows"),
            (dn, "rows"),
            (par, "whole"),
            (spread, "whole"),
        ],
        [
            row_out(inner, F32),
            out((steps, inner, LANES), BF16, "block"),
            state_out,
            out((8, rows), F32, "lanes"),
        ],
        [pltpu.VMEM((inner, LANES), F32)],
        micros=8,
        mega=12,
    )
    other_stat = swapped(stat)
    inner_all = inner * lax.axis_size("tp")
    half = width // 2
    keep, send, gwo, small_gate, dy, dz, de, exits, packet = call(
        functools.partial(gate_back_kernel, counts, inner_all),
        steps,
        info,
        [
            (stat, "lanes"),
            (other_stat, "lanes"),
            (y, "rows"),
            (z, "rows"),
            (dn, "rows"),
            (cotangent, "rows"),
            (cum, "rows"),
            (bc, "rows"),
            (xc, "rows"),
            (hb, "block"),
            (decay, "block"),
            (w2, wo_spec),
            (par, "whole"),
            (spread, "whole"),
        ],
        [
            row_out(half, BF16),
            row_out(half, BF16),
            out((width, inner), BF16, "whole"),
            out((8, inner), F32, "whole"),
            row_out(inner, BF16),
            row_out(inner, BF16),
            row_out(LANES, F32),
            state_out,
            packet_out,
        ],
        [
            pltpu.VMEM((width, inner), F32),
            pltpu.VMEM((inner, LANES), F32),
            pltpu.VMEM((8, LANES), F32),
        ],
        reverse=True,
        micros=15,
        mega=14,
    )
    packets = [(shifted(packet, "ctx", -step), "whole") for step in range(1, ctx_count)]
    dxc, dcq, dbq, row_sums, col_sums, *g2 = call(
        functools.partial(intra_back_kernel, counts, heads, dp_count),
        steps,
        info,
        [
            (dy, "rows"),
            (dz, "rows"),
            (xc, "rows"),
            (bc, "rows"),
            (cum, "rows"),
            (pre_step, "rows"),
            (hb, "block"),
            (normed, "rows"),
            (gwo, "whole"),
            (par, "whole"),
            (spread, "whole"),
        ],
        [
            row_out(inner, BF16),
            row_out(LANES, F32),
            row_out(LANES, F32),
            row_out(LANES, F32),
            row_out(LANES, F32),
        ]
        + [out((width // parts, 2 * inner), BF16, "whole")] * parts,
        [pltpu.VMEM((width, inner), F32), pltpu.VMEM((LANES, BLOCK), F32)],
        micros=18,
        mega=14,
    )
    with jax.named_scope("reduce_gate_weights"):
        total2 = ctx_sum(g2) if parts > 1 else g2[0]
    packed, back, *g1 = call(
        functools.partial(state_back_kernel, counts, heads, dp_count, len(packets), parts),
        steps,
        info,
        packets
        + [
            (exits, "block"),
            (h, "block"),
            (xc, "rows"),
            (bc, "rows"),
            (cum, "rows"),
            (pre_step, "rows"),
            (de, "rows"),
            (dxc, "rows"),
            (dcq, "rows"),
            (dbq, "rows"),
            (row_sums, "rows"),
            (col_sums, "rows"),
            (decay, "block"),
            (v, "rows"),
            (v, "tail"),
            (halo_v, "whole"),
            (halo_normed, "whole"),
            (normed, "rows"),
            (small_gate, "whole"),
            (par, "whole"),
            (dtp, "whole"),
            (spread, "whole"),
        ],
        [row_out(channels + LANES, BF16), out((16, channels), BF16, "whole")]
        + [out((width // parts, channels + LANES), BF16, "whole")] * parts,
        [
            pltpu.VMEM((inner, LANES), F32),
            pltpu.VMEM((8, LANES), F32),
            pltpu.VMEM((8 + BLOCK, channels), F32),
            pltpu.VMEM((8 + BLOCK, channels), F32),
            pltpu.VMEM((width, channels + LANES), F32),
            pltpu.VMEM((8, channels), F32),
        ],
        reverse=True,
        micros=25,
        mega=20,
    )
    with jax.named_scope("reduce_gate_weights"):
        if parts > 1:
            total2 = total2.reshape(dp_count, part_rows, 2 * inner)
            total2 = halved(total2, 1) if dp_count > 1 else total2
        else:
            total2 = whole_sum(total2)
    norm_rows = part_rows * dp_count
    if parts > 1:
        g1 = [g1[0]] + [partnered(g1[mask], "ctx", mask) for mask in range(1, parts)]
        packed, g1[1], total2 = lax.optimization_barrier((packed, g1[1], total2))
        mask = 2
        while mask < dp_count:
            total2 = halved(total2, mask)
            mask *= 2
        total2 = total2[0].astype(BF16)
    partial, halo_grad, norm_part = call(
        functools.partial(input_back_kernel, counts, dp_count, parts),
        steps,
        info,
        [
            (packed, "rows"),
            (back, "whole"),
            (dz, "rows"),
            (w2, wz_spec),
            (tokens, "rows"),
            (halo, "whole"),
            (w1, "whole"),
            (par, "whole"),
        ],
        [
            row_out(width, BF16),
            out((8, width), F32, "whole"),
            out((norm_rows, LANES), F32, "whole"),
        ],
        [pltpu.VMEM((8, width), F32)],
        micros=5,
        mega=12,
    )
    other = swapped(partial)
    with jax.named_scope("reduce_input_weights"):
        norm_part = jnp.pad(norm_part, ((0, 0), (channels, 0)))
        if parts > 1:
            total1 = sum(piece.astype(F32) for piece in g1) + norm_part
            total1, total2 = lax.optimization_barrier((total1, total2))
            total1 = dp_sum(total1)
            total2 = doubled(total2, 1)
            total1, total2 = lax.optimization_barrier((total1, total2))
            mask = 2
            while mask < ctx_count:
                total2 = doubled(total2, mask)
                mask *= 2
        else:
            total1 = whole_sum((g1[0].astype(F32) + norm_part).astype(BF16))
        across = swapped(total1[:, inner:])
        across, halo_grad, send = lax.optimization_barrier((across, halo_grad, send))
        lane = np.arange(3 * LANES) - 2 * LANES
        both = (lane < 0) | ((lane >= STATE_TAPS) & (lane < BY_HEAD))
        both = both | ((lane >= NORM) & (lane < NORM + shard // part_rows))
        summed = total1[:, inner:] + jnp.where(both[None, :], across, 0)
        total1 = jnp.concatenate([total1[:, :inner], summed], axis=1)
    size = ctx_count * 2
    back = [(s, s - 2) for s in range(2, size)]
    cross = [(s, (s - 2) ^ 1) for s in range(2, size)]
    halo_a = lax.ppermute(halo_grad, ("ctx", "tp"), back)
    halo_b = lax.ppermute(halo_grad, ("ctx", "tp"), cross)
    received = swapped(send)
    grad_tokens, layer_out = call(
        functools.partial(finish_kernel, counts),
        steps,
        info,
        [
            (partial, "rows"),
            (other, "rows"),
            (halo_a, "whole"),
            (halo_b, "whole"),
            (keep, "rows"),
            (received, "rows"),
            (tokens, "rows"),
            (cotangent, "rows"),
            (par, "whole"),
        ],
        [row_out(width, F32), row_out(half, F32)],
        micros=5,
        mega=10,
    )
    with jax.named_scope("last_hop"):
        if parts > 1:
            total1 = exchanged(total1, "ctx")
            total1[-1], grad_tokens = lax.optimization_barrier((total1[-1], grad_tokens))
        else:
            total1 = [total1]
    each = HEAD // dp_count
    part_bc = bias_bc.shape[0]
    tall = -(-shard // LANES) * LANES

    def final(*sizes):
        return out(sizes, F32, "whole")

    grad_wz, grad_wo = call(
        functools.partial(unpack_gate_kernel, counts, parts),
        1,
        info,
        [(total2, "whole")],
        [final(shard, inner), final(shard, inner)],
        micros=2,
        mega=8,
    )
    (
        grad_wx, grad_wbc, grad_wdt, grad_norm, grad_taps, grad_bias, grad_state_taps, grad_state_bias,
        grad_dt_bias, grad_a_log, grad_skip, grad_gate,
    ) = call(
        functools.partial(unpack_input_kernel, counts, heads, parts),
        1,
        info,
        [(value, "whole") for value in total1],
        [
            final(shard, inner),
            final(shard, 2 * LANES),
            final(heads, shard),
            final(1, shard),
            final(heads, CONV, each),
            final(heads, each),
            final(CONV, part_bc),
            final(1, part_bc),
            final(1, heads),
            final(1, heads),
            final(1, heads),
            final(heads, each),
        ],
        [pltpu.VMEM((tall, channels + LANES), F32)],
        micros=2,
        mega=8,
    )
    return (
        layer_out,
        grad_tokens,
        grad_norm[0],
        grad_wz,
        grad_wx,
        grad_wbc,
        grad_wdt.T,
        grad_taps.transpose(1, 0, 2),
        grad_bias,
        grad_state_taps,
        grad_state_bias[0],
        grad_dt_bias[0],
        grad_a_log[0],
        grad_skip[0],
        grad_gate,
        grad_wo.T,
    )


def solution(mesh):
    shards = P(("dp", "ctx"), None)
    return jax.shard_map(
        body,
        mesh=mesh,
        in_specs=(
            shards,
            shards,
            P("dp", None),
            P("dp", None),
            P("dp"),
            P("dp", "tp"),
            P("dp", "tp"),
            P("dp", None),
            P("dp", "tp"),
            P(None, "tp", "dp"),
            P("tp", "dp"),
            P(None, "dp"),
            P("dp"),
            P("tp"),
            P("tp"),
            P("tp"),
            P("tp", "dp"),
            P("tp", "dp"),
        ),
        out_specs=(
            P(("dp", "ctx"), "tp"),
            shards,
            P("dp"),
            P("dp", "tp"),
            P("dp", "tp"),
            P("dp", None),
            P("dp", "tp"),
            P(None, "tp", "dp"),
            P("tp", "dp"),
            P(None, "dp"),
            P("dp"),
            P("tp"),
            P("tp"),
            P("tp"),
            P("tp", "dp"),
            P("tp", "dp"),
        ),
        check_vma=False,
    )
```
